32 devices in a mesh: pole: 2 (over y), wave: 16 (over z, x, core).
Axes of the slice: x: 2, y: 2, z: 4, core: 2. Of those that a mesh axis runs over, the one named last changes fastest.
Arguments:
- tendency: bfloat16 [6, 2560, 32, 128], P('pole', 'wave'), may hold values from -6 to 6
- spectral_state: bfloat16 [6, 32, 128, 1280], P('pole', 'wave'), may hold values from -6 to 6
- legendre: bfloat16 [32, 1280, 2560], P('wave'), may hold values from -0.15625 to 0.15625
- gauss_weights: float32 [2560], P('wave'), may hold values from 0.35 to 1.05
- block_inverses: bfloat16 [64, 18, 32, 1280], P('pole', None, 'wave'), may hold values from -0.21875 to 0.21875
- pole_coeffs: float32 [64, 2], P('pole'), may hold values from -4 to 4
- wavenumbers: int32 [32], P('wave'), may hold values from 0 to 1279, as said below
Outputs:
- grid_state: bfloat16 [6, 2560, 32, 128], P('pole', 'wave')
The draws below stay inside these ranges and needn't reach their ends.
Inputs may be any that keep to these rules, and one draw needn't show every extreme that they name: `wavenumbers`: entries 2 i and 2 i + 1 hold w and 1279 - w for some w below 640; all entries differ, and 0 is among them.
All inputs are finite; a program needn't handle non-finite values.
Results may differ from the reference program's by a relative error of at most 0.0062.
Values may be sent and summed in bfloat16 or wider, within the bound.
No kernel may reach another device: no remote copies, remote signals or barrier semaphores. Data moves between devices by JAX's collectives and lax.ppermute only.
A program may use at most 128 MiB of HBM per device.

```python
import jax
import jax.numpy as jnp
from jax import lax

NSPEC = 1280
NLAT = 2560
PAIRS = 64
MEMBERS = 128
M = 32


def draw_wavenumbers(key, part):
    halfway = NSPEC // 2
    device_count = M // 2
    shuffled = jax.random.permutation(jax.random.fold_in(key, 11), halfway - 1) + 1
    chosen = jnp.concatenate([jnp.zeros((1,), jnp.int32), shuffled[:device_count - 1].astype(jnp.int32)])
    chosen = jax.random.permutation(jax.random.fold_in(key, 12), chosen)
    paired = jnp.stack([chosen, NSPEC - 1 - chosen], axis=1)
    return paired.reshape(-1).astype(jnp.int32)


def shard_levels(key, dims, pieces, low, high):
    def one(position, blocks):
        heights = jax.random.uniform(jax.random.fold_in(jax.random.fold_in(key, 6), position), (blocks,), jnp.float32, low / len(pieces), high / len(pieces))
        return jnp.repeat(jnp.exp(heights), dims[position] // blocks).reshape((-1,) + (1,) * (len(dims) - position - 1))

    loudness = one(*pieces[0])
    for cut in pieces[1:]:
        loudness = loudness * one(*cut)
    return loudness


def scatter_about(stream_key, dims, spread, most, cuts=(), kind=jnp.bfloat16):
    entries = jax.random.normal(stream_key, dims, jnp.float32) * spread
    if len(cuts) > 0:
        entries = shard_levels(stream_key, dims, cuts, -0.22, 0.18) * entries
    return jnp.clip(entries, min=-most, max=most).astype(kind)


def setup_inputs(seed: int = 0) -> dict:
    keys = jax.random.split(jax.random.key(seed), 8)
    return {
        "tendency": scatter_about(keys[0], (6, NLAT, M, MEMBERS), 1.0, 6.0, ((0, 2), (1, 16))),
        "spectral_state": scatter_about(keys[1], (6, M, MEMBERS, NSPEC), 1.0, 6.0, ((0, 2), (1, 16))),
        "legendre": scatter_about(keys[2], (M, NSPEC, NLAT), NSPEC ** -0.5, 0.15625, ((0, 16),)),
        "gauss_weights": jnp.clip(0.35 + 0.699999958 * jax.random.uniform(keys[3], (NLAT,), jnp.float32) ** shard_levels(keys[3], (NLAT,), ((0, 16),), -0.2, 0.2), 0.35, 1.05),
        "block_inverses": scatter_about(keys[4], (PAIRS, 18, M, NSPEC), (PAIRS * 12) ** -0.5, 0.21875, ((0, 2), (2, 16))),
        "pole_coeffs": scatter_about(keys[5], (PAIRS, 2), 1.0, 4.0, ((0, 2),), jnp.float32),
        "wavenumbers": draw_wavenumbers(jax.random.fold_in(keys[7], 71), 0),
    }


def mix_rows(real_matrix, imag_matrix, leading, trailing, orientation):
    summed = jnp.zeros(leading.shape, jnp.float32)
    for column in range(3):
        summed = summed + real_matrix[:, column, :, None, :] * leading[column][None]
        summed = summed + orientation * imag_matrix[:, column, :, None, :] * trailing[column][None]
    return summed


def reference(tendency, spectral_state, legendre, gauss_weights, block_inverses, pole_coeffs, wavenumbers):
    weighted = (tendency.astype(jnp.float32) * gauss_weights[None, :, None, None]).astype(jnp.bfloat16)

    def analyse(slot_index):
        grid_slot = lax.dynamic_index_in_dim(weighted, slot_index, 2, keepdims=False).astype(jnp.float32)
        legendre_slot = lax.dynamic_index_in_dim(legendre, slot_index, 0, keepdims=False).astype(jnp.float32)
        return jnp.einsum('rje,nj->ren', grid_slot, legendre_slot)

    spectral_tend = jnp.transpose(lax.map(analyse, jnp.arange(M, dtype=jnp.int32)), (1, 0, 2, 3))
    degree = jnp.arange(NSPEC, dtype=jnp.int32)
    live_mask = (degree[None, :] >= wavenumbers[:, None]).astype(jnp.float32)
    forced = ((spectral_state.astype(jnp.float32) + spectral_tend) * live_mask[None, :, None, :]).astype(jnp.bfloat16)

    def add_pair(summed, pair_data):
        inverse, coefficient = pair_data
        inverse = inverse.astype(jnp.float32).reshape(2, 3, 3, M, NSPEC)
        real_part = coefficient[0] * inverse[0] - coefficient[1] * inverse[1]
        imag_part = coefficient[0] * inverse[1] + coefficient[1] * inverse[0]
        return (summed[0] + real_part, summed[1] + imag_part), None

    zeros_matrix = jnp.zeros((3, 3, M, NSPEC), jnp.float32)
    matrices, unused = lax.scan(add_pair, (zeros_matrix, zeros_matrix), (block_inverses, pole_coeffs))
    real_matrix, imag_matrix = matrices
    forced_wide = forced.astype(jnp.float32)
    real_rows = mix_rows(real_matrix, imag_matrix, forced_wide[:3], forced_wide[3:], -1.0)
    imag_rows = mix_rows(real_matrix, imag_matrix, forced_wide[3:], forced_wide[:3], 1.0)
    advanced = jnp.concatenate([real_rows, imag_rows], axis=0).astype(jnp.bfloat16)

    def synthesise(slot_index):
        spectra = lax.dynamic_index_in_dim(advanced, slot_index, 1, keepdims=False).astype(jnp.float32)
        legendre_slot = lax.dynamic_index_in_dim(legendre, slot_index, 0, keepdims=False).astype(jnp.float32)
        return jnp.einsum('ren,nj->rje', spectra, legendre_slot)

    synthesized = lax.map(synthesise, jnp.arange(M, dtype=jnp.int32))
    return jnp.transpose(synthesized, (1, 2, 0, 3)).astype(jnp.bfloat16)
```

```python
import jax
import jax.numpy as jnp
from jax import lax
from jax.sharding import PartitionSpec as P


def mix_rows(real_matrix, imag_matrix, leading, trailing, orientation):
    summed = 0.0
    for column in range(3):
        summed = summed + real_matrix[:, column, None, :] * leading[column][None]
        summed = summed + (orientation * imag_matrix[:, column, None, :]) * trailing[column][None]
    return summed


def per_device(
    tendency, spectral_state, legendre, gauss_weights, block_inverses, pole_coeffs, wavenumbers
):
    rows, lats, slots, members = tendency.shape
    local_slots, nspec = legendre.shape[:2]
    owners = slots // local_slots
    pole_index = lax.axis_index("pole")
    orientation = (2 * pole_index - 1).astype(jnp.float32)
    split = tendency.reshape(rows, lats, owners, local_slots, members)

    def send(slot):
        weighted = (split[:, :, :, slot, :].astype(jnp.float32) * gauss_weights[None, :, None, None]).astype(
            jnp.bfloat16
        )
        return lax.all_to_all(weighted, "wave", split_axis=2, concat_axis=1, tiled=True)

    received = [send(slot) for slot in range(local_slots)]

    local_pairs = block_inverses.shape[0]
    flat_inverse = block_inverses.reshape(local_pairs, -1).astype(jnp.float32)
    weighted_sums = jnp.dot(pole_coeffs.T, flat_inverse, precision=lax.Precision.HIGHEST)
    weighted_sums = weighted_sums.reshape(2, 2, 3, 3, local_slots, nspec)
    real_matrix = weighted_sums[0, 0] - weighted_sums[1, 1]
    imag_matrix = weighted_sums[0, 1] + weighted_sums[1, 0]
    real_matrix, imag_matrix = lax.psum((real_matrix, imag_matrix), "pole")

    degree = jnp.arange(nspec, dtype=jnp.int32)
    outputs = []
    for slot in range(local_slots):
        grid = received[slot].reshape(rows, -1, members)
        spectral_tend = jnp.einsum(
            "rje,nj->ren", grid, legendre[slot], preferred_element_type=jnp.float32
        )
        live = (degree >= wavenumbers[slot]).astype(jnp.float32)
        forced = ((spectral_state[:, slot].astype(jnp.float32) + spectral_tend) * live).astype(jnp.bfloat16)
        other = lax.ppermute(forced, "pole", [(0, 1), (1, 0)])
        advanced = mix_rows(
            real_matrix[:, :, slot],
            imag_matrix[:, :, slot],
            forced.astype(jnp.float32),
            other.astype(jnp.float32),
            orientation,
        ).astype(jnp.bfloat16)
        synthesized = jnp.einsum(
            "ren,nj->rje", advanced, legendre[slot], preferred_element_type=jnp.float32
        ).astype(jnp.bfloat16)
        outputs.append(
            lax.all_to_all(
                synthesized.reshape(rows, -1, 1, members), "wave", split_axis=1, concat_axis=2, tiled=True
            )
        )
    return jnp.stack(outputs, axis=3).reshape(tendency.shape)


def solution(mesh):
    in_specs = (
        P("pole", "wave", None, None),
        P("pole", "wave", None, None),
        P("wave", None, None),
        P("wave"),
        P("pole", None, "wave", None),
        P("pole", None),
        P("wave"),
    )
    out_specs = P("pole", "wave", None, None)
    return jax.shard_map(
        per_device, mesh=mesh, in_specs=in_specs, out_specs=out_specs, check_vma=False
    )
```

```python
import jax
import jax.numpy as jnp
from jax import lax
from jax.sharding import PartitionSpec as P


def mix_rows(real_matrix, imag_matrix, leading, trailing, orientation):
    summed = 0.0
    for column in range(3):
        summed = summed + real_matrix[:, column, None, :] * leading[column][None]
        summed = summed + (orientation * imag_matrix[:, column, None, :]) * trailing[column][None]
    return summed


def exchange_blocks(blocks, me, owners):
    pieces = [lax.dynamic_index_in_dim(blocks, me, 0, keepdims=False)]
    order = sorted(range(1, owners), key=lambda k: -k)
    got = {0: pieces[0]}
    for k in order:
        sent = lax.dynamic_index_in_dim(blocks, me ^ k, 0, keepdims=False)
        got[k] = lax.ppermute(sent, "wave", [(d, d ^ k) for d in range(owners)])
    stacked = jnp.stack([got[k] for k in range(owners)])
    return jnp.take(stacked, me ^ jnp.arange(owners), axis=0, unique_indices=True, mode="clip")


def per_device(
    tendency, spectral_state, legendre, gauss_weights, block_inverses, pole_coeffs, wavenumbers
):
    rows, lats, slots, members = tendency.shape
    local_slots, nspec, nlat = legendre.shape
    owners = slots // local_slots
    pole_index = lax.axis_index("pole")
    me = lax.axis_index("wave")
    orientation = (2 * pole_index - 1).astype(jnp.float32)
    weighted = (tendency.astype(jnp.float32) * gauss_weights[None, :, None, None]).astype(jnp.bfloat16)
    weighted = jnp.transpose(weighted, (2, 0, 1, 3)).reshape(owners, local_slots, rows, lats, members)

    def swap(blocks, slot):
        if slot == 0:
            return lax.all_to_all(blocks, "wave", split_axis=0, concat_axis=0, tiled=True)
        return exchange_blocks(blocks, me, owners)

    received = [swap(weighted[:, slot], slot) for slot in range(local_slots)]

    local_pairs = block_inverses.shape[0]
    flat_inverse = block_inverses.reshape(local_pairs, -1).astype(jnp.float32)
    weighted_sums = jnp.dot(pole_coeffs.T, flat_inverse, precision=lax.Precision.HIGHEST)
    weighted_sums = weighted_sums.reshape(2, 2, 3, 3, local_slots, nspec)
    real_matrix = weighted_sums[0, 0] - weighted_sums[1, 1]
    imag_matrix = weighted_sums[0, 1] + weighted_sums[1, 0]
    real_matrix, imag_matrix = lax.psum((real_matrix, imag_matrix), "pole")

    outputs = []
    for slot in range(local_slots):
        low = nspec // 2 if slot % 2 else 0
        degree = jnp.arange(low, nspec, dtype=jnp.int32)
        table = legendre[slot, low:]
        grid = jnp.transpose(received[slot], (1, 0, 2, 3)).reshape(rows, nlat, members)
        spectral_tend = jnp.einsum("rje,nj->ren", grid, table, preferred_element_type=jnp.float32)
        live = (degree >= wavenumbers[slot]).astype(jnp.float32)
        forced = ((spectral_state[:, slot, :, low:].astype(jnp.float32) + spectral_tend) * live).astype(jnp.bfloat16)
        other = lax.ppermute(forced, "pole", [(0, 1), (1, 0)])
        advanced = mix_rows(
            real_matrix[:, :, slot, low:],
            imag_matrix[:, :, slot, low:],
            forced.astype(jnp.float32),
            other.astype(jnp.float32),
            orientation,
        ).astype(jnp.bfloat16)
        synthesized = jnp.einsum("ren,nj->rje", advanced, table, preferred_element_type=jnp.float32)
        blocks = synthesized.astype(jnp.bfloat16).reshape(rows, owners, lats, members)
        outputs.append(swap(jnp.transpose(blocks, (1, 0, 2, 3)), slot))
    out = jnp.stack(outputs, axis=1).reshape(slots, rows, lats, members)
    return jnp.transpose(out, (1, 2, 0, 3))


def solution(mesh):
    in_specs = (
        P("pole", "wave", None, None),
        P("pole", "wave", None, None),
        P("wave", None, None),
        P("wave"),
        P("pole", None, "wave", None),
        P("pole", None),
        P("wave"),
    )
    out_specs = P("pole", "wave", None, None)
    return jax.shard_map(
        per_device, mesh=mesh, in_specs=in_specs, out_specs=out_specs, check_vma=False
    )
```

```python
import functools

import jax
import jax.numpy as jnp
from jax import lax
from jax.experimental import pallas as pl
from jax.experimental.pallas import tpu as pltpu
from jax.sharding import PartitionSpec as P

BF16 = jnp.bfloat16
F32 = jnp.float32
VMEM_LIMIT = 56 * 1024 * 1024
CORES = 2
ROWS = 16


def params(semantics=None):
    return pltpu.CompilerParams(vmem_limit_bytes=VMEM_LIMIT, dimension_semantics=semantics)


def weigh_kernel(slot, local_slots, me_ref, gauss_ref, tendency_ref, *rest):
    outs, wide = rest[:-1], rest[-1]
    _, lats, slots, members = tendency_ref.shape
    wide[...] = tendency_ref[0].astype(F32).reshape(lats * slots, members)
    chip = me_ref[0] // CORES
    for k, out in enumerate(outs):
        for core in range(CORES):
            row = ((chip ^ k) * CORES + core) * local_slots + slot
            picked = wide[pl.ds(row, lats, stride=slots), :]
            out[core, 0] = (picked * gauss_ref[...]).astype(BF16)


def weigh(tendency, gauss, me, slot, local_slots):
    rows, lats, slots, members = tendency.shape
    chips = slots // local_slots // CORES
    piece = pl.BlockSpec((CORES, 1, lats, members), lambda r, m: (0, r, 0, 0))
    return pl.pallas_call(
        functools.partial(weigh_kernel, slot, local_slots),
        out_shape=[jax.ShapeDtypeStruct((CORES, rows, lats, members), BF16)] * chips,
        grid_spec=pltpu.PrefetchScalarGridSpec(
            num_scalar_prefetch=1,
            grid=(rows,),
            in_specs=[
                pl.BlockSpec((lats, members), lambda r, m: (0, 0)),
                pl.BlockSpec((1, lats, slots, members), lambda r, m: (r, 0, 0, 0)),
            ],
            out_specs=[piece] * chips,
            scratch_shapes=[pltpu.VMEM((lats * slots, members), F32)],
        ),
        compiler_params=params(),
        cost_estimate=pl.CostEstimate(flops=tendency.size, bytes_accessed=3 * tendency.size, transcendentals=0),
        name="weigh",
    )(me, gauss, tendency)


def run_copies(copies):
    for copy in copies:
        copy.start()
    for copy in copies:
        copy.wait()


def pick_kernel(me_ref, *rest):
    ins, out, sems = rest[:-2], rest[-2], rest[-1]
    mate = (CORES - 1) - me_ref[0] % CORES
    run_copies([pltpu.make_async_copy(ref.at[mate], out.at[k], sems.at[k]) for k, ref in enumerate(ins)])


def pick(messages, me):
    anywhere = pl.BlockSpec(memory_space=pl.ANY)
    shape = (len(messages),) + messages[0].shape[1:]
    size = 4 * len(messages) * messages[0].size // CORES
    return pl.pallas_call(
        pick_kernel,
        out_shape=jax.ShapeDtypeStruct(shape, BF16),
        in_specs=[pl.BlockSpec(memory_space=pltpu.SMEM)] + [anywhere] * len(messages),
        out_specs=anywhere,
        scratch_shapes=[pltpu.SemaphoreType.DMA((len(messages),))],
        compiler_params=params(),
        cost_estimate=pl.CostEstimate(flops=0, bytes_accessed=size, transcendentals=0),
        name="pick",
    )(me, *messages)


def pair_kernel(own, mate, *rest):
    outs, sems = rest[:-1], rest[-1]
    copies = []
    for k, out in enumerate(outs):
        copies.append(pltpu.make_async_copy(own.at[k], out.at[0], sems.at[0, k]))
        copies.append(pltpu.make_async_copy(mate.at[k], out.at[1], sems.at[1, k]))
    run_copies(copies)


def pair(own, mate):
    anywhere = pl.BlockSpec(memory_space=pl.ANY)
    chips = own.shape[0]
    return pl.pallas_call(
        pair_kernel,
        out_shape=[jax.ShapeDtypeStruct((CORES,) + own.shape[1:], BF16)] * chips,
        in_specs=[anywhere] * 2,
        out_specs=[anywhere] * chips,
        scratch_shapes=[pltpu.SemaphoreType.DMA((CORES, chips))],
        compiler_params=params(),
        cost_estimate=pl.CostEstimate(flops=0, bytes_accessed=8 * own.size, transcendentals=0),
        name="pair",
    )(own, mate)


def ordered(here, chips):
    owner = jnp.arange(chips * CORES, dtype=jnp.int32)
    return ((owner // CORES) ^ (here // CORES)) * CORES + (owner % CORES ^ here % CORES)


def analyse_kernel(slot, low, chips, lats, me_ref, wave_ref, table_ref, state_ref, *rest):
    messages, mate, out, grid, sems = rest[:-4], rest[-4], rest[-3], rest[-2], rest[-1]
    rows = out.shape[0]
    members = out.shape[1]
    width = table_ref.shape[1]
    step = pl.program_id(0)

    @pl.when(step == 0)
    def _():
        chip, core = me_ref[0] // CORES, me_ref[0] % CORES
        copies = []
        if not messages:
            copies.append(pltpu.make_async_copy(mate, grid, sems.at[0, 0, 0]))
        for k in range(len(messages)):
            for source in range(CORES):
                origin = (chip ^ k) * CORES + (core if source == 0 else CORES - 1 - core)
                start = pl.multiple_of(origin * lats, lats)
                block = messages[k].at[core] if source == 0 else mate.at[k]
                for r in range(rows):
                    target = grid.at[pl.ds(start, lats), pl.ds(r * members, members)]
                    copies.append(pltpu.make_async_copy(block.at[r], target, sems.at[source, k, r]))
        run_copies(copies)

    sums = jnp.dot(table_ref[0], grid[...], preferred_element_type=F32)
    degree = lax.broadcasted_iota(jnp.int32, (members, width), 1) + (low + step * width)
    live = degree >= wave_ref[slot]
    for r in range(rows):
        tend = sums[:, r * members : (r + 1) * members].T
        total = state_ref[r, 0].astype(F32) + tend
        out[r] = jnp.where(live, total, 0.0).astype(BF16)


def analyse(messages, mate, table, state, wave, me, slot, low, width):
    chips = len(messages)
    _, rows, lats, members = messages[0].shape
    nspec, nlat = table.shape[1:]
    first = low // width
    if lats % ROWS:
        own = jnp.stack([lax.dynamic_index_in_dim(m, me[0] % CORES, 0, keepdims=False) for m in messages])
        blocks = jnp.stack([own, mate], axis=1).reshape(chips * CORES, rows, lats, members)
        blocks = jnp.take(blocks, ordered(me[0], chips), axis=0)
        messages, mate = [], jnp.transpose(blocks, (0, 2, 1, 3)).reshape(nlat, rows * members)
    anywhere = pl.BlockSpec(memory_space=pl.ANY)
    smem = pl.BlockSpec(memory_space=pltpu.SMEM)
    return pl.pallas_call(
        functools.partial(analyse_kernel, slot, low, chips, lats),
        out_shape=jax.ShapeDtypeStruct((rows, members, nspec - low), BF16),
        grid=((nspec - low) // width,),
        in_specs=[
            smem,
            smem,
            pl.BlockSpec((1, width, nlat), lambda i: (slot, first + i, 0)),
            pl.BlockSpec((rows, 1, members, width), lambda i: (0, slot, 0, first + i)),
        ]
        + [anywhere] * (len(messages) + 1),
        out_specs=pl.BlockSpec((rows, members, width), lambda i: (0, 0, i)),
        scratch_shapes=[
            pltpu.VMEM((nlat, rows * members), BF16),
            pltpu.SemaphoreType.DMA((CORES, chips, rows)),
        ],
        compiler_params=params(),
        cost_estimate=pl.CostEstimate(
            flops=2 * (nspec - low) * nlat * rows * members, bytes_accessed=2 * nspec * nlat, transcendentals=0
        ),
        name="analyse",
    )(me, wave, table, state, *messages, mate)


def synthesise_kernel(chips, lats, me_ref, matrix_ref, own_ref, other_ref, table_ref, *rest):
    outs, (mixed, grid, sems) = rest[:-3], rest[-3:]
    rows, members, _ = own_ref.shape
    width = table_ref.shape[2]
    step = pl.program_id(0)

    @pl.when(step == 0)
    def _():
        for f in range(rows):
            total = 0.0
            for g in range(rows):
                total = total + matrix_ref[f * rows + g : f * rows + g + 1, :] * own_ref[g].astype(F32)
                line = rows * rows + f * rows + g
                total = total + matrix_ref[line : line + 1, :] * other_ref[g].astype(F32)
            mixed[f * members : (f + 1) * members, :] = total.astype(BF16)

    sums = jnp.dot(mixed[...], table_ref[0], preferred_element_type=F32)
    start = pl.multiple_of(step * width, width)
    for r in range(rows):
        grid[r, pl.ds(start, width), :] = sums[r * members : (r + 1) * members, :].T.astype(BF16)

    @pl.when(step == pl.num_programs(0) - 1)
    def _():
        chip, core = me_ref[0] // CORES, me_ref[0] % CORES
        copies = []
        if len(outs) == 1:
            copies.append(pltpu.make_async_copy(grid, outs[0], sems.at[0, 0, 0]))
        for k in range(chips if len(outs) > 1 else 0):
            for target, out in enumerate(outs):
                owner = (chip ^ k) * CORES + (core if target == 0 else CORES - 1 - core)
                here = pl.ds(pl.multiple_of(owner * lats, lats), lats)
                for r in range(rows):
                    copies.append(pltpu.make_async_copy(grid.at[r, here, :], out.at[k, r], sems.at[target, k, r]))
        run_copies(copies)


def synthesise(matrix, own, other, table, me, slot, low, chips, width):
    rows, members, count = own.shape
    nlat = table.shape[2]
    lats = nlat // chips // CORES
    anywhere = pl.BlockSpec(memory_space=pl.ANY)
    whole = pl.BlockSpec((rows, members, count), lambda j: (0, 0, 0))
    shapes = [jax.ShapeDtypeStruct((chips, rows, lats, members), BF16)] * CORES
    if lats % ROWS:
        shapes = [jax.ShapeDtypeStruct((rows, nlat, members), BF16)]
    outs = pl.pallas_call(
        functools.partial(synthesise_kernel, chips, lats),
        out_shape=shapes,
        grid=(nlat // width,),
        in_specs=[
            pl.BlockSpec(memory_space=pltpu.SMEM),
            pl.BlockSpec(matrix.shape, lambda j: (0, 0)),
            whole,
            whole,
            pl.BlockSpec((1, count, width), lambda j: (slot, low // count, j)),
        ],
        out_specs=[anywhere] * len(shapes),
        scratch_shapes=[
            pltpu.VMEM((rows * members, count), BF16),
            pltpu.VMEM((rows, nlat, members), BF16),
            pltpu.SemaphoreType.DMA((CORES, chips, rows)),
        ],
        compiler_params=params(),
        cost_estimate=pl.CostEstimate(
            flops=2 * count * nlat * rows * members, bytes_accessed=2 * count * nlat, transcendentals=0
        ),
        name="synthesise",
    )(me, matrix, own, other, table)
    if lats % ROWS:
        blocks = jnp.transpose(outs[0].reshape(rows, chips * CORES, lats, members), (1, 0, 2, 3))
        blocks = jnp.take(blocks, ordered(me[0], chips), axis=0).reshape(chips, CORES, rows, lats, members)
        outs = [blocks[:, 0], blocks[:, 1]]
    return outs


def assemble_kernel(chips, local_slots, me_ref, *rest):
    ins, out, wide = rest[:-2], rest[-2], rest[-1]
    _, lats, slots, members = out.shape
    chip, core = me_ref[0] // CORES, me_ref[0] % CORES
    for slot in range(local_slots):
        for k in range(chips):
            for source in range(CORES):
                origin = (chip ^ k) * CORES + (core if source == 0 else CORES - 1 - core)
                block = ins[slot * chips + k][source, 0]
                wide[pl.ds(origin * local_slots + slot, lats, stride=slots), :] = block.astype(F32)
    out[0] = wide[...].astype(BF16).reshape(lats, slots, members)


def assemble(pieces, me):
    local_slots, chips = len(pieces), len(pieces[0])
    _, rows, lats, members = pieces[0][0].shape
    slots = local_slots * chips * CORES
    piece = pl.BlockSpec((CORES, 1, lats, members), lambda r, m: (0, r, 0, 0))
    return pl.pallas_call(
        functools.partial(assemble_kernel, chips, local_slots),
        out_shape=jax.ShapeDtypeStruct((rows, lats, slots, members), BF16),
        grid_spec=pltpu.PrefetchScalarGridSpec(
            num_scalar_prefetch=1,
            grid=(rows,),
            in_specs=[piece] * (chips * local_slots),
            out_specs=pl.BlockSpec((1, lats, slots, members), lambda r, m: (r, 0, 0, 0)),
            scratch_shapes=[pltpu.VMEM((lats * slots, members), F32)],
        ),
        compiler_params=params(),
        name="assemble",
    )(me, *[block for slot in pieces for block in slot])


def between_chips(messages, chips):
    half = chips // 2
    order = []
    for near, far in zip([0] + list(range(1, half)), range(half, chips)):
        order += [far, near]
    got = {0: messages[0]}
    for k in [k for k in order if k > 0]:
        moves = [(d, d ^ (k * CORES)) for d in range(chips * CORES)]
        got[k] = lax.ppermute(messages[k], "wave", moves)
    return [got[k] for k in range(chips)]


def between_cores(blocks, owners):
    return lax.ppermute(blocks, "wave", [(d, d ^ 1) for d in range(owners)])


def per_device(
    tendency, spectral_state, legendre, gauss_weights, block_inverses, pole_coeffs, wavenumbers
):
    rows, lats, slots, members = tendency.shape
    local_slots, nspec, nlat = legendre.shape
    owners = slots // local_slots
    chips = owners // CORES
    me = lax.axis_index("wave").astype(jnp.int32).reshape(1)
    pole_index = lax.axis_index("pole")
    orientation = (2 * pole_index - 1).astype(F32)
    gauss = jnp.broadcast_to(gauss_weights[:, None], (lats, members))
    received = [
        between_chips(weigh(tendency, gauss, me, slot, local_slots), chips) for slot in range(local_slots)
    ]

    local_pairs = block_inverses.shape[0]
    flat_inverse = block_inverses.reshape(local_pairs, -1).astype(F32)
    weighted_sums = jnp.dot(pole_coeffs.T, flat_inverse, precision=lax.Precision.HIGHEST)
    weighted_sums = weighted_sums.reshape(2, 2, rows, rows, local_slots, nspec)
    real_matrix = weighted_sums[0, 0] - weighted_sums[1, 1]
    imag_matrix = weighted_sums[0, 1] + weighted_sums[1, 0]
    real_matrix, imag_matrix = lax.psum((real_matrix, imag_matrix), "pole")
    matrices = jnp.concatenate([real_matrix, orientation * imag_matrix]).reshape(2 * rows * rows, local_slots, nspec)

    sent = []
    for slot in range(local_slots):
        low = nspec // 2 if slot % 2 else 0
        mate = between_cores(pick(received[slot], me), owners)
        forced = analyse(received[slot], mate, legendre, spectral_state, wavenumbers, me, slot, low, nspec // 2)
        other = lax.ppermute(forced, "pole", [(0, 1), (1, 0)])
        own, for_mate = synthesise(matrices[:, slot, low:], forced, other, legendre, me, slot, low, chips, nlat // 5)
        sent.append(between_chips(pair(own, between_cores(for_mate, owners)), chips))
    return assemble(sent, me)


def solution(mesh):
    in_specs = (
        P("pole", "wave", None, None),
        P("pole", "wave", None, None),
        P("wave", None, None),
        P("wave"),
        P("pole", None, "wave", None),
        P("pole", None),
        P("wave"),
    )
    out_specs = P("pole", "wave", None, None)
    return jax.shard_map(
        per_device, mesh=mesh, in_specs=in_specs, out_specs=out_specs, check_vma=False
    )
```

```python
import functools
import math

import jax
import jax.numpy as jnp
from jax import lax
from jax.experimental import pallas as pl
from jax.experimental.pallas import tpu as pltpu
from jax.sharding import PartitionSpec as P

BF16 = jnp.bfloat16
F32 = jnp.float32
CORES = 2
PERMUTED = (1,)
ANYWHERE = pl.BlockSpec(memory_space=pl.ANY)
IN_SMEM = pl.BlockSpec(memory_space=pltpu.SMEM)
TOKEN = jax.ShapeDtypeStruct((8, 128), F32)


def call(kernel, name, flops, size, mib=40, **kwargs):
    return pl.pallas_call(
        kernel,
        name=name,
        compiler_params=pltpu.CompilerParams(vmem_limit_bytes=mib * 1024 * 1024),
        cost_estimate=pl.CostEstimate(flops=int(flops), bytes_accessed=int(size), transcendentals=0),
        **kwargs,
    )


def run_copies(copies):
    for copy in copies:
        copy.start()
    for copy in copies:
        copy.wait()


def owner_of(me, k, other):
    core = me % CORES
    return ((me // CORES) ^ k) * CORES + (CORES - 1 - core if other else core)


def swap_matrix(rows, columns, picked):
    width = rows * columns
    target = lax.broadcasted_iota(jnp.int32, (len(picked) * rows, width), 0)
    source = lax.broadcasted_iota(jnp.int32, (len(picked) * rows, width), 1)
    step = picked[1] - picked[0] if len(picked) > 1 else 1
    column = (target // rows) * step + picked[0]
    return (source == (target % rows) * columns + column).astype(BF16)


def weigh_kernel(slot, local_slots, permuted, me_ref, gauss_ref, tendency_ref, *rest):
    _, lats, slots, members = tendency_ref.shape
    outs, blocks = (rest[:-1], rest[-1]) if permuted else (rest, None)
    depth, breadth = math.gcd(lats, 16), 16
    matrix = swap_matrix(depth, breadth, range(slot, breadth, local_slots))
    owners = breadth // local_slots
    for j in range(0, lats, depth):
        scale = gauss_ref[j : j + depth, :]
        for s in range(0, slots, 2 * breadth):
            halves = [
                tendency_ref[0, j : j + depth, s + h : s + h + breadth, :].reshape(depth * breadth, members)
                for h in (0, breadth)
            ]
            turned = jnp.dot(matrix, jnp.concatenate(halves, axis=1), preferred_element_type=F32)
            for h in range(2):
                for i in range(owners):
                    value = turned[i * depth : (i + 1) * depth, h * members : (h + 1) * members]
                    owner = (s + h * breadth) // local_slots + i
                    value = (value * scale).astype(BF16)
                    if permuted:
                        blocks[owner, j : j + depth, :] = value
                    else:
                        outs[0][owner, 0, j : j + depth, :] = value
    if permuted:
        for k, out in enumerate(outs):
            for core in range(CORES):
                out[core, 0] = blocks[((me_ref[0] // CORES) ^ k) * CORES + core]


def weigh(tendency, gauss, me, slot, local_slots, permuted):
    rows, lats, slots, members = tendency.shape
    owners = slots // local_slots
    count, chips = (CORES, owners // CORES) if permuted else (owners, 1)
    piece = pl.BlockSpec((count, 1, lats, members), lambda r, m: (0, r, 0, 0))
    return call(
        functools.partial(weigh_kernel, slot, local_slots, permuted),
        "weigh",
        2 * 128 * tendency.size,
        3 * tendency.size,
        out_shape=[jax.ShapeDtypeStruct((count, rows, lats, members), BF16)] * chips,
        grid_spec=pltpu.PrefetchScalarGridSpec(
            num_scalar_prefetch=1,
            grid=(rows,),
            in_specs=[
                pl.BlockSpec((lats, members), lambda r, m: (0, 0)),
                pl.BlockSpec((1, lats, slots, members), lambda r, m: (r, 0, 0, 0)),
            ],
            out_specs=[piece] * chips,
            scratch_shapes=[pltpu.VMEM((owners, lats, members), BF16)] if permuted else [],
        ),
    )(me, gauss, tendency)


def pick_kernel(me_ref, *rest):
    ins, out = rest[:-1], rest[-1]
    for k, ref in enumerate(ins):
        out[k] = ref[0]


def pick(messages, me):
    _, rows, lats, members = messages[0].shape
    chips = len(messages)
    shape = (chips, rows, lats, members)
    return call(
        pick_kernel,
        "pick",
        0,
        4 * math.prod(shape),
        out_shape=jax.ShapeDtypeStruct(shape, BF16),
        grid_spec=pltpu.PrefetchScalarGridSpec(
            num_scalar_prefetch=1,
            grid=(rows,),
            in_specs=[
                pl.BlockSpec((1, 1, lats, members), lambda r, m: (CORES - 1 - m[0] % CORES, r, 0, 0))
            ]
            * chips,
            out_specs=pl.BlockSpec((chips, 1, lats, members), lambda r, m: (0, r, 0, 0)),
        ),
    )(me, *messages)


def pair_kernel(mate_ref, *rest):
    chips = mate_ref.shape[0]
    outs, sems = rest[chips:-1], rest[-1]
    run_copies([pltpu.make_async_copy(mate_ref.at[k], out.at[1], sems.at[k]) for k, out in enumerate(outs)])


def pair(messages, mate):
    chips = len(messages)
    return call(
        pair_kernel,
        "pair",
        0,
        4 * mate.size,
        out_shape=[jax.ShapeDtypeStruct(m.shape, m.dtype) for m in messages],
        in_specs=[pl.BlockSpec(mate.shape, lambda: (0, 0, 0, 0))] + [ANYWHERE] * chips,
        out_specs=[ANYWHERE] * chips,
        scratch_shapes=[pltpu.SemaphoreType.DMA((chips,))],
        input_output_aliases={k + 1: k for k in range(chips)},
    )(mate, *messages)


def analyse_kernel(slot, low, count, me_ref, wave_ref, token_ref, table_ref, state_ref, *rest):
    blocks, out, grid, sems = rest[:count], rest[count], rest[count + 1], rest[count + 2]
    rows, members, _ = out.shape
    owners, lats, _ = grid.shape
    width = table_ref.shape[1]
    step = pl.program_id(0)

    @pl.when(step == 0)
    def _():
        copies = []
        for r in range(rows):
            lanes = pl.ds(r * members, members)
            if count == 1:
                copies.append(pltpu.make_async_copy(blocks[0].at[:, r], grid.at[:, :, lanes], sems.at[0, r]))
            for k in range(count - 1):
                for other in range(CORES):
                    target = grid.at[owner_of(me_ref[0], k, other), :, lanes]
                    source = blocks[-1].at[k, r] if other else blocks[k].at[me_ref[0] % CORES, r]
                    copies.append(pltpu.make_async_copy(source, target, sems.at[CORES * k + other, r]))
        run_copies(copies)

    field = grid[...].reshape(owners * lats, rows * members)
    sums = jnp.dot(table_ref[0], field, preferred_element_type=F32)
    degree = lax.broadcasted_iota(jnp.int32, (members, width), 1) + (low + step * width)
    live = degree >= wave_ref[slot]
    for r in range(rows):
        total = state_ref[r, 0].astype(F32) + sums[:, r * members : (r + 1) * members].T
        out[r] = jnp.where(live, total, 0.0).astype(BF16)


def analyse(blocks, table, state, wave, me, token, slot, low, width):
    _, rows, lats, members = blocks[0].shape
    nspec, nlat = table.shape[1:]
    owners = nlat // lats
    first = low // width
    if lats % 16:
        blocks = [lay_in_place(blocks, me[0], owners)]
        blocks[0] = jnp.transpose(blocks[0], (1, 0, 2, 3)).reshape(1, rows, nlat, members)
        owners, lats = 1, nlat
    return call(
        functools.partial(analyse_kernel, slot, low, len(blocks)),
        "analyse",
        2 * (nspec - low) * nlat * rows * members,
        2 * (nspec - low) * nlat,
        out_shape=jax.ShapeDtypeStruct((rows, members, nspec - low), BF16),
        grid=((nspec - low) // width,),
        in_specs=[
            IN_SMEM,
            IN_SMEM,
            ANYWHERE,
            pl.BlockSpec((1, width, nlat), lambda i: (slot, first + i, 0)),
            pl.BlockSpec((rows, 1, members, width), lambda i: (0, slot, 0, first + i)),
        ]
        + [ANYWHERE] * len(blocks),
        out_specs=pl.BlockSpec((rows, members, width), lambda i: (0, 0, i)),
        scratch_shapes=[
            pltpu.VMEM((owners, lats, rows * members), BF16),
            pltpu.SemaphoreType.DMA((owners, rows)),
        ],
    )(me, wave, token, table, state, *blocks)


def lay_in_place(blocks, here, owners):
    if len(blocks) == 1:
        return blocks[0]
    own = [lax.dynamic_index_in_dim(m, here % CORES, 0, keepdims=False) for m in blocks[:-1]]
    both = jnp.stack([jnp.stack(own), blocks[-1]], axis=1).reshape((owners,) + own[0].shape)
    order = jnp.arange(owners, dtype=jnp.int32)
    order = ((order // CORES) ^ (here // CORES)) * CORES + (order % CORES ^ here % CORES)
    return jnp.take(both, order, axis=0)


def synthesise_kernel(permuted, me_ref, matrix_ref, own_ref, other_ref, table_ref, *rest):
    rows, members, _ = own_ref.shape
    width = table_ref.shape[2]
    step = pl.program_id(0)
    outs, token_ref, mixed = rest[: permuted + 1], rest[permuted + 1], rest[permuted + 2]

    @pl.when(step == 0)
    def _():
        token_ref[...] = jnp.zeros_like(token_ref)
        for f in range(rows):
            total = 0.0
            for g in range(rows):
                total = total + matrix_ref[f * rows + g : f * rows + g + 1, :] * own_ref[g].astype(F32)
                line = rows * rows + f * rows + g
                total = total + matrix_ref[line : line + 1, :] * other_ref[g].astype(F32)
            mixed[f * members : (f + 1) * members, :] = total.astype(BF16)

    sums = jnp.dot(mixed[...], table_ref[0], preferred_element_type=F32)
    grid = rest[permuted + 3] if permuted else outs[0]
    lats = grid.shape[2]
    each = width // lats
    for r in range(rows):
        turned = sums[r * members : (r + 1) * members, :].T.reshape(each, lats, members).astype(BF16)
        if permuted:
            grid[pl.ds(step * each, each), r] = turned
        else:
            grid[:, r] = turned

    if permuted:
        sems = rest[-1]

        @pl.when(step == pl.num_programs(0) - 1)
        def _():
            copies = []
            for k in range(permuted):
                for other in range(CORES):
                    source = grid.at[owner_of(me_ref[0], k, other)]
                    target = outs[-1].at[k] if other else outs[k].at[0]
                    copies.append(pltpu.make_async_copy(source, target, sems.at[k, other]))
            run_copies(copies)


def synthesise(matrix, own, other, table, me, slot, low, lats, permuted):
    rows, members, count = own.shape
    nlat = table.shape[2]
    owners = nlat // lats
    width = math.lcm(lats, 128)
    chips = owners // CORES if permuted else 0
    whole = pl.BlockSpec((rows, members, count), lambda j: (0, 0, 0))
    shapes = [jax.ShapeDtypeStruct((owners, rows, lats, members), BF16)]
    specs = [pl.BlockSpec((width // lats, rows, lats, members), lambda j: (j, 0, 0, 0))]
    scratch = [pltpu.VMEM((rows * members, count), BF16)]
    if permuted:
        shapes = [jax.ShapeDtypeStruct((CORES, rows, lats, members), BF16)] * chips
        shapes += [jax.ShapeDtypeStruct((chips, rows, lats, members), BF16)]
        specs = [ANYWHERE] * (chips + 1)
        scratch += [pltpu.VMEM((owners, rows, lats, members), BF16), pltpu.SemaphoreType.DMA((chips, CORES))]
    return call(
        functools.partial(synthesise_kernel, chips),
        "synthesise",
        2 * count * nlat * rows * members,
        2 * count * nlat,
        out_shape=shapes + [TOKEN],
        grid=(nlat // width,),
        in_specs=[
            IN_SMEM,
            pl.BlockSpec(matrix.shape, lambda j: (0, 0)),
            whole,
            whole,
            pl.BlockSpec((1, count, width), lambda j: (slot, low // count, j)),
        ],
        out_specs=specs + [pl.BlockSpec(TOKEN.shape, lambda j: (0, 0))],
        scratch_shapes=scratch,
    )(me, matrix, own, other, table)


def assemble_kernel(counts, me_ref, *rest):
    ins, out, blocks = rest[: sum(counts)], rest[sum(counts)], rest[sum(counts) + 1 :]
    _, lats, slots, members = out.shape
    local_slots = len(counts)
    views, used, spare = [], 0, 0
    for count in counts:
        refs = ins[used : used + count]
        used += count
        if count == 1:
            views.append(lambda owner, j, ref=refs[0]: ref[owner, 0, j, :])
            continue
        for k, ref in enumerate(refs):
            for other in range(CORES):
                blocks[spare][owner_of(me_ref[0], k, other)] = ref[other, 0]
        views.append(lambda owner, j, ref=blocks[spare]: ref[owner, j, :])
        spare += 1
    depth, breadth = math.gcd(lats, 16), 16
    matrix = swap_matrix(breadth, depth, range(depth))
    for start in range(0, lats, depth):
        j = slice(start, start + depth)
        for s in range(0, slots, 2 * breadth):
            halves = [
                jnp.concatenate(
                    [views[i % local_slots](i // local_slots, j) for i in range(s + h, s + h + breadth)], axis=0
                )
                for h in (0, breadth)
            ]
            turned = jnp.dot(matrix, jnp.concatenate(halves, axis=1), preferred_element_type=F32).astype(BF16)
            for h in range(2):
                value = turned[:, h * members : (h + 1) * members].reshape(depth, breadth, members)
                out[0, j, s + h * breadth : s + (h + 1) * breadth, :] = value


def assemble(pieces, me, lats):
    local_slots = len(pieces)
    _, rows, _, members = pieces[0][0].shape
    owners = max(len(p) * p[0].shape[0] for p in pieces)
    slots = local_slots * owners
    flat = [block for slot in pieces for block in slot]
    moved = sum(len(p) > 1 for p in pieces)
    return call(
        functools.partial(assemble_kernel, [len(p) for p in pieces]),
        "assemble",
        2 * 256 * rows * lats * slots * members,
        4 * rows * lats * slots * members,
        out_shape=jax.ShapeDtypeStruct((rows, lats, slots, members), BF16),
        grid_spec=pltpu.PrefetchScalarGridSpec(
            num_scalar_prefetch=1,
            grid=(rows,),
            in_specs=[
                pl.BlockSpec((block.shape[0], 1, lats, members), lambda r, m: (0, r, 0, 0)) for block in flat
            ],
            out_specs=pl.BlockSpec((1, lats, slots, members), lambda r, m: (r, 0, 0, 0)),
            scratch_shapes=[pltpu.VMEM((owners, lats, members), BF16)] * moved,
        ),
    )(me, *flat)


def between_chips(messages):
    chips = len(messages)
    got = [messages[0]]
    for k in range(1, chips):
        got.append(lax.ppermute(messages[k], "wave", [(d, d ^ (k * CORES)) for d in range(chips * CORES)]))
    return got


def between_cores(blocks, owners):
    return lax.ppermute(blocks, "wave", [(d, d ^ 1) for d in range(owners)])


def to_all(blocks):
    return lax.all_to_all(blocks, "wave", split_axis=0, concat_axis=0, tiled=True)


def per_device(
    tendency, spectral_state, legendre, gauss_weights, block_inverses, pole_coeffs, wavenumbers
):
    rows, lats, slots, members = tendency.shape
    local_slots, nspec, nlat = legendre.shape
    owners = slots // local_slots
    me = lax.axis_index("wave").astype(jnp.int32).reshape(1)
    pole_index = lax.axis_index("pole")
    orientation = (2 * pole_index - 1).astype(F32)
    gauss = jnp.broadcast_to(gauss_weights[:, None], (lats, members))
    received = []
    for slot in range(local_slots):
        permuted = slot in PERMUTED
        blocks = weigh(tendency, gauss, me, slot, local_slots, permuted)
        received.append(between_chips(blocks) if permuted else [to_all(blocks[0])])

    local_pairs = block_inverses.shape[0]
    flat_inverse = block_inverses.reshape(local_pairs, -1).astype(F32)
    weighted_sums = jnp.dot(pole_coeffs.T, flat_inverse, precision=lax.Precision.HIGHEST)
    weighted_sums = weighted_sums.reshape(2, 2, rows, rows, local_slots, nspec)
    real_matrix = weighted_sums[0, 0] - weighted_sums[1, 1]
    imag_matrix = weighted_sums[0, 1] + weighted_sums[1, 0]
    real_matrix, imag_matrix = lax.psum((real_matrix, imag_matrix), "pole")
    matrices = jnp.concatenate([real_matrix, orientation * imag_matrix]).reshape(2 * rows * rows, local_slots, nspec)

    sent = []
    token = jnp.zeros(TOKEN.shape, TOKEN.dtype)
    for slot in range(local_slots):
        permuted = slot in PERMUTED
        low = nspec // 2 if slot % 2 else 0
        blocks = received[slot]
        if permuted:
            blocks = blocks + [between_cores(pick(blocks, me), owners)]
        forced = analyse(blocks, legendre, spectral_state, wavenumbers, me, token, slot, low, nspec // 2)
        other = lax.ppermute(forced, "pole", [(0, 1), (1, 0)])
        matrix = matrices[:, slot, low:]
        *blocks, token = synthesise(matrix, forced, other, legendre, me, slot, low, lats, permuted)
        if permuted:
            sent.append(between_chips(pair(blocks[:-1], between_cores(blocks[-1], owners))))
        else:
            sent.append([to_all(blocks[0])])
    return assemble(sent, me, lats)


def solution(mesh):
    in_specs = (
        P("pole", "wave", None, None),
        P("pole", "wave", None, None),
        P("wave", None, None),
        P("wave"),
        P("pole", None, "wave", None),
        P("pole", None),
        P("wave"),
    )
    out_specs = P("pole", "wave", None, None)
    return jax.shard_map(
        per_device, mesh=mesh, in_specs=in_specs, out_specs=out_specs, check_vma=False
    )
```

```python
import functools
import math

import jax
import jax.numpy as jnp
from jax import lax
from jax.experimental import pallas as pl
from jax.experimental.pallas import tpu as pltpu
from jax.sharding import PartitionSpec as P

BF16 = jnp.bfloat16
F32 = jnp.float32
CORES = 2
PERMUTED = ()
ANYWHERE = pl.BlockSpec(memory_space=pl.ANY)
IN_SMEM = pl.BlockSpec(memory_space=pltpu.SMEM)
TOKEN = jax.ShapeDtypeStruct((8, 128), F32)


def call(kernel, name, flops, size, mib=40, **kwargs):
    return pl.pallas_call(
        kernel,
        name=name,
        compiler_params=pltpu.CompilerParams(vmem_limit_bytes=mib * 1024 * 1024),
        cost_estimate=pl.CostEstimate(flops=int(flops), bytes_accessed=int(size), transcendentals=0),
        **kwargs,
    )


def run_copies(copies):
    for copy in copies:
        copy.start()
    for copy in copies:
        copy.wait()


def owner_of(me, k, other):
    core = me % CORES
    return ((me // CORES) ^ k) * CORES + (CORES - 1 - core if other else core)


def swap_matrix(rows, columns, picked):
    width = rows * columns
    target = lax.broadcasted_iota(jnp.int32, (len(picked) * rows, width), 0)
    source = lax.broadcasted_iota(jnp.int32, (len(picked) * rows, width), 1)
    step = picked[1] - picked[0] if len(picked) > 1 else 1
    column = (target // rows) * step + picked[0]
    return (source == (target % rows) * columns + column).astype(BF16)


def weigh_kernel(slot, local_slots, permuted, me_ref, gauss_ref, tendency_ref, *rest):
    _, lats, slots, members = tendency_ref.shape
    outs, blocks = (rest[:-1], rest[-1]) if permuted else (rest, None)
    depth, breadth = math.gcd(lats, 16), 16
    matrix = swap_matrix(depth, breadth, range(slot, breadth, local_slots))
    owners = breadth // local_slots
    for j in range(0, lats, depth):
        scale = gauss_ref[j : j + depth, :]
        for s in range(0, slots, 2 * breadth):
            halves = [
                tendency_ref[0, j : j + depth, s + h : s + h + breadth, :].reshape(depth * breadth, members)
                for h in (0, breadth)
            ]
            turned = jnp.dot(matrix, jnp.concatenate(halves, axis=1), preferred_element_type=F32)
            for h in range(2):
                for i in range(owners):
                    value = turned[i * depth : (i + 1) * depth, h * members : (h + 1) * members]
                    owner = (s + h * breadth) // local_slots + i
                    value = (value * scale).astype(BF16)
                    if permuted:
                        blocks[owner, j : j + depth, :] = value
                    else:
                        outs[0][owner, 0, j : j + depth, :] = value
    if permuted:
        for k, out in enumerate(outs):
            for core in range(CORES):
                out[core, 0] = blocks[((me_ref[0] // CORES) ^ k) * CORES + core]


def weigh(tendency, gauss, me, slot, local_slots, permuted):
    rows, lats, slots, members = tendency.shape
    owners = slots // local_slots
    count, chips = (CORES, owners // CORES) if permuted else (owners, 1)
    piece = pl.BlockSpec((count, 1, lats, members), lambda r, m: (0, r, 0, 0))
    return call(
        functools.partial(weigh_kernel, slot, local_slots, permuted),
        "weigh",
        2 * 128 * tendency.size,
        3 * tendency.size,
        out_shape=[jax.ShapeDtypeStruct((count, rows, lats, members), BF16)] * chips,
        grid_spec=pltpu.PrefetchScalarGridSpec(
            num_scalar_prefetch=1,
            grid=(rows,),
            in_specs=[
                pl.BlockSpec((lats, members), lambda r, m: (0, 0)),
                pl.BlockSpec((1, lats, slots, members), lambda r, m: (r, 0, 0, 0)),
            ],
            out_specs=[piece] * chips,
            scratch_shapes=[pltpu.VMEM((owners, lats, members), BF16)] if permuted else [],
        ),
    )(me, gauss, tendency)


def pick_kernel(me_ref, *rest):
    ins, out = rest[:-1], rest[-1]
    for k, ref in enumerate(ins):
        out[k] = ref[0]


def pick(messages, me):
    _, rows, lats, members = messages[0].shape
    chips = len(messages)
    shape = (chips, rows, lats, members)
    return call(
        pick_kernel,
        "pick",
        0,
        4 * math.prod(shape),
        out_shape=jax.ShapeDtypeStruct(shape, BF16),
        grid_spec=pltpu.PrefetchScalarGridSpec(
            num_scalar_prefetch=1,
            grid=(rows,),
            in_specs=[
                pl.BlockSpec((1, 1, lats, members), lambda r, m: (CORES - 1 - m[0] % CORES, r, 0, 0))
            ]
            * chips,
            out_specs=pl.BlockSpec((chips, 1, lats, members), lambda r, m: (0, r, 0, 0)),
        ),
    )(me, *messages)


def pair_kernel(mate_ref, *rest):
    chips = mate_ref.shape[0]
    outs, sems = rest[chips:-1], rest[-1]
    run_copies([pltpu.make_async_copy(mate_ref.at[k], out.at[1], sems.at[k]) for k, out in enumerate(outs)])


def pair(messages, mate):
    chips = len(messages)
    return call(
        pair_kernel,
        "pair",
        0,
        4 * mate.size,
        out_shape=[jax.ShapeDtypeStruct(m.shape, m.dtype) for m in messages],
        in_specs=[pl.BlockSpec(mate.shape, lambda: (0, 0, 0, 0))] + [ANYWHERE] * chips,
        out_specs=[ANYWHERE] * chips,
        scratch_shapes=[pltpu.SemaphoreType.DMA((chips,))],
        input_output_aliases={k + 1: k for k in range(chips)},
    )(mate, *messages)


def analyse_kernel(slot, low, count, me_ref, wave_ref, token_ref, table_ref, state_ref, *rest):
    blocks, out, grid, sems = rest[:count], rest[count], rest[count + 1], rest[count + 2]
    rows, members, _ = out.shape
    owners, lats, _ = grid.shape
    width = table_ref.shape[1]
    step = pl.program_id(0)

    @pl.when(step == 0)
    def _():
        copies = []
        for r in range(rows):
            lanes = pl.ds(r * members, members)
            if count == 1:
                copies.append(pltpu.make_async_copy(blocks[0].at[:, r], grid.at[:, :, lanes], sems.at[0, r]))
            for k in range(count - 1):
                for other in range(CORES):
                    target = grid.at[owner_of(me_ref[0], k, other), :, lanes]
                    source = blocks[-1].at[k, r] if other else blocks[k].at[me_ref[0] % CORES, r]
                    copies.append(pltpu.make_async_copy(source, target, sems.at[CORES * k + other, r]))
        run_copies(copies)

    field = grid[...].reshape(owners * lats, rows * members)
    sums = jnp.dot(table_ref[0], field, preferred_element_type=F32)
    degree = lax.broadcasted_iota(jnp.int32, (members, width), 1) + (low + step * width)
    live = degree >= wave_ref[slot]
    for r in range(rows):
        total = state_ref[r, 0].astype(F32) + sums[:, r * members : (r + 1) * members].T
        out[r] = jnp.where(live, total, 0.0).astype(BF16)


def analyse(blocks, table, state, wave, me, token, slot, low, width):
    _, rows, lats, members = blocks[0].shape
    nspec, nlat = table.shape[1:]
    owners = nlat // lats
    first = low // width
    if lats % 16:
        blocks = [lay_in_place(blocks, me[0], owners)]
        blocks[0] = jnp.transpose(blocks[0], (1, 0, 2, 3)).reshape(1, rows, nlat, members)
        owners, lats = 1, nlat
    return call(
        functools.partial(analyse_kernel, slot, low, len(blocks)),
        "analyse",
        2 * (nspec - low) * nlat * rows * members,
        2 * (nspec - low) * nlat,
        out_shape=jax.ShapeDtypeStruct((rows, members, nspec - low), BF16),
        grid=((nspec - low) // width,),
        in_specs=[
            IN_SMEM,
            IN_SMEM,
            ANYWHERE,
            pl.BlockSpec((1, width, nlat), lambda i: (slot, first + i, 0)),
            pl.BlockSpec((rows, 1, members, width), lambda i: (0, slot, 0, first + i)),
        ]
        + [ANYWHERE] * len(blocks),
        out_specs=pl.BlockSpec((rows, members, width), lambda i: (0, 0, i)),
        scratch_shapes=[
            pltpu.VMEM((owners, lats, rows * members), BF16),
            pltpu.SemaphoreType.DMA((owners, rows)),
        ],
    )(me, wave, token, table, state, *blocks)


def lay_in_place(blocks, here, owners):
    if len(blocks) == 1:
        return blocks[0]
    own = [lax.dynamic_index_in_dim(m, here % CORES, 0, keepdims=False) for m in blocks[:-1]]
    both = jnp.stack([jnp.stack(own), blocks[-1]], axis=1).reshape((owners,) + own[0].shape)
    order = jnp.arange(owners, dtype=jnp.int32)
    order = ((order // CORES) ^ (here // CORES)) * CORES + (order % CORES ^ here % CORES)
    return jnp.take(both, order, axis=0)


def synthesise_kernel(permuted, me_ref, matrix_ref, own_ref, other_ref, table_ref, *rest):
    rows, members, _ = own_ref.shape
    width = table_ref.shape[2]
    step = pl.program_id(0)
    outs, token_ref, mixed = rest[: permuted + 1], rest[permuted + 1], rest[permuted + 2]

    @pl.when(step == 0)
    def _():
        token_ref[...] = jnp.zeros_like(token_ref)
        for f in range(rows):
            total = 0.0
            for g in range(rows):
                total = total + matrix_ref[f * rows + g : f * rows + g + 1, :] * own_ref[g].astype(F32)
                line = rows * rows + f * rows + g
                total = total + matrix_ref[line : line + 1, :] * other_ref[g].astype(F32)
            mixed[f * members : (f + 1) * members, :] = total.astype(BF16)

    sums = jnp.dot(mixed[...], table_ref[0], preferred_element_type=F32)
    grid = rest[permuted + 3] if permuted else outs[0]
    lats = grid.shape[2]
    each = width // lats
    for r in range(rows):
        turned = sums[r * members : (r + 1) * members, :].T.reshape(each, lats, members).astype(BF16)
        if permuted:
            grid[pl.ds(step * each, each), r] = turned
        else:
            grid[:, r] = turned

    if permuted:
        sems = rest[-1]

        @pl.when(step == pl.num_programs(0) - 1)
        def _():
            copies = []
            for k in range(permuted):
                for other in range(CORES):
                    source = grid.at[owner_of(me_ref[0], k, other)]
                    target = outs[-1].at[k] if other else outs[k].at[0]
                    copies.append(pltpu.make_async_copy(source, target, sems.at[k, other]))
            run_copies(copies)


def synthesise(matrix, own, other, table, me, slot, low, lats, permuted):
    rows, members, count = own.shape
    nlat = table.shape[2]
    owners = nlat // lats
    width = math.lcm(lats, 128)
    chips = owners // CORES if permuted else 0
    whole = pl.BlockSpec((rows, members, count), lambda j: (0, 0, 0))
    shapes = [jax.ShapeDtypeStruct((owners, rows, lats, members), BF16)]
    specs = [pl.BlockSpec((width // lats, rows, lats, members), lambda j: (j, 0, 0, 0))]
    scratch = [pltpu.VMEM((rows * members, count), BF16)]
    if permuted:
        shapes = [jax.ShapeDtypeStruct((CORES, rows, lats, members), BF16)] * chips
        shapes += [jax.ShapeDtypeStruct((chips, rows, lats, members), BF16)]
        specs = [ANYWHERE] * (chips + 1)
        scratch += [pltpu.VMEM((owners, rows, lats, members), BF16), pltpu.SemaphoreType.DMA((chips, CORES))]
    return call(
        functools.partial(synthesise_kernel, chips),
        "synthesise",
        2 * count * nlat * rows * members,
        2 * count * nlat,
        out_shape=shapes + [TOKEN],
        grid=(nlat // width,),
        in_specs=[
            IN_SMEM,
            pl.BlockSpec(matrix.shape, lambda j: (0, 0)),
            whole,
            whole,
            pl.BlockSpec((1, count, width), lambda j: (slot, low // count, j)),
        ],
        out_specs=specs + [pl.BlockSpec(TOKEN.shape, lambda j: (0, 0))],
        scratch_shapes=scratch,
    )(me, matrix, own, other, table)


def assemble_kernel(counts, me_ref, *rest):
    ins, out, blocks = rest[: sum(counts)], rest[sum(counts)], rest[sum(counts) + 1 :]
    _, lats, slots, members = out.shape
    local_slots = len(counts)
    views, used, spare = [], 0, 0
    for count in counts:
        refs = ins[used : used + count]
        used += count
        if count == 1:
            views.append(lambda owner, j, ref=refs[0]: ref[owner, 0, j, :])
            continue
        for k, ref in enumerate(refs):
            for other in range(CORES):
                blocks[spare][owner_of(me_ref[0], k, other)] = ref[other, 0]
        views.append(lambda owner, j, ref=blocks[spare]: ref[owner, j, :])
        spare += 1
    depth, breadth = math.gcd(lats, 16), 16
    matrix = swap_matrix(breadth, depth, range(depth))
    for start in range(0, lats, depth):
        j = slice(start, start + depth)
        for s in range(0, slots, 2 * breadth):
            halves = [
                jnp.concatenate(
                    [views[i % local_slots](i // local_slots, j) for i in range(s + h, s + h + breadth)], axis=0
                )
                for h in (0, breadth)
            ]
            turned = jnp.dot(matrix, jnp.concatenate(halves, axis=1), preferred_element_type=F32).astype(BF16)
            for h in range(2):
                value = turned[:, h * members : (h + 1) * members].reshape(depth, breadth, members)
                out[0, j, s + h * breadth : s + (h + 1) * breadth, :] = value


def assemble(pieces, me, lats):
    local_slots = len(pieces)
    _, rows, _, members = pieces[0][0].shape
    owners = max(len(p) * p[0].shape[0] for p in pieces)
    slots = local_slots * owners
    flat = [block for slot in pieces for block in slot]
    moved = sum(len(p) > 1 for p in pieces)
    return call(
        functools.partial(assemble_kernel, [len(p) for p in pieces]),
        "assemble",
        2 * 256 * rows * lats * slots * members,
        4 * rows * lats * slots * members,
        out_shape=jax.ShapeDtypeStruct((rows, lats, slots, members), BF16),
        grid_spec=pltpu.PrefetchScalarGridSpec(
            num_scalar_prefetch=1,
            grid=(rows,),
            in_specs=[
                pl.BlockSpec((block.shape[0], 1, lats, members), lambda r, m: (0, r, 0, 0)) for block in flat
            ],
            out_specs=pl.BlockSpec((1, lats, slots, members), lambda r, m: (r, 0, 0, 0)),
            scratch_shapes=[pltpu.VMEM((owners, lats, members), BF16)] * moved,
        ),
    )(me, *flat)


def between_chips(messages):
    chips = len(messages)
    got = [messages[0]]
    for k in range(1, chips):
        got.append(lax.ppermute(messages[k], "wave", [(d, d ^ (k * CORES)) for d in range(chips * CORES)]))
    return got


def between_cores(blocks, owners):
    return lax.ppermute(blocks, "wave", [(d, d ^ 1) for d in range(owners)])


def to_all(blocks):
    return lax.all_to_all(blocks, "wave", split_axis=0, concat_axis=0, tiled=True)


def per_device(
    tendency, spectral_state, legendre, gauss_weights, block_inverses, pole_coeffs, wavenumbers
):
    rows, lats, slots, members = tendency.shape
    local_slots, nspec, nlat = legendre.shape
    owners = slots // local_slots
    me = lax.axis_index("wave").astype(jnp.int32).reshape(1)
    pole_index = lax.axis_index("pole")
    orientation = (2 * pole_index - 1).astype(F32)
    gauss = jnp.broadcast_to(gauss_weights[:, None], (lats, members))
    received = []
    for slot in range(local_slots):
        permuted = slot in PERMUTED
        blocks = weigh(tendency, gauss, me, slot, local_slots, permuted)
        received.append(between_chips(blocks) if permuted else [to_all(blocks[0])])

    local_pairs = block_inverses.shape[0]
    flat_inverse = block_inverses.reshape(local_pairs, -1).astype(F32)
    weighted_sums = jnp.dot(pole_coeffs.T, flat_inverse, precision=lax.Precision.HIGHEST)
    weighted_sums = weighted_sums.reshape(2, 2, rows, rows, local_slots, nspec)
    real_matrix = weighted_sums[0, 0] - weighted_sums[1, 1]
    imag_matrix = weighted_sums[0, 1] + weighted_sums[1, 0]
    real_matrix, imag_matrix = lax.psum((real_matrix, imag_matrix), "pole")
    matrices = jnp.concatenate([real_matrix, orientation * imag_matrix]).reshape(2 * rows * rows, local_slots, nspec)

    sent = []
    token = jnp.zeros(TOKEN.shape, TOKEN.dtype)
    for slot in range(local_slots):
        permuted = slot in PERMUTED
        low = nspec // 2 if slot % 2 else 0
        blocks = received[slot]
        if permuted:
            blocks = blocks + [between_cores(pick(blocks, me), owners)]
        forced = analyse(blocks, legendre, spectral_state, wavenumbers, me, token, slot, low, nspec // 2)
        other = lax.ppermute(forced, "pole", [(0, 1), (1, 0)])
        matrix = matrices[:, slot, low:]
        *blocks, token = synthesise(matrix, forced, other, legendre, me, slot, low, lats, permuted)
        if permuted:
            sent.append(between_chips(pair(blocks[:-1], between_cores(blocks[-1], owners))))
        else:
            sent.append([to_all(blocks[0])])
    return assemble(sent, me, lats)


def solution(mesh):
    in_specs = (
        P("pole", "wave", None, None),
        P("pole", "wave", None, None),
        P("wave", None, None),
        P("wave"),
        P("pole", None, "wave", None),
        P("pole", None),
        P("wave"),
    )
    out_specs = P("pole", "wave", None, None)
    return jax.shard_map(
        per_device, mesh=mesh, in_specs=in_specs, out_specs=out_specs, check_vma=False
    )
```

```python
import functools
import math

import jax
import jax.numpy as jnp
from jax import lax
from jax.experimental import pallas as pl
from jax.experimental.pallas import tpu as pltpu
from jax.sharding import PartitionSpec as P

BF16 = jnp.bfloat16
F32 = jnp.float32
CORES = 2
PERMUTED = ()
ANYWHERE = pl.BlockSpec(memory_space=pl.ANY)
IN_SMEM = pl.BlockSpec(memory_space=pltpu.SMEM)
TOKEN = jax.ShapeDtypeStruct((8, 128), F32)


def call(kernel, name, flops, size, mib=40, **kwargs):
    return pl.pallas_call(
        kernel,
        name=name,
        compiler_params=pltpu.CompilerParams(vmem_limit_bytes=mib * 1024 * 1024),
        cost_estimate=pl.CostEstimate(flops=int(flops), bytes_accessed=int(size), transcendentals=0),
        **kwargs,
    )


def run_copies(copies):
    for copy in copies:
        copy.start()
    for copy in copies:
        copy.wait()


def owner_of(me, k, other):
    core = me % CORES
    return ((me // CORES) ^ k) * CORES + (CORES - 1 - core if other else core)


def swap_matrix(rows, columns, picked):
    width = rows * columns
    target = lax.broadcasted_iota(jnp.int32, (len(picked) * rows, width), 0)
    source = lax.broadcasted_iota(jnp.int32, (len(picked) * rows, width), 1)
    step = picked[1] - picked[0] if len(picked) > 1 else 1
    column = (target // rows) * step + picked[0]
    return (source == (target % rows) * columns + column).astype(BF16)


def weigh_kernel(slot, local_slots, permuted, me_ref, gauss_ref, tendency_ref, *rest):
    _, lats, slots, members = tendency_ref.shape
    outs, blocks = (rest[:-1], rest[-1]) if permuted else (rest, None)
    outs, token_ref = outs[:-1], outs[-1]
    token_ref[...] = jnp.zeros_like(token_ref)
    depth, breadth = math.gcd(lats, 16), 16
    matrix = swap_matrix(depth, breadth, range(slot, breadth, local_slots))
    owners = breadth // local_slots
    for j in range(0, lats, depth):
        scale = gauss_ref[j : j + depth, :]
        for s in range(0, slots, 2 * breadth):
            halves = [
                tendency_ref[0, j : j + depth, s + h : s + h + breadth, :].reshape(depth * breadth, members)
                for h in (0, breadth)
            ]
            turned = jnp.dot(matrix, jnp.concatenate(halves, axis=1), preferred_element_type=F32)
            for h in range(2):
                for i in range(owners):
                    value = turned[i * depth : (i + 1) * depth, h * members : (h + 1) * members]
                    owner = (s + h * breadth) // local_slots + i
                    value = (value * scale).astype(BF16)
                    if permuted:
                        blocks[owner, j : j + depth, :] = value
                    else:
                        outs[0][owner, 0, j : j + depth, :] = value
    if permuted:
        for k, out in enumerate(outs):
            for core in range(CORES):
                out[core, 0] = blocks[((me_ref[0] // CORES) ^ k) * CORES + core]


def weigh(tendency, gauss, me, slot, local_slots, permuted):
    rows, lats, slots, members = tendency.shape
    owners = slots // local_slots
    count, chips = (CORES, owners // CORES) if permuted else (owners, 1)
    piece = pl.BlockSpec((count, 1, lats, members), lambda r, m: (0, r, 0, 0))
    return call(
        functools.partial(weigh_kernel, slot, local_slots, permuted),
        "weigh",
        2 * 128 * tendency.size,
        3 * tendency.size,
        58,
        out_shape=[jax.ShapeDtypeStruct((count, rows, lats, members), BF16)] * chips + [TOKEN],
        grid_spec=pltpu.PrefetchScalarGridSpec(
            num_scalar_prefetch=1,
            grid=(rows,),
            in_specs=[
                pl.BlockSpec((lats, members), lambda r, m: (0, 0)),
                pl.BlockSpec((1, lats, slots, members), lambda r, m: (r, 0, 0, 0)),
            ],
            out_specs=[piece] * chips + [pl.BlockSpec(TOKEN.shape, lambda r, m: (0, 0))],
            scratch_shapes=[pltpu.VMEM((owners, lats, members), BF16)] if permuted else [],
        ),
    )(me, gauss, tendency)


def pick_kernel(me_ref, *rest):
    ins, out = rest[:-1], rest[-1]
    for k, ref in enumerate(ins):
        out[k] = ref[0]


def pick(messages, me):
    _, rows, lats, members = messages[0].shape
    chips = len(messages)
    shape = (chips, rows, lats, members)
    return call(
        pick_kernel,
        "pick",
        0,
        4 * math.prod(shape),
        out_shape=jax.ShapeDtypeStruct(shape, BF16),
        grid_spec=pltpu.PrefetchScalarGridSpec(
            num_scalar_prefetch=1,
            grid=(rows,),
            in_specs=[
                pl.BlockSpec((1, 1, lats, members), lambda r, m: (CORES - 1 - m[0] % CORES, r, 0, 0))
            ]
            * chips,
            out_specs=pl.BlockSpec((chips, 1, lats, members), lambda r, m: (0, r, 0, 0)),
        ),
    )(me, *messages)


def pair_kernel(mate_ref, *rest):
    chips = mate_ref.shape[0]
    outs, sems = rest[chips:-1], rest[-1]
    run_copies([pltpu.make_async_copy(mate_ref.at[k], out.at[1], sems.at[k]) for k, out in enumerate(outs)])


def pair(messages, mate):
    chips = len(messages)
    return call(
        pair_kernel,
        "pair",
        0,
        4 * mate.size,
        out_shape=[jax.ShapeDtypeStruct(m.shape, m.dtype) for m in messages],
        in_specs=[pl.BlockSpec(mate.shape, lambda: (0, 0, 0, 0))] + [ANYWHERE] * chips,
        out_specs=[ANYWHERE] * chips,
        scratch_shapes=[pltpu.SemaphoreType.DMA((chips,))],
        input_output_aliases={k + 1: k for k in range(chips)},
    )(mate, *messages)


def analyse_kernel(slot, low, count, me_ref, wave_ref, token_ref, table_ref, state_ref, *rest):
    blocks, out, grid, sems = rest[:count], rest[count], rest[count + 1], rest[count + 2]
    rows, members, _ = out.shape
    owners, lats, _ = grid.shape
    width = table_ref.shape[1]
    step = pl.program_id(0)

    @pl.when(step == 0)
    def _():
        copies = []
        for r in range(rows):
            lanes = pl.ds(r * members, members)
            if count == 1:
                copies.append(pltpu.make_async_copy(blocks[0].at[:, r], grid.at[:, :, lanes], sems.at[0, r]))
            for k in range(count - 1):
                for other in range(CORES):
                    target = grid.at[owner_of(me_ref[0], k, other), :, lanes]
                    source = blocks[-1].at[k, r] if other else blocks[k].at[me_ref[0] % CORES, r]
                    copies.append(pltpu.make_async_copy(source, target, sems.at[CORES * k + other, r]))
        run_copies(copies)

    field = grid[...].reshape(owners * lats, rows * members)
    sums = jnp.dot(table_ref[0], field, preferred_element_type=F32)
    degree = lax.broadcasted_iota(jnp.int32, (members, width), 1) + (low + step * width)
    live = degree >= wave_ref[slot]
    for r in range(rows):
        total = state_ref[r, 0].astype(F32) + sums[:, r * members : (r + 1) * members].T
        out[r] = jnp.where(live, total, 0.0).astype(BF16)


def analyse(blocks, table, state, wave, me, token, slot, low, width):
    _, rows, lats, members = blocks[0].shape
    nspec, nlat = table.shape[1:]
    owners = nlat // lats
    first = low // width
    if lats % 16:
        blocks = [lay_in_place(blocks, me[0], owners)]
        blocks[0] = jnp.transpose(blocks[0], (1, 0, 2, 3)).reshape(1, rows, nlat, members)
        owners, lats = 1, nlat
    return call(
        functools.partial(analyse_kernel, slot, low, len(blocks)),
        "analyse",
        2 * (nspec - low) * nlat * rows * members,
        2 * (nspec - low) * nlat,
        out_shape=jax.ShapeDtypeStruct((rows, members, nspec - low), BF16),
        grid=((nspec - low) // width,),
        in_specs=[
            IN_SMEM,
            IN_SMEM,
            ANYWHERE,
            pl.BlockSpec((1, width, nlat), lambda i: (slot, first + i, 0)),
            pl.BlockSpec((rows, 1, members, width), lambda i: (0, slot, 0, first + i)),
        ]
        + [ANYWHERE] * len(blocks),
        out_specs=pl.BlockSpec((rows, members, width), lambda i: (0, 0, i)),
        scratch_shapes=[
            pltpu.VMEM((owners, lats, rows * members), BF16),
            pltpu.SemaphoreType.DMA((owners, rows)),
        ],
    )(me, wave, token, table, state, *blocks)


def lay_in_place(blocks, here, owners):
    if len(blocks) == 1:
        return blocks[0]
    own = [lax.dynamic_index_in_dim(m, here % CORES, 0, keepdims=False) for m in blocks[:-1]]
    both = jnp.stack([jnp.stack(own), blocks[-1]], axis=1).reshape((owners,) + own[0].shape)
    order = jnp.arange(owners, dtype=jnp.int32)
    order = ((order // CORES) ^ (here // CORES)) * CORES + (order % CORES ^ here % CORES)
    return jnp.take(both, order, axis=0)


def sum_pairs_kernel(coeff_ref, token_ref, inverse_ref, out_ref):
    pairs, entries = inverse_ref.shape[:2]
    half = entries // 2

    def one(entry, carry):
        real = imag = 0.0
        for k in range(pairs):
            first, second = inverse_ref[k, entry].astype(F32), inverse_ref[k, half + entry].astype(F32)
            a, b = coeff_ref[k, 0], coeff_ref[k, 1]
            real = real + (a * first - b * second)
            imag = imag + (a * second + b * first)
        out_ref[entry] = real
        out_ref[half + entry] = imag
        return carry

    lax.fori_loop(0, half, one, 0)


def sum_pairs(block_inverses, pole_coeffs, token):
    return call(
        sum_pairs_kernel,
        "sum_pairs",
        4 * block_inverses.size,
        2 * block_inverses.size,
        out_shape=jax.ShapeDtypeStruct(block_inverses.shape[1:], F32),
        in_specs=[IN_SMEM, ANYWHERE, pl.BlockSpec(block_inverses.shape, lambda: (0, 0, 0, 0))],
        out_specs=pl.BlockSpec(block_inverses.shape[1:], lambda: (0, 0, 0)),
    )(pole_coeffs, token, block_inverses)


def synthesise_kernel(slot, low, permuted, me_ref, sign_ref, here_ref, there_ref, own_ref, other_ref, table_ref, *rest):
    rows, members, _ = own_ref.shape
    width = table_ref.shape[2]
    step = pl.program_id(0)
    outs, token_ref, mixed = rest[: permuted + 1], rest[permuted + 1], rest[permuted + 2]

    @pl.when(step == 0)
    def _():
        token_ref[...] = jnp.zeros_like(token_ref)

        def line(entry):
            return here_ref[entry, slot : slot + 1, low:] + there_ref[entry, slot : slot + 1, low:]

        for f in range(rows):
            total = 0.0
            for g in range(rows):
                total = total + line(f * rows + g) * own_ref[g].astype(F32)
                total = total + sign_ref[0] * line(rows * rows + f * rows + g) * other_ref[g].astype(F32)
            mixed[f * members : (f + 1) * members, :] = total.astype(BF16)

    sums = jnp.dot(mixed[...], table_ref[0], preferred_element_type=F32)
    grid = rest[permuted + 3] if permuted else outs[0]
    lats = grid.shape[2]
    each = width // lats
    for r in range(rows):
        turned = sums[r * members : (r + 1) * members, :].T.reshape(each, lats, members).astype(BF16)
        if permuted:
            grid[pl.ds(step * each, each), r] = turned
        else:
            grid[:, r] = turned

    if permuted:
        sems = rest[-1]

        @pl.when(step == pl.num_programs(0) - 1)
        def _():
            copies = []
            for k in range(permuted):
                for other in range(CORES):
                    source = grid.at[owner_of(me_ref[0], k, other)]
                    target = outs[-1].at[k] if other else outs[k].at[0]
                    copies.append(pltpu.make_async_copy(source, target, sems.at[k, other]))
            run_copies(copies)


def synthesise(here, there, sign, own, other, table, me, slot, low, lats, permuted):
    rows, members, count = own.shape
    nlat = table.shape[2]
    owners = nlat // lats
    width = math.lcm(lats, 128)
    chips = owners // CORES if permuted else 0
    matrix = pl.BlockSpec(here.shape, lambda j: (0, 0, 0))
    whole = pl.BlockSpec((rows, members, count), lambda j: (0, 0, 0))
    shapes = [jax.ShapeDtypeStruct((owners, rows, lats, members), BF16)]
    specs = [pl.BlockSpec((width // lats, rows, lats, members), lambda j: (j, 0, 0, 0))]
    scratch = [pltpu.VMEM((rows * members, count), BF16)]
    if permuted:
        shapes = [jax.ShapeDtypeStruct((CORES, rows, lats, members), BF16)] * chips
        shapes += [jax.ShapeDtypeStruct((chips, rows, lats, members), BF16)]
        specs = [ANYWHERE] * (chips + 1)
        scratch += [pltpu.VMEM((owners, rows, lats, members), BF16), pltpu.SemaphoreType.DMA((chips, CORES))]
    return call(
        functools.partial(synthesise_kernel, slot, low, chips),
        "synthesise",
        2 * count * nlat * rows * members,
        2 * count * nlat,
        out_shape=shapes + [TOKEN],
        grid=(nlat // width,),
        in_specs=[
            IN_SMEM,
            IN_SMEM,
            matrix,
            matrix,
            whole,
            whole,
            pl.BlockSpec((1, count, width), lambda j: (slot, low // count, j)),
        ],
        out_specs=specs + [pl.BlockSpec(TOKEN.shape, lambda j: (0, 0))],
        scratch_shapes=scratch,
    )(me, sign, here, there, own, other, table)


def assemble_kernel(counts, me_ref, *rest):
    ins, out, blocks = rest[: sum(counts)], rest[sum(counts)], rest[sum(counts) + 1 :]
    _, lats, slots, members = out.shape
    local_slots = len(counts)
    views, used, spare = [], 0, 0
    for count in counts:
        refs = ins[used : used + count]
        used += count
        if count == 1:
            views.append(lambda owner, j, ref=refs[0]: ref[owner, 0, j, :])
            continue
        for k, ref in enumerate(refs):
            for other in range(CORES):
                blocks[spare][owner_of(me_ref[0], k, other)] = ref[other, 0]
        views.append(lambda owner, j, ref=blocks[spare]: ref[owner, j, :])
        spare += 1
    depth, breadth = math.gcd(lats, 16), 16
    matrix = swap_matrix(breadth, depth, range(depth))
    for start in range(0, lats, depth):
        j = slice(start, start + depth)
        for s in range(0, slots, 2 * breadth):
            halves = [
                jnp.concatenate(
                    [views[i % local_slots](i // local_slots, j) for i in range(s + h, s + h + breadth)], axis=0
                )
                for h in (0, breadth)
            ]
            turned = jnp.dot(matrix, jnp.concatenate(halves, axis=1), preferred_element_type=F32).astype(BF16)
            for h in range(2):
                value = turned[:, h * members : (h + 1) * members].reshape(depth, breadth, members)
                out[0, j, s + h * breadth : s + (h + 1) * breadth, :] = value


def assemble(pieces, me, lats):
    local_slots = len(pieces)
    _, rows, _, members = pieces[0][0].shape
    owners = max(len(p) * p[0].shape[0] for p in pieces)
    slots = local_slots * owners
    flat = [block for slot in pieces for block in slot]
    moved = sum(len(p) > 1 for p in pieces)
    return call(
        functools.partial(assemble_kernel, [len(p) for p in pieces]),
        "assemble",
        2 * 256 * rows * lats * slots * members,
        4 * rows * lats * slots * members,
        out_shape=jax.ShapeDtypeStruct((rows, lats, slots, members), BF16),
        grid_spec=pltpu.PrefetchScalarGridSpec(
            num_scalar_prefetch=1,
            grid=(rows,),
            in_specs=[
                pl.BlockSpec((block.shape[0], 1, lats, members), lambda r, m: (0, r, 0, 0)) for block in flat
            ],
            out_specs=pl.BlockSpec((1, lats, slots, members), lambda r, m: (r, 0, 0, 0)),
            scratch_shapes=[pltpu.VMEM((owners, lats, members), BF16)] * moved,
        ),
    )(me, *flat)


def between_chips(messages):
    chips = len(messages)
    got = [messages[0]]
    for k in range(1, chips):
        got.append(lax.ppermute(messages[k], "wave", [(d, d ^ (k * CORES)) for d in range(chips * CORES)]))
    return got


def between_cores(blocks, owners):
    return lax.ppermute(blocks, "wave", [(d, d ^ 1) for d in range(owners)])


def to_all(blocks):
    return lax.all_to_all(blocks, "wave", split_axis=0, concat_axis=0, tiled=True)


def per_device(
    tendency, spectral_state, legendre, gauss_weights, block_inverses, pole_coeffs, wavenumbers
):
    rows, lats, slots, members = tendency.shape
    local_slots, nspec, nlat = legendre.shape
    owners = slots // local_slots
    me = lax.axis_index("wave").astype(jnp.int32).reshape(1)
    pole_index = lax.axis_index("pole")
    sign = (2 * pole_index - 1).astype(F32).reshape(1)
    gauss = jnp.broadcast_to(gauss_weights[:, None], (lats, members))
    received, tokens = [], []
    for slot in range(local_slots):
        permuted = slot in PERMUTED
        *blocks, token = weigh(tendency, gauss, me, slot, local_slots, permuted)
        tokens.append(token)
        received.append(between_chips(blocks) if permuted else [to_all(blocks[0])])

    here = sum_pairs(block_inverses, pole_coeffs, tokens[0])
    there = lax.ppermute(here, "pole", [(0, 1), (1, 0)])
    sent = []
    token = there
    for slot in range(local_slots):
        permuted = slot in PERMUTED
        low = nspec // 2 if slot % 2 else 0
        blocks = received[slot]
        if permuted:
            blocks = blocks + [between_cores(pick(blocks, me), owners)]
        forced = analyse(blocks, legendre, spectral_state, wavenumbers, me, token, slot, low, nspec // 2)
        other = lax.ppermute(forced, "pole", [(0, 1), (1, 0)])
        *blocks, token = synthesise(here, there, sign, forced, other, legendre, me, slot, low, lats, permuted)
        if permuted:
            sent.append(between_chips(pair(blocks[:-1], between_cores(blocks[-1], owners))))
        else:
            sent.append([to_all(blocks[0])])
    return assemble(sent, me, lats)


def solution(mesh):
    in_specs = (
        P("pole", "wave", None, None),
        P("pole", "wave", None, None),
        P("wave", None, None),
        P("wave"),
        P("pole", None, "wave", None),
        P("pole", None),
        P("wave"),
    )
    out_specs = P("pole", "wave", None, None)
    return jax.shard_map(
        per_device, mesh=mesh, in_specs=in_specs, out_specs=out_specs, check_vma=False
    )
```

```python
import functools
import math

import jax
import jax.numpy as jnp
from jax import lax
from jax.experimental import pallas as pl
from jax.experimental.pallas import tpu as pltpu
from jax.sharding import PartitionSpec as P

BF16 = jnp.bfloat16
F32 = jnp.float32
CORES = 2
PERMUTED = ()
ANYWHERE = pl.BlockSpec(memory_space=pl.ANY)
IN_SMEM = pl.BlockSpec(memory_space=pltpu.SMEM)
TOKEN = jax.ShapeDtypeStruct((8, 128), F32)


def call(kernel, name, flops, size, mib=40, **kwargs):
    return pl.pallas_call(
        kernel,
        name=name,
        compiler_params=pltpu.CompilerParams(vmem_limit_bytes=mib * 1024 * 1024),
        cost_estimate=pl.CostEstimate(flops=int(flops), bytes_accessed=int(size), transcendentals=0),
        **kwargs,
    )


def run_copies(copies):
    for copy in copies:
        copy.start()
    for copy in copies:
        copy.wait()


def owner_of(me, k, other):
    core = me % CORES
    return ((me // CORES) ^ k) * CORES + (CORES - 1 - core if other else core)


def swap_matrix(rows, columns, picked):
    width = rows * columns
    target = lax.broadcasted_iota(jnp.int32, (len(picked) * rows, width), 0)
    source = lax.broadcasted_iota(jnp.int32, (len(picked) * rows, width), 1)
    step = picked[1] - picked[0] if len(picked) > 1 else 1
    column = (target // rows) * step + picked[0]
    return (source == (target % rows) * columns + column).astype(BF16)


def weigh_kernel(slot, local_slots, permuted, waits, me_ref, gauss_ref, tendency_ref, *rest):
    _, lats, slots, members = tendency_ref.shape
    rest = rest[waits:]
    first = pl.program_id(1) * lats
    outs, blocks = (rest[:-1], rest[-1]) if permuted else (rest, None)
    outs, token_ref = outs[:-1], outs[-1]
    token_ref[...] = jnp.zeros_like(token_ref)
    depth, breadth = math.gcd(lats, 16), 16
    matrix = swap_matrix(depth, breadth, range(slot, breadth, local_slots))
    owners = breadth // local_slots
    for j in range(0, lats, depth):
        line = jnp.broadcast_to(gauss_ref[...], (depth, gauss_ref.shape[1]))
        here = lax.broadcasted_iota(jnp.int32, line.shape, 0) + (first + j)
        mine = lax.broadcasted_iota(jnp.int32, line.shape, 1) == here
        scale = jnp.sum(jnp.where(mine, line, 0.0), axis=1, keepdims=True)
        for s in range(0, slots, 2 * breadth):
            halves = [
                tendency_ref[0, j : j + depth, s + h : s + h + breadth, :].reshape(depth * breadth, members)
                for h in (0, breadth)
            ]
            turned = jnp.dot(matrix, jnp.concatenate(halves, axis=1), preferred_element_type=F32)
            for h in range(2):
                for i in range(owners):
                    value = turned[i * depth : (i + 1) * depth, h * members : (h + 1) * members]
                    owner = (s + h * breadth) // local_slots + i
                    value = (value * scale).astype(BF16)
                    if permuted:
                        blocks[owner, j : j + depth, :] = value
                    else:
                        outs[0][owner, 0, j : j + depth, :] = value
    if permuted:
        for k, out in enumerate(outs):
            for core in range(CORES):
                out[core, 0] = blocks[((me_ref[0] // CORES) ^ k) * CORES + core]


def lat_block(lats):
    return lats // 2 if lats % 32 == 0 else lats


def weigh(tendency, gauss, me, slot, local_slots, permuted, waits):
    rows, lats, slots, members = tendency.shape
    each = lat_block(lats)
    owners = slots // local_slots
    count, chips = (CORES, owners // CORES) if permuted else (owners, 1)
    piece = pl.BlockSpec((count, 1, each, members), lambda r, j, m: (0, r, j, 0))
    return call(
        functools.partial(weigh_kernel, slot, local_slots, permuted, len(waits)),
        "weigh",
        2 * 128 * tendency.size,
        3 * tendency.size,
        58,
        out_shape=[jax.ShapeDtypeStruct((count, rows, lats, members), BF16)] * chips + [TOKEN],
        grid_spec=pltpu.PrefetchScalarGridSpec(
            num_scalar_prefetch=1,
            grid=(rows, lats // each),
            in_specs=[
                pl.BlockSpec((1, lats), lambda r, j, m: (0, 0)),
                pl.BlockSpec((1, each, slots, members), lambda r, j, m: (r, j, 0, 0)),
            ]
            + [ANYWHERE] * len(waits),
            out_specs=[piece] * chips + [pl.BlockSpec(TOKEN.shape, lambda r, j, m: (0, 0))],
            scratch_shapes=[pltpu.VMEM((owners, each, members), BF16)] if permuted else [],
        ),
    )(me, gauss, tendency, *waits)


def pick_kernel(waits, me_ref, *rest):
    ins, out = rest[waits:-1], rest[-1]
    for k, ref in enumerate(ins):
        out[k] = ref[0]


def pick(messages, me, waits):
    _, rows, lats, members = messages[0].shape
    chips = len(messages)
    shape = (chips, rows, lats, members)
    return call(
        functools.partial(pick_kernel, len(waits)),
        "pick",
        0,
        4 * math.prod(shape),
        out_shape=jax.ShapeDtypeStruct(shape, BF16),
        grid_spec=pltpu.PrefetchScalarGridSpec(
            num_scalar_prefetch=1,
            grid=(rows,),
            in_specs=[ANYWHERE] * len(waits)
            + [
                pl.BlockSpec((1, 1, lats, members), lambda r, m: (CORES - 1 - m[0] % CORES, r, 0, 0))
            ]
            * chips,
            out_specs=pl.BlockSpec((chips, 1, lats, members), lambda r, m: (0, r, 0, 0)),
        ),
    )(me, *waits, *messages)


def pair_kernel(mate_ref, *rest):
    chips = mate_ref.shape[0]
    outs, sems = rest[chips:-1], rest[-1]
    run_copies([pltpu.make_async_copy(mate_ref.at[k], out.at[1], sems.at[k]) for k, out in enumerate(outs)])


def pair(messages, mate):
    chips = len(messages)
    return call(
        pair_kernel,
        "pair",
        0,
        4 * mate.size,
        out_shape=[jax.ShapeDtypeStruct(m.shape, m.dtype) for m in messages],
        in_specs=[pl.BlockSpec(mate.shape, lambda: (0, 0, 0, 0))] + [ANYWHERE] * chips,
        out_specs=[ANYWHERE] * chips,
        scratch_shapes=[pltpu.SemaphoreType.DMA((chips,))],
        input_output_aliases={k + 1: k for k in range(chips)},
    )(mate, *messages)


def analyse_kernel(slot, low, count, me_ref, wave_ref, token_ref, table_ref, state_ref, *rest):
    blocks, out, grid, sems = rest[:count], rest[count], rest[count + 1], rest[count + 2]
    rows, members, _ = out.shape
    owners, lats, _ = grid.shape
    width = table_ref.shape[1]
    step = pl.program_id(0)

    @pl.when(step == 0)
    def _():
        copies = []
        for r in range(rows):
            lanes = pl.ds(r * members, members)
            if count == 1:
                copies.append(pltpu.make_async_copy(blocks[0].at[:, r], grid.at[:, :, lanes], sems.at[0, r]))
            for k in range(count - 1):
                for other in range(CORES):
                    target = grid.at[owner_of(me_ref[0], k, other), :, lanes]
                    source = blocks[-1].at[k, r] if other else blocks[k].at[me_ref[0] % CORES, r]
                    copies.append(pltpu.make_async_copy(source, target, sems.at[CORES * k + other, r]))
        run_copies(copies)

    field = grid[...].reshape(owners * lats, rows * members)
    sums = jnp.dot(table_ref[0], field, preferred_element_type=F32)
    degree = lax.broadcasted_iota(jnp.int32, (members, width), 1) + (low + step * width)
    live = degree >= wave_ref[slot]
    for r in range(rows):
        total = state_ref[r, 0].astype(F32) + sums[:, r * members : (r + 1) * members].T
        out[r] = jnp.where(live, total, 0.0).astype(BF16)


def analyse(blocks, table, state, wave, me, token, slot, low, width):
    _, rows, lats, members = blocks[0].shape
    nspec, nlat = table.shape[1:]
    owners = nlat // lats
    first = low // width
    if lats % 16:
        blocks = [lay_in_place(blocks, me[0], owners)]
        blocks[0] = jnp.transpose(blocks[0], (1, 0, 2, 3)).reshape(1, rows, nlat, members)
        owners, lats = 1, nlat
    return call(
        functools.partial(analyse_kernel, slot, low, len(blocks)),
        "analyse",
        2 * (nspec - low) * nlat * rows * members,
        2 * (nspec - low) * nlat,
        out_shape=jax.ShapeDtypeStruct((rows, members, nspec - low), BF16),
        grid=((nspec - low) // width,),
        in_specs=[
            IN_SMEM,
            IN_SMEM,
            ANYWHERE,
            pl.BlockSpec((1, width, nlat), lambda i: (slot, first + i, 0)),
            pl.BlockSpec((rows, 1, members, width), lambda i: (0, slot, 0, first + i)),
        ]
        + [ANYWHERE] * len(blocks),
        out_specs=pl.BlockSpec((rows, members, width), lambda i: (0, 0, i)),
        scratch_shapes=[
            pltpu.VMEM((owners, lats, rows * members), BF16),
            pltpu.SemaphoreType.DMA((owners, rows)),
        ],
    )(me, wave, token, table, state, *blocks)


def lay_in_place(blocks, here, owners):
    if len(blocks) == 1:
        return blocks[0]
    own = [lax.dynamic_index_in_dim(m, here % CORES, 0, keepdims=False) for m in blocks[:-1]]
    both = jnp.stack([jnp.stack(own), blocks[-1]], axis=1).reshape((owners,) + own[0].shape)
    order = jnp.arange(owners, dtype=jnp.int32)
    order = ((order // CORES) ^ (here // CORES)) * CORES + (order % CORES ^ here % CORES)
    return jnp.take(both, order, axis=0)


def sum_pairs_kernel(coeff_ref, token_ref, inverse_ref, out_ref):
    pairs, entries = inverse_ref.shape[:2]
    half = entries // 2

    def one(entry, carry):
        real = imag = 0.0
        for k in range(pairs):
            first, second = inverse_ref[k, entry].astype(F32), inverse_ref[k, half + entry].astype(F32)
            a, b = coeff_ref[k, 0], coeff_ref[k, 1]
            real = real + (a * first - b * second)
            imag = imag + (a * second + b * first)
        out_ref[entry] = real
        out_ref[half + entry] = imag
        return carry

    lax.fori_loop(0, half, one, 0)


def sum_pairs(block_inverses, pole_coeffs, token):
    return call(
        sum_pairs_kernel,
        "sum_pairs",
        4 * block_inverses.size,
        2 * block_inverses.size,
        out_shape=jax.ShapeDtypeStruct(block_inverses.shape[1:], F32),
        in_specs=[IN_SMEM, ANYWHERE, pl.BlockSpec(block_inverses.shape, lambda: (0, 0, 0, 0))],
        out_specs=pl.BlockSpec(block_inverses.shape[1:], lambda: (0, 0, 0)),
    )(pole_coeffs, token, block_inverses)


def synthesise_kernel(slot, low, permuted, me_ref, sign_ref, here_ref, there_ref, own_ref, other_ref, table_ref, *rest):
    rows, members, _ = own_ref.shape
    width = table_ref.shape[2]
    step = pl.program_id(0)
    outs, token_ref, mixed = rest[: permuted + 1], rest[permuted + 1], rest[permuted + 2]

    @pl.when(step == 0)
    def _():
        token_ref[...] = jnp.zeros_like(token_ref)

        def line(entry):
            return here_ref[entry, slot : slot + 1, low:] + there_ref[entry, slot : slot + 1, low:]

        for f in range(rows):
            total = 0.0
            for g in range(rows):
                total = total + line(f * rows + g) * own_ref[g].astype(F32)
                total = total + sign_ref[0] * line(rows * rows + f * rows + g) * other_ref[g].astype(F32)
            mixed[f * members : (f + 1) * members, :] = total.astype(BF16)

    sums = jnp.dot(mixed[...], table_ref[0], preferred_element_type=F32)
    grid = rest[permuted + 3] if permuted else outs[0]
    lats = grid.shape[2]
    each = width // lats
    for r in range(rows):
        turned = sums[r * members : (r + 1) * members, :].T.reshape(each, lats, members).astype(BF16)
        if permuted:
            grid[pl.ds(step * each, each), r] = turned
        else:
            grid[:, r] = turned

    if permuted:
        sems = rest[-1]

        @pl.when(step == pl.num_programs(0) - 1)
        def _():
            copies = []
            for k in range(permuted):
                for other in range(CORES):
                    source = grid.at[owner_of(me_ref[0], k, other)]
                    target = outs[-1].at[k] if other else outs[k].at[0]
                    copies.append(pltpu.make_async_copy(source, target, sems.at[k, other]))
            run_copies(copies)


def synthesise(here, there, sign, own, other, table, me, slot, low, lats, permuted):
    rows, members, count = own.shape
    nlat = table.shape[2]
    owners = nlat // lats
    width = math.lcm(lats, 128)
    chips = owners // CORES if permuted else 0
    matrix = pl.BlockSpec(here.shape, lambda j: (0, 0, 0))
    whole = pl.BlockSpec((rows, members, count), lambda j: (0, 0, 0))
    shapes = [jax.ShapeDtypeStruct((owners, rows, lats, members), BF16)]
    specs = [pl.BlockSpec((width // lats, rows, lats, members), lambda j: (j, 0, 0, 0))]
    scratch = [pltpu.VMEM((rows * members, count), BF16)]
    if permuted:
        shapes = [jax.ShapeDtypeStruct((CORES, rows, lats, members), BF16)] * chips
        shapes += [jax.ShapeDtypeStruct((chips, rows, lats, members), BF16)]
        specs = [ANYWHERE] * (chips + 1)
        scratch += [pltpu.VMEM((owners, rows, lats, members), BF16), pltpu.SemaphoreType.DMA((chips, CORES))]
    return call(
        functools.partial(synthesise_kernel, slot, low, chips),
        "synthesise",
        2 * count * nlat * rows * members,
        2 * count * nlat,
        out_shape=shapes + [TOKEN],
        grid=(nlat // width,),
        in_specs=[
            IN_SMEM,
            IN_SMEM,
            matrix,
            matrix,
            whole,
            whole,
            pl.BlockSpec((1, count, width), lambda j: (slot, low // count, j)),
        ],
        out_specs=specs + [pl.BlockSpec(TOKEN.shape, lambda j: (0, 0))],
        scratch_shapes=scratch,
    )(me, sign, here, there, own, other, table)


def assemble_kernel(counts, me_ref, *rest):
    ins, out, blocks = rest[: sum(counts)], rest[sum(counts)], rest[sum(counts) + 1 :]
    _, lats, slots, members = out.shape
    local_slots = len(counts)
    views, used, spare = [], 0, 0
    for count in counts:
        refs = ins[used : used + count]
        used += count
        if count == 1:
            views.append(lambda owner, j, ref=refs[0]: ref[owner, 0, j, :])
            continue
        for k, ref in enumerate(refs):
            for other in range(CORES):
                blocks[spare][owner_of(me_ref[0], k, other)] = ref[other, 0]
        views.append(lambda owner, j, ref=blocks[spare]: ref[owner, j, :])
        spare += 1
    depth, breadth = math.gcd(lats, 16), 16
    matrix = swap_matrix(breadth, depth, range(depth))
    for start in range(0, lats, depth):
        j = slice(start, start + depth)
        for s in range(0, slots, 2 * breadth):
            halves = [
                jnp.concatenate(
                    [views[i % local_slots](i // local_slots, j) for i in range(s + h, s + h + breadth)], axis=0
                )
                for h in (0, breadth)
            ]
            turned = jnp.dot(matrix, jnp.concatenate(halves, axis=1), preferred_element_type=F32).astype(BF16)
            for h in range(2):
                value = turned[:, h * members : (h + 1) * members].reshape(depth, breadth, members)
                out[0, j, s + h * breadth : s + (h + 1) * breadth, :] = value


def assemble(pieces, me, lats):
    local_slots = len(pieces)
    _, rows, _, members = pieces[0][0].shape
    owners = max(len(p) * p[0].shape[0] for p in pieces)
    slots = local_slots * owners
    each = lat_block(lats)
    flat = [block for slot in pieces for block in slot]
    moved = sum(len(p) > 1 for p in pieces)
    return call(
        functools.partial(assemble_kernel, [len(p) for p in pieces]),
        "assemble",
        2 * 256 * rows * lats * slots * members,
        4 * rows * lats * slots * members,
        out_shape=jax.ShapeDtypeStruct((rows, lats, slots, members), BF16),
        grid_spec=pltpu.PrefetchScalarGridSpec(
            num_scalar_prefetch=1,
            grid=(rows, lats // each),
            in_specs=[
                pl.BlockSpec((block.shape[0], 1, each, members), lambda r, j, m: (0, r, j, 0)) for block in flat
            ],
            out_specs=pl.BlockSpec((1, each, slots, members), lambda r, j, m: (r, j, 0, 0)),
            scratch_shapes=[pltpu.VMEM((owners, each, members), BF16)] * moved,
        ),
    )(me, *flat)


def between_chips(messages):
    chips = len(messages)
    got = [messages[0]]
    for k in range(1, chips):
        got.append(lax.ppermute(messages[k], "wave", [(d, d ^ (k * CORES)) for d in range(chips * CORES)]))
    return got


def between_cores(blocks, owners):
    return lax.ppermute(blocks, "wave", [(d, d ^ 1) for d in range(owners)])


def to_all(blocks):
    return lax.all_to_all(blocks, "wave", split_axis=0, concat_axis=0, tiled=True)


def per_device(
    tendency, spectral_state, legendre, gauss_weights, block_inverses, pole_coeffs, wavenumbers
):
    rows, lats, slots, members = tendency.shape
    local_slots, nspec, nlat = legendre.shape
    owners = slots // local_slots
    me = lax.axis_index("wave").astype(jnp.int32).reshape(1)
    pole_index = lax.axis_index("pole")
    sign = (2 * pole_index - 1).astype(F32).reshape(1)
    received, waits = [], []
    for slot in range(local_slots):
        permuted = slot in PERMUTED
        *blocks, token = weigh(tendency, gauss_weights[None], me, slot, local_slots, permuted, waits)
        received.append(between_chips(blocks) if permuted else [to_all(blocks[0])])
        if slot == 0:
            here = sum_pairs(block_inverses, pole_coeffs, token)
            there = lax.ppermute(here, "pole", [(0, 1), (1, 0)])
            waits = [here if permuted else there]

    sent = []
    for slot in range(local_slots):
        permuted = slot in PERMUTED
        low = nspec // 2 if slot % 2 else 0
        blocks = received[slot]
        if permuted:
            blocks = blocks + [between_cores(pick(blocks, me, [token, there]), owners)]
        forced = analyse(blocks, legendre, spectral_state, wavenumbers, me, token, slot, low, nspec // 2)
        other = lax.ppermute(forced, "pole", [(0, 1), (1, 0)])
        *blocks, token = synthesise(here, there, sign, forced, other, legendre, me, slot, low, lats, permuted)
        if permuted:
            sent.append(between_chips(pair(blocks[:-1], between_cores(blocks[-1], owners))))
        else:
            sent.append([to_all(blocks[0])])
    return assemble(sent, me, lats)


def solution(mesh):
    in_specs = (
        P("pole", "wave", None, None),
        P("pole", "wave", None, None),
        P("wave", None, None),
        P("wave"),
        P("pole", None, "wave", None),
        P("pole", None),
        P("wave"),
    )
    out_specs = P("pole", "wave", None, None)
    return jax.shard_map(
        per_device, mesh=mesh, in_specs=in_specs, out_specs=out_specs, check_vma=False
    )
```

```python
import functools
import math

import jax
import jax.numpy as jnp
import numpy as np
from jax import lax
from jax.experimental import pallas as pl
from jax.experimental.pallas import tpu as pltpu
from jax.sharding import PartitionSpec as P

BF16 = jnp.bfloat16
F32 = jnp.float32
CORES = 2
PERMUTED = (0, 1)
ANYWHERE = pl.BlockSpec(memory_space=pl.ANY)
IN_SMEM = pl.BlockSpec(memory_space=pltpu.SMEM)
TOKEN = jax.ShapeDtypeStruct((8, 128), F32)


def call(kernel, name, flops, size, mib=40, **kwargs):
    return pl.pallas_call(
        kernel,
        name=name,
        compiler_params=pltpu.CompilerParams(vmem_limit_bytes=mib * 1024 * 1024),
        cost_estimate=pl.CostEstimate(flops=int(flops), bytes_accessed=int(size), transcendentals=0),
        **kwargs,
    )


def run_copies(copies):
    for copy in copies:
        copy.start()
    for copy in copies:
        copy.wait()


def owner_of(me, k, other):
    core = me % CORES
    return ((me // CORES) ^ k) * CORES + (CORES - 1 - core if other else core)


def swap_matrix(rows, columns, picked):
    matrix = np.zeros((len(picked), rows, rows, columns), np.float32)
    for i, c in enumerate(picked):
        matrix[i, np.arange(rows), np.arange(rows), c] = 1.0
    return jnp.asarray(matrix.reshape(len(picked) * rows, rows * columns), BF16)


def weigh_kernel(slot, local_slots, permuted, waits, me_ref, matrix_ref, gauss_ref, tendency_ref, *rest):
    _, lats, slots, members = tendency_ref.shape
    rest, column = rest[waits:-1], rest[-1]
    first = pl.program_id(1) * lats
    outs, blocks = (rest[:-1], rest[-1]) if permuted else (rest, None)
    outs, token_ref = outs[:-1], outs[-1]
    token_ref[...] = jnp.zeros_like(token_ref)
    depth, breadth = math.gcd(lats, 16), 16
    matrix = matrix_ref[...]
    owners = breadth // local_slots

    @pl.when((pl.program_id(0) == 0) & (pl.program_id(1) == 0))
    def _():
        total = gauss_ref.shape[1]
        for j in range(0, total, depth):
            line = jnp.broadcast_to(gauss_ref[...], (depth, total))
            here = lax.broadcasted_iota(jnp.int32, line.shape, 0) + j
            mine = lax.broadcasted_iota(jnp.int32, line.shape, 1) == here
            value = jnp.sum(jnp.where(mine, line, 0.0), axis=1, keepdims=True)
            column[j : j + depth, :] = jnp.broadcast_to(value, (depth, members))

    for j in range(0, lats, depth):
        scale = column[pl.ds(pl.multiple_of(first + j, depth), depth), :]
        for s in range(0, slots, 2 * breadth):
            halves = [
                tendency_ref[0, j : j + depth, s + h : s + h + breadth, :].reshape(depth * breadth, members)
                for h in (0, breadth)
            ]
            turned = jnp.dot(matrix, jnp.concatenate(halves, axis=1), preferred_element_type=F32)
            for h in range(2):
                for i in range(owners):
                    value = turned[i * depth : (i + 1) * depth, h * members : (h + 1) * members]
                    owner = (s + h * breadth) // local_slots + i
                    value = (value * scale).astype(BF16)
                    if permuted:
                        blocks[owner, j : j + depth, :] = value
                    else:
                        outs[0][owner, 0, j : j + depth, :] = value
    if permuted:
        for k, out in enumerate(outs):
            for core in range(CORES):
                out[core, 0] = blocks[((me_ref[0] // CORES) ^ k) * CORES + core]


def lat_block(lats):
    return lats // 2 if lats % 32 == 0 else lats


def weigh(tendency, gauss, me, slot, local_slots, permuted, waits):
    rows, lats, slots, members = tendency.shape
    each = lat_block(lats)
    matrix = swap_matrix(math.gcd(each, 16), 16, range(slot, 16, local_slots))
    owners = slots // local_slots
    count, chips = (CORES, owners // CORES) if permuted else (owners, 1)
    piece = pl.BlockSpec((count, 1, each, members), lambda r, j, m: (0, r, j, 0))
    return call(
        functools.partial(weigh_kernel, slot, local_slots, permuted, len(waits)),
        "weigh",
        2 * 128 * tendency.size,
        3 * tendency.size,
        58,
        out_shape=[jax.ShapeDtypeStruct((count, rows, lats, members), BF16)] * chips + [TOKEN],
        grid_spec=pltpu.PrefetchScalarGridSpec(
            num_scalar_prefetch=1,
            grid=(rows, lats // each),
            in_specs=[
                pl.BlockSpec(matrix.shape, lambda r, j, m: (0, 0)),
                pl.BlockSpec((1, lats), lambda r, j, m: (0, 0)),
                pl.BlockSpec((1, each, slots, members), lambda r, j, m: (r, j, 0, 0)),
            ]
            + [ANYWHERE] * len(waits),
            out_specs=[piece] * chips + [pl.BlockSpec(TOKEN.shape, lambda r, j, m: (0, 0))],
            scratch_shapes=([pltpu.VMEM((owners, each, members), BF16)] if permuted else [])
            + [pltpu.VMEM((lats, members), F32)],
        ),
    )(me, matrix, gauss, tendency, *waits)


def pick_kernel(waits, me_ref, *rest):
    ins, out = rest[waits:-1], rest[-1]
    for k, ref in enumerate(ins):
        out[k] = ref[0]


def pick(messages, me, waits):
    _, rows, lats, members = messages[0].shape
    chips = len(messages)
    shape = (chips, rows, lats, members)
    return call(
        functools.partial(pick_kernel, len(waits)),
        "pick",
        0,
        4 * math.prod(shape),
        out_shape=jax.ShapeDtypeStruct(shape, BF16),
        grid_spec=pltpu.PrefetchScalarGridSpec(
            num_scalar_prefetch=1,
            grid=(rows,),
            in_specs=[ANYWHERE] * len(waits)
            + [
                pl.BlockSpec((1, 1, lats, members), lambda r, m: (CORES - 1 - m[0] % CORES, r, 0, 0))
            ]
            * chips,
            out_specs=pl.BlockSpec((chips, 1, lats, members), lambda r, m: (0, r, 0, 0)),
        ),
    )(me, *waits, *messages)


def pair_kernel(mate_ref, *rest):
    chips = mate_ref.shape[0]
    outs, sems = rest[chips:-1], rest[-1]
    run_copies([pltpu.make_async_copy(mate_ref.at[k], out.at[1], sems.at[k]) for k, out in enumerate(outs)])


def pair(messages, mate):
    chips = len(messages)
    return call(
        pair_kernel,
        "pair",
        0,
        4 * mate.size,
        out_shape=[jax.ShapeDtypeStruct(m.shape, m.dtype) for m in messages],
        in_specs=[pl.BlockSpec(mate.shape, lambda: (0, 0, 0, 0))] + [ANYWHERE] * chips,
        out_specs=[ANYWHERE] * chips,
        scratch_shapes=[pltpu.SemaphoreType.DMA((chips,))],
        input_output_aliases={k + 1: k for k in range(chips)},
    )(mate, *messages)


def analyse_kernel(slot, low, count, me_ref, wave_ref, token_ref, table_ref, state_ref, *rest):
    blocks, out, grid, sems = rest[:count], rest[count], rest[count + 1], rest[count + 2]
    rows, members, _ = out.shape
    owners, lats, _ = grid.shape
    width = table_ref.shape[1]
    step = pl.program_id(0)

    @pl.when(step == 0)
    def _():
        copies = []
        for r in range(rows):
            lanes = pl.ds(r * members, members)
            if count == 1:
                copies.append(pltpu.make_async_copy(blocks[0].at[:, r], grid.at[:, :, lanes], sems.at[0, r]))
            for k in range(count - 1):
                for other in range(CORES):
                    target = grid.at[owner_of(me_ref[0], k, other), :, lanes]
                    source = blocks[-1].at[k, r] if other else blocks[k].at[me_ref[0] % CORES, r]
                    copies.append(pltpu.make_async_copy(source, target, sems.at[CORES * k + other, r]))
        run_copies(copies)

    field = grid[...].reshape(owners * lats, rows * members)
    sums = jnp.dot(table_ref[0], field, preferred_element_type=F32)
    degree = lax.broadcasted_iota(jnp.int32, (members, width), 1) + (low + step * width)
    live = degree >= wave_ref[slot]
    for r in range(rows):
        total = state_ref[r, 0].astype(F32) + sums[:, r * members : (r + 1) * members].T
        out[r] = jnp.where(live, total, 0.0).astype(BF16)


def analyse(blocks, table, state, wave, me, token, slot, low, width):
    _, rows, lats, members = blocks[0].shape
    nspec, nlat = table.shape[1:]
    owners = nlat // lats
    first = low // width
    if lats % 16:
        blocks = [lay_in_place(blocks, me[0], owners)]
        blocks[0] = jnp.transpose(blocks[0], (1, 0, 2, 3)).reshape(1, rows, nlat, members)
        owners, lats = 1, nlat
    return call(
        functools.partial(analyse_kernel, slot, low, len(blocks)),
        "analyse",
        2 * (nspec - low) * nlat * rows * members,
        2 * (nspec - low) * nlat,
        out_shape=jax.ShapeDtypeStruct((rows, members, nspec - low), BF16),
        grid=((nspec - low) // width,),
        in_specs=[
            IN_SMEM,
            IN_SMEM,
            ANYWHERE,
            pl.BlockSpec((1, width, nlat), lambda i: (slot, first + i, 0)),
            pl.BlockSpec((rows, 1, members, width), lambda i: (0, slot, 0, first + i)),
        ]
        + [ANYWHERE] * len(blocks),
        out_specs=pl.BlockSpec((rows, members, width), lambda i: (0, 0, i)),
        scratch_shapes=[
            pltpu.VMEM((owners, lats, rows * members), BF16),
            pltpu.SemaphoreType.DMA((owners, rows)),
        ],
    )(me, wave, token, table, state, *blocks)


def lay_in_place(blocks, here, owners):
    if len(blocks) == 1:
        return blocks[0]
    own = [lax.dynamic_index_in_dim(m, here % CORES, 0, keepdims=False) for m in blocks[:-1]]
    both = jnp.stack([jnp.stack(own), blocks[-1]], axis=1).reshape((owners,) + own[0].shape)
    order = jnp.arange(owners, dtype=jnp.int32)
    order = ((order // CORES) ^ (here // CORES)) * CORES + (order % CORES ^ here % CORES)
    return jnp.take(both, order, axis=0)


def sum_pairs_kernel(coeff_ref, token_ref, inverse_ref, out_ref):
    pairs, entries = inverse_ref.shape[:2]
    half = entries // 2

    def one(entry, carry):
        real = imag = 0.0
        for k in range(pairs):
            first, second = inverse_ref[k, entry].astype(F32), inverse_ref[k, half + entry].astype(F32)
            a, b = coeff_ref[k, 0], coeff_ref[k, 1]
            real = real + (a * first - b * second)
            imag = imag + (a * second + b * first)
        out_ref[entry] = real
        out_ref[half + entry] = imag
        return carry

    lax.fori_loop(0, half, one, 0)


def sum_pairs(block_inverses, pole_coeffs, token):
    return call(
        sum_pairs_kernel,
        "sum_pairs",
        4 * block_inverses.size,
        2 * block_inverses.size,
        out_shape=jax.ShapeDtypeStruct(block_inverses.shape[1:], F32),
        in_specs=[IN_SMEM, ANYWHERE, pl.BlockSpec(block_inverses.shape, lambda: (0, 0, 0, 0))],
        out_specs=pl.BlockSpec(block_inverses.shape[1:], lambda: (0, 0, 0)),
    )(pole_coeffs, token, block_inverses)


def synthesise_kernel(slot, low, permuted, me_ref, sign_ref, here_ref, there_ref, own_ref, other_ref, table_ref, *rest):
    rows, members, _ = own_ref.shape
    width = table_ref.shape[2]
    step = pl.program_id(0)
    outs, token_ref, mixed = rest[: permuted + 1], rest[permuted + 1], rest[permuted + 2]

    @pl.when(step == 0)
    def _():
        token_ref[...] = jnp.zeros_like(token_ref)

        def line(entry):
            return here_ref[entry, slot : slot + 1, low:] + there_ref[entry, slot : slot + 1, low:]

        for f in range(rows):
            total = 0.0
            for g in range(rows):
                total = total + line(f * rows + g) * own_ref[g].astype(F32)
                total = total + sign_ref[0] * line(rows * rows + f * rows + g) * other_ref[g].astype(F32)
            mixed[f * members : (f + 1) * members, :] = total.astype(BF16)

    sums = jnp.dot(mixed[...], table_ref[0], preferred_element_type=F32)
    grid = rest[permuted + 3] if permuted else outs[0]
    lats = grid.shape[2]
    each = width // lats
    for r in range(rows):
        turned = sums[r * members : (r + 1) * members, :].T.reshape(each, lats, members).astype(BF16)
        if permuted:
            grid[pl.ds(step * each, each), r] = turned
        else:
            grid[:, r] = turned

    if permuted:
        sems = rest[-1]

        @pl.when(step == pl.num_programs(0) - 1)
        def _():
            copies = []
            for k in range(permuted):
                for other in range(CORES):
                    source = grid.at[owner_of(me_ref[0], k, other)]
                    target = outs[-1].at[k] if other else outs[k].at[0]
                    copies.append(pltpu.make_async_copy(source, target, sems.at[k, other]))
            run_copies(copies)


def synthesise(here, there, sign, own, other, table, me, slot, low, lats, permuted):
    rows, members, count = own.shape
    nlat = table.shape[2]
    owners = nlat // lats
    width = math.lcm(lats, 128)
    chips = owners // CORES if permuted else 0
    matrix = pl.BlockSpec(here.shape, lambda j: (0, 0, 0))
    whole = pl.BlockSpec((rows, members, count), lambda j: (0, 0, 0))
    shapes = [jax.ShapeDtypeStruct((owners, rows, lats, members), BF16)]
    specs = [pl.BlockSpec((width // lats, rows, lats, members), lambda j: (j, 0, 0, 0))]
    scratch = [pltpu.VMEM((rows * members, count), BF16)]
    if permuted:
        shapes = [jax.ShapeDtypeStruct((CORES, rows, lats, members), BF16)] * chips
        shapes += [jax.ShapeDtypeStruct((chips, rows, lats, members), BF16)]
        specs = [ANYWHERE] * (chips + 1)
        scratch += [pltpu.VMEM((owners, rows, lats, members), BF16), pltpu.SemaphoreType.DMA((chips, CORES))]
    return call(
        functools.partial(synthesise_kernel, slot, low, chips),
        "synthesise",
        2 * count * nlat * rows * members,
        2 * count * nlat,
        out_shape=shapes + [TOKEN],
        grid=(nlat // width,),
        in_specs=[
            IN_SMEM,
            IN_SMEM,
            matrix,
            matrix,
            whole,
            whole,
            pl.BlockSpec((1, count, width), lambda j: (slot, low // count, j)),
        ],
        out_specs=specs + [pl.BlockSpec(TOKEN.shape, lambda j: (0, 0))],
        scratch_shapes=scratch,
    )(me, sign, here, there, own, other, table)


def assemble_kernel(counts, me_ref, matrix_ref, *rest):
    ins, out, blocks = rest[: sum(counts)], rest[sum(counts)], rest[sum(counts) + 1 :]
    _, lats, slots, members = out.shape
    local_slots = len(counts)
    views, used, spare = [], 0, 0
    for count in counts:
        refs = ins[used : used + count]
        used += count
        if count == 1:
            views.append(lambda owner, j, ref=refs[0]: ref[owner, 0, j, :])
            continue
        for k, ref in enumerate(refs):
            for other in range(CORES):
                blocks[spare][owner_of(me_ref[0], k, other)] = ref[other, 0]
        views.append(lambda owner, j, ref=blocks[spare]: ref[owner, j, :])
        spare += 1
    depth, breadth = math.gcd(lats, 16), 16
    matrix = matrix_ref[...]
    for start in range(0, lats, depth):
        j = slice(start, start + depth)
        for s in range(0, slots, 2 * breadth):
            halves = [
                jnp.concatenate(
                    [views[i % local_slots](i // local_slots, j) for i in range(s + h, s + h + breadth)], axis=0
                )
                for h in (0, breadth)
            ]
            turned = jnp.dot(matrix, jnp.concatenate(halves, axis=1), preferred_element_type=F32).astype(BF16)
            for h in range(2):
                value = turned[:, h * members : (h + 1) * members].reshape(depth, breadth, members)
                out[0, j, s + h * breadth : s + (h + 1) * breadth, :] = value


def assemble(pieces, me, lats):
    local_slots = len(pieces)
    _, rows, _, members = pieces[0][0].shape
    owners = max(len(p) * p[0].shape[0] for p in pieces)
    slots = local_slots * owners
    each = lat_block(lats)
    matrix = swap_matrix(16, math.gcd(each, 16), range(math.gcd(each, 16)))
    flat = [block for slot in pieces for block in slot]
    moved = sum(len(p) > 1 for p in pieces)
    return call(
        functools.partial(assemble_kernel, [len(p) for p in pieces]),
        "assemble",
        2 * 256 * rows * lats * slots * members,
        4 * rows * lats * slots * members,
        out_shape=jax.ShapeDtypeStruct((rows, lats, slots, members), BF16),
        grid_spec=pltpu.PrefetchScalarGridSpec(
            num_scalar_prefetch=1,
            grid=(rows, lats // each),
            in_specs=[pl.BlockSpec(matrix.shape, lambda r, j, m: (0, 0))]
            + [
                pl.BlockSpec((block.shape[0], 1, each, members), lambda r, j, m: (0, r, j, 0)) for block in flat
            ],
            out_specs=pl.BlockSpec((1, each, slots, members), lambda r, j, m: (r, j, 0, 0)),
            scratch_shapes=[pltpu.VMEM((owners, each, members), BF16)] * moved,
        ),
    )(me, matrix, *flat)


def between_chips(messages):
    chips = len(messages)
    got = [messages[0]]
    for k in range(1, chips):
        got.append(lax.ppermute(messages[k], "wave", [(d, d ^ (k * CORES)) for d in range(chips * CORES)]))
    return got


def between_cores(blocks, owners):
    return lax.ppermute(blocks, "wave", [(d, d ^ 1) for d in range(owners)])


def to_all(blocks):
    return lax.all_to_all(blocks, "wave", split_axis=0, concat_axis=0, tiled=True)


def per_device(
    tendency, spectral_state, legendre, gauss_weights, block_inverses, pole_coeffs, wavenumbers
):
    rows, lats, slots, members = tendency.shape
    local_slots, nspec, nlat = legendre.shape
    owners = slots // local_slots
    me = lax.axis_index("wave").astype(jnp.int32).reshape(1)
    pole_index = lax.axis_index("pole")
    sign = (2 * pole_index - 1).astype(F32).reshape(1)
    received, waits = [], []
    for slot in range(local_slots):
        permuted = slot in PERMUTED
        *blocks, token = weigh(tendency, gauss_weights[None], me, slot, local_slots, permuted, waits)
        received.append(between_chips(blocks) if permuted else [to_all(blocks[0])])
        if slot == 0:
            here = sum_pairs(block_inverses, pole_coeffs, token)
            there = lax.ppermute(here, "pole", [(0, 1), (1, 0)])
            waits = [here if permuted else there]

    sent = []
    for slot in range(local_slots):
        permuted = slot in PERMUTED
        low = nspec // 2 if slot % 2 else 0
        blocks = received[slot]
        if permuted:
            blocks = blocks + [between_cores(pick(blocks, me, [token, there]), owners)]
        forced = analyse(blocks, legendre, spectral_state, wavenumbers, me, token, slot, low, nspec // 2)
        other = lax.ppermute(forced, "pole", [(0, 1), (1, 0)])
        *blocks, token = synthesise(here, there, sign, forced, other, legendre, me, slot, low, lats, permuted)
        if permuted:
            sent.append(between_chips(pair(blocks[:-1], between_cores(blocks[-1], owners))))
        else:
            sent.append([to_all(blocks[0])])
    return assemble(sent, me, lats)


def solution(mesh):
    in_specs = (
        P("pole", "wave", None, None),
        P("pole", "wave", None, None),
        P("wave", None, None),
        P("wave"),
        P("pole", None, "wave", None),
        P("pole", None),
        P("wave"),
    )
    out_specs = P("pole", "wave", None, None)
    return jax.shard_map(
        per_device, mesh=mesh, in_specs=in_specs, out_specs=out_specs, check_vma=False
    )
```

```python
import functools
import math

import jax
import jax.numpy as jnp
import numpy as np
from jax import lax
from jax.experimental import pallas as pl
from jax.experimental.pallas import tpu as pltpu
from jax.sharding import PartitionSpec as P

BF16 = jnp.bfloat16
F32 = jnp.float32
CORES = 2
ANYWHERE = pl.BlockSpec(memory_space=pl.ANY)
IN_SMEM = pl.BlockSpec(memory_space=pltpu.SMEM)
TOKEN = jax.ShapeDtypeStruct((8, 128), F32)


def call(kernel, name, flops, size, mib=40, **kwargs):
    return pl.pallas_call(
        kernel,
        name=name,
        compiler_params=pltpu.CompilerParams(vmem_limit_bytes=mib * 1024 * 1024),
        cost_estimate=pl.CostEstimate(flops=int(flops), bytes_accessed=int(size), transcendentals=0),
        **kwargs,
    )


def run_copies(copies):
    for copy in copies:
        copy.start()
    for copy in copies:
        copy.wait()


def owner_of(me, k, other):
    core = me % CORES
    return ((me // CORES) ^ k) * CORES + (CORES - 1 - core if other else core)


def partners(chips):
    return [0] + list(range(chips // 2, chips)) + list(range(1, chips // 2))


def swap_matrix(rows, columns, picked):
    matrix = np.zeros((len(picked), rows, rows, columns), np.float32)
    for i, c in enumerate(picked):
        matrix[i, np.arange(rows), np.arange(rows), c] = 1.0
    return jnp.asarray(matrix.reshape(len(picked) * rows, rows * columns), BF16)


def weigh_kernel(slot, local_slots, permuted, waits, me_ref, matrix_ref, gauss_ref, tendency_ref, *rest):
    _, lats, slots, members = tendency_ref.shape
    rest, column = rest[waits:-1], rest[-1]
    first = pl.program_id(1) * lats
    outs, blocks = (rest[:-1], rest[-1]) if permuted else (rest, None)
    outs, token_ref = outs[:-1], outs[-1]
    token_ref[...] = jnp.zeros_like(token_ref)
    depth, breadth = math.gcd(lats, 16), 16
    matrix = matrix_ref[...]
    owners = breadth // local_slots

    @pl.when((pl.program_id(0) == 0) & (pl.program_id(1) == 0))
    def _():
        total = gauss_ref.shape[1]
        for j in range(0, total, depth):
            line = jnp.broadcast_to(gauss_ref[...], (depth, total))
            here = lax.broadcasted_iota(jnp.int32, line.shape, 0) + j
            mine = lax.broadcasted_iota(jnp.int32, line.shape, 1) == here
            value = jnp.sum(jnp.where(mine, line, 0.0), axis=1, keepdims=True)
            column[j : j + depth, :] = jnp.broadcast_to(value, (depth, members))

    for j in range(0, lats, depth):
        scale = column[pl.ds(pl.multiple_of(first + j, depth), depth), :]
        for s in range(0, slots, 2 * breadth):
            halves = [
                tendency_ref[0, j : j + depth, s + h : s + h + breadth, :].reshape(depth * breadth, members)
                for h in (0, breadth)
            ]
            turned = jnp.dot(matrix, jnp.concatenate(halves, axis=1), preferred_element_type=F32)
            for h in range(2):
                for i in range(owners):
                    value = turned[i * depth : (i + 1) * depth, h * members : (h + 1) * members]
                    owner = (s + h * breadth) // local_slots + i
                    value = (value * scale).astype(BF16)
                    if permuted:
                        blocks[owner, j : j + depth, :] = value
                    else:
                        outs[0][owner, 0, j : j + depth, :] = value
    if permuted:
        for k, out in zip(partners(len(outs)), outs):
            for core in range(CORES):
                out[core, 0] = blocks[((me_ref[0] // CORES) ^ k) * CORES + core]


def lat_block(lats):
    return lats // 2 if lats % 32 == 0 else lats


def weigh(tendency, gauss, me, slot, local_slots, permuted, waits):
    rows, lats, slots, members = tendency.shape
    each = lat_block(lats)
    matrix = swap_matrix(math.gcd(each, 16), 16, range(slot, 16, local_slots))
    owners = slots // local_slots
    count, chips = (CORES, owners // CORES) if permuted else (owners, 1)
    piece = pl.BlockSpec((count, 1, each, members), lambda r, j, m: (0, r, j, 0))
    return call(
        functools.partial(weigh_kernel, slot, local_slots, permuted, len(waits)),
        "weigh",
        2 * 128 * tendency.size,
        3 * tendency.size,
        58,
        out_shape=[jax.ShapeDtypeStruct((count, rows, lats, members), BF16)] * chips + [TOKEN],
        grid_spec=pltpu.PrefetchScalarGridSpec(
            num_scalar_prefetch=1,
            grid=(rows, lats // each),
            in_specs=[
                pl.BlockSpec(matrix.shape, lambda r, j, m: (0, 0)),
                pl.BlockSpec((1, lats), lambda r, j, m: (0, 0)),
                pl.BlockSpec((1, each, slots, members), lambda r, j, m: (r, j, 0, 0)),
            ]
            + [ANYWHERE] * len(waits),
            out_specs=[piece] * chips + [pl.BlockSpec(TOKEN.shape, lambda r, j, m: (0, 0))],
            scratch_shapes=([pltpu.VMEM((owners, each, members), BF16)] if permuted else [])
            + [pltpu.VMEM((lats, members), F32)],
        ),
    )(me, matrix, gauss, tendency, *waits)


def pick_kernel(waits, me_ref, *rest):
    ins, out = rest[waits:-1], rest[-1]
    for k, ref in enumerate(ins):
        out[k] = ref[0]


def pick(messages, me, waits):
    _, rows, lats, members = messages[0].shape
    chips = len(messages)
    shape = (chips, rows, lats, members)
    return call(
        functools.partial(pick_kernel, len(waits)),
        "pick",
        0,
        4 * math.prod(shape),
        out_shape=jax.ShapeDtypeStruct(shape, BF16),
        grid_spec=pltpu.PrefetchScalarGridSpec(
            num_scalar_prefetch=1,
            grid=(rows,),
            in_specs=[ANYWHERE] * len(waits)
            + [
                pl.BlockSpec((1, 1, lats, members), lambda r, m: (CORES - 1 - m[0] % CORES, r, 0, 0))
            ]
            * chips,
            out_specs=pl.BlockSpec((chips, 1, lats, members), lambda r, m: (0, r, 0, 0)),
        ),
    )(me, *waits, *messages)


def pair_kernel(mate_ref, *rest):
    chips = mate_ref.shape[0]
    outs, token_ref, sems = rest[-2 - chips : -2], rest[-2], rest[-1]
    token_ref[...] = jnp.zeros_like(token_ref)
    run_copies([pltpu.make_async_copy(mate_ref.at[k], out.at[1], sems.at[k]) for k, out in enumerate(outs)])


def pair(messages, mate, waits):
    chips = len(messages)
    return call(
        pair_kernel,
        "pair",
        0,
        4 * mate.size,
        out_shape=[jax.ShapeDtypeStruct(m.shape, m.dtype) for m in messages] + [TOKEN],
        in_specs=[pl.BlockSpec(mate.shape, lambda: (0, 0, 0, 0))] + [ANYWHERE] * (chips + len(waits)),
        out_specs=[ANYWHERE] * chips + [pl.BlockSpec(TOKEN.shape, lambda: (0, 0))],
        scratch_shapes=[pltpu.SemaphoreType.DMA((chips,))],
        input_output_aliases={k + 1: k for k in range(chips)},
    )(mate, *messages, *waits)


def analyse_kernel(slot, low, count, me_ref, wave_ref, token_ref, table_ref, state_ref, *rest):
    blocks, out, grid, sems = rest[:count], rest[count], rest[count + 1], rest[count + 2]
    rows, members, _ = out.shape
    owners, lats, _ = grid.shape
    width = table_ref.shape[1]
    step = pl.program_id(0)

    @pl.when(step == 0)
    def _():
        copies = []
        for r in range(rows):
            lanes = pl.ds(r * members, members)
            if count == 1:
                copies.append(pltpu.make_async_copy(blocks[0].at[:, r], grid.at[:, :, lanes], sems.at[0, r]))
            for i, k in enumerate(partners(count - 1) if count > 1 else []):
                for other in range(CORES):
                    target = grid.at[owner_of(me_ref[0], k, other), :, lanes]
                    source = blocks[-1].at[i, r] if other else blocks[i].at[me_ref[0] % CORES, r]
                    copies.append(pltpu.make_async_copy(source, target, sems.at[CORES * i + other, r]))
        run_copies(copies)

    field = grid[...].reshape(owners * lats, rows * members)
    sums = jnp.dot(table_ref[0], field, preferred_element_type=F32)
    degree = lax.broadcasted_iota(jnp.int32, (members, width), 1) + (low + step * width)
    live = degree >= wave_ref[slot]
    for r in range(rows):
        total = state_ref[r, 0].astype(F32) + sums[:, r * members : (r + 1) * members].T
        out[r] = jnp.where(live, total, 0.0).astype(BF16)


def analyse(blocks, table, state, wave, me, token, slot, low, width):
    _, rows, lats, members = blocks[0].shape
    nspec, nlat = table.shape[1:]
    owners = nlat // lats
    first = low // width
    if lats % 16:
        blocks = [lay_in_place(blocks, me[0], owners)]
        blocks[0] = jnp.transpose(blocks[0], (1, 0, 2, 3)).reshape(1, rows, nlat, members)
        owners, lats = 1, nlat
    return call(
        functools.partial(analyse_kernel, slot, low, len(blocks)),
        "analyse",
        2 * (nspec - low) * nlat * rows * members,
        2 * (nspec - low) * nlat,
        out_shape=jax.ShapeDtypeStruct((rows, members, nspec - low), BF16),
        grid=((nspec - low) // width,),
        in_specs=[
            IN_SMEM,
            IN_SMEM,
            ANYWHERE,
            pl.BlockSpec((1, width, nlat), lambda i: (slot, first + i, 0)),
            pl.BlockSpec((rows, 1, members, width), lambda i: (0, slot, 0, first + i)),
        ]
        + [ANYWHERE] * len(blocks),
        out_specs=pl.BlockSpec((rows, members, width), lambda i: (0, 0, i)),
        scratch_shapes=[
            pltpu.VMEM((owners, lats, rows * members), BF16),
            pltpu.SemaphoreType.DMA((owners, rows)),
        ],
    )(me, wave, token, table, state, *blocks)


def lay_in_place(blocks, here, owners):
    if len(blocks) == 1:
        return blocks[0]
    own = [lax.dynamic_index_in_dim(m, here % CORES, 0, keepdims=False) for m in blocks[:-1]]
    place = np.argsort(partners(len(own)))
    both = jnp.stack([jnp.stack(own)[place], blocks[-1][place]], axis=1).reshape((owners,) + own[0].shape)
    order = jnp.arange(owners, dtype=jnp.int32)
    order = ((order // CORES) ^ (here // CORES)) * CORES + (order % CORES ^ here % CORES)
    return jnp.take(both, order, axis=0)


def sum_pairs_kernel(coeff_ref, token_ref, inverse_ref, out_ref):
    pairs, entries = inverse_ref.shape[:2]
    half = entries // 2

    def one(entry, carry):
        real = imag = 0.0
        for k in range(pairs):
            first, second = inverse_ref[k, entry].astype(F32), inverse_ref[k, half + entry].astype(F32)
            a, b = coeff_ref[k, 0], coeff_ref[k, 1]
            real = real + (a * first - b * second)
            imag = imag + (a * second + b * first)
        out_ref[entry] = real
        out_ref[half + entry] = imag
        return carry

    lax.fori_loop(0, half, one, 0)


def sum_pairs(block_inverses, pole_coeffs, token):
    return call(
        sum_pairs_kernel,
        "sum_pairs",
        4 * block_inverses.size,
        2 * block_inverses.size,
        out_shape=jax.ShapeDtypeStruct(block_inverses.shape[1:], F32),
        in_specs=[IN_SMEM, ANYWHERE, pl.BlockSpec(block_inverses.shape, lambda: (0, 0, 0, 0))],
        out_specs=pl.BlockSpec(block_inverses.shape[1:], lambda: (0, 0, 0)),
    )(pole_coeffs, token, block_inverses)


def synthesise_kernel(slot, low, permuted, me_ref, sign_ref, here_ref, there_ref, own_ref, other_ref, table_ref, *rest):
    rows, members, _ = own_ref.shape
    width = table_ref.shape[2]
    step = pl.program_id(0)
    outs, token_ref, mixed = rest[: permuted + 1], rest[permuted + 1], rest[permuted + 2]

    @pl.when(step == 0)
    def _():
        token_ref[...] = jnp.zeros_like(token_ref)

        def line(entry):
            return here_ref[entry, slot : slot + 1, low:] + there_ref[entry, slot : slot + 1, low:]

        for f in range(rows):
            total = 0.0
            for g in range(rows):
                total = total + line(f * rows + g) * own_ref[g].astype(F32)
                total = total + sign_ref[0] * line(rows * rows + f * rows + g) * other_ref[g].astype(F32)
            mixed[f * members : (f + 1) * members, :] = total.astype(BF16)

    sums = jnp.dot(mixed[...], table_ref[0], preferred_element_type=F32)
    grid = rest[permuted + 3] if permuted else outs[0]
    lats = grid.shape[2]
    each = width // lats
    for r in range(rows):
        turned = sums[r * members : (r + 1) * members, :].T.reshape(each, lats, members).astype(BF16)
        if permuted:
            grid[pl.ds(step * each, each), r] = turned
        else:
            grid[:, r] = turned

    if permuted:
        sems = rest[-1]

        @pl.when(step == pl.num_programs(0) - 1)
        def _():
            copies = []
            for i, k in enumerate(partners(permuted)):
                for other in range(CORES):
                    source = grid.at[owner_of(me_ref[0], k, other)]
                    target = outs[-1].at[i] if other else outs[i].at[0]
                    copies.append(pltpu.make_async_copy(source, target, sems.at[i, other]))
            run_copies(copies)


def synthesise(here, there, sign, own, other, table, me, slot, low, lats, permuted):
    rows, members, count = own.shape
    nlat = table.shape[2]
    owners = nlat // lats
    width = math.lcm(lats, 128)
    chips = owners // CORES if permuted else 0
    matrix = pl.BlockSpec(here.shape, lambda j: (0, 0, 0))
    whole = pl.BlockSpec((rows, members, count), lambda j: (0, 0, 0))
    shapes = [jax.ShapeDtypeStruct((owners, rows, lats, members), BF16)]
    specs = [pl.BlockSpec((width // lats, rows, lats, members), lambda j: (j, 0, 0, 0))]
    scratch = [pltpu.VMEM((rows * members, count), BF16)]
    if permuted:
        shapes = [jax.ShapeDtypeStruct((CORES, rows, lats, members), BF16)] * chips
        shapes += [jax.ShapeDtypeStruct((chips, rows, lats, members), BF16)]
        specs = [ANYWHERE] * (chips + 1)
        scratch += [pltpu.VMEM((owners, rows, lats, members), BF16), pltpu.SemaphoreType.DMA((chips, CORES))]
    return call(
        functools.partial(synthesise_kernel, slot, low, chips),
        "synthesise",
        2 * count * nlat * rows * members,
        2 * count * nlat,
        out_shape=shapes + [TOKEN],
        grid=(nlat // width,),
        in_specs=[
            IN_SMEM,
            IN_SMEM,
            matrix,
            matrix,
            whole,
            whole,
            pl.BlockSpec((1, count, width), lambda j: (slot, low // count, j)),
        ],
        out_specs=specs + [pl.BlockSpec(TOKEN.shape, lambda j: (0, 0))],
        scratch_shapes=scratch,
    )(me, sign, here, there, own, other, table)


def assemble_kernel(counts, me_ref, matrix_ref, *rest):
    ins, out, blocks = rest[: sum(counts)], rest[sum(counts)], rest[sum(counts) + 1 :]
    _, lats, slots, members = out.shape
    local_slots = len(counts)
    views, used, spare = [], 0, 0
    for count in counts:
        refs = ins[used : used + count]
        used += count
        if count == 1:
            views.append(lambda owner, j, ref=refs[0]: ref[owner, 0, j, :])
            continue
        for k, ref in zip(partners(count), refs):
            for other in range(CORES):
                blocks[spare][owner_of(me_ref[0], k, other)] = ref[other, 0]
        views.append(lambda owner, j, ref=blocks[spare]: ref[owner, j, :])
        spare += 1
    depth, breadth = math.gcd(lats, 16), 16
    matrix = matrix_ref[...]
    for start in range(0, lats, depth):
        j = slice(start, start + depth)
        for s in range(0, slots, 2 * breadth):
            halves = [
                jnp.concatenate(
                    [views[i % local_slots](i // local_slots, j) for i in range(s + h, s + h + breadth)], axis=0
                )
                for h in (0, breadth)
            ]
            turned = jnp.dot(matrix, jnp.concatenate(halves, axis=1), preferred_element_type=F32).astype(BF16)
            for h in range(2):
                value = turned[:, h * members : (h + 1) * members].reshape(depth, breadth, members)
                out[0, j, s + h * breadth : s + (h + 1) * breadth, :] = value


def assemble(pieces, me, lats):
    local_slots = len(pieces)
    _, rows, _, members = pieces[0][0].shape
    owners = max(len(p) * p[0].shape[0] for p in pieces)
    slots = local_slots * owners
    each = lat_block(lats)
    matrix = swap_matrix(16, math.gcd(each, 16), range(math.gcd(each, 16)))
    flat = [block for slot in pieces for block in slot]
    moved = sum(len(p) > 1 for p in pieces)
    return call(
        functools.partial(assemble_kernel, [len(p) for p in pieces]),
        "assemble",
        2 * 256 * rows * lats * slots * members,
        4 * rows * lats * slots * members,
        out_shape=jax.ShapeDtypeStruct((rows, lats, slots, members), BF16),
        grid_spec=pltpu.PrefetchScalarGridSpec(
            num_scalar_prefetch=1,
            grid=(rows, lats // each),
            in_specs=[pl.BlockSpec(matrix.shape, lambda r, j, m: (0, 0))]
            + [
                pl.BlockSpec((block.shape[0], 1, each, members), lambda r, j, m: (0, r, j, 0)) for block in flat
            ],
            out_specs=pl.BlockSpec((1, each, slots, members), lambda r, j, m: (r, j, 0, 0)),
            scratch_shapes=[pltpu.VMEM((owners, each, members), BF16)] * moved,
        ),
    )(me, matrix, *flat)


def between_chips(messages):
    chips = len(messages)
    got = [messages[0]]
    for k, message in list(zip(partners(chips), messages))[1:]:
        got.append(lax.ppermute(message, "wave", [(d, d ^ (k * CORES)) for d in range(chips * CORES)]))
    return got


def between_cores(blocks, owners):
    return lax.ppermute(blocks, "wave", [(d, d ^ 1) for d in range(owners)])


def to_all(blocks):
    return lax.all_to_all(blocks, "wave", split_axis=0, concat_axis=0, tiled=True)


def per_device(
    tendency, spectral_state, legendre, gauss_weights, block_inverses, pole_coeffs, wavenumbers
):
    rows, lats, slots, members = tendency.shape
    local_slots, nspec, nlat = legendre.shape
    owners = slots // local_slots
    me = lax.axis_index("wave").astype(jnp.int32).reshape(1)
    pole_index = lax.axis_index("pole")
    sign = (2 * pole_index - 1).astype(F32).reshape(1)
    order = list(range(local_slots))[::-1]
    received, waits = {}, []
    for slot in order:
        permuted = slot == order[0]
        *blocks, token = weigh(tendency, gauss_weights[None], me, slot, local_slots, permuted, waits)
        received[slot] = between_chips(blocks) if permuted else [to_all(blocks[0])]
        if permuted:
            here = sum_pairs(block_inverses, pole_coeffs, token)
            there = lax.ppermute(here, "pole", [(0, 1), (1, 0)])
            waits = [here, received[slot][1]]

    sent = {}
    for slot in order:
        incoming = slot == order[0]
        low = nspec // 2 if slot % 2 else 0
        blocks = received[slot]
        if incoming:
            blocks = blocks + [between_cores(pick(blocks, me, [token, there]), owners)]
        forced = analyse(blocks, legendre, spectral_state, wavenumbers, me, token, slot, low, nspec // 2)
        other = lax.ppermute(forced, "pole", [(0, 1), (1, 0)])
        *blocks, token = synthesise(here, there, sign, forced, other, legendre, me, slot, low, lats, not incoming)
        if incoming:
            sent[slot] = [to_all(blocks[0])]
        else:
            *blocks, token = pair(blocks[:-1], between_cores(blocks[-1], owners), [])
            sent[slot] = between_chips(blocks)
    return assemble([sent[slot] for slot in range(local_slots)], me, lats)


def solution(mesh):
    in_specs = (
        P("pole", "wave", None, None),
        P("pole", "wave", None, None),
        P("wave", None, None),
        P("wave"),
        P("pole", None, "wave", None),
        P("pole", None),
        P("wave"),
    )
    out_specs = P("pole", "wave", None, None)
    return jax.shard_map(
        per_device, mesh=mesh, in_specs=in_specs, out_specs=out_specs, check_vma=False
    )
```

```python
import functools
import math

import jax
import jax.numpy as jnp
import numpy as np
from jax import lax
from jax.experimental import pallas as pl
from jax.experimental.pallas import tpu as pltpu
from jax.sharding import PartitionSpec as P

BF16 = jnp.bfloat16
F32 = jnp.float32
CORES = 2
ANYWHERE = pl.BlockSpec(memory_space=pl.ANY)
IN_SMEM = pl.BlockSpec(memory_space=pltpu.SMEM)
TOKEN = jax.ShapeDtypeStruct((8, 128), F32)


def call(kernel, name, flops, size, mib=40, **kwargs):
    return pl.pallas_call(
        kernel,
        name=name,
        compiler_params=pltpu.CompilerParams(vmem_limit_bytes=mib * 1024 * 1024),
        cost_estimate=pl.CostEstimate(flops=int(flops), bytes_accessed=int(size), transcendentals=0),
        **kwargs,
    )


def run_copies(copies):
    for copy in copies:
        copy.start()
    for copy in copies:
        copy.wait()


def split_cores(values, core):
    even = [values[i] for i in range(0, len(values), CORES)]
    odd = [values[i] for i in range(1, len(values), CORES)]
    mine = [jnp.where(core == 0, a, b) for a, b in zip(even, odd)]
    others = [jnp.where(core == 0, b, a) for a, b in zip(even, odd)]
    return mine, others


def swap_matrix(rows, columns, picked):
    matrix = np.zeros((len(picked), rows, rows, columns), np.float32)
    for i, c in enumerate(picked):
        matrix[i, np.arange(rows), np.arange(rows), c] = 1.0
    return jnp.asarray(matrix.reshape(len(picked) * rows, rows * columns), BF16)


def weigh_kernel(slot, local_slots, split, waits, me_ref, matrix_ref, gauss_ref, tendency_ref, *rest):
    _, lats, slots, members = tendency_ref.shape
    outs, token_ref, column = rest[waits:-2], rest[-2], rest[-1]
    token_ref[...] = jnp.zeros_like(token_ref)
    first = pl.program_id(1) * lats
    depth, breadth = math.gcd(lats, 16), 16
    matrix = matrix_ref[...]
    owners = breadth // local_slots
    core = me_ref[0] % CORES

    @pl.when((pl.program_id(0) == 0) & (pl.program_id(1) == 0))
    def _():
        total = gauss_ref.shape[1]
        for j in range(0, total, depth):
            line = jnp.broadcast_to(gauss_ref[...], (depth, total))
            here = lax.broadcasted_iota(jnp.int32, line.shape, 0) + j
            mine = lax.broadcasted_iota(jnp.int32, line.shape, 1) == here
            value = jnp.sum(jnp.where(mine, line, 0.0), axis=1, keepdims=True)
            column[j : j + depth, :] = jnp.broadcast_to(value, (depth, members))

    for j in range(0, lats, depth):
        scale = column[pl.ds(pl.multiple_of(first + j, depth), depth), :]
        for s in range(0, slots, 2 * breadth):
            halves = [
                tendency_ref[0, j : j + depth, s + h : s + h + breadth, :].reshape(depth * breadth, members)
                for h in (0, breadth)
            ]
            turned = jnp.dot(matrix, jnp.concatenate(halves, axis=1), preferred_element_type=F32)
            values = [
                turned[i * depth : (i + 1) * depth, h * members : (h + 1) * members] * scale
                for h in range(2)
                for i in range(owners)
            ]
            start = s // local_slots
            if split:
                mine, others = split_cores(values, core)
                for i, (a, b) in enumerate(zip(mine, others)):
                    outs[0][start // CORES + i, 0, 0, j : j + depth, :] = a.astype(BF16)
                    outs[1][start // CORES + i, 0, j : j + depth, :] = b.astype(BF16)
            else:
                for i, value in enumerate(values):
                    chip, target = divmod(start + i, CORES)
                    outs[0][chip, target, 0, j : j + depth, :] = value.astype(BF16)


def lat_block(lats):
    return lats // 2 if lats % 32 == 0 else lats


def weigh(tendency, gauss, me, slot, local_slots, split, waits):
    rows, lats, slots, members = tendency.shape
    each = lat_block(lats)
    matrix = swap_matrix(math.gcd(each, 16), 16, range(slot, 16, local_slots))
    chips = slots // local_slots // CORES
    shapes = [jax.ShapeDtypeStruct((chips, CORES, rows, lats, members), BF16)]
    specs = [pl.BlockSpec((chips, CORES, 1, each, members), lambda r, j, m: (0, 0, r, j, 0))]
    if split:
        shapes += [jax.ShapeDtypeStruct((chips, rows, lats, members), BF16)]
        specs = [pl.BlockSpec((chips, 1, 1, each, members), lambda r, j, m: (0, m[0] % CORES, r, j, 0))]
        specs += [pl.BlockSpec((chips, 1, each, members), lambda r, j, m: (0, r, j, 0))]
    return call(
        functools.partial(weigh_kernel, slot, local_slots, split, len(waits)),
        "weigh",
        2 * 128 * tendency.size,
        3 * tendency.size,
        58,
        out_shape=shapes + [TOKEN],
        grid_spec=pltpu.PrefetchScalarGridSpec(
            num_scalar_prefetch=1,
            grid=(rows, lats // each),
            in_specs=[
                pl.BlockSpec(matrix.shape, lambda r, j, m: (0, 0)),
                pl.BlockSpec((1, lats), lambda r, j, m: (0, 0)),
                pl.BlockSpec((1, each, slots, members), lambda r, j, m: (r, j, 0, 0)),
            ]
            + [ANYWHERE] * len(waits),
            out_specs=specs + [pl.BlockSpec(TOKEN.shape, lambda r, j, m: (0, 0))],
            scratch_shapes=[pltpu.VMEM((lats, members), F32)],
        ),
    )(me, matrix, gauss, tendency, *waits)


def pick_kernel(me_ref, token_ref, in_ref, out_ref):
    out_ref[...] = in_ref[:, 0]


def pick(blocks, me, token):
    chips, _, rows, lats, members = blocks.shape
    return call(
        pick_kernel,
        "pick",
        0,
        2 * blocks.size,
        out_shape=jax.ShapeDtypeStruct((chips, rows, lats, members), BF16),
        grid_spec=pltpu.PrefetchScalarGridSpec(
            num_scalar_prefetch=1,
            grid=(rows,),
            in_specs=[
                ANYWHERE,
                pl.BlockSpec((chips, 1, 1, lats, members), lambda r, m: (0, CORES - 1 - m[0] % CORES, r, 0, 0))
            ],
            out_specs=pl.BlockSpec((chips, 1, lats, members), lambda r, m: (0, r, 0, 0)),
        ),
    )(me, token, blocks)


def pair_kernel(me_ref, mate_ref, blocks_ref, out_ref, token_ref, sem):
    token_ref[...] = jnp.zeros_like(token_ref)
    other = CORES - 1 - me_ref[0] % CORES
    run_copies([pltpu.make_async_copy(mate_ref, out_ref.at[:, other], sem)])


def pair(blocks, mate, me):
    return call(
        pair_kernel,
        "pair",
        0,
        4 * mate.size,
        out_shape=[jax.ShapeDtypeStruct(blocks.shape, blocks.dtype), TOKEN],
        in_specs=[IN_SMEM, pl.BlockSpec(mate.shape, lambda: (0, 0, 0, 0)), ANYWHERE],
        out_specs=[ANYWHERE, pl.BlockSpec(TOKEN.shape, lambda: (0, 0))],
        scratch_shapes=[pltpu.SemaphoreType.DMA],
        input_output_aliases={2: 0},
    )(me, mate, blocks)


def analyse_kernel(slot, low, count, me_ref, wave_ref, token_ref, table_ref, state_ref, *rest):
    blocks, out, grid, sems = rest[:count], rest[count], rest[count + 1], rest[count + 2]
    rows, members, _ = out.shape
    chips, cores, lats, _ = grid.shape
    width = table_ref.shape[1]
    step = pl.program_id(0)

    @pl.when(step == 0)
    def _():
        copies = []
        core = me_ref[0] % CORES
        for r in range(rows):
            lanes = pl.ds(r * members, members)
            if count == 1:
                copies.append(pltpu.make_async_copy(blocks[0].at[:, :, r], grid.at[:, :, :, lanes], sems.at[0, r]))
            else:
                target = grid.at[:, core, :, lanes]
                copies.append(pltpu.make_async_copy(blocks[0].at[:, core, r], target, sems.at[0, r]))
                target = grid.at[:, CORES - 1 - core, :, lanes]
                copies.append(pltpu.make_async_copy(blocks[1].at[:, r], target, sems.at[1, r]))
        run_copies(copies)

    field = grid[...].reshape(chips * cores * lats, rows * members)
    sums = jnp.dot(table_ref[0], field, preferred_element_type=F32)
    degree = lax.broadcasted_iota(jnp.int32, (members, width), 1) + (low + step * width)
    live = degree >= wave_ref[slot]
    for r in range(rows):
        total = state_ref[r, 0].astype(F32) + sums[:, r * members : (r + 1) * members].T
        out[r] = jnp.where(live, total, 0.0).astype(BF16)


def analyse(blocks, table, state, wave, me, token, slot, low, width):
    chips, _, rows, lats, members = blocks[0].shape
    nspec, nlat = table.shape[1:]
    first = low // width
    cores = CORES
    if lats % 16:
        if len(blocks) > 1:
            core = me[0] % CORES
            own = lax.dynamic_index_in_dim(blocks[0], core, 1, keepdims=False)
            pairs = [jnp.where(core == 0, own, blocks[1]), jnp.where(core == 0, blocks[1], own)]
            blocks = [jnp.stack(pairs, axis=1)]
        laid = jnp.transpose(blocks[0], (2, 0, 1, 3, 4)).reshape(1, 1, rows, nlat, members)
        blocks, chips, cores, lats = [laid], 1, 1, nlat
    return call(
        functools.partial(analyse_kernel, slot, low, len(blocks)),
        "analyse",
        2 * (nspec - low) * nlat * rows * members,
        2 * (nspec - low) * nlat,
        out_shape=jax.ShapeDtypeStruct((rows, members, nspec - low), BF16),
        grid=((nspec - low) // width,),
        in_specs=[
            IN_SMEM,
            IN_SMEM,
            ANYWHERE,
            pl.BlockSpec((1, width, nlat), lambda i: (slot, first + i, 0)),
            pl.BlockSpec((rows, 1, members, width), lambda i: (0, slot, 0, first + i)),
        ]
        + [ANYWHERE] * len(blocks),
        out_specs=pl.BlockSpec((rows, members, width), lambda i: (0, 0, i)),
        scratch_shapes=[
            pltpu.VMEM((chips, cores, lats, rows * members), BF16),
            pltpu.SemaphoreType.DMA((CORES, rows)),
        ],
    )(me, wave, token, table, state, *blocks)


def sum_pairs_kernel(coeff_ref, token_ref, inverse_ref, out_ref):
    pairs, entries = inverse_ref.shape[:2]
    half = entries // 2

    def one(entry, carry):
        real = imag = 0.0
        for k in range(pairs):
            first, second = inverse_ref[k, entry].astype(F32), inverse_ref[k, half + entry].astype(F32)
            a, b = coeff_ref[k, 0], coeff_ref[k, 1]
            real = real + (a * first - b * second)
            imag = imag + (a * second + b * first)
        out_ref[entry] = real
        out_ref[half + entry] = imag
        return carry

    lax.fori_loop(0, half, one, 0)


def sum_pairs(block_inverses, pole_coeffs, token):
    return call(
        sum_pairs_kernel,
        "sum_pairs",
        4 * block_inverses.size,
        2 * block_inverses.size,
        out_shape=jax.ShapeDtypeStruct(block_inverses.shape[1:], F32),
        in_specs=[IN_SMEM, ANYWHERE, pl.BlockSpec(block_inverses.shape, lambda: (0, 0, 0, 0))],
        out_specs=pl.BlockSpec(block_inverses.shape[1:], lambda: (0, 0, 0)),
    )(pole_coeffs, token, block_inverses)


def synthesise_kernel(slot, low, me_ref, sign_ref, here_ref, there_ref, own_ref, other_ref, table_ref, *rest):
    rows, members, _ = own_ref.shape
    step = pl.program_id(0)
    own_out, mate_out, mixed = rest

    @pl.when(step == 0)
    def _():
        def line(entry):
            return here_ref[entry, slot : slot + 1, low:] + there_ref[entry, slot : slot + 1, low:]

        for f in range(rows):
            total = 0.0
            for g in range(rows):
                total = total + line(f * rows + g) * own_ref[g].astype(F32)
                total = total + sign_ref[0] * line(rows * rows + f * rows + g) * other_ref[g].astype(F32)
            mixed[f * members : (f + 1) * members, :] = total.astype(BF16)

    sums = jnp.dot(mixed[...], table_ref[0], preferred_element_type=F32)
    lats = own_out.shape[3]
    for r in range(rows):
        turned = sums[r * members : (r + 1) * members, :].T
        values = [turned[i : i + lats] for i in range(0, turned.shape[0], lats)]
        mine, others = split_cores(values, me_ref[0] % CORES)
        for i, (a, b) in enumerate(zip(mine, others)):
            own_out[i, 0, r] = a.astype(BF16)
            mate_out[i, r] = b.astype(BF16)


def synthesise(here, there, sign, own, other, table, me, slot, low, lats):
    rows, members, count = own.shape
    nlat = table.shape[2]
    width = math.lcm(CORES * lats, 128)
    chips, each = nlat // lats // CORES, width // lats // CORES
    matrix = pl.BlockSpec(here.shape, lambda j, m: (0, 0, 0))
    whole = pl.BlockSpec((rows, members, count), lambda j, m: (0, 0, 0))
    smem = pl.BlockSpec(memory_space=pltpu.SMEM)
    return call(
        functools.partial(synthesise_kernel, slot, low),
        "synthesise",
        2 * count * nlat * rows * members,
        2 * count * nlat,
        out_shape=[
            jax.ShapeDtypeStruct((chips, CORES, rows, lats, members), BF16),
            jax.ShapeDtypeStruct((chips, rows, lats, members), BF16),
        ],
        grid_spec=pltpu.PrefetchScalarGridSpec(
            num_scalar_prefetch=1,
            grid=(nlat // width,),
            in_specs=[
                smem,
                matrix,
                matrix,
                whole,
                whole,
                pl.BlockSpec((1, count, width), lambda j, m: (slot, low // count, j)),
            ],
            out_specs=[
                pl.BlockSpec((each, 1, rows, lats, members), lambda j, m: (j, m[0] % CORES, 0, 0, 0)),
                pl.BlockSpec((each, rows, lats, members), lambda j, m: (j, 0, 0, 0)),
            ],
            scratch_shapes=[pltpu.VMEM((rows * members, count), BF16)],
        ),
    )(me, sign, here, there, own, other, table)


def assemble_kernel(matrix_ref, *rest):
    ins, out = rest[:-1], rest[-1]
    _, lats, slots, members = out.shape
    local_slots = len(ins)
    depth, breadth = math.gcd(lats, 16), 16
    matrix = matrix_ref[...]
    for start in range(0, lats, depth):
        j = slice(start, start + depth)
        for s in range(0, slots, 2 * breadth):
            halves = []
            for h in (0, breadth):
                columns = [divmod(i, local_slots) for i in range(s + h, s + h + breadth)]
                columns = [ins[slot][owner // CORES, owner % CORES, 0, j, :] for owner, slot in columns]
                halves.append(jnp.concatenate(columns, axis=0))
            turned = jnp.dot(matrix, jnp.concatenate(halves, axis=1), preferred_element_type=F32).astype(BF16)
            for h in range(2):
                value = turned[:, h * members : (h + 1) * members].reshape(depth, breadth, members)
                out[0, j, s + h * breadth : s + (h + 1) * breadth, :] = value


def assemble(pieces):
    chips, cores, rows, lats, members = pieces[0].shape
    slots = len(pieces) * chips * cores
    each = lat_block(lats)
    matrix = swap_matrix(16, math.gcd(each, 16), range(math.gcd(each, 16)))
    piece = pl.BlockSpec((chips, cores, 1, each, members), lambda r, j: (0, 0, r, j, 0))
    return call(
        assemble_kernel,
        "assemble",
        2 * 256 * rows * lats * slots * members,
        4 * rows * lats * slots * members,
        out_shape=jax.ShapeDtypeStruct((rows, lats, slots, members), BF16),
        grid=(rows, lats // each),
        in_specs=[pl.BlockSpec(matrix.shape, lambda r, j: (0, 0))] + [piece] * len(pieces),
        out_specs=pl.BlockSpec((1, each, slots, members), lambda r, j: (r, j, 0, 0)),
    )(matrix, *pieces)


def between_cores(blocks, owners):
    return lax.ppermute(blocks, "wave", [(d, d ^ 1) for d in range(owners)])


def between_chips(blocks, owners):
    groups = [list(range(core, owners, CORES)) for core in range(CORES)]
    return lax.all_to_all(blocks, "wave", split_axis=0, concat_axis=0, axis_index_groups=groups, tiled=True)


def per_device(
    tendency, spectral_state, legendre, gauss_weights, block_inverses, pole_coeffs, wavenumbers
):
    rows, lats, slots, members = tendency.shape
    local_slots, nspec, nlat = legendre.shape
    owners = slots // local_slots
    me = lax.axis_index("wave").astype(jnp.int32).reshape(1)
    pole_index = lax.axis_index("pole")
    sign = (2 * pole_index - 1).astype(F32).reshape(1)
    order = list(range(local_slots))[::-1]
    received, waits = {}, []
    for slot in order:
        early = slot == order[0]
        *blocks, token = weigh(tendency, gauss_weights[None], me, slot, local_slots, not early, waits)
        if early:
            received[slot] = between_chips(blocks[0], owners)
            here = sum_pairs(block_inverses, pole_coeffs, token)
            there = lax.ppermute(here, "pole", [(0, 1), (1, 0)])
            waits = [there]
        else:
            blocks, token = pair(blocks[0], between_cores(blocks[1], owners), me)
            received[slot] = between_chips(blocks, owners)

    sent = {}
    for slot in order:
        low = nspec // 2 if slot % 2 else 0
        blocks = [received[slot]]
        if slot == order[0]:
            blocks.append(between_cores(pick(blocks[0], me, token), owners))
        forced = analyse(blocks, legendre, spectral_state, wavenumbers, me, token, slot, low, nspec // 2)
        other = lax.ppermute(forced, "pole", [(0, 1), (1, 0)])
        own, for_mate = synthesise(here, there, sign, forced, other, legendre, me, slot, low, lats)
        blocks, token = pair(own, between_cores(for_mate, owners), me)
        sent[slot] = between_chips(blocks, owners)
    return assemble([sent[slot] for slot in range(local_slots)])


def solution(mesh):
    in_specs = (
        P("pole", "wave", None, None),
        P("pole", "wave", None, None),
        P("wave", None, None),
        P("wave"),
        P("pole", None, "wave", None),
        P("pole", None),
        P("wave"),
    )
    out_specs = P("pole", "wave", None, None)
    return jax.shard_map(
        per_device, mesh=mesh, in_specs=in_specs, out_specs=out_specs, check_vma=False
    )
```

```python
import functools
import math

import jax
import jax.numpy as jnp
import numpy as np
from jax import lax
from jax.experimental import pallas as pl
from jax.experimental.pallas import tpu as pltpu
from jax.sharding import PartitionSpec as P

BF16 = jnp.bfloat16
F32 = jnp.float32
CORES = 2
ANYWHERE = pl.BlockSpec(memory_space=pl.ANY)
IN_SMEM = pl.BlockSpec(memory_space=pltpu.SMEM)
TOKEN = jax.ShapeDtypeStruct((8, 128), F32)


def call(kernel, name, flops, size, mib=40, **kwargs):
    return pl.pallas_call(
        kernel,
        name=name,
        compiler_params=pltpu.CompilerParams(vmem_limit_bytes=mib * 1024 * 1024),
        cost_estimate=pl.CostEstimate(flops=int(flops), bytes_accessed=int(size), transcendentals=0),
        **kwargs,
    )


def run_copies(copies):
    for copy in copies:
        copy.start()
    for copy in copies:
        copy.wait()


def partners(chips):
    return [0] + list(range(chips // 2, chips)) + list(range(1, chips // 2))


def split_cores(values, core):
    even = [values[i] for i in range(0, len(values), CORES)]
    odd = [values[i] for i in range(1, len(values), CORES)]
    mine = [jnp.where(core == 0, a, b) for a, b in zip(even, odd)]
    others = [jnp.where(core == 0, b, a) for a, b in zip(even, odd)]
    return mine, others


def swap_matrix(rows, columns, picked):
    matrix = np.zeros((len(picked), rows, rows, columns), np.float32)
    for i, c in enumerate(picked):
        matrix[i, np.arange(rows), np.arange(rows), c] = 1.0
    return jnp.asarray(matrix.reshape(len(picked) * rows, rows * columns), BF16)


def weigh_kernel(slot, local_slots, split, waits, me_ref, matrix_ref, gauss_ref, tendency_ref, *rest):
    outs, token_ref, (column, held, done, in_sems, out_sems) = rest[waits:-6], rest[-6], rest[-5:]
    rows, lats, slots, members = held.shape
    each = in_sems.shape[1]
    size = lats // each
    copies = []
    for r in range(rows):
        for i in range(each):
            part = pl.ds(i * size, size)
            copies.append(pltpu.make_async_copy(tendency_ref.at[r, part], held.at[r, part], in_sems.at[r, i]))
            copies[-1].start()
    token_ref[...] = jnp.zeros_like(token_ref)
    depth, breadth = math.gcd(size, 16), 16
    matrix = matrix_ref[...]
    owners = breadth // local_slots
    core = me_ref[0] % CORES
    for j in range(0, lats, depth):
        line = jnp.broadcast_to(gauss_ref[...], (depth, lats))
        here = lax.broadcasted_iota(jnp.int32, line.shape, 0) + j
        mine = lax.broadcasted_iota(jnp.int32, line.shape, 1) == here
        value = jnp.sum(jnp.where(mine, line, 0.0), axis=1, keepdims=True)
        column[j : j + depth, :] = jnp.broadcast_to(value, (depth, members))
    results = []
    for r in range(rows):
        for j in range(0, lats, depth):
            if j % size == 0:
                copies[r * each + j // size].wait()
            scale = column[j : j + depth, :]
            for s in range(0, slots, 2 * breadth):
                halves = [
                    held[r, j : j + depth, s + h : s + h + breadth, :].reshape(depth * breadth, members)
                    for h in (0, breadth)
                ]
                turned = jnp.dot(matrix, jnp.concatenate(halves, axis=1), preferred_element_type=F32)
                values = [
                    turned[i * depth : (i + 1) * depth, h * members : (h + 1) * members] * scale
                    for h in range(2)
                    for i in range(owners)
                ]
                start = s // local_slots
                if split:
                    mine, others = split_cores(values, core)
                    for i, (a, b) in enumerate(zip(mine, others)):
                        done[start // CORES + i, 0, r, j : j + depth, :] = a.astype(BF16)
                        done[start // CORES + i, 1, r, j : j + depth, :] = b.astype(BF16)
                else:
                    for i, value in enumerate(values):
                        chip, target = divmod(start + i, CORES)
                        done[chip, target, r, j : j + depth, :] = value.astype(BF16)
        if split:
            results.append(pltpu.make_async_copy(done.at[:, 0, r], outs[0].at[:, core, r], out_sems.at[0, r]))
            results.append(pltpu.make_async_copy(done.at[:, 1, r], outs[1].at[:, r], out_sems.at[1, r]))
            results[-2].start()
        else:
            results.append(pltpu.make_async_copy(done.at[:, :, r], outs[0].at[:, :, r], out_sems.at[0, r]))
        results[-1].start()
    for copy in results:
        copy.wait()


def lat_block(lats):
    return lats // 2 if lats % 32 == 0 else lats


def weigh(tendency, gauss, me, slot, local_slots, split, waits):
    rows, lats, slots, members = tendency.shape
    each = lats // lat_block(lats)
    depth = math.gcd(lats // each, 16)
    matrix = swap_matrix(depth, 16, range(slot, 16, local_slots))
    chips = slots // local_slots // CORES
    shapes = [jax.ShapeDtypeStruct((chips, CORES, rows, lats, members), BF16)]
    if split:
        shapes += [jax.ShapeDtypeStruct((chips, rows, lats, members), BF16)]
    return call(
        functools.partial(weigh_kernel, slot, local_slots, split, len(waits)),
        "weigh",
        2 * 128 * tendency.size,
        3 * tendency.size,
        58,
        out_shape=shapes + [TOKEN],
        in_specs=[
            IN_SMEM,
            pl.BlockSpec(matrix.shape, lambda: (0, 0)),
            pl.BlockSpec((1, lats), lambda: (0, 0)),
            ANYWHERE,
        ]
        + [ANYWHERE] * len(waits),
        out_specs=[ANYWHERE] * len(shapes) + [pl.BlockSpec(TOKEN.shape, lambda: (0, 0))],
        scratch_shapes=[
            pltpu.VMEM((lats, members), F32),
            pltpu.VMEM((rows, lats, slots, members), BF16),
            pltpu.VMEM((chips, CORES, rows, lats, members), BF16),
            pltpu.SemaphoreType.DMA((rows, each)),
            pltpu.SemaphoreType.DMA((CORES, rows)),
        ],
    )(me, matrix, gauss, tendency, *waits)


def pick_kernel(me_ref, token_ref, in_ref, out_ref):
    out_ref[...] = in_ref[:, 0]


def pick(blocks, me, token):
    chips, _, rows, lats, members = blocks.shape
    return call(
        pick_kernel,
        "pick",
        0,
        2 * blocks.size,
        out_shape=jax.ShapeDtypeStruct((chips, rows, lats, members), BF16),
        grid_spec=pltpu.PrefetchScalarGridSpec(
            num_scalar_prefetch=1,
            grid=(rows,),
            in_specs=[
                ANYWHERE,
                pl.BlockSpec((chips, 1, 1, lats, members), lambda r, m: (0, CORES - 1 - m[0] % CORES, r, 0, 0))
            ],
            out_specs=pl.BlockSpec((chips, 1, lats, members), lambda r, m: (0, r, 0, 0)),
        ),
    )(me, token, blocks)


def pair_kernel(me_ref, mate_ref, blocks_ref, out_ref, token_ref, sem):
    token_ref[...] = jnp.zeros_like(token_ref)
    other = CORES - 1 - me_ref[0] % CORES
    run_copies([pltpu.make_async_copy(mate_ref, out_ref.at[:, other], sem)])


def pair(blocks, mate, me):
    return call(
        pair_kernel,
        "pair",
        0,
        4 * mate.size,
        out_shape=[jax.ShapeDtypeStruct(blocks.shape, blocks.dtype), TOKEN],
        in_specs=[IN_SMEM, pl.BlockSpec(mate.shape, lambda: (0, 0, 0, 0)), ANYWHERE],
        out_specs=[ANYWHERE, pl.BlockSpec(TOKEN.shape, lambda: (0, 0))],
        scratch_shapes=[pltpu.SemaphoreType.DMA],
        input_output_aliases={2: 0},
    )(me, mate, blocks)


def pair_messages_kernel(me_ref, mate_ref, *rest):
    chips = mate_ref.shape[0]
    outs, sems = rest[chips:-1], rest[-1]
    chip, other = me_ref[0] // CORES, CORES - 1 - me_ref[0] % CORES
    run_copies(
        [
            pltpu.make_async_copy(mate_ref.at[chip ^ k], out.at[other], sems.at[i])
            for i, (k, out) in enumerate(zip(partners(chips), outs))
        ]
    )


def pair_messages(messages, mate, me):
    chips = len(messages)
    return call(
        pair_messages_kernel,
        "pair",
        0,
        4 * mate.size,
        out_shape=[jax.ShapeDtypeStruct(m.shape, m.dtype) for m in messages],
        in_specs=[IN_SMEM, pl.BlockSpec(mate.shape, lambda: (0, 0, 0, 0))] + [ANYWHERE] * chips,
        out_specs=[ANYWHERE] * chips,
        scratch_shapes=[pltpu.SemaphoreType.DMA((chips,))],
        input_output_aliases={i + 2: i for i in range(chips)},
    )(me, mate, *messages)


def analyse_kernel(slot, low, count, me_ref, wave_ref, token_ref, table_ref, state_ref, *rest):
    blocks, out, grid, sems = rest[:count], rest[count], rest[count + 1], rest[count + 2]
    rows, members, _ = out.shape
    chips, cores, lats, _ = grid.shape
    width = table_ref.shape[1]
    step = pl.program_id(0)

    @pl.when(step == 0)
    def _():
        copies = []
        core = me_ref[0] % CORES
        for r in range(rows):
            lanes = pl.ds(r * members, members)
            if count == 1:
                copies.append(pltpu.make_async_copy(blocks[0].at[:, :, r], grid.at[:, :, :, lanes], sems.at[0, r]))
            else:
                target = grid.at[:, core, :, lanes]
                copies.append(pltpu.make_async_copy(blocks[0].at[:, core, r], target, sems.at[0, r]))
                target = grid.at[:, CORES - 1 - core, :, lanes]
                copies.append(pltpu.make_async_copy(blocks[1].at[:, r], target, sems.at[1, r]))
        run_copies(copies)

    field = grid[...].reshape(chips * cores * lats, rows * members)
    sums = jnp.dot(table_ref[0], field, preferred_element_type=F32)
    degree = lax.broadcasted_iota(jnp.int32, (members, width), 1) + (low + step * width)
    live = degree >= wave_ref[slot]
    for r in range(rows):
        total = state_ref[r, 0].astype(F32) + sums[:, r * members : (r + 1) * members].T
        out[r] = jnp.where(live, total, 0.0).astype(BF16)


def analyse(blocks, table, state, wave, me, token, slot, low, width):
    chips, _, rows, lats, members = blocks[0].shape
    nspec, nlat = table.shape[1:]
    first = low // width
    cores = CORES
    if lats % 16:
        if len(blocks) > 1:
            core = me[0] % CORES
            own = lax.dynamic_index_in_dim(blocks[0], core, 1, keepdims=False)
            pairs = [jnp.where(core == 0, own, blocks[1]), jnp.where(core == 0, blocks[1], own)]
            blocks = [jnp.stack(pairs, axis=1)]
        laid = jnp.transpose(blocks[0], (2, 0, 1, 3, 4)).reshape(1, 1, rows, nlat, members)
        blocks, chips, cores, lats = [laid], 1, 1, nlat
    return call(
        functools.partial(analyse_kernel, slot, low, len(blocks)),
        "analyse",
        2 * (nspec - low) * nlat * rows * members,
        2 * (nspec - low) * nlat,
        out_shape=jax.ShapeDtypeStruct((rows, members, nspec - low), BF16),
        grid=((nspec - low) // width,),
        in_specs=[
            IN_SMEM,
            IN_SMEM,
            ANYWHERE,
            pl.BlockSpec((1, width, nlat), lambda i: (slot, first + i, 0)),
            pl.BlockSpec((rows, 1, members, width), lambda i: (0, slot, 0, first + i)),
        ]
        + [ANYWHERE] * len(blocks),
        out_specs=pl.BlockSpec((rows, members, width), lambda i: (0, 0, i)),
        scratch_shapes=[
            pltpu.VMEM((chips, cores, lats, rows * members), BF16),
            pltpu.SemaphoreType.DMA((CORES, rows)),
        ],
    )(me, wave, token, table, state, *blocks)


def sum_pairs_kernel(coeff_ref, token_ref, inverse_ref, out_ref):
    pairs, entries = inverse_ref.shape[:2]
    half = entries // 2

    def one(entry, carry):
        real = imag = 0.0
        for k in range(pairs):
            first, second = inverse_ref[k, entry].astype(F32), inverse_ref[k, half + entry].astype(F32)
            a, b = coeff_ref[k, 0], coeff_ref[k, 1]
            real = real + (a * first - b * second)
            imag = imag + (a * second + b * first)
        out_ref[entry] = real
        out_ref[half + entry] = imag
        return carry

    lax.fori_loop(0, half, one, 0)


def sum_pairs(block_inverses, pole_coeffs, token):
    return call(
        sum_pairs_kernel,
        "sum_pairs",
        4 * block_inverses.size,
        2 * block_inverses.size,
        out_shape=jax.ShapeDtypeStruct(block_inverses.shape[1:], F32),
        in_specs=[IN_SMEM, ANYWHERE, pl.BlockSpec(block_inverses.shape, lambda: (0, 0, 0, 0))],
        out_specs=pl.BlockSpec(block_inverses.shape[1:], lambda: (0, 0, 0)),
    )(pole_coeffs, token, block_inverses)


def synthesise_kernel(slot, low, apart, me_ref, sign_ref, here_ref, there_ref, own_ref, other_ref, table_ref, *rest):
    rows, members, _ = own_ref.shape
    step = pl.program_id(0)
    if apart:
        outs, mate_out, mixed, held, sems = rest[:-4], rest[-4], rest[-3], rest[-2], rest[-1]
    else:
        own_out, mate_out, mixed = rest

    @pl.when(step == 0)
    def _():
        def line(entry):
            return here_ref[entry, slot : slot + 1, low:] + there_ref[entry, slot : slot + 1, low:]

        for f in range(rows):
            total = 0.0
            for g in range(rows):
                total = total + line(f * rows + g) * own_ref[g].astype(F32)
                total = total + sign_ref[0] * line(rows * rows + f * rows + g) * other_ref[g].astype(F32)
            mixed[f * members : (f + 1) * members, :] = total.astype(BF16)

    sums = jnp.dot(mixed[...], table_ref[0], preferred_element_type=F32)
    lats = mate_out.shape[2]
    each = mate_out.shape[0]
    for r in range(rows):
        turned = sums[r * members : (r + 1) * members, :].T
        values = [turned[i : i + lats] for i in range(0, turned.shape[0], lats)]
        mine, others = split_cores(values, me_ref[0] % CORES)
        for i, (a, b) in enumerate(zip(mine, others)):
            if apart:
                held[step * each + i, r] = a.astype(BF16)
            else:
                own_out[i, 0, r] = a.astype(BF16)
            mate_out[i, r] = b.astype(BF16)

    if apart:
        chip, core = me_ref[0] // CORES, me_ref[0] % CORES
        copies = []
        for i, (k, out) in enumerate(zip(partners(len(outs)), outs)):
            copies.append(pltpu.make_async_copy(held.at[chip ^ k], out.at[core], sems.at[i]))
            pl.when((chip ^ k) // each == step)(copies[-1].start)

        @pl.when(step == pl.num_programs(0) - 1)
        def _():
            for copy in copies:
                copy.wait()


def synthesise(here, there, sign, own, other, table, me, slot, low, lats, apart):
    rows, members, count = own.shape
    nlat = table.shape[2]
    width = math.lcm(CORES * lats, 128)
    chips, each = nlat // lats // CORES, width // lats // CORES
    matrix = pl.BlockSpec(here.shape, lambda j, m: (0, 0, 0))
    whole = pl.BlockSpec((rows, members, count), lambda j, m: (0, 0, 0))
    smem = pl.BlockSpec(memory_space=pltpu.SMEM)
    shapes = [jax.ShapeDtypeStruct((chips, CORES, rows, lats, members), BF16)]
    specs = [pl.BlockSpec((each, 1, rows, lats, members), lambda j, m: (j, m[0] % CORES, 0, 0, 0))]
    scratch = [pltpu.VMEM((rows * members, count), BF16)]
    if apart:
        shapes = [jax.ShapeDtypeStruct((CORES, rows, lats, members), BF16)] * chips
        specs = [ANYWHERE] * chips
        scratch += [pltpu.VMEM((chips, rows, lats, members), BF16), pltpu.SemaphoreType.DMA((chips,))]
    return call(
        functools.partial(synthesise_kernel, slot, low, apart),
        "synthesise",
        2 * count * nlat * rows * members,
        2 * count * nlat,
        out_shape=shapes + [jax.ShapeDtypeStruct((chips, rows, lats, members), BF16)],
        grid_spec=pltpu.PrefetchScalarGridSpec(
            num_scalar_prefetch=1,
            grid=(nlat // width,),
            in_specs=[
                smem,
                matrix,
                matrix,
                whole,
                whole,
                pl.BlockSpec((1, count, width), lambda j, m: (slot, low // count, j)),
            ],
            out_specs=specs + [pl.BlockSpec((each, rows, lats, members), lambda j, m: (j, 0, 0, 0))],
            scratch_shapes=scratch,
        ),
    )(me, sign, here, there, own, other, table)


def assemble_kernel(counts, me_ref, matrix_ref, *rest):
    ins, out_ref, (held, done, in_sems, out_sems) = rest[: sum(counts)], rest[-5], rest[-4:]
    rows, lats, slots, members = done.shape
    local_slots = len(counts)
    chip = me_ref[0] // CORES
    each = out_sems.shape[1]
    depth, breadth = math.gcd(lats // each, 16), 16
    size = lats // each
    copies, used = [], 0
    for r in range(rows):
        copies.append([])
        used = 0
        for slot, count in enumerate(counts):
            refs = ins[used : used + count]
            used += count
            if count == 1:
                copies[r].append(
                    pltpu.make_async_copy(refs[0].at[:, :, r], held.at[slot, :, :, r], in_sems.at[r, slot, 0])
                )
                continue
            for i, (k, ref) in enumerate(zip(partners(count), refs)):
                copies[r].append(
                    pltpu.make_async_copy(ref.at[:, r], held.at[slot, chip ^ k, :, r], in_sems.at[r, slot, i])
                )
        for copy in copies[r]:
            copy.start()
    matrix = matrix_ref[...]
    results = []
    for r in range(rows):
        for copy in copies[r]:
            copy.wait()
        for start in range(0, lats, depth):
            j = slice(start, start + depth)
            for s in range(0, slots, 2 * breadth):
                halves = []
                for h in (0, breadth):
                    columns = [divmod(i, local_slots) for i in range(s + h, s + h + breadth)]
                    columns = [held[slot, owner // CORES, owner % CORES, r, j, :] for owner, slot in columns]
                    halves.append(jnp.concatenate(columns, axis=0))
                turned = jnp.dot(matrix, jnp.concatenate(halves, axis=1), preferred_element_type=F32).astype(BF16)
                for h in range(2):
                    value = turned[:, h * members : (h + 1) * members].reshape(depth, breadth, members)
                    done[r, j, s + h * breadth : s + (h + 1) * breadth, :] = value
            if (start + depth) % size == 0:
                part = pl.ds(start + depth - size, size)
                results.append(
                    pltpu.make_async_copy(done.at[r, part], out_ref.at[r, part], out_sems.at[r, start // size])
                )
                results[-1].start()
    for copy in results:
        copy.wait()


def assemble(pieces, me):
    rows, lats, members = pieces[0][0].shape[-3:]
    chips = max(len(p) if len(p) > 1 else p[0].shape[0] for p in pieces)
    slots = len(pieces) * chips * CORES
    each = lats // lat_block(lats)
    matrix = swap_matrix(16, math.gcd(lats // each, 16), range(math.gcd(lats // each, 16)))
    flat = [block for slot in pieces for block in slot]
    return call(
        functools.partial(assemble_kernel, [len(p) for p in pieces]),
        "assemble",
        2 * 256 * rows * lats * slots * members,
        4 * rows * lats * slots * members,
        out_shape=jax.ShapeDtypeStruct((rows, lats, slots, members), BF16),
        in_specs=[IN_SMEM, pl.BlockSpec(matrix.shape, lambda: (0, 0))] + [ANYWHERE] * len(flat),
        out_specs=ANYWHERE,
        scratch_shapes=[
            pltpu.VMEM((len(pieces), chips, CORES, rows, lats, members), BF16),
            pltpu.VMEM((rows, lats, slots, members), BF16),
            pltpu.SemaphoreType.DMA((rows, len(pieces), chips)),
            pltpu.SemaphoreType.DMA((rows, each)),
        ],
    )(me, matrix, *flat)


def between_cores(blocks, owners):
    return lax.ppermute(blocks, "wave", [(d, d ^ 1) for d in range(owners)])


def by_permutes(messages):
    owners = len(messages) * CORES
    got = [messages[0]]
    for k, message in list(zip(partners(len(messages)), messages))[1:]:
        got.append(lax.ppermute(message, "wave", [(d, d ^ (k * CORES)) for d in range(owners)]))
    return got


def between_chips(blocks, owners):
    groups = [list(range(core, owners, CORES)) for core in range(CORES)]
    return lax.all_to_all(blocks, "wave", split_axis=0, concat_axis=0, axis_index_groups=groups, tiled=True)


def per_device(
    tendency, spectral_state, legendre, gauss_weights, block_inverses, pole_coeffs, wavenumbers
):
    rows, lats, slots, members = tendency.shape
    local_slots, nspec, nlat = legendre.shape
    owners = slots // local_slots
    me = lax.axis_index("wave").astype(jnp.int32).reshape(1)
    pole_index = lax.axis_index("pole")
    sign = (2 * pole_index - 1).astype(F32).reshape(1)
    order = list(range(local_slots))[::-1]
    received, waits = {}, []
    for slot in order:
        early = slot == order[0]
        *blocks, token = weigh(tendency, gauss_weights[None], me, slot, local_slots, not early, waits)
        if early:
            received[slot] = between_chips(blocks[0], owners)
            here = sum_pairs(block_inverses, pole_coeffs, token)
            there = lax.ppermute(here, "pole", [(0, 1), (1, 0)])
            waits = [there]
        else:
            blocks, token = pair(blocks[0], between_cores(blocks[1], owners), me)
            received[slot] = between_chips(blocks, owners)

    sent = {}
    for slot in order:
        low = nspec // 2 if slot % 2 else 0
        blocks = [received[slot]]
        if slot == order[0]:
            blocks.append(between_cores(pick(blocks[0], me, token), owners))
        forced = analyse(blocks, legendre, spectral_state, wavenumbers, me, token, slot, low, nspec // 2)
        other = lax.ppermute(forced, "pole", [(0, 1), (1, 0)])
        last = slot == order[-1]
        *own, for_mate = synthesise(here, there, sign, forced, other, legendre, me, slot, low, lats, last)
        mate = between_cores(for_mate, owners)
        if last:
            sent[slot] = by_permutes(pair_messages(own, mate, me))
        else:
            blocks, token = pair(own[0], mate, me)
            sent[slot] = [between_chips(blocks, owners)]
    return assemble([sent[slot] for slot in range(local_slots)], me)


def solution(mesh):
    in_specs = (
        P("pole", "wave", None, None),
        P("pole", "wave", None, None),
        P("wave", None, None),
        P("wave"),
        P("pole", None, "wave", None),
        P("pole", None),
        P("wave"),
    )
    out_specs = P("pole", "wave", None, None)
    return jax.shard_map(
        per_device, mesh=mesh, in_specs=in_specs, out_specs=out_specs, check_vma=False
    )
```

```python
import functools
import math

import jax
import jax.numpy as jnp
from jax import lax
from jax.experimental import pallas as pl
from jax.experimental.pallas import tpu as pltpu
from jax.sharding import PartitionSpec as P

BF16 = jnp.bfloat16
F32 = jnp.float32
CORES = 2
ANYWHERE = pl.BlockSpec(memory_space=pl.ANY)
IN_SMEM = pl.BlockSpec(memory_space=pltpu.SMEM)
TOKEN = jax.ShapeDtypeStruct((8, 128), F32)


def call(kernel, name, flops, size, mib=40, **kwargs):
    return pl.pallas_call(
        kernel,
        name=name,
        compiler_params=pltpu.CompilerParams(vmem_limit_bytes=mib * 1024 * 1024),
        cost_estimate=pl.CostEstimate(flops=int(flops), bytes_accessed=int(size), transcendentals=0),
        **kwargs,
    )


def run_copies(copies):
    for copy in copies:
        copy.start()
    for copy in copies:
        copy.wait()


def partners(chips):
    return [0] + list(range(chips // 2, chips)) + list(range(1, chips // 2))


def split_cores(values, core):
    even = [values[i] for i in range(0, len(values), CORES)]
    odd = [values[i] for i in range(1, len(values), CORES)]
    mine = [jnp.where(core == 0, a, b) for a, b in zip(even, odd)]
    others = [jnp.where(core == 0, b, a) for a, b in zip(even, odd)]
    return mine, others


def swap_matrix(rows, columns, step, skip):
    shape = (rows * columns // step, rows * columns)
    shift = rows.bit_length() - 1
    target = lax.broadcasted_iota(jnp.int32, shape, 0)
    source = lax.broadcasted_iota(jnp.int32, shape, 1)
    wanted = (target & (rows - 1)) * columns + (target >> shift) * step + skip
    return jnp.where(source == wanted, 1.0, 0.0).astype(BF16)


def weigh_kernel(slot, local_slots, split, waits, me_ref, gauss_any, tendency_ref, *rest):
    outs, token_ref, (gauss_ref, column, held, done, gauss_sem, in_sems, out_sems) = rest[waits:-8], rest[-8], rest[-7:]
    line_copy = pltpu.make_async_copy(gauss_any, gauss_ref, gauss_sem)
    line_copy.start()
    rows, lats, slots, members = held.shape
    each = in_sems.shape[1]
    size = lats // each
    copies = []
    for r in range(rows):
        for i in range(each):
            part = pl.ds(i * size, size)
            copies.append(pltpu.make_async_copy(tendency_ref.at[r, part], held.at[r, part], in_sems.at[r, i]))
            copies[-1].start()
    token_ref[...] = jnp.zeros_like(token_ref)
    depth, breadth = math.gcd(size, 16), 16
    matrix = swap_matrix(depth, breadth, local_slots, slot)
    owners = breadth // local_slots
    core = me_ref[0] % CORES
    line_copy.wait()
    for j in range(0, lats, depth):
        line = jnp.broadcast_to(gauss_ref[...], (depth, lats))
        here = lax.broadcasted_iota(jnp.int32, line.shape, 0) + j
        mine = lax.broadcasted_iota(jnp.int32, line.shape, 1) == here
        value = jnp.sum(jnp.where(mine, line, 0.0), axis=1, keepdims=True)
        column[j : j + depth, :] = jnp.broadcast_to(value, (depth, members))
    results = []
    for r in range(rows):
        for j in range(0, lats, depth):
            if j % size == 0:
                copies[r * each + j // size].wait()
            scale = column[j : j + depth, :]
            for s in range(0, slots, 2 * breadth):
                halves = [
                    held[r, j : j + depth, s + h : s + h + breadth, :].reshape(depth * breadth, members)
                    for h in (0, breadth)
                ]
                turned = jnp.dot(matrix, jnp.concatenate(halves, axis=1), preferred_element_type=F32)
                values = [
                    turned[i * depth : (i + 1) * depth, h * members : (h + 1) * members] * scale
                    for h in range(2)
                    for i in range(owners)
                ]
                start = s // local_slots
                if split:
                    mine, others = split_cores(values, core)
                    for i, (a, b) in enumerate(zip(mine, others)):
                        done[start // CORES + i, 0, r, j : j + depth, :] = a.astype(BF16)
                        done[start // CORES + i, 1, r, j : j + depth, :] = b.astype(BF16)
                else:
                    for i, value in enumerate(values):
                        chip, target = divmod(start + i, CORES)
                        done[chip, target, r, j : j + depth, :] = value.astype(BF16)
        if split:
            results.append(pltpu.make_async_copy(done.at[:, 0, r], outs[0].at[:, core, r], out_sems.at[0, r]))
            results.append(pltpu.make_async_copy(done.at[:, 1, r], outs[1].at[:, r], out_sems.at[1, r]))
            results[-2].start()
        else:
            results.append(pltpu.make_async_copy(done.at[:, :, r], outs[0].at[:, :, r], out_sems.at[0, r]))
        results[-1].start()
    for copy in results:
        copy.wait()


def lat_block(lats):
    return lats // 2 if lats % 32 == 0 else lats


def weigh(tendency, gauss, me, slot, local_slots, split, waits):
    rows, lats, slots, members = tendency.shape
    each = lats // lat_block(lats)
    chips = slots // local_slots // CORES
    shapes = [jax.ShapeDtypeStruct((chips, CORES, rows, lats, members), BF16)]
    if split:
        shapes += [jax.ShapeDtypeStruct((chips, rows, lats, members), BF16)]
    return call(
        functools.partial(weigh_kernel, slot, local_slots, split, len(waits)),
        "weigh",
        2 * 128 * tendency.size,
        3 * tendency.size,
        58,
        out_shape=shapes + [TOKEN],
        in_specs=[IN_SMEM] + [ANYWHERE] * (2 + len(waits)),
        out_specs=[ANYWHERE] * len(shapes) + [pl.BlockSpec(TOKEN.shape, lambda: (0, 0))],
        scratch_shapes=[
            pltpu.VMEM((1, lats), F32),
            pltpu.VMEM((lats, members), F32),
            pltpu.VMEM((rows, lats, slots, members), BF16),
            pltpu.VMEM((chips, CORES, rows, lats, members), BF16),
            pltpu.SemaphoreType.DMA,
            pltpu.SemaphoreType.DMA((rows, each)),
            pltpu.SemaphoreType.DMA((CORES, rows)),
        ],
    )(me, gauss, tendency, *waits)


def pick_kernel(me_ref, token_ref, in_ref, out_ref):
    out_ref[...] = in_ref[:, 0]


def pick(blocks, me, token):
    chips, _, rows, lats, members = blocks.shape
    return call(
        pick_kernel,
        "pick",
        0,
        2 * blocks.size,
        out_shape=jax.ShapeDtypeStruct((chips, rows, lats, members), BF16),
        grid_spec=pltpu.PrefetchScalarGridSpec(
            num_scalar_prefetch=1,
            grid=(rows,),
            in_specs=[
                ANYWHERE,
                pl.BlockSpec((chips, 1, 1, lats, members), lambda r, m: (0, CORES - 1 - m[0] % CORES, r, 0, 0))
            ],
            out_specs=pl.BlockSpec((chips, 1, lats, members), lambda r, m: (0, r, 0, 0)),
        ),
    )(me, token, blocks)


def pair_kernel(me_ref, mate_ref, blocks_ref, out_ref, token_ref, sem):
    token_ref[...] = jnp.zeros_like(token_ref)
    other = CORES - 1 - me_ref[0] % CORES
    run_copies([pltpu.make_async_copy(mate_ref, out_ref.at[:, other], sem)])


def pair(blocks, mate, me):
    return call(
        pair_kernel,
        "pair",
        0,
        4 * mate.size,
        out_shape=[jax.ShapeDtypeStruct(blocks.shape, blocks.dtype), TOKEN],
        in_specs=[IN_SMEM, pl.BlockSpec(mate.shape, lambda: (0, 0, 0, 0)), ANYWHERE],
        out_specs=[ANYWHERE, pl.BlockSpec(TOKEN.shape, lambda: (0, 0))],
        scratch_shapes=[pltpu.SemaphoreType.DMA],
        input_output_aliases={2: 0},
    )(me, mate, blocks)


def pair_messages_kernel(me_ref, mate_ref, *rest):
    chips = mate_ref.shape[0]
    outs, sems = rest[chips:-1], rest[-1]
    chip, other = me_ref[0] // CORES, CORES - 1 - me_ref[0] % CORES
    run_copies(
        [
            pltpu.make_async_copy(mate_ref.at[chip ^ k], out.at[other], sems.at[i])
            for i, (k, out) in enumerate(zip(partners(chips), outs))
        ]
    )


def pair_messages(messages, mate, me):
    chips = len(messages)
    return call(
        pair_messages_kernel,
        "pair",
        0,
        4 * mate.size,
        out_shape=[jax.ShapeDtypeStruct(m.shape, m.dtype) for m in messages],
        in_specs=[IN_SMEM, pl.BlockSpec(mate.shape, lambda: (0, 0, 0, 0))] + [ANYWHERE] * chips,
        out_specs=[ANYWHERE] * chips,
        scratch_shapes=[pltpu.SemaphoreType.DMA((chips,))],
        input_output_aliases={i + 2: i for i in range(chips)},
    )(me, mate, *messages)


def analyse_kernel(slot, low, count, me_ref, wave_ref, token_ref, table_ref, state_ref, *rest):
    blocks, out, grid = rest[:count], rest[count], rest[count + 1]
    rows, members, _ = out.shape
    chips, cores, lats, _ = grid.shape
    width = table_ref.shape[1]
    step = pl.program_id(0)

    @pl.when(step == 0)
    def _():
        core = me_ref[0] % CORES
        for r in range(rows):
            lanes = slice(r * members, (r + 1) * members)
            if count == 1:
                grid[:, :, :, lanes] = blocks[0][:, :, r]
            else:
                grid[:, core, :, lanes] = blocks[0][:, 0, r]
                grid[:, CORES - 1 - core, :, lanes] = blocks[1][:, r]

    field = grid[...].reshape(chips * cores * lats, rows * members)
    sums = jnp.dot(table_ref[0], field, preferred_element_type=F32)
    degree = lax.broadcasted_iota(jnp.int32, (members, width), 1) + (low + step * width)
    live = degree >= wave_ref[slot]
    for r in range(rows):
        total = state_ref[r, 0].astype(F32) + sums[:, r * members : (r + 1) * members].T
        out[r] = jnp.where(live, total, 0.0).astype(BF16)


def analyse(blocks, table, state, wave, me, token, slot, low, width):
    chips, _, rows, lats, members = blocks[0].shape
    nspec, nlat = table.shape[1:]
    first = low // width
    cores = CORES
    if lats % 16:
        if len(blocks) > 1:
            core = me[0] % CORES
            own = lax.dynamic_index_in_dim(blocks[0], core, 1, keepdims=False)
            pairs = [jnp.where(core == 0, own, blocks[1]), jnp.where(core == 0, blocks[1], own)]
            blocks = [jnp.stack(pairs, axis=1)]
        laid = jnp.transpose(blocks[0], (2, 0, 1, 3, 4)).reshape(1, 1, rows, nlat, members)
        blocks, chips, cores, lats = [laid], 1, 1, nlat
    windows = [pl.BlockSpec(blocks[0].shape, lambda i, m: (0, 0, 0, 0, 0))]
    if len(blocks) > 1:
        shape = (chips, 1) + blocks[0].shape[2:]
        windows = [pl.BlockSpec(shape, lambda i, m: (0, m[0] % CORES, 0, 0, 0))]
        windows += [pl.BlockSpec(blocks[1].shape, lambda i, m: (0, 0, 0, 0))]
    return call(
        functools.partial(analyse_kernel, slot, low, len(blocks)),
        "analyse",
        2 * (nspec - low) * nlat * rows * members,
        2 * (nspec - low) * nlat,
        out_shape=jax.ShapeDtypeStruct((rows, members, nspec - low), BF16),
        grid_spec=pltpu.PrefetchScalarGridSpec(
            num_scalar_prefetch=1,
            grid=((nspec - low) // width,),
            in_specs=[
                IN_SMEM,
                ANYWHERE,
                pl.BlockSpec((1, width, nlat), lambda i, m: (slot, first + i, 0)),
                pl.BlockSpec((rows, 1, members, width), lambda i, m: (0, slot, 0, first + i)),
            ]
            + windows,
            out_specs=pl.BlockSpec((rows, members, width), lambda i, m: (0, 0, i)),
            scratch_shapes=[pltpu.VMEM((chips, cores, lats, rows * members), BF16)],
        ),
    )(me, wave, token, table, state, *blocks)


def sum_pairs_kernel(coeff_ref, token_ref, inverse_ref, out_ref):
    pairs, entries = inverse_ref.shape[:2]
    half = entries // 2

    def one(entry, carry):
        real = imag = 0.0
        for k in range(pairs):
            first, second = inverse_ref[k, entry].astype(F32), inverse_ref[k, half + entry].astype(F32)
            a, b = coeff_ref[k, 0], coeff_ref[k, 1]
            real = real + (a * first - b * second)
            imag = imag + (a * second + b * first)
        out_ref[entry] = real
        out_ref[half + entry] = imag
        return carry

    lax.fori_loop(0, half, one, 0)


def sum_pairs(block_inverses, pole_coeffs, token):
    return call(
        sum_pairs_kernel,
        "sum_pairs",
        4 * block_inverses.size,
        2 * block_inverses.size,
        out_shape=jax.ShapeDtypeStruct(block_inverses.shape[1:], F32),
        in_specs=[IN_SMEM, ANYWHERE, pl.BlockSpec(block_inverses.shape, lambda: (0, 0, 0, 0))],
        out_specs=pl.BlockSpec(block_inverses.shape[1:], lambda: (0, 0, 0)),
    )(pole_coeffs, token, block_inverses)


def synthesise_kernel(slot, low, apart, me_ref, sign_ref, here_ref, there_ref, own_ref, other_ref, table_ref, *rest):
    rows, members, _ = own_ref.shape
    step = pl.program_id(0)
    if apart:
        outs, mate_out, mixed, held, sems = rest[:-4], rest[-4], rest[-3], rest[-2], rest[-1]
    else:
        own_out, mate_out, mixed = rest

    @pl.when(step == 0)
    def _():
        count = own_ref.shape[2]
        for n in range(0, count, 128):
            lanes = slice(low + n, low + n + 128)
            lines = [
                here_ref[entry, slot : slot + 1, lanes] + there_ref[entry, slot : slot + 1, lanes]
                for entry in range(2 * rows * rows)
            ]
            lines[rows * rows :] = [sign_ref[0] * line for line in lines[rows * rows :]]
            for e in range(0, members, 32):
                part = (slice(e, e + 32), slice(n, n + 128))
                owns = [own_ref[(g,) + part].astype(F32) for g in range(rows)]
                others = [other_ref[(g,) + part].astype(F32) for g in range(rows)]
                for f in range(rows):
                    total = 0.0
                    for g in range(rows):
                        total = total + lines[f * rows + g] * owns[g]
                        total = total + lines[rows * rows + f * rows + g] * others[g]
                    mixed[f * members + e : f * members + e + 32, n : n + 128] = total.astype(BF16)

    sums = jnp.dot(mixed[...], table_ref[0], preferred_element_type=F32)
    lats = mate_out.shape[2]
    each = mate_out.shape[0]
    for r in range(rows):
        turned = sums[r * members : (r + 1) * members, :].astype(BF16).T
        values = [turned[i : i + lats] for i in range(0, turned.shape[0], lats)]
        mine, others = split_cores(values, me_ref[0] % CORES)
        for i, (a, b) in enumerate(zip(mine, others)):
            if apart:
                held[step * each + i, r] = a
            else:
                own_out[i, 0, r] = a
            mate_out[i, r] = b

    if apart:
        chip, core = me_ref[0] // CORES, me_ref[0] % CORES
        copies = []
        for i, (k, out) in enumerate(zip(partners(len(outs)), outs)):
            copies.append(pltpu.make_async_copy(held.at[chip ^ k], out.at[core], sems.at[i]))
            pl.when((chip ^ k) // each == step)(copies[-1].start)

        @pl.when(step == pl.num_programs(0) - 1)
        def _():
            for copy in copies:
                copy.wait()


def synthesise(here, there, sign, own, other, table, me, slot, low, lats, apart):
    rows, members, count = own.shape
    nlat = table.shape[2]
    width = math.lcm(CORES * lats, 128)
    chips, each = nlat // lats // CORES, width // lats // CORES
    matrix = pl.BlockSpec(here.shape, lambda j, m: (0, 0, 0))
    whole = pl.BlockSpec((rows, members, count), lambda j, m: (0, 0, 0))
    smem = pl.BlockSpec(memory_space=pltpu.SMEM)
    shapes = [jax.ShapeDtypeStruct((chips, CORES, rows, lats, members), BF16)]
    specs = [pl.BlockSpec((each, 1, rows, lats, members), lambda j, m: (j, m[0] % CORES, 0, 0, 0))]
    scratch = [pltpu.VMEM((rows * members, count), BF16)]
    if apart:
        shapes = [jax.ShapeDtypeStruct((CORES, rows, lats, members), BF16)] * chips
        specs = [ANYWHERE] * chips
        scratch += [pltpu.VMEM((chips, rows, lats, members), BF16), pltpu.SemaphoreType.DMA((chips,))]
    return call(
        functools.partial(synthesise_kernel, slot, low, apart),
        "synthesise",
        2 * count * nlat * rows * members,
        2 * count * nlat,
        out_shape=shapes + [jax.ShapeDtypeStruct((chips, rows, lats, members), BF16)],
        grid_spec=pltpu.PrefetchScalarGridSpec(
            num_scalar_prefetch=1,
            grid=(nlat // width,),
            in_specs=[
                smem,
                matrix,
                matrix,
                whole,
                whole,
                pl.BlockSpec((1, count, width), lambda j, m: (slot, low // count, j)),
            ],
            out_specs=specs + [pl.BlockSpec((each, rows, lats, members), lambda j, m: (j, 0, 0, 0))],
            scratch_shapes=scratch,
        ),
    )(me, sign, here, there, own, other, table)


def assemble_kernel(counts, me_ref, *rest):
    ins, out, (held, matrix) = rest[: sum(counts)], rest[-3], rest[-2:]
    _, lats, slots, members = out.shape
    local_slots = len(counts)
    chip = me_ref[0] // CORES
    depth, breadth = math.gcd(lats, 16), 16

    @pl.when((pl.program_id(0) == 0) & (pl.program_id(1) == 0))
    def _():
        matrix[...] = swap_matrix(breadth, depth, 1, 0)

    views, used = [], 0
    for count in counts:
        refs = ins[used : used + count]
        used += count
        if count == 1:
            views.append(lambda owner, j, ref=refs[0]: ref[owner // CORES, owner % CORES, 0, j, :])
        else:
            for k, ref in zip(partners(count), refs):
                held[chip ^ k] = ref[:, 0]
            views.append(lambda owner, j: held[owner // CORES, owner % CORES, j, :])
    for start in range(0, lats, depth):
        j = slice(start, start + depth)
        for s in range(0, slots, 2 * breadth):
            halves = []
            for h in (0, breadth):
                columns = [divmod(i, local_slots) for i in range(s + h, s + h + breadth)]
                halves.append(jnp.concatenate([views[slot](owner, j) for owner, slot in columns], axis=0))
            turned = jnp.dot(matrix[...], jnp.concatenate(halves, axis=1), preferred_element_type=F32).astype(BF16)
            for h in range(2):
                value = turned[:, h * members : (h + 1) * members].reshape(depth, breadth, members)
                out[0, j, s + h * breadth : s + (h + 1) * breadth, :] = value


def assemble(pieces, me):
    rows, lats, members = pieces[0][0].shape[-3:]
    chips = max(len(p) if len(p) > 1 else p[0].shape[0] for p in pieces)
    slots = len(pieces) * chips * CORES
    each = lat_block(lats)
    side = 16 * math.gcd(each, 16)
    flat = [block for slot in pieces for block in slot]

    def window(block):
        lead = block.shape[:-3]
        return pl.BlockSpec(lead + (1, each, members), lambda r, j, m: (0,) * len(lead) + (r, j, 0))

    return call(
        functools.partial(assemble_kernel, [len(p) for p in pieces]),
        "assemble",
        2 * 256 * rows * lats * slots * members,
        4 * rows * lats * slots * members,
        out_shape=jax.ShapeDtypeStruct((rows, lats, slots, members), BF16),
        grid_spec=pltpu.PrefetchScalarGridSpec(
            num_scalar_prefetch=1,
            grid=(rows, lats // each),
            in_specs=[window(block) for block in flat],
            out_specs=pl.BlockSpec((1, each, slots, members), lambda r, j, m: (r, j, 0, 0)),
            scratch_shapes=[pltpu.VMEM((chips, CORES, each, members), BF16), pltpu.VMEM((side, side), BF16)],
        ),
    )(me, *flat)


def between_cores(blocks, owners):
    return lax.ppermute(blocks, "wave", [(d, d ^ 1) for d in range(owners)])


def by_permutes(messages):
    owners = len(messages) * CORES
    got = [messages[0]]
    for k, message in list(zip(partners(len(messages)), messages))[1:]:
        got.append(lax.ppermute(message, "wave", [(d, d ^ (k * CORES)) for d in range(owners)]))
    return got


def between_chips(blocks, owners):
    groups = [list(range(core, owners, CORES)) for core in range(CORES)]
    return lax.all_to_all(blocks, "wave", split_axis=0, concat_axis=0, axis_index_groups=groups, tiled=True)


def per_device(
    tendency, spectral_state, legendre, gauss_weights, block_inverses, pole_coeffs, wavenumbers
):
    rows, lats, slots, members = tendency.shape
    local_slots, nspec, nlat = legendre.shape
    owners = slots // local_slots
    me = lax.axis_index("wave").astype(jnp.int32).reshape(1)
    pole_index = lax.axis_index("pole")
    sign = (2 * pole_index - 1).astype(F32).reshape(1)
    order = list(range(local_slots))[::-1]
    received, waits = {}, []
    for slot in order:
        early = slot == order[0]
        *blocks, token = weigh(tendency, gauss_weights[None], me, slot, local_slots, not early, waits)
        if early:
            received[slot] = between_chips(blocks[0], owners)
            here = sum_pairs(block_inverses, pole_coeffs, token)
            there = lax.ppermute(here, "pole", [(0, 1), (1, 0)])
            waits = [there]
        else:
            blocks, token = pair(blocks[0], between_cores(blocks[1], owners), me)
            received[slot] = between_chips(blocks, owners)

    sent = {}
    for slot in order:
        low = nspec // 2 if slot % 2 else 0
        blocks = [received[slot]]
        if slot == order[0]:
            blocks.append(between_cores(pick(blocks[0], me, token), owners))
        forced = analyse(blocks, legendre, spectral_state, wavenumbers, me, token, slot, low, nspec // 2)
        other = lax.ppermute(forced, "pole", [(0, 1), (1, 0)])
        last = slot == order[-1]
        *own, for_mate = synthesise(here, there, sign, forced, other, legendre, me, slot, low, lats, last)
        mate = between_cores(for_mate, owners)
        if last:
            sent[slot] = by_permutes(pair_messages(own, mate, me))
        else:
            blocks, token = pair(own[0], mate, me)
            sent[slot] = [between_chips(blocks, owners)]
    return assemble([sent[slot] for slot in range(local_slots)], me)


def solution(mesh):
    in_specs = (
        P("pole", "wave", None, None),
        P("pole", "wave", None, None),
        P("wave", None, None),
        P("wave"),
        P("pole", None, "wave", None),
        P("pole", None),
        P("wave"),
    )
    out_specs = P("pole", "wave", None, None)
    return jax.shard_map(
        per_device, mesh=mesh, in_specs=in_specs, out_specs=out_specs, check_vma=False
    )
```

```python
import functools
import math

import jax
import jax.numpy as jnp
from jax import lax
from jax.experimental import pallas as pl
from jax.experimental.pallas import tpu as pltpu
from jax.sharding import PartitionSpec as P

BF16 = jnp.bfloat16
F32 = jnp.float32
CORES = 2
ANYWHERE = pl.BlockSpec(memory_space=pl.ANY)
IN_SMEM = pl.BlockSpec(memory_space=pltpu.SMEM)
TOKEN = jax.ShapeDtypeStruct((8, 128), F32)


def call(kernel, name, flops, size, mib=40, **kwargs):
    return pl.pallas_call(
        kernel,
        name=name,
        compiler_params=pltpu.CompilerParams(vmem_limit_bytes=mib * 1024 * 1024),
        cost_estimate=pl.CostEstimate(flops=int(flops), bytes_accessed=int(size), transcendentals=0),
        **kwargs,
    )


def run_copies(copies):
    for copy in copies:
        copy.start()
    for copy in copies:
        copy.wait()


def partners(chips):
    return [0] + list(range(chips // 2, chips)) + list(range(1, chips // 2))


def split_cores(values, core):
    even = [values[i] for i in range(0, len(values), CORES)]
    odd = [values[i] for i in range(1, len(values), CORES)]
    mine = [jnp.where(core == 0, a, b) for a, b in zip(even, odd)]
    others = [jnp.where(core == 0, b, a) for a, b in zip(even, odd)]
    return mine, others


def swap_matrix(rows, columns, step, skip):
    shape = (rows * columns // step, rows * columns)
    shift = rows.bit_length() - 1
    target = lax.broadcasted_iota(jnp.int32, shape, 0)
    source = lax.broadcasted_iota(jnp.int32, shape, 1)
    wanted = (target & (rows - 1)) * columns + (target >> shift) * step + skip
    return jnp.where(source == wanted, 1.0, 0.0).astype(BF16)


def weigh_kernel(slot, local_slots, split, waits, me_ref, gauss_any, tendency_ref, *rest):
    outs, token_ref, (gauss_ref, column, held, done, gauss_sem, in_sems, out_sems) = rest[waits:-8], rest[-8], rest[-7:]
    line_copy = pltpu.make_async_copy(gauss_any, gauss_ref, gauss_sem)
    line_copy.start()
    rows, lats, slots, members = held.shape
    each = in_sems.shape[1]
    size = lats // each
    copies = []
    for r in range(rows):
        for i in range(each):
            part = pl.ds(i * size, size)
            copies.append(pltpu.make_async_copy(tendency_ref.at[r, part], held.at[r, part], in_sems.at[r, i]))
            copies[-1].start()
    token_ref[...] = jnp.zeros_like(token_ref)
    depth, breadth = math.gcd(size, 16), 16
    matrix = swap_matrix(depth, breadth, local_slots, slot)
    owners = breadth // local_slots
    core = me_ref[0] % CORES
    line_copy.wait()
    for j in range(0, lats, depth):
        line = jnp.broadcast_to(gauss_ref[...], (depth, lats))
        here = lax.broadcasted_iota(jnp.int32, line.shape, 0) + j
        mine = lax.broadcasted_iota(jnp.int32, line.shape, 1) == here
        value = jnp.sum(jnp.where(mine, line, 0.0), axis=1, keepdims=True)
        column[j : j + depth, :] = jnp.broadcast_to(value, (depth, members))
    results = []
    for r in range(rows):
        for j in range(0, lats, depth):
            if j % size == 0:
                copies[r * each + j // size].wait()
            scale = column[j : j + depth, :]
            for s in range(0, slots, 2 * breadth):
                halves = [
                    held[r, j : j + depth, s + h : s + h + breadth, :].reshape(depth * breadth, members)
                    for h in (0, breadth)
                ]
                turned = jnp.dot(matrix, jnp.concatenate(halves, axis=1), preferred_element_type=F32)
                values = [
                    turned[i * depth : (i + 1) * depth, h * members : (h + 1) * members] * scale
                    for h in range(2)
                    for i in range(owners)
                ]
                start = s // local_slots
                if split:
                    mine, others = split_cores(values, core)
                    for i, (a, b) in enumerate(zip(mine, others)):
                        done[start // CORES + i, 0, r, j : j + depth, :] = a.astype(BF16)
                        done[start // CORES + i, 1, r, j : j + depth, :] = b.astype(BF16)
                else:
                    for i, value in enumerate(values):
                        chip, target = divmod(start + i, CORES)
                        done[chip, target, r, j : j + depth, :] = value.astype(BF16)
        if split:
            results.append(pltpu.make_async_copy(done.at[:, 0, r], outs[0].at[:, core, r], out_sems.at[0, r]))
            results.append(pltpu.make_async_copy(done.at[:, 1, r], outs[1].at[:, r], out_sems.at[1, r]))
            results[-2].start()
        else:
            results.append(pltpu.make_async_copy(done.at[:, :, r], outs[0].at[:, :, r], out_sems.at[0, r]))
        results[-1].start()
    for copy in results:
        copy.wait()


def lat_block(lats):
    return lats // 2 if lats % 32 == 0 else lats


def weigh(tendency, gauss, me, slot, local_slots, split, waits):
    rows, lats, slots, members = tendency.shape
    each = lats // lat_block(lats)
    chips = slots // local_slots // CORES
    shapes = [jax.ShapeDtypeStruct((chips, CORES, rows, lats, members), BF16)]
    if split:
        shapes += [jax.ShapeDtypeStruct((chips, rows, lats, members), BF16)]
    return call(
        functools.partial(weigh_kernel, slot, local_slots, split, len(waits)),
        "weigh",
        2 * 128 * tendency.size,
        3 * tendency.size,
        58,
        out_shape=shapes + [TOKEN],
        in_specs=[IN_SMEM] + [ANYWHERE] * (2 + len(waits)),
        out_specs=[ANYWHERE] * len(shapes) + [pl.BlockSpec(TOKEN.shape, lambda: (0, 0))],
        scratch_shapes=[
            pltpu.VMEM((1, lats), F32),
            pltpu.VMEM((lats, members), F32),
            pltpu.VMEM((rows, lats, slots, members), BF16),
            pltpu.VMEM((chips, CORES, rows, lats, members), BF16),
            pltpu.SemaphoreType.DMA,
            pltpu.SemaphoreType.DMA((rows, each)),
            pltpu.SemaphoreType.DMA((CORES, rows)),
        ],
    )(me, gauss, tendency, *waits)


def pick_kernel(me_ref, token_ref, in_ref, out_ref):
    out_ref[...] = in_ref[:, 0]


def pick(blocks, me, token):
    chips, _, rows, lats, members = blocks.shape
    return call(
        pick_kernel,
        "pick",
        0,
        2 * blocks.size,
        out_shape=jax.ShapeDtypeStruct((chips, rows, lats, members), BF16),
        grid_spec=pltpu.PrefetchScalarGridSpec(
            num_scalar_prefetch=1,
            grid=(rows,),
            in_specs=[
                ANYWHERE,
                pl.BlockSpec((chips, 1, 1, lats, members), lambda r, m: (0, CORES - 1 - m[0] % CORES, r, 0, 0))
            ],
            out_specs=pl.BlockSpec((chips, 1, lats, members), lambda r, m: (0, r, 0, 0)),
        ),
    )(me, token, blocks)


def pair_kernel(me_ref, mate_ref, blocks_ref, out_ref, token_ref, sem):
    token_ref[...] = jnp.zeros_like(token_ref)
    other = CORES - 1 - me_ref[0] % CORES
    run_copies([pltpu.make_async_copy(mate_ref, out_ref.at[:, other], sem)])


def pair(blocks, mate, me):
    return call(
        pair_kernel,
        "pair",
        0,
        4 * mate.size,
        out_shape=[jax.ShapeDtypeStruct(blocks.shape, blocks.dtype), TOKEN],
        in_specs=[IN_SMEM, pl.BlockSpec(mate.shape, lambda: (0, 0, 0, 0)), ANYWHERE],
        out_specs=[ANYWHERE, pl.BlockSpec(TOKEN.shape, lambda: (0, 0))],
        scratch_shapes=[pltpu.SemaphoreType.DMA],
        input_output_aliases={2: 0},
    )(me, mate, blocks)


def pair_messages_kernel(first, waits, me_ref, mate_ref, *rest):
    count = (len(rest) - 1 - waits) // 2
    outs, sems = rest[-1 - count : -1], rest[-1]
    chip, other = me_ref[0] // CORES, CORES - 1 - me_ref[0] % CORES
    wanted = partners(mate_ref.shape[0])[first : first + count]
    run_copies(
        [
            pltpu.make_async_copy(mate_ref.at[chip ^ k], out.at[other], sems.at[i])
            for i, (k, out) in enumerate(zip(wanted, outs))
        ]
    )


def pair_messages(messages, mate, me, first, waits):
    count = len(messages)
    return call(
        functools.partial(pair_messages_kernel, first, len(waits)),
        "pair",
        0,
        4 * mate.size,
        out_shape=[jax.ShapeDtypeStruct(m.shape, m.dtype) for m in messages],
        in_specs=[IN_SMEM, pl.BlockSpec(mate.shape, lambda: (0, 0, 0, 0))] + [ANYWHERE] * (count + len(waits)),
        out_specs=[ANYWHERE] * count,
        scratch_shapes=[pltpu.SemaphoreType.DMA((count,))],
        input_output_aliases={i + 2: i for i in range(count)},
    )(me, mate, *messages, *waits)


def analyse_kernel(slot, low, me_ref, wave_ref, token_ref, table_ref, state_ref, *rest):
    blocks, out, (grid, table, state, table_sems, state_sem) = rest[:-6], rest[-6], rest[-5:]
    rows, members, width = out.shape
    chips, cores, lats, _ = grid.shape
    cuts = [0] + list(range(width % 256, width + 1, 256))
    cuts = sorted(set(cuts))
    copies = []
    for i, (start, end) in enumerate(zip(cuts, cuts[1:])):
        source = table_ref.at[slot, pl.ds(low + start, end - start)]
        copies.append(pltpu.make_async_copy(source, table.at[pl.ds(start, end - start)], table_sems.at[i]))
        copies[-1].start()
    state_copy = pltpu.make_async_copy(state_ref.at[:, slot, :, pl.ds(low, width)], state, state_sem)
    state_copy.start()
    core = me_ref[0] % CORES
    for r in range(rows):
        lanes = slice(r * members, (r + 1) * members)
        if len(blocks) == 1:
            grid[:, :, :, lanes] = blocks[0][:, :, r]
        else:
            grid[:, core, :, lanes] = blocks[0][:, 0, r]
            grid[:, CORES - 1 - core, :, lanes] = blocks[1][:, r]
    field = grid[...].reshape(chips * cores * lats, rows * members)
    state_copy.wait()
    for copy, start, end in zip(copies, cuts, cuts[1:]):
        copy.wait()
        sums = jnp.dot(table[start:end], field, preferred_element_type=F32)
        degree = lax.broadcasted_iota(jnp.int32, (members, end - start), 1) + (low + start)
        live = degree >= wave_ref[slot]
        for r in range(rows):
            total = state[r, :, start:end].astype(F32) + sums[:, r * members : (r + 1) * members].T
            out[r, :, start:end] = jnp.where(live, total, 0.0).astype(BF16)


def analyse(blocks, table, state, wave, me, token, slot, low, width):
    chips, _, rows, lats, members = blocks[0].shape
    nlat = table.shape[2]
    cores = CORES
    if lats % 16:
        if len(blocks) > 1:
            core = me[0] % CORES
            own = lax.dynamic_index_in_dim(blocks[0], core, 1, keepdims=False)
            pairs = [jnp.where(core == 0, own, blocks[1]), jnp.where(core == 0, blocks[1], own)]
            blocks = [jnp.stack(pairs, axis=1)]
        laid = jnp.transpose(blocks[0], (2, 0, 1, 3, 4)).reshape(1, 1, rows, nlat, members)
        blocks, chips, cores, lats = [laid], 1, 1, nlat
    windows = [pl.BlockSpec(blocks[0].shape, lambda i, m: (0, 0, 0, 0, 0))]
    if len(blocks) > 1:
        shape = (chips, 1) + blocks[0].shape[2:]
        windows = [pl.BlockSpec(shape, lambda i, m: (0, m[0] % CORES, 0, 0, 0))]
        windows += [pl.BlockSpec(blocks[1].shape, lambda i, m: (0, 0, 0, 0))]
    in_hbm = pl.BlockSpec(memory_space=pltpu.HBM)
    return call(
        functools.partial(analyse_kernel, slot, low),
        "analyse",
        2 * width * nlat * rows * members,
        2 * width * nlat,
        out_shape=jax.ShapeDtypeStruct((rows, members, width), BF16),
        grid_spec=pltpu.PrefetchScalarGridSpec(
            num_scalar_prefetch=1,
            grid=(1,),
            in_specs=[IN_SMEM, ANYWHERE, in_hbm, in_hbm] + windows,
            out_specs=pl.BlockSpec((rows, members, width), lambda i, m: (0, 0, 0)),
            scratch_shapes=[
                pltpu.VMEM((chips, cores, lats, rows * members), BF16),
                pltpu.VMEM((width, nlat), BF16),
                pltpu.VMEM((rows, members, width), BF16),
                pltpu.SemaphoreType.DMA((width // 256 + 1,)),
                pltpu.SemaphoreType.DMA,
            ],
        ),
    )(me, wave, token, table, state, *blocks)


def sum_pairs_kernel(coeff_ref, token_ref, inverse_ref, out_ref):
    pairs, entries = inverse_ref.shape[:2]
    half = entries // 2

    def one(entry, carry):
        real = imag = 0.0
        for k in range(pairs):
            first, second = inverse_ref[k, entry].astype(F32), inverse_ref[k, half + entry].astype(F32)
            a, b = coeff_ref[k, 0], coeff_ref[k, 1]
            real = real + (a * first - b * second)
            imag = imag + (a * second + b * first)
        out_ref[entry] = real
        out_ref[half + entry] = imag
        return carry

    lax.fori_loop(0, half, one, 0)


def sum_pairs(block_inverses, pole_coeffs, token):
    return call(
        sum_pairs_kernel,
        "sum_pairs",
        4 * block_inverses.size,
        2 * block_inverses.size,
        out_shape=jax.ShapeDtypeStruct(block_inverses.shape[1:], F32),
        in_specs=[IN_SMEM, ANYWHERE, pl.BlockSpec(block_inverses.shape, lambda: (0, 0, 0, 0))],
        out_specs=pl.BlockSpec(block_inverses.shape[1:], lambda: (0, 0, 0)),
    )(pole_coeffs, token, block_inverses)


def synthesise_kernel(
    slot, low, apart, more, partial, me_ref, sign_ref, here_ref, there_ref, own_ref, other_ref, table_ref, *rest
):
    rows, members, _ = own_ref.shape
    step = pl.program_id(0)
    if partial:
        partial_ref, rest = rest[0], rest[1:]
    if more:
        sums_out, mixed = rest
    elif apart:
        outs, mate_out, mixed, held, sems = rest[:-4], rest[-4], rest[-3], rest[-2], rest[-1]
    else:
        own_out, mate_out, mixed = rest

    @pl.when(step == 0)
    def _():
        count = own_ref.shape[2]
        for n in range(0, count, 128):
            lanes = slice(low + n, low + n + 128)
            lines = [
                here_ref[entry, slot : slot + 1, lanes] + there_ref[entry, slot : slot + 1, lanes]
                for entry in range(2 * rows * rows)
            ]
            lines[rows * rows :] = [sign_ref[0] * line for line in lines[rows * rows :]]
            for e in range(0, members, 32):
                part = (slice(e, e + 32), slice(n, n + 128))
                owns = [own_ref[(g,) + part].astype(F32) for g in range(rows)]
                others = [other_ref[(g,) + part].astype(F32) for g in range(rows)]
                for f in range(rows):
                    total = 0.0
                    for g in range(rows):
                        total = total + lines[f * rows + g] * owns[g]
                        total = total + lines[rows * rows + f * rows + g] * others[g]
                    mixed[f * members + e : f * members + e + 32, n : n + 128] = total.astype(BF16)

    sums = jnp.dot(mixed[...], table_ref[0], preferred_element_type=F32)
    if partial:
        sums = sums + partial_ref[...]
    if more:
        sums_out[...] = sums
        return
    lats = mate_out.shape[2]
    each = mate_out.shape[0]
    for r in range(rows):
        turned = sums[r * members : (r + 1) * members, :].astype(BF16).T
        values = [turned[i : i + lats] for i in range(0, turned.shape[0], lats)]
        mine, others = split_cores(values, me_ref[0] % CORES)
        for i, (a, b) in enumerate(zip(mine, others)):
            if apart:
                held[step * each + i, r] = a
            else:
                own_out[i, 0, r] = a
            mate_out[i, r] = b

    if apart:
        chip, core = me_ref[0] // CORES, me_ref[0] % CORES
        copies = []
        for i, (k, out) in enumerate(zip(partners(len(outs)), outs)):
            copies.append(pltpu.make_async_copy(held.at[chip ^ k], out.at[core], sems.at[i]))
            pl.when((chip ^ k) // each == step)(copies[-1].start)

        @pl.when(step == pl.num_programs(0) - 1)
        def _():
            for copy in copies:
                copy.wait()


def synthesise(here, there, sign, own, other, table, me, slot, low, lats, apart, more, partial):
    rows, members, count = own.shape
    nlat = table.shape[2]
    width = math.lcm(CORES * lats, 128)
    chips, each = nlat // lats // CORES, width // lats // CORES
    matrix = pl.BlockSpec(here.shape, lambda j, m: (0, 0, 0))
    whole = pl.BlockSpec((rows, members, count), lambda j, m: (0, 0, 0))
    smem = pl.BlockSpec(memory_space=pltpu.SMEM)
    shapes = [jax.ShapeDtypeStruct((chips, CORES, rows, lats, members), BF16)]
    specs = [pl.BlockSpec((each, 1, rows, lats, members), lambda j, m: (j, m[0] % CORES, 0, 0, 0))]
    scratch = [pltpu.VMEM((rows * members, count), BF16)]
    shapes += [jax.ShapeDtypeStruct((chips, rows, lats, members), BF16)]
    specs += [pl.BlockSpec((each, rows, lats, members), lambda j, m: (j, 0, 0, 0))]
    sums = pl.BlockSpec((rows * members, width), lambda j, m: (0, j))
    if more:
        shapes, specs = [jax.ShapeDtypeStruct((rows * members, nlat), F32)], [sums]
    elif apart:
        shapes[:1] = [jax.ShapeDtypeStruct((CORES, rows, lats, members), BF16)] * chips
        specs[:1] = [ANYWHERE] * chips
        scratch += [pltpu.VMEM((chips, rows, lats, members), BF16), pltpu.SemaphoreType.DMA((chips,))]
    return call(
        functools.partial(synthesise_kernel, slot, low, apart, more, len(partial)),
        "synthesise",
        2 * count * nlat * rows * members,
        2 * count * nlat,
        out_shape=shapes,
        grid_spec=pltpu.PrefetchScalarGridSpec(
            num_scalar_prefetch=1,
            grid=(nlat // width,),
            in_specs=[
                smem,
                matrix,
                matrix,
                whole,
                whole,
                pl.BlockSpec((1, count, width), lambda j, m: (slot, low // count, j)),
            ]
            + [sums] * len(partial),
            out_specs=specs,
            scratch_shapes=scratch,
        ),
    )(me, sign, here, there, own, other, table, *partial)


def assemble_kernel(counts, me_ref, *rest):
    ins, out, (held, matrix) = rest[: sum(counts)], rest[-3], rest[-2:]
    _, lats, slots, members = out.shape
    local_slots = len(counts)
    chip = me_ref[0] // CORES
    depth, breadth = math.gcd(lats, 16), 16

    @pl.when((pl.program_id(0) == 0) & (pl.program_id(1) == 0))
    def _():
        matrix[...] = swap_matrix(breadth, depth, 1, 0)

    views, used = [], 0
    for count in counts:
        refs = ins[used : used + count]
        used += count
        if count == 1:
            views.append(lambda owner, j, ref=refs[0]: ref[owner // CORES, owner % CORES, 0, j, :])
        else:
            for k, ref in zip(partners(count), refs):
                held[chip ^ k] = ref[:, 0]
            views.append(lambda owner, j: held[owner // CORES, owner % CORES, j, :])
    for start in range(0, lats, depth):
        j = slice(start, start + depth)
        for s in range(0, slots, 2 * breadth):
            halves = []
            for h in (0, breadth):
                columns = [divmod(i, local_slots) for i in range(s + h, s + h + breadth)]
                halves.append(jnp.concatenate([views[slot](owner, j) for owner, slot in columns], axis=0))
            turned = jnp.dot(matrix[...], jnp.concatenate(halves, axis=1), preferred_element_type=F32).astype(BF16)
            for h in range(2):
                value = turned[:, h * members : (h + 1) * members].reshape(depth, breadth, members)
                out[0, j, s + h * breadth : s + (h + 1) * breadth, :] = value


def assemble(pieces, me):
    rows, lats, members = pieces[0][0].shape[-3:]
    chips = max(len(p) if len(p) > 1 else p[0].shape[0] for p in pieces)
    slots = len(pieces) * chips * CORES
    each = lat_block(lats)
    side = 16 * math.gcd(each, 16)
    flat = [block for slot in pieces for block in slot]

    def window(block):
        lead = block.shape[:-3]
        return pl.BlockSpec(lead + (1, each, members), lambda r, j, m: (0,) * len(lead) + (r, j, 0))

    return call(
        functools.partial(assemble_kernel, [len(p) for p in pieces]),
        "assemble",
        2 * 256 * rows * lats * slots * members,
        4 * rows * lats * slots * members,
        out_shape=jax.ShapeDtypeStruct((rows, lats, slots, members), BF16),
        grid_spec=pltpu.PrefetchScalarGridSpec(
            num_scalar_prefetch=1,
            grid=(rows, lats // each),
            in_specs=[window(block) for block in flat],
            out_specs=pl.BlockSpec((1, each, slots, members), lambda r, j, m: (r, j, 0, 0)),
            scratch_shapes=[pltpu.VMEM((chips, CORES, each, members), BF16), pltpu.VMEM((side, side), BF16)],
        ),
    )(me, *flat)


def between_cores(blocks, owners):
    return lax.ppermute(blocks, "wave", [(d, d ^ 1) for d in range(owners)])


def by_permutes(messages):
    owners = len(messages) * CORES
    got = [messages[0]]
    for k, message in list(zip(partners(len(messages)), messages))[1:]:
        got.append(lax.ppermute(message, "wave", [(d, d ^ (k * CORES)) for d in range(owners)]))
    return got


def between_chips(blocks, owners):
    groups = [list(range(core, owners, CORES)) for core in range(CORES)]
    return lax.all_to_all(blocks, "wave", split_axis=0, concat_axis=0, axis_index_groups=groups, tiled=True)


def per_device(
    tendency, spectral_state, legendre, gauss_weights, block_inverses, pole_coeffs, wavenumbers
):
    rows, lats, slots, members = tendency.shape
    local_slots, nspec, nlat = legendre.shape
    owners = slots // local_slots
    me = lax.axis_index("wave").astype(jnp.int32).reshape(1)
    pole_index = lax.axis_index("pole")
    sign = (2 * pole_index - 1).astype(F32).reshape(1)
    order = list(range(local_slots))[::-1]
    received, waits = {}, []
    for slot in order:
        early = slot == order[0]
        *blocks, token = weigh(tendency, gauss_weights[None], me, slot, local_slots, not early, waits)
        if early:
            received[slot] = between_chips(blocks[0], owners)
            here = sum_pairs(block_inverses, pole_coeffs, token)
            there = lax.ppermute(here, "pole", [(0, 1), (1, 0)])
            waits = [there]
        else:
            blocks, token = pair(blocks[0], between_cores(blocks[1], owners), me)
            received[slot] = between_chips(blocks, owners)

    sent = {}
    for slot in order:
        half = nspec // 2
        lows = [half] if slot % 2 else [0, half]
        blocks = [received[slot]]
        if slot == order[0]:
            blocks.append(between_cores(pick(blocks[0], me, token), owners))
        forced = [analyse(blocks, legendre, spectral_state, wavenumbers, me, token, slot, low, half) for low in lows]
        others = [lax.ppermute(part, "pole", [(0, 1), (1, 0)]) for part in forced]
        last = slot == order[-1]
        own = []
        for low, part, other in zip(lows, forced, others):
            more = low != lows[-1]
            own = synthesise(here, there, sign, part, other, legendre, me, slot, low, lats, last, more, own)
        *own, for_mate = own
        mate = between_cores(for_mate, owners)
        if last:
            far = len(own) // 2 + 1
            own = list(pair_messages(own[:far], mate, me, 0, [])) + list(
                pair_messages(own[far:], mate, me, far, sent[order[0]])
            )
            sent[slot] = by_permutes(own)
        else:
            blocks, token = pair(own[0], mate, me)
            sent[slot] = [between_chips(blocks, owners)]
    return assemble([sent[slot] for slot in range(local_slots)], me)


def solution(mesh):
    in_specs = (
        P("pole", "wave", None, None),
        P("pole", "wave", None, None),
        P("wave", None, None),
        P("wave"),
        P("pole", None, "wave", None),
        P("pole", None),
        P("wave"),
    )
    out_specs = P("pole", "wave", None, None)
    return jax.shard_map(
        per_device, mesh=mesh, in_specs=in_specs, out_specs=out_specs, check_vma=False
    )
```

```python
import functools
import math

import jax
import jax.numpy as jnp
from jax import lax
from jax.experimental import pallas as pl
from jax.experimental.pallas import tpu as pltpu
from jax.sharding import PartitionSpec as P

BF16 = jnp.bfloat16
F32 = jnp.float32
CORES = 2
ANYWHERE = pl.BlockSpec(memory_space=pl.ANY)
IN_SMEM = pl.BlockSpec(memory_space=pltpu.SMEM)
IN_HBM = pl.BlockSpec(memory_space=pltpu.HBM)
TOKEN = jax.ShapeDtypeStruct((8, 128), F32)


def call(kernel, name, flops, size, mib=40, **kwargs):
    return pl.pallas_call(
        kernel,
        name=name,
        compiler_params=pltpu.CompilerParams(vmem_limit_bytes=mib * 1024 * 1024),
        cost_estimate=pl.CostEstimate(flops=int(flops), bytes_accessed=int(size), transcendentals=0),
        **kwargs,
    )


def run_copies(copies):
    for copy in copies:
        copy.start()
    for copy in copies:
        copy.wait()


def partners(chips):
    return [0] + list(range(chips // 2, chips)) + list(range(1, chips // 2))


def split_cores(values, core):
    even = [values[i] for i in range(0, len(values), CORES)]
    odd = [values[i] for i in range(1, len(values), CORES)]
    mine = [jnp.where(core == 0, a, b) for a, b in zip(even, odd)]
    others = [jnp.where(core == 0, b, a) for a, b in zip(even, odd)]
    return mine, others


def swap_matrix(rows, columns, step, skip):
    shape = (rows * columns // step, rows * columns)
    shift = rows.bit_length() - 1
    target = lax.broadcasted_iota(jnp.int32, shape, 0)
    source = lax.broadcasted_iota(jnp.int32, shape, 1)
    wanted = (target & (rows - 1)) * columns + (target >> shift) * step + skip
    return jnp.where(source == wanted, 1.0, 0.0).astype(BF16)


def weigh_kernel(slot, local_slots, split, waits, me_ref, gauss_any, tendency_ref, *rest):
    outs, token_ref, (gauss_ref, column, held, done, gauss_sem, in_sems, out_sems) = rest[waits:-8], rest[-8], rest[-7:]
    line_copy = pltpu.make_async_copy(gauss_any, gauss_ref, gauss_sem)
    line_copy.start()
    rows, lats, slots, members = held.shape
    each = in_sems.shape[1]
    size = lats // each
    copies = []
    for r in range(rows):
        for i in range(each):
            part = pl.ds(i * size, size)
            copies.append(pltpu.make_async_copy(tendency_ref.at[r, part], held.at[r, part], in_sems.at[r, i]))
            copies[-1].start()
    token_ref[...] = jnp.zeros_like(token_ref)
    depth, breadth = math.gcd(size, 16), 16
    matrix = swap_matrix(depth, breadth, local_slots, slot)
    owners = breadth // local_slots
    core = me_ref[0] % CORES
    line_copy.wait()
    for j in range(0, lats, depth):
        line = jnp.broadcast_to(gauss_ref[...], (depth, lats))
        here = lax.broadcasted_iota(jnp.int32, line.shape, 0) + j
        mine = lax.broadcasted_iota(jnp.int32, line.shape, 1) == here
        value = jnp.sum(jnp.where(mine, line, 0.0), axis=1, keepdims=True)
        column[j : j + depth, :] = jnp.broadcast_to(value, (depth, members))
    results = []
    for r in range(rows):
        for j in range(0, lats, depth):
            if j % size == 0:
                copies[r * each + j // size].wait()
            scale = column[j : j + depth, :]
            for s in range(0, slots, 2 * breadth):
                halves = [
                    held[r, j : j + depth, s + h : s + h + breadth, :].reshape(depth * breadth, members)
                    for h in (0, breadth)
                ]
                turned = jnp.dot(matrix, jnp.concatenate(halves, axis=1), preferred_element_type=F32)
                values = [
                    turned[i * depth : (i + 1) * depth, h * members : (h + 1) * members] * scale
                    for h in range(2)
                    for i in range(owners)
                ]
                start = s // local_slots
                if split:
                    mine, others = split_cores(values, core)
                    for i, (a, b) in enumerate(zip(mine, others)):
                        done[start // CORES + i, 0, r, j : j + depth, :] = a.astype(BF16)
                        done[start // CORES + i, 1, r, j : j + depth, :] = b.astype(BF16)
                else:
                    for i, value in enumerate(values):
                        chip, target = divmod(start + i, CORES)
                        done[chip, target, r, j : j + depth, :] = value.astype(BF16)
        if split:
            results.append(pltpu.make_async_copy(done.at[:, 0, r], outs[0].at[:, core, r], out_sems.at[0, r]))
            results.append(pltpu.make_async_copy(done.at[:, 1, r], outs[1].at[:, r], out_sems.at[1, r]))
            results[-2].start()
        else:
            results.append(pltpu.make_async_copy(done.at[:, :, r], outs[0].at[:, :, r], out_sems.at[0, r]))
        results[-1].start()
    for copy in results:
        copy.wait()


def lat_block(lats):
    return lats // 2 if lats % 32 == 0 else lats


def weigh(tendency, gauss, me, slot, local_slots, split, waits):
    rows, lats, slots, members = tendency.shape
    each = lats // lat_block(lats)
    chips = slots // local_slots // CORES
    shapes = [jax.ShapeDtypeStruct((chips, CORES, rows, lats, members), BF16)]
    if split:
        shapes += [jax.ShapeDtypeStruct((chips, rows, lats, members), BF16)]
    return call(
        functools.partial(weigh_kernel, slot, local_slots, split, len(waits)),
        "weigh",
        2 * 128 * tendency.size,
        3 * tendency.size,
        58,
        out_shape=shapes + [TOKEN],
        in_specs=[IN_SMEM] + [ANYWHERE] * (2 + len(waits)),
        out_specs=[ANYWHERE] * len(shapes) + [pl.BlockSpec(TOKEN.shape, lambda: (0, 0))],
        scratch_shapes=[
            pltpu.VMEM((1, lats), F32),
            pltpu.VMEM((lats, members), F32),
            pltpu.VMEM((rows, lats, slots, members), BF16),
            pltpu.VMEM((chips, CORES, rows, lats, members), BF16),
            pltpu.SemaphoreType.DMA,
            pltpu.SemaphoreType.DMA((rows, each)),
            pltpu.SemaphoreType.DMA((CORES, rows)),
        ],
    )(me, gauss, tendency, *waits)


def pick_kernel(me_ref, token_ref, in_ref, out_ref, held, in_sems, out_sems):
    other = CORES - 1 - me_ref[0] % CORES
    rows = held.shape[1]
    fetched = [pltpu.make_async_copy(in_ref.at[:, other, r], held.at[:, r], in_sems.at[r]) for r in range(rows)]
    stored = [pltpu.make_async_copy(held.at[:, r], out_ref.at[:, r], out_sems.at[r]) for r in range(rows)]
    for copy in fetched:
        copy.start()
    for fetch, store in zip(fetched, stored):
        fetch.wait()
        store.start()
    for copy in stored:
        copy.wait()


def pick(blocks, me, token):
    chips, _, rows, lats, members = blocks.shape
    shape = (chips, rows, lats, members)
    return call(
        pick_kernel,
        "pick",
        0,
        2 * blocks.size,
        out_shape=jax.ShapeDtypeStruct(shape, BF16),
        in_specs=[IN_SMEM, ANYWHERE, IN_HBM],
        out_specs=IN_HBM,
        scratch_shapes=[
            pltpu.VMEM(shape, BF16),
            pltpu.SemaphoreType.DMA((rows,)),
            pltpu.SemaphoreType.DMA((rows,)),
        ],
    )(me, token, blocks)


def pair_kernel(me_ref, mate_ref, blocks_ref, out_ref, token_ref, sem):
    token_ref[...] = jnp.zeros_like(token_ref)
    other = CORES - 1 - me_ref[0] % CORES
    run_copies([pltpu.make_async_copy(mate_ref, out_ref.at[:, other], sem)])


def pair(blocks, mate, me):
    return call(
        pair_kernel,
        "pair",
        0,
        4 * mate.size,
        out_shape=[jax.ShapeDtypeStruct(blocks.shape, blocks.dtype), TOKEN],
        in_specs=[IN_SMEM, pl.BlockSpec(mate.shape, lambda: (0, 0, 0, 0)), ANYWHERE],
        out_specs=[ANYWHERE, pl.BlockSpec(TOKEN.shape, lambda: (0, 0))],
        scratch_shapes=[pltpu.SemaphoreType.DMA],
        input_output_aliases={2: 0},
    )(me, mate, blocks)


def pair_messages_kernel(first, waits, me_ref, mate_ref, *rest):
    count = (len(rest) - 1 - waits) // 2
    outs, sems = rest[-1 - count : -1], rest[-1]
    chip, other = me_ref[0] // CORES, CORES - 1 - me_ref[0] % CORES
    wanted = partners(mate_ref.shape[0])[first : first + count]
    run_copies(
        [
            pltpu.make_async_copy(mate_ref.at[chip ^ k], out.at[other], sems.at[i])
            for i, (k, out) in enumerate(zip(wanted, outs))
        ]
    )


def pair_messages(messages, mate, me, first, waits):
    count = len(messages)
    return call(
        functools.partial(pair_messages_kernel, first, len(waits)),
        "pair",
        0,
        4 * mate.size,
        out_shape=[jax.ShapeDtypeStruct(m.shape, m.dtype) for m in messages],
        in_specs=[IN_SMEM, pl.BlockSpec(mate.shape, lambda: (0, 0, 0, 0))] + [ANYWHERE] * (count + len(waits)),
        out_specs=[ANYWHERE] * count,
        scratch_shapes=[pltpu.SemaphoreType.DMA((count,))],
        input_output_aliases={i + 2: i for i in range(count)},
    )(me, mate, *messages, *waits)


def analyse_kernel(slot, low, me_ref, wave_ref, token_ref, table_ref, state_ref, *rest):
    blocks, out, (grid, table, state, table_sems, state_sem, block_sems) = rest[:-7], rest[-7], rest[-6:]
    rows, members, width = out.shape
    chips, cores, lats, _ = grid.shape
    core = me_ref[0] % CORES
    moves = []
    for r in range(rows):
        lanes = pl.ds(r * members, members)
        if len(blocks) == 1:
            moves.append(pltpu.make_async_copy(blocks[0].at[:, :, r], grid.at[:, :, :, lanes], block_sems.at[0, r]))
        else:
            target = grid.at[:, core, :, lanes]
            moves.append(pltpu.make_async_copy(blocks[0].at[:, core, r], target, block_sems.at[0, r]))
            target = grid.at[:, CORES - 1 - core, :, lanes]
            moves.append(pltpu.make_async_copy(blocks[1].at[:, r], target, block_sems.at[1, r]))
    cuts = sorted(set([0] + list(range(width % 256, width + 1, 256))))
    copies = []
    for i, (start, end) in enumerate(zip(cuts, cuts[1:])):
        source = table_ref.at[slot, pl.ds(low + start, end - start)]
        copies.append(pltpu.make_async_copy(source, table.at[pl.ds(start, end - start)], table_sems.at[i]))
    state_copy = pltpu.make_async_copy(state_ref.at[:, slot, :, pl.ds(low, width)], state, state_sem)
    for move in moves + copies + [state_copy]:
        move.start()
    for move in moves:
        move.wait()
    field = grid[...].reshape(chips * cores * lats, rows * members)
    state_copy.wait()
    for copy, start, end in zip(copies, cuts, cuts[1:]):
        copy.wait()
        sums = jnp.dot(table[start:end], field, preferred_element_type=F32)
        degree = lax.broadcasted_iota(jnp.int32, (members, end - start), 1) + (low + start)
        live = degree >= wave_ref[slot]
        for r in range(rows):
            total = state[r, :, start:end].astype(F32) + sums[:, r * members : (r + 1) * members].T
            out[r, :, start:end] = jnp.where(live, total, 0.0).astype(BF16)


def analyse(blocks, table, state, wave, me, token, slot, low, width):
    chips, _, rows, lats, members = blocks[0].shape
    nlat = table.shape[2]
    cores = CORES
    if lats % 16:
        if len(blocks) > 1:
            core = me[0] % CORES
            own = lax.dynamic_index_in_dim(blocks[0], core, 1, keepdims=False)
            pairs = [jnp.where(core == 0, own, blocks[1]), jnp.where(core == 0, blocks[1], own)]
            blocks = [jnp.stack(pairs, axis=1)]
        laid = jnp.transpose(blocks[0], (2, 0, 1, 3, 4)).reshape(1, 1, rows, nlat, members)
        blocks, chips, cores, lats = [laid], 1, 1, nlat
    return call(
        functools.partial(analyse_kernel, slot, low),
        "analyse",
        2 * width * nlat * rows * members,
        2 * width * nlat,
        out_shape=jax.ShapeDtypeStruct((rows, members, width), BF16),
        grid_spec=pltpu.PrefetchScalarGridSpec(
            num_scalar_prefetch=1,
            grid=(1,),
            in_specs=[IN_SMEM, ANYWHERE] + [IN_HBM] * (2 + len(blocks)),
            out_specs=pl.BlockSpec((rows, members, width), lambda i, m: (0, 0, 0)),
            scratch_shapes=[
                pltpu.VMEM((chips, cores, lats, rows * members), BF16),
                pltpu.VMEM((width, nlat), BF16),
                pltpu.VMEM((rows, members, width), BF16),
                pltpu.SemaphoreType.DMA((width // 256 + 1,)),
                pltpu.SemaphoreType.DMA,
                pltpu.SemaphoreType.DMA((CORES, rows)),
            ],
        ),
    )(me, wave, token, table, state, *blocks)


def sum_pairs_kernel(coeff_ref, token_ref, inverse_ref, out_ref):
    pairs, entries = inverse_ref.shape[:2]
    half = entries // 2

    def one(entry, carry):
        real = imag = 0.0
        for k in range(pairs):
            first, second = inverse_ref[k, entry].astype(F32), inverse_ref[k, half + entry].astype(F32)
            a, b = coeff_ref[k, 0], coeff_ref[k, 1]
            real = real + (a * first - b * second)
            imag = imag + (a * second + b * first)
        out_ref[entry] = real
        out_ref[half + entry] = imag
        return carry

    lax.fori_loop(0, half, one, 0)


def sum_pairs(block_inverses, pole_coeffs, token):
    return call(
        sum_pairs_kernel,
        "sum_pairs",
        4 * block_inverses.size,
        2 * block_inverses.size,
        out_shape=jax.ShapeDtypeStruct(block_inverses.shape[1:], F32),
        in_specs=[IN_SMEM, ANYWHERE, pl.BlockSpec(block_inverses.shape, lambda: (0, 0, 0, 0))],
        out_specs=pl.BlockSpec(block_inverses.shape[1:], lambda: (0, 0, 0)),
    )(pole_coeffs, token, block_inverses)


def synthesise_kernel(
    slot, low, apart, more, partial, me_ref, sign_ref, here_ref, there_ref, own_ref, other_ref, table_ref, *rest
):
    rows, members, _ = own_ref.shape
    step = pl.program_id(0)
    if partial:
        partial_ref, rest = rest[0], rest[1:]
    if more:
        sums_out, mixed = rest
    elif apart:
        outs, mate_out, mixed, held, sems = rest[:-4], rest[-4], rest[-3], rest[-2], rest[-1]
    else:
        own_out, mate_out, mixed = rest

    @pl.when(step == 0)
    def _():
        count = own_ref.shape[2]
        for n in range(0, count, 128):
            lanes = slice(low + n, low + n + 128)
            lines = [
                here_ref[entry, slot : slot + 1, lanes] + there_ref[entry, slot : slot + 1, lanes]
                for entry in range(2 * rows * rows)
            ]
            lines[rows * rows :] = [sign_ref[0] * line for line in lines[rows * rows :]]
            for e in range(0, members, 32):
                part = (slice(e, e + 32), slice(n, n + 128))
                owns = [own_ref[(g,) + part].astype(F32) for g in range(rows)]
                others = [other_ref[(g,) + part].astype(F32) for g in range(rows)]
                for f in range(rows):
                    total = 0.0
                    for g in range(rows):
                        total = total + lines[f * rows + g] * owns[g]
                        total = total + lines[rows * rows + f * rows + g] * others[g]
                    mixed[f * members + e : f * members + e + 32, n : n + 128] = total.astype(BF16)

    sums = jnp.dot(mixed[...], table_ref[0], preferred_element_type=F32)
    if partial:
        sums = sums + partial_ref[...]
    if more:
        sums_out[...] = sums
        return
    lats = mate_out.shape[2]
    each = mate_out.shape[0]
    for r in range(rows):
        turned = sums[r * members : (r + 1) * members, :].astype(BF16).T
        values = [turned[i : i + lats] for i in range(0, turned.shape[0], lats)]
        mine, others = split_cores(values, me_ref[0] % CORES)
        for i, (a, b) in enumerate(zip(mine, others)):
            if apart:
                held[step * each + i, r] = a
            else:
                own_out[i, 0, r] = a
            mate_out[i, r] = b

    if apart:
        chip, core = me_ref[0] // CORES, me_ref[0] % CORES
        copies = []
        for i, (k, out) in enumerate(zip(partners(len(outs)), outs)):
            copies.append(pltpu.make_async_copy(held.at[chip ^ k], out.at[core], sems.at[i]))
            pl.when((chip ^ k) // each == step)(copies[-1].start)

        @pl.when(step == pl.num_programs(0) - 1)
        def _():
            for copy in copies:
                copy.wait()


def synthesise(here, there, sign, own, other, table, me, slot, low, lats, apart, more, partial):
    rows, members, count = own.shape
    nlat = table.shape[2]
    width = math.lcm(CORES * lats, 128)
    chips, each = nlat // lats // CORES, width // lats // CORES
    matrix = pl.BlockSpec(here.shape, lambda j, m: (0, 0, 0))
    whole = pl.BlockSpec((rows, members, count), lambda j, m: (0, 0, 0))
    smem = pl.BlockSpec(memory_space=pltpu.SMEM)
    shapes = [jax.ShapeDtypeStruct((chips, CORES, rows, lats, members), BF16)]
    specs = [pl.BlockSpec((each, 1, rows, lats, members), lambda j, m: (j, m[0] % CORES, 0, 0, 0))]
    scratch = [pltpu.VMEM((rows * members, count), BF16)]
    shapes += [jax.ShapeDtypeStruct((chips, rows, lats, members), BF16)]
    specs += [pl.BlockSpec((each, rows, lats, members), lambda j, m: (j, 0, 0, 0))]
    sums = pl.BlockSpec((rows * members, width), lambda j, m: (0, j))
    if more:
        shapes, specs = [jax.ShapeDtypeStruct((rows * members, nlat), F32)], [sums]
    elif apart:
        shapes[:1] = [jax.ShapeDtypeStruct((CORES, rows, lats, members), BF16)] * chips
        specs[:1] = [ANYWHERE] * chips
        scratch += [pltpu.VMEM((chips, rows, lats, members), BF16), pltpu.SemaphoreType.DMA((chips,))]
    return call(
        functools.partial(synthesise_kernel, slot, low, apart, more, len(partial)),
        "synthesise",
        2 * count * nlat * rows * members,
        2 * count * nlat,
        out_shape=shapes,
        grid_spec=pltpu.PrefetchScalarGridSpec(
            num_scalar_prefetch=1,
            grid=(nlat // width,),
            in_specs=[
                smem,
                matrix,
                matrix,
                whole,
                whole,
                pl.BlockSpec((1, count, width), lambda j, m: (slot, low // count, j)),
            ]
            + [sums] * len(partial),
            out_specs=specs,
            scratch_shapes=scratch,
        ),
    )(me, sign, here, there, own, other, table, *partial)


def assemble_kernel(counts, me_ref, *rest):
    ins, out_ref, (held, done, in_sems, out_sems) = rest[: sum(counts)], rest[-5], rest[-4:]
    rows, lats, slots, members = done.shape
    local_slots = len(counts)
    chip = me_ref[0] // CORES
    each = out_sems.shape[1]
    size = lats // each
    depth, breadth = math.gcd(size, 16), 16
    copies = []
    for r in range(rows):
        copies.append([])
        used = 0
        for slot, count in enumerate(counts):
            refs = ins[used : used + count]
            used += count
            if count == 1:
                target = held.at[slot, :, :, r]
                copies[r].append(pltpu.make_async_copy(refs[0].at[:, :, r], target, in_sems.at[r, slot, 0]))
                continue
            for i, (k, ref) in enumerate(zip(partners(count), refs)):
                target = held.at[slot, chip ^ k, :, r]
                copies[r].append(pltpu.make_async_copy(ref.at[:, r], target, in_sems.at[r, slot, i]))
        for copy in copies[r]:
            copy.start()
    matrix = swap_matrix(breadth, depth, 1, 0)
    results = []
    for r in range(rows):
        for copy in copies[r]:
            copy.wait()
        for start in range(0, lats, depth):
            j = slice(start, start + depth)
            for s in range(0, slots, 2 * breadth):
                halves = []
                for h in (0, breadth):
                    columns = [divmod(i, local_slots) for i in range(s + h, s + h + breadth)]
                    columns = [held[slot, owner // CORES, owner % CORES, r, j, :] for owner, slot in columns]
                    halves.append(jnp.concatenate(columns, axis=0))
                turned = jnp.dot(matrix, jnp.concatenate(halves, axis=1), preferred_element_type=F32).astype(BF16)
                for h in range(2):
                    value = turned[:, h * members : (h + 1) * members].reshape(depth, breadth, members)
                    done[r, j, s + h * breadth : s + (h + 1) * breadth, :] = value
            if (start + depth) % size == 0:
                part = pl.ds(start + depth - size, size)
                target = out_ref.at[r, part]
                results.append(pltpu.make_async_copy(done.at[r, part], target, out_sems.at[r, start // size]))
                results[-1].start()
    for copy in results:
        copy.wait()


def assemble(pieces, me):
    rows, lats, members = pieces[0][0].shape[-3:]
    chips = max(len(p) if len(p) > 1 else p[0].shape[0] for p in pieces)
    slots = len(pieces) * chips * CORES
    flat = [block for slot in pieces for block in slot]
    return call(
        functools.partial(assemble_kernel, [len(p) for p in pieces]),
        "assemble",
        2 * 256 * rows * lats * slots * members,
        4 * rows * lats * slots * members,
        out_shape=jax.ShapeDtypeStruct((rows, lats, slots, members), BF16),
        in_specs=[IN_SMEM] + [IN_HBM] * len(flat),
        out_specs=IN_HBM,
        scratch_shapes=[
            pltpu.VMEM((len(pieces), chips, CORES, rows, lats, members), BF16),
            pltpu.VMEM((rows, lats, slots, members), BF16),
            pltpu.SemaphoreType.DMA((rows, len(pieces), chips)),
            pltpu.SemaphoreType.DMA((rows, lats // lat_block(lats))),
        ],
    )(me, *flat)


def between_cores(blocks, owners):
    return lax.ppermute(blocks, "wave", [(d, d ^ 1) for d in range(owners)])


def by_permutes(messages):
    owners = len(messages) * CORES
    got = [messages[0]]
    for k, message in list(zip(partners(len(messages)), messages))[1:]:
        got.append(lax.ppermute(message, "wave", [(d, d ^ (k * CORES)) for d in range(owners)]))
    return got


def between_chips(blocks, owners):
    groups = [list(range(core, owners, CORES)) for core in range(CORES)]
    return lax.all_to_all(blocks, "wave", split_axis=0, concat_axis=0, axis_index_groups=groups, tiled=True)


def per_device(
    tendency, spectral_state, legendre, gauss_weights, block_inverses, pole_coeffs, wavenumbers
):
    rows, lats, slots, members = tendency.shape
    local_slots, nspec, nlat = legendre.shape
    owners = slots // local_slots
    me = lax.axis_index("wave").astype(jnp.int32).reshape(1)
    pole_index = lax.axis_index("pole")
    sign = (2 * pole_index - 1).astype(F32).reshape(1)
    order = list(range(local_slots))[::-1]
    received, waits = {}, []
    for slot in order:
        early = slot == order[0]
        *blocks, token = weigh(tendency, gauss_weights[None], me, slot, local_slots, not early, waits)
        if early:
            received[slot] = between_chips(blocks[0], owners)
            here = sum_pairs(block_inverses, pole_coeffs, token)
            there = lax.ppermute(here, "pole", [(0, 1), (1, 0)])
            waits = [there]
        else:
            blocks, token = pair(blocks[0], between_cores(blocks[1], owners), me)
            received[slot] = between_chips(blocks, owners)

    sent = {}
    for slot in order:
        half = nspec // 2
        lows = [half] if slot % 2 else [0, half]
        blocks = [received[slot]]
        if slot == order[0]:
            blocks.append(between_cores(pick(blocks[0], me, token), owners))
        forced = [analyse(blocks, legendre, spectral_state, wavenumbers, me, token, slot, low, half) for low in lows]
        others = [lax.ppermute(part, "pole", [(0, 1), (1, 0)]) for part in forced]
        last = slot == order[-1]
        own = []
        for low, part, other in zip(lows, forced, others):
            more = low != lows[-1]
            own = synthesise(here, there, sign, part, other, legendre, me, slot, low, lats, last, more, own)
        *own, for_mate = own
        mate = between_cores(for_mate, owners)
        if last:
            far = len(own) // 2 + 1
            own = list(pair_messages(own[:far], mate, me, 0, [])) + list(
                pair_messages(own[far:], mate, me, far, sent[order[0]])
            )
            sent[slot] = by_permutes(own)
        else:
            blocks, token = pair(own[0], mate, me)
            sent[slot] = [between_chips(blocks, owners)]
    return assemble([sent[slot] for slot in range(local_slots)], me)


def solution(mesh):
    in_specs = (
        P("pole", "wave", None, None),
        P("pole", "wave", None, None),
        P("wave", None, None),
        P("wave"),
        P("pole", None, "wave", None),
        P("pole", None),
        P("wave"),
    )
    out_specs = P("pole", "wave", None, None)
    return jax.shard_map(
        per_device, mesh=mesh, in_specs=in_specs, out_specs=out_specs, check_vma=False
    )
```

```python
import functools
import math

import jax
import jax.numpy as jnp
from jax import lax
from jax.experimental import pallas as pl
from jax.experimental.pallas import tpu as pltpu
from jax.sharding import PartitionSpec as P

BF16 = jnp.bfloat16
F32 = jnp.float32
CORES = 2
ANYWHERE = pl.BlockSpec(memory_space=pl.ANY)
IN_SMEM = pl.BlockSpec(memory_space=pltpu.SMEM)
IN_HBM = pl.BlockSpec(memory_space=pltpu.HBM)
IN_VMEM = pl.BlockSpec(memory_space=pltpu.VMEM)
TOKEN = jax.ShapeDtypeStruct((8, 128), F32)


def call(kernel, name, flops, size, mib=40, **kwargs):
    return pl.pallas_call(
        kernel,
        name=name,
        compiler_params=pltpu.CompilerParams(vmem_limit_bytes=mib * 1024 * 1024),
        cost_estimate=pl.CostEstimate(flops=int(flops), bytes_accessed=int(size), transcendentals=0),
        **kwargs,
    )


def run_copies(copies):
    for copy in copies:
        copy.start()
    for copy in copies:
        copy.wait()


def partners(chips):
    return [0] + list(range(chips // 2, chips)) + list(range(1, chips // 2))


def split_cores(values, core):
    even = [values[i] for i in range(0, len(values), CORES)]
    odd = [values[i] for i in range(1, len(values), CORES)]
    mine = [jnp.where(core == 0, a, b) for a, b in zip(even, odd)]
    others = [jnp.where(core == 0, b, a) for a, b in zip(even, odd)]
    return mine, others


def swap_matrix(rows, columns, step, skip):
    shape = (rows * columns // step, rows * columns)
    shift = rows.bit_length() - 1
    target = lax.broadcasted_iota(jnp.int32, shape, 0)
    source = lax.broadcasted_iota(jnp.int32, shape, 1)
    wanted = (target & (rows - 1)) * columns + (target >> shift) * step + skip
    return jnp.where(source == wanted, 1.0, 0.0).astype(BF16)


def weigh_kernel(slot, local_slots, split, waits, me_ref, gauss_any, tendency_ref, *rest):
    outs, token_ref, (gauss_ref, column, held, done, gauss_sem, in_sems, out_sems) = rest[waits:-8], rest[-8], rest[-7:]
    line_copy = pltpu.make_async_copy(gauss_any, gauss_ref, gauss_sem)
    line_copy.start()
    rows, lats, slots, members = held.shape
    each = in_sems.shape[1]
    size = lats // each
    copies = []
    for r in range(rows):
        for i in range(each):
            part = pl.ds(i * size, size)
            copies.append(pltpu.make_async_copy(tendency_ref.at[r, part], held.at[r, part], in_sems.at[r, i]))
            copies[-1].start()
    token_ref[...] = jnp.zeros_like(token_ref)
    depth, breadth = math.gcd(size, 16), 16
    matrix = swap_matrix(depth, breadth, local_slots, slot)
    owners = breadth // local_slots
    core = me_ref[0] % CORES
    line_copy.wait()
    for j in range(0, lats, depth):
        line = jnp.broadcast_to(gauss_ref[...], (depth, lats))
        here = lax.broadcasted_iota(jnp.int32, line.shape, 0) + j
        mine = lax.broadcasted_iota(jnp.int32, line.shape, 1) == here
        value = jnp.sum(jnp.where(mine, line, 0.0), axis=1, keepdims=True)
        column[j : j + depth, :] = jnp.broadcast_to(value, (depth, members))
    results = []
    for r in range(rows):
        for j in range(0, lats, depth):
            if j % size == 0:
                copies[r * each + j // size].wait()
            scale = column[j : j + depth, :]
            for s in range(0, slots, 2 * breadth):
                halves = [
                    held[r, j : j + depth, s + h : s + h + breadth, :].reshape(depth * breadth, members)
                    for h in (0, breadth)
                ]
                turned = jnp.dot(matrix, jnp.concatenate(halves, axis=1), preferred_element_type=F32)
                values = [
                    turned[i * depth : (i + 1) * depth, h * members : (h + 1) * members] * scale
                    for h in range(2)
                    for i in range(owners)
                ]
                start = s // local_slots
                if split:
                    mine, others = split_cores(values, core)
                    for i, (a, b) in enumerate(zip(mine, others)):
                        done[start // CORES + i, 0, r, j : j + depth, :] = a.astype(BF16)
                        done[start // CORES + i, 1, r, j : j + depth, :] = b.astype(BF16)
                else:
                    for i, value in enumerate(values):
                        chip, target = divmod(start + i, CORES)
                        done[chip, target, r, j : j + depth, :] = value.astype(BF16)
            if (j + depth) % size == 0:
                part = pl.ds(j + depth - size, size)
                source, target = done.at[:, :, r, part], outs[0].at[:, :, r, part]
                if split:
                    source, target = done.at[:, 0, r, part], outs[0].at[:, core, r, part]
                    other = pltpu.make_async_copy(
                        done.at[:, 1, r, part], outs[1].at[:, r, part], out_sems.at[1, r, j // size]
                    )
                    other.start()
                    results.append(other)
                results.append(pltpu.make_async_copy(source, target, out_sems.at[0, r, j // size]))
                results[-1].start()
    for copy in results:
        copy.wait()


def lat_block(lats):
    return lats // 2 if lats % 32 == 0 else lats


def weigh(tendency, gauss, me, slot, local_slots, split, waits):
    rows, lats, slots, members = tendency.shape
    each = lats // lat_block(lats)
    chips = slots // local_slots // CORES
    shapes = [jax.ShapeDtypeStruct((chips, CORES, rows, lats, members), BF16)]
    if split:
        shapes += [jax.ShapeDtypeStruct((chips, rows, lats, members), BF16)]
    return call(
        functools.partial(weigh_kernel, slot, local_slots, split, len(waits)),
        "weigh",
        2 * 128 * tendency.size,
        3 * tendency.size,
        58,
        out_shape=shapes + [TOKEN],
        in_specs=[IN_SMEM] + [ANYWHERE] * (2 + len(waits)),
        out_specs=[ANYWHERE] * len(shapes) + [pl.BlockSpec(TOKEN.shape, lambda: (0, 0))],
        scratch_shapes=[
            pltpu.VMEM((1, lats), F32),
            pltpu.VMEM((lats, members), F32),
            pltpu.VMEM((rows, lats, slots, members), BF16),
            pltpu.VMEM((chips, CORES, rows, lats, members), BF16),
            pltpu.SemaphoreType.DMA,
            pltpu.SemaphoreType.DMA((rows, each)),
            pltpu.SemaphoreType.DMA((CORES, rows, each)),
        ],
    )(me, gauss, tendency, *waits)


def pair_kernel(me_ref, mate_ref, blocks_ref, out_ref, token_ref, sem):
    token_ref[...] = jnp.zeros_like(token_ref)
    other = CORES - 1 - me_ref[0] % CORES
    run_copies([pltpu.make_async_copy(mate_ref, out_ref.at[:, other], sem)])


def pair(blocks, mate, me):
    return call(
        pair_kernel,
        "pair",
        0,
        4 * mate.size,
        out_shape=[jax.ShapeDtypeStruct(blocks.shape, blocks.dtype), TOKEN],
        in_specs=[IN_SMEM, pl.BlockSpec(mate.shape, lambda: (0, 0, 0, 0)), ANYWHERE],
        out_specs=[ANYWHERE, pl.BlockSpec(TOKEN.shape, lambda: (0, 0))],
        scratch_shapes=[pltpu.SemaphoreType.DMA],
        input_output_aliases={2: 0},
    )(me, mate, blocks)


def pair_messages_kernel(first, waits, me_ref, mate_ref, *rest):
    count = (len(rest) - 1 - waits) // 2
    outs, sems = rest[-1 - count : -1], rest[-1]
    chip, other = me_ref[0] // CORES, CORES - 1 - me_ref[0] % CORES
    wanted = partners(mate_ref.shape[0])[first : first + count]
    run_copies(
        [
            pltpu.make_async_copy(mate_ref.at[chip ^ k], out.at[other], sems.at[i])
            for i, (k, out) in enumerate(zip(wanted, outs))
        ]
    )


def pair_messages(messages, mate, me, first, waits):
    count = len(messages)
    return call(
        functools.partial(pair_messages_kernel, first, len(waits)),
        "pair",
        0,
        4 * mate.size,
        out_shape=[jax.ShapeDtypeStruct(m.shape, m.dtype) for m in messages],
        in_specs=[IN_SMEM, pl.BlockSpec(mate.shape, lambda: (0, 0, 0, 0))] + [ANYWHERE] * (count + len(waits)),
        out_specs=[ANYWHERE] * count,
        scratch_shapes=[pltpu.SemaphoreType.DMA((count,))],
        input_output_aliases={i + 2: i for i in range(count)},
    )(me, mate, *messages, *waits)


def analyse_kernel(slot, low, wave_ref, token_ref, table_ref, state_ref, blocks_ref, out, *scratch):
    grid, table, state, table_sems, state_sem, block_sems = scratch
    rows, members, width = out.shape
    chips, cores, lats, _ = grid.shape
    moves = []
    for r in range(rows):
        target = grid.at[:, :, :, pl.ds(r * members, members)]
        moves.append(pltpu.make_async_copy(blocks_ref.at[:, :, r], target, block_sems.at[r]))
    cuts = sorted(set([0] + list(range(width % 256, width + 1, 256))))
    copies = []
    for i, (start, end) in enumerate(zip(cuts, cuts[1:])):
        source = table_ref.at[slot, pl.ds(low + start, end - start)]
        copies.append(pltpu.make_async_copy(source, table.at[pl.ds(start, end - start)], table_sems.at[i]))
    state_copy = pltpu.make_async_copy(state_ref.at[:, slot, :, pl.ds(low, width)], state, state_sem)
    for move in moves + copies + [state_copy]:
        move.start()
    for move in moves:
        move.wait()
    field = grid[...].reshape(chips * cores * lats, rows * members)
    state_copy.wait()
    for copy, start, end in zip(copies, cuts, cuts[1:]):
        copy.wait()
        sums = jnp.dot(table[start:end], field, preferred_element_type=F32)
        degree = lax.broadcasted_iota(jnp.int32, (members, end - start), 1) + (low + start)
        live = degree >= wave_ref[slot]
        for r in range(rows):
            total = state[r, :, start:end].astype(F32) + sums[:, r * members : (r + 1) * members].T
            out[r, :, start:end] = jnp.where(live, total, 0.0).astype(BF16)


def analyse(blocks, table, state, wave, token, slot, low, width):
    chips, cores, rows, lats, members = blocks.shape
    nlat = table.shape[2]
    if lats % 16:
        blocks = jnp.transpose(blocks, (2, 0, 1, 3, 4)).reshape(1, 1, rows, nlat, members)
        chips, cores, lats = 1, 1, nlat
    return call(
        functools.partial(analyse_kernel, slot, low),
        "analyse",
        2 * width * nlat * rows * members,
        2 * width * nlat,
        out_shape=jax.ShapeDtypeStruct((rows, members, width), BF16),
        in_specs=[IN_SMEM, ANYWHERE] + [IN_HBM] * 3,
        out_specs=pl.BlockSpec((rows, members, width), lambda: (0, 0, 0)),
        scratch_shapes=[
            pltpu.VMEM((chips, cores, lats, rows * members), BF16),
            pltpu.VMEM((width, nlat), BF16),
            pltpu.VMEM((rows, members, width), BF16),
            pltpu.SemaphoreType.DMA((width // 256 + 1,)),
            pltpu.SemaphoreType.DMA,
            pltpu.SemaphoreType.DMA((rows,)),
        ],
    )(wave, token, table, state, blocks)


def sum_pairs_kernel(coeff_ref, token_ref, inverse_ref, out_ref):
    pairs, entries = inverse_ref.shape[:2]
    half = entries // 2

    def one(entry, carry):
        real = imag = 0.0
        for k in range(pairs):
            first, second = inverse_ref[k, entry].astype(F32), inverse_ref[k, half + entry].astype(F32)
            a, b = coeff_ref[k, 0], coeff_ref[k, 1]
            real = real + (a * first - b * second)
            imag = imag + (a * second + b * first)
        out_ref[entry] = real
        out_ref[half + entry] = imag
        return carry

    lax.fori_loop(0, half, one, 0)


def sum_pairs(block_inverses, pole_coeffs, token):
    return call(
        sum_pairs_kernel,
        "sum_pairs",
        4 * block_inverses.size,
        2 * block_inverses.size,
        out_shape=jax.ShapeDtypeStruct(block_inverses.shape[1:], F32),
        in_specs=[IN_SMEM, ANYWHERE, pl.BlockSpec(block_inverses.shape, lambda: (0, 0, 0, 0))],
        out_specs=pl.BlockSpec(block_inverses.shape[1:], lambda: (0, 0, 0)),
    )(pole_coeffs, token, block_inverses)


def synthesise_kernel(
    slot, low, apart, more, partial, me_ref, sign_ref, here_ref, there_ref, own_ref, other_ref, table_ref, *rest
):
    rows, members, _ = own_ref.shape
    step = pl.program_id(0)
    if partial:
        partial_ref, rest = rest[0], rest[1:]
    if more:
        sums_out, mixed = rest
    elif apart:
        outs, mate_out, mixed, held, sems = rest[:-4], rest[-4], rest[-3], rest[-2], rest[-1]
    else:
        own_out, mate_out, mixed = rest

    @pl.when(step == 0)
    def _():
        count = own_ref.shape[2]
        for n in range(0, count, 128):
            lanes = slice(low + n, low + n + 128)
            lines = [
                here_ref[entry, slot : slot + 1, lanes] + there_ref[entry, slot : slot + 1, lanes]
                for entry in range(2 * rows * rows)
            ]
            lines[rows * rows :] = [sign_ref[0] * line for line in lines[rows * rows :]]
            for e in range(0, members, 32):
                part = (slice(e, e + 32), slice(n, n + 128))
                owns = [own_ref[(g,) + part].astype(F32) for g in range(rows)]
                others = [other_ref[(g,) + part].astype(F32) for g in range(rows)]
                for f in range(rows):
                    total = 0.0
                    for g in range(rows):
                        total = total + lines[f * rows + g] * owns[g]
                        total = total + lines[rows * rows + f * rows + g] * others[g]
                    mixed[f * members + e : f * members + e + 32, n : n + 128] = total.astype(BF16)

    sums = jnp.dot(mixed[...], table_ref[0], preferred_element_type=F32)
    if partial:
        sums = sums + partial_ref[...]
    if more:
        sums_out[...] = sums
        return
    lats = mate_out.shape[2]
    each = mate_out.shape[0]
    for r in range(rows):
        turned = sums[r * members : (r + 1) * members, :].astype(BF16).T
        values = [turned[i : i + lats] for i in range(0, turned.shape[0], lats)]
        mine, others = split_cores(values, me_ref[0] % CORES)
        for i, (a, b) in enumerate(zip(mine, others)):
            if apart:
                held[step * each + i, r] = a
            else:
                own_out[i, 0, r] = a
            mate_out[i, r] = b

    if apart:
        chip, core = me_ref[0] // CORES, me_ref[0] % CORES
        copies = []
        for i, (k, out) in enumerate(zip(partners(len(outs)), outs)):
            copies.append(pltpu.make_async_copy(held.at[chip ^ k], out.at[core], sems.at[i]))
            pl.when((chip ^ k) // each == step)(copies[-1].start)

        @pl.when(step == pl.num_programs(0) - 1)
        def _():
            for copy in copies:
                copy.wait()


def synthesise(here, there, sign, own, other, table, me, slot, low, lats, apart, more, partial):
    rows, members, count = own.shape
    nlat = table.shape[2]
    width = math.lcm(CORES * lats, 128)
    chips, each = nlat // lats // CORES, width // lats // CORES
    matrix = pl.BlockSpec(here.shape, lambda j, m: (0, 0, 0))
    whole = pl.BlockSpec((rows, members, count), lambda j, m: (0, 0, 0))
    smem = pl.BlockSpec(memory_space=pltpu.SMEM)
    shapes = [jax.ShapeDtypeStruct((chips, CORES, rows, lats, members), BF16)]
    specs = [pl.BlockSpec((each, 1, rows, lats, members), lambda j, m: (j, m[0] % CORES, 0, 0, 0))]
    scratch = [pltpu.VMEM((rows * members, count), BF16)]
    shapes += [jax.ShapeDtypeStruct((chips, rows, lats, members), BF16)]
    specs += [pl.BlockSpec((each, rows, lats, members), lambda j, m: (j, 0, 0, 0))]
    sums = pl.BlockSpec((rows * members, width), lambda j, m: (0, j))
    if more:
        shapes, specs = [jax.ShapeDtypeStruct((rows * members, nlat), F32)], [sums]
    elif apart:
        shapes[:1] = [jax.ShapeDtypeStruct((CORES, rows, lats, members), BF16)] * chips
        specs[:1] = [ANYWHERE] * chips
        scratch += [pltpu.VMEM((chips, rows, lats, members), BF16), pltpu.SemaphoreType.DMA((chips,))]
    return call(
        functools.partial(synthesise_kernel, slot, low, apart, more, len(partial)),
        "synthesise",
        2 * count * nlat * rows * members,
        2 * count * nlat,
        out_shape=shapes,
        grid_spec=pltpu.PrefetchScalarGridSpec(
            num_scalar_prefetch=1,
            grid=(nlat // width,),
            in_specs=[
                smem,
                matrix,
                matrix,
                whole,
                whole,
                pl.BlockSpec((1, count, width), lambda j, m: (slot, low // count, j)),
            ]
            + [sums] * len(partial),
            out_specs=specs,
            scratch_shapes=scratch,
        ),
    )(me, sign, here, there, own, other, table, *partial)


def assemble_kernel(counts, me_ref, *rest):
    ins, out_ref, (held, done, in_sems, out_sems) = rest[: sum(counts)], rest[-5], rest[-4:]
    rows, lats, slots, members = done.shape
    local_slots = len(counts)
    chip = me_ref[0] // CORES
    each = out_sems.shape[1]
    size = lats // each
    depth, breadth = math.gcd(size, 16), 16
    copies, whole = [], {}
    for r in range(rows):
        copies.append([])
        used = 0
        for slot, count in enumerate(counts):
            refs = ins[used : used + count]
            used += count
            if count == 1:
                whole[slot] = refs[0]
                continue
            if r == 0:
                held[slot, chip] = refs[0][...]
            for i, (k, ref) in list(enumerate(zip(partners(count), refs)))[1:]:
                target = held.at[slot, chip ^ k, :, r]
                copies[r].append(pltpu.make_async_copy(ref.at[:, r], target, in_sems.at[r, slot, i]))
        for copy in copies[r]:
            copy.start()
    matrix = swap_matrix(breadth, depth, 1, 0)
    results = []
    for r in range(rows):
        for copy in copies[r]:
            copy.wait()
        for start in range(0, lats, depth):
            j = slice(start, start + depth)
            for s in range(0, slots, 2 * breadth):
                halves = []
                for h in (0, breadth):
                    columns = [divmod(i, local_slots) for i in range(s + h, s + h + breadth)]
                    columns = [
                        whole.get(slot, held.at[slot])[owner // CORES, owner % CORES, r, j, :]
                        for owner, slot in columns
                    ]
                    halves.append(jnp.concatenate(columns, axis=0))
                turned = jnp.dot(matrix, jnp.concatenate(halves, axis=1), preferred_element_type=F32).astype(BF16)
                for h in range(2):
                    value = turned[:, h * members : (h + 1) * members].reshape(depth, breadth, members)
                    done[r, j, s + h * breadth : s + (h + 1) * breadth, :] = value
            if (start + depth) % size == 0:
                part = pl.ds(start + depth - size, size)
                target = out_ref.at[r, part]
                results.append(pltpu.make_async_copy(done.at[r, part], target, out_sems.at[r, start // size]))
                results[-1].start()
    for copy in results:
        copy.wait()


def assemble(pieces, me):
    rows, lats, members = pieces[0][0].shape[-3:]
    chips = max(len(p) if len(p) > 1 else p[0].shape[0] for p in pieces)
    slots = len(pieces) * chips * CORES
    flat = [block for slot in pieces for block in slot]
    return call(
        functools.partial(assemble_kernel, [len(p) for p in pieces]),
        "assemble",
        2 * 256 * rows * lats * slots * members,
        4 * rows * lats * slots * members,
        out_shape=jax.ShapeDtypeStruct((rows, lats, slots, members), BF16),
        in_specs=[IN_SMEM]
        + [IN_VMEM if i == 0 else IN_HBM for p in pieces for i in range(len(p))],
        out_specs=IN_HBM,
        scratch_shapes=[
            pltpu.VMEM((len(pieces), chips, CORES, rows, lats, members), BF16),
            pltpu.VMEM((rows, lats, slots, members), BF16),
            pltpu.SemaphoreType.DMA((rows, len(pieces), chips)),
            pltpu.SemaphoreType.DMA((rows, lats // lat_block(lats))),
        ],
    )(me, *flat)


def between_cores(blocks, owners):
    return lax.ppermute(blocks, "wave", [(d, d ^ 1) for d in range(owners)])


def by_permutes(messages):
    owners = len(messages) * CORES
    got = [messages[0]]
    for k, message in list(zip(partners(len(messages)), messages))[1:]:
        got.append(lax.ppermute(message, "wave", [(d, d ^ (k * CORES)) for d in range(owners)]))
    return got


def between_all(blocks):
    flat = blocks.reshape((-1,) + blocks.shape[2:])
    return lax.all_to_all(flat, "wave", split_axis=0, concat_axis=0, tiled=True).reshape(blocks.shape)


def between_chips(blocks, owners):
    groups = [list(range(core, owners, CORES)) for core in range(CORES)]
    return lax.all_to_all(blocks, "wave", split_axis=0, concat_axis=0, axis_index_groups=groups, tiled=True)


def per_device(
    tendency, spectral_state, legendre, gauss_weights, block_inverses, pole_coeffs, wavenumbers
):
    rows, lats, slots, members = tendency.shape
    local_slots, nspec, nlat = legendre.shape
    owners = slots // local_slots
    me = lax.axis_index("wave").astype(jnp.int32).reshape(1)
    pole_index = lax.axis_index("pole")
    sign = (2 * pole_index - 1).astype(F32).reshape(1)
    order = list(range(local_slots))[::-1]
    received, waits = {}, []
    for slot in order:
        early = slot == order[0]
        *blocks, token = weigh(tendency, gauss_weights[None], me, slot, local_slots, not early, waits)
        if early:
            received[slot] = between_all(blocks[0])
            here = sum_pairs(block_inverses, pole_coeffs, token)
            there = lax.ppermute(here, "pole", [(0, 1), (1, 0)])
            waits = [there]
        else:
            blocks, token = pair(blocks[0], between_cores(blocks[1], owners), me)
            received[slot] = between_chips(blocks, owners)

    sent = {}
    for slot in order:
        half = nspec // 2
        lows = [half] if slot % 2 else [0, half]
        forced = [analyse(received[slot], legendre, spectral_state, wavenumbers, token, slot, low, half) for low in lows]
        others = [lax.ppermute(part, "pole", [(0, 1), (1, 0)]) for part in forced]
        last = slot == order[-1]
        own = []
        for low, part, other in zip(lows, forced, others):
            more = low != lows[-1]
            own = synthesise(here, there, sign, part, other, legendre, me, slot, low, lats, last, more, own)
        *own, for_mate = own
        mate = between_cores(for_mate, owners)
        if last:
            far = len(own) // 2 + 1
            own = list(pair_messages(own[:far], mate, me, 0, [])) + list(
                pair_messages(own[far:], mate, me, far, sent[order[0]])
            )
            sent[slot] = by_permutes(own)
        else:
            blocks, token = pair(own[0], mate, me)
            sent[slot] = [between_chips(blocks, owners)]
    return assemble([sent[slot] for slot in range(local_slots)], me)


def solution(mesh):
    in_specs = (
        P("pole", "wave", None, None),
        P("pole", "wave", None, None),
        P("wave", None, None),
        P("wave"),
        P("pole", None, "wave", None),
        P("pole", None),
        P("wave"),
    )
    out_specs = P("pole", "wave", None, None)
    return jax.shard_map(
        per_device, mesh=mesh, in_specs=in_specs, out_specs=out_specs, check_vma=False
    )
```

```python
import functools
import math

import jax
import jax.numpy as jnp
from jax import lax
from jax.experimental import pallas as pl
from jax.experimental.pallas import tpu as pltpu
from jax.sharding import PartitionSpec as P

BF16 = jnp.bfloat16
F32 = jnp.float32
CORES = 2
ANYWHERE = pl.BlockSpec(memory_space=pl.ANY)
IN_SMEM = pl.BlockSpec(memory_space=pltpu.SMEM)
IN_HBM = pl.BlockSpec(memory_space=pltpu.HBM)
IN_VMEM = pl.BlockSpec(memory_space=pltpu.VMEM)
TOKEN = jax.ShapeDtypeStruct((8, 128), F32)


def call(kernel, name, flops, size, mib=40, **kwargs):
    return pl.pallas_call(
        kernel,
        name=name,
        compiler_params=pltpu.CompilerParams(vmem_limit_bytes=mib * 1024 * 1024),
        cost_estimate=pl.CostEstimate(flops=int(flops), bytes_accessed=int(size), transcendentals=0),
        **kwargs,
    )


def in_hbm(array):
    return pltpu.with_memory_space_constraint(array, pltpu.HBM)


def run_copies(copies):
    for copy in copies:
        copy.start()
    for copy in copies:
        copy.wait()


def partners(chips):
    return [0] + list(range(chips // 2, chips)) + list(range(1, chips // 2))


def split_cores(values, core):
    even = [values[i] for i in range(0, len(values), CORES)]
    odd = [values[i] for i in range(1, len(values), CORES)]
    mine = [jnp.where(core == 0, a, b) for a, b in zip(even, odd)]
    others = [jnp.where(core == 0, b, a) for a, b in zip(even, odd)]
    return mine, others


def swap_matrix(rows, columns, step, skip):
    shape = (rows * columns // step, rows * columns)
    shift = rows.bit_length() - 1
    target = lax.broadcasted_iota(jnp.int32, shape, 0)
    source = lax.broadcasted_iota(jnp.int32, shape, 1)
    wanted = (target & (rows - 1)) * columns + (target >> shift) * step + skip
    return jnp.where(source == wanted, 1.0, 0.0).astype(BF16)


def weigh_kernel(slot, local_slots, split, waits, me_ref, gauss_any, tendency_ref, *rest):
    outs, token_ref, (gauss_ref, column, held, done, gauss_sem, in_sems, out_sems) = rest[waits:-8], rest[-8], rest[-7:]
    line_copy = pltpu.make_async_copy(gauss_any, gauss_ref, gauss_sem)
    line_copy.start()
    rows, lats, slots, members = held.shape
    each = in_sems.shape[1]
    size = lats // each
    copies = []
    for r in range(rows):
        for i in range(each):
            part = pl.ds(i * size, size)
            copies.append(pltpu.make_async_copy(tendency_ref.at[r, part], held.at[r, part], in_sems.at[r, i]))
            copies[-1].start()
    token_ref[...] = jnp.zeros_like(token_ref)
    depth, breadth = math.gcd(size, 16), 16
    matrix = swap_matrix(depth, breadth, local_slots, slot)
    owners = breadth // local_slots
    core = me_ref[0] % CORES
    line_copy.wait()
    for j in range(0, lats, depth):
        line = jnp.broadcast_to(gauss_ref[...], (depth, lats))
        here = lax.broadcasted_iota(jnp.int32, line.shape, 0) + j
        mine = lax.broadcasted_iota(jnp.int32, line.shape, 1) == here
        value = jnp.sum(jnp.where(mine, line, 0.0), axis=1, keepdims=True)
        column[j : j + depth, :] = jnp.broadcast_to(value, (depth, members))
    results = []
    for r in range(rows):
        for j in range(0, lats, depth):
            if j % size == 0:
                copies[r * each + j // size].wait()
            scale = column[j : j + depth, :]
            for s in range(0, slots, 2 * breadth):
                halves = [
                    held[r, j : j + depth, s + h : s + h + breadth, :].reshape(depth * breadth, members)
                    for h in (0, breadth)
                ]
                turned = jnp.dot(matrix, jnp.concatenate(halves, axis=1), preferred_element_type=F32)
                values = [
                    turned[i * depth : (i + 1) * depth, h * members : (h + 1) * members] * scale
                    for h in range(2)
                    for i in range(owners)
                ]
                start = s // local_slots
                if split:
                    mine, others = split_cores(values, core)
                    for i, (a, b) in enumerate(zip(mine, others)):
                        done[start // CORES + i, 0, r, j : j + depth, :] = a.astype(BF16)
                        done[start // CORES + i, 1, r, j : j + depth, :] = b.astype(BF16)
                else:
                    for i, value in enumerate(values):
                        chip, target = divmod(start + i, CORES)
                        done[chip, target, r, j : j + depth, :] = value.astype(BF16)
            if (j + depth) % size == 0:
                part = pl.ds(j + depth - size, size)
                source, target = done.at[:, :, r, part], outs[0].at[:, :, r, part]
                if split:
                    source, target = done.at[:, 0, r, part], outs[0].at[:, core, r, part]
                    other = pltpu.make_async_copy(
                        done.at[:, 1, r, part], outs[1].at[:, r, part], out_sems.at[1, r, j // size]
                    )
                    other.start()
                    results.append(other)
                results.append(pltpu.make_async_copy(source, target, out_sems.at[0, r, j // size]))
                results[-1].start()
    for copy in results:
        copy.wait()


def lat_block(lats):
    return lats // 2 if lats % 32 == 0 else lats


def weigh(tendency, gauss, me, slot, local_slots, split, waits):
    rows, lats, slots, members = tendency.shape
    each = lats // lat_block(lats)
    chips = slots // local_slots // CORES
    shapes = [jax.ShapeDtypeStruct((chips, CORES, rows, lats, members), BF16)]
    if split:
        shapes += [jax.ShapeDtypeStruct((chips, rows, lats, members), BF16)]
    return call(
        functools.partial(weigh_kernel, slot, local_slots, split, len(waits)),
        "weigh",
        2 * 128 * tendency.size,
        3 * tendency.size,
        58,
        out_shape=shapes + [TOKEN],
        in_specs=[IN_SMEM] + [ANYWHERE] * (2 + len(waits)),
        out_specs=[ANYWHERE] * len(shapes) + [pl.BlockSpec(TOKEN.shape, lambda: (0, 0))],
        scratch_shapes=[
            pltpu.VMEM((1, lats), F32),
            pltpu.VMEM((lats, members), F32),
            pltpu.VMEM((rows, lats, slots, members), BF16),
            pltpu.VMEM((chips, CORES, rows, lats, members), BF16),
            pltpu.SemaphoreType.DMA,
            pltpu.SemaphoreType.DMA((rows, each)),
            pltpu.SemaphoreType.DMA((CORES, rows, each)),
        ],
    )(me, gauss, tendency, *waits)


def pick_kernel(me_ref, token_ref, in_ref, out_ref, held, in_sems, out_sems):
    other = CORES - 1 - me_ref[0] % CORES
    rows = held.shape[1]
    fetched = [pltpu.make_async_copy(in_ref.at[:, other, r], held.at[:, r], in_sems.at[r]) for r in range(rows)]
    stored = [pltpu.make_async_copy(held.at[:, r], out_ref.at[:, r], out_sems.at[r]) for r in range(rows)]
    for copy in fetched:
        copy.start()
    for fetch, store in zip(fetched, stored):
        fetch.wait()
        store.start()
    for copy in stored:
        copy.wait()


def pick(blocks, me, token):
    chips, _, rows, lats, members = blocks.shape
    shape = (chips, rows, lats, members)
    return call(
        pick_kernel,
        "pick",
        0,
        2 * blocks.size,
        out_shape=jax.ShapeDtypeStruct(shape, BF16),
        in_specs=[IN_SMEM, ANYWHERE, IN_HBM],
        out_specs=IN_HBM,
        scratch_shapes=[
            pltpu.VMEM(shape, BF16),
            pltpu.SemaphoreType.DMA((rows,)),
            pltpu.SemaphoreType.DMA((rows,)),
        ],
    )(me, token, in_hbm(blocks))


def pair_kernel(me_ref, mate_ref, blocks_ref, out_ref, token_ref, sem):
    token_ref[...] = jnp.zeros_like(token_ref)
    other = CORES - 1 - me_ref[0] % CORES
    run_copies([pltpu.make_async_copy(mate_ref, out_ref.at[:, other], sem)])


def pair(blocks, mate, me):
    return call(
        pair_kernel,
        "pair",
        0,
        4 * mate.size,
        out_shape=[jax.ShapeDtypeStruct(blocks.shape, blocks.dtype), TOKEN],
        in_specs=[IN_SMEM, pl.BlockSpec(mate.shape, lambda: (0, 0, 0, 0)), ANYWHERE],
        out_specs=[ANYWHERE, pl.BlockSpec(TOKEN.shape, lambda: (0, 0))],
        scratch_shapes=[pltpu.SemaphoreType.DMA],
        input_output_aliases={2: 0},
    )(me, mate, blocks)


def pair_messages_kernel(first, waits, me_ref, mate_ref, *rest):
    count = (len(rest) - 1 - waits) // 2
    outs, sems = rest[-1 - count : -1], rest[-1]
    chip, other = me_ref[0] // CORES, CORES - 1 - me_ref[0] % CORES
    wanted = partners(mate_ref.shape[0])[first : first + count]
    run_copies(
        [
            pltpu.make_async_copy(mate_ref.at[chip ^ k], out.at[other], sems.at[i])
            for i, (k, out) in enumerate(zip(wanted, outs))
        ]
    )


def pair_messages(messages, mate, me, first, waits):
    count = len(messages)
    return call(
        functools.partial(pair_messages_kernel, first, len(waits)),
        "pair",
        0,
        4 * mate.size,
        out_shape=[jax.ShapeDtypeStruct(m.shape, m.dtype) for m in messages],
        in_specs=[IN_SMEM, pl.BlockSpec(mate.shape, lambda: (0, 0, 0, 0))] + [ANYWHERE] * (count + len(waits)),
        out_specs=[ANYWHERE] * count,
        scratch_shapes=[pltpu.SemaphoreType.DMA((count,))],
        input_output_aliases={i + 2: i for i in range(count)},
    )(me, mate, *messages, *waits)


def analyse_kernel(slot, low, me_ref, wave_ref, token_ref, table_ref, state_ref, *rest):
    blocks, out, (grid, table, state, table_sems, state_sem, block_sems) = rest[:-7], rest[-7], rest[-6:]
    rows, members, width = out.shape
    chips, cores, lats, _ = grid.shape
    core = me_ref[0] % CORES
    moves = []
    for r in range(rows):
        lanes = pl.ds(r * members, members)
        if len(blocks) == 1:
            moves.append(pltpu.make_async_copy(blocks[0].at[:, :, r], grid.at[:, :, :, lanes], block_sems.at[0, r]))
        else:
            target = grid.at[:, core, :, lanes]
            moves.append(pltpu.make_async_copy(blocks[0].at[:, core, r], target, block_sems.at[0, r]))
            target = grid.at[:, CORES - 1 - core, :, lanes]
            moves.append(pltpu.make_async_copy(blocks[1].at[:, r], target, block_sems.at[1, r]))
    cuts = sorted(set([0] + list(range(width % 256, width + 1, 256))))
    copies = []
    for i, (start, end) in enumerate(zip(cuts, cuts[1:])):
        source = table_ref.at[slot, pl.ds(low + start, end - start)]
        copies.append(pltpu.make_async_copy(source, table.at[pl.ds(start, end - start)], table_sems.at[i]))
    state_copy = pltpu.make_async_copy(state_ref.at[:, slot, :, pl.ds(low, width)], state, state_sem)
    for move in moves + copies + [state_copy]:
        move.start()
    for move in moves:
        move.wait()
    field = grid[...].reshape(chips * cores * lats, rows * members)
    state_copy.wait()
    for copy, start, end in zip(copies, cuts, cuts[1:]):
        copy.wait()
        sums = jnp.dot(table[start:end], field, preferred_element_type=F32)
        degree = lax.broadcasted_iota(jnp.int32, (members, end - start), 1) + (low + start)
        live = degree >= wave_ref[slot]
        for r in range(rows):
            total = state[r, :, start:end].astype(F32) + sums[:, r * members : (r + 1) * members].T
            out[r, :, start:end] = jnp.where(live, total, 0.0).astype(BF16)


def analyse(blocks, table, state, wave, me, token, slot, low, width):
    chips, _, rows, lats, members = blocks[0].shape
    nlat = table.shape[2]
    cores = CORES
    if lats % 16:
        if len(blocks) > 1:
            core = me[0] % CORES
            own = lax.dynamic_index_in_dim(blocks[0], core, 1, keepdims=False)
            pairs = [jnp.where(core == 0, own, blocks[1]), jnp.where(core == 0, blocks[1], own)]
            blocks = [jnp.stack(pairs, axis=1)]
        laid = jnp.transpose(blocks[0], (2, 0, 1, 3, 4)).reshape(1, 1, rows, nlat, members)
        blocks, chips, cores, lats = [laid], 1, 1, nlat
    return call(
        functools.partial(analyse_kernel, slot, low),
        "analyse",
        2 * width * nlat * rows * members,
        2 * width * nlat,
        out_shape=jax.ShapeDtypeStruct((rows, members, width), BF16),
        grid_spec=pltpu.PrefetchScalarGridSpec(
            num_scalar_prefetch=1,
            grid=(1,),
            in_specs=[IN_SMEM, ANYWHERE] + [IN_HBM] * (2 + len(blocks)),
            out_specs=pl.BlockSpec((rows, members, width), lambda i, m: (0, 0, 0)),
            scratch_shapes=[
                pltpu.VMEM((chips, cores, lats, rows * members), BF16),
                pltpu.VMEM((width, nlat), BF16),
                pltpu.VMEM((rows, members, width), BF16),
                pltpu.SemaphoreType.DMA((width // 256 + 1,)),
                pltpu.SemaphoreType.DMA,
                pltpu.SemaphoreType.DMA((CORES, rows)),
            ],
        ),
    )(me, wave, token, in_hbm(table), in_hbm(state), in_hbm(blocks[0]), *blocks[1:])


def sum_pairs_kernel(coeff_ref, token_ref, inverse_ref, out_ref):
    pairs, entries = inverse_ref.shape[:2]
    half = entries // 2

    def one(entry, carry):
        real = imag = 0.0
        for k in range(pairs):
            first, second = inverse_ref[k, entry].astype(F32), inverse_ref[k, half + entry].astype(F32)
            a, b = coeff_ref[k, 0], coeff_ref[k, 1]
            real = real + (a * first - b * second)
            imag = imag + (a * second + b * first)
        out_ref[entry] = real
        out_ref[half + entry] = imag
        return carry

    lax.fori_loop(0, half, one, 0)


def sum_pairs(block_inverses, pole_coeffs, token):
    return call(
        sum_pairs_kernel,
        "sum_pairs",
        4 * block_inverses.size,
        2 * block_inverses.size,
        out_shape=jax.ShapeDtypeStruct(block_inverses.shape[1:], F32),
        in_specs=[IN_SMEM, ANYWHERE, pl.BlockSpec(block_inverses.shape, lambda: (0, 0, 0, 0))],
        out_specs=pl.BlockSpec(block_inverses.shape[1:], lambda: (0, 0, 0)),
    )(pole_coeffs, token, block_inverses)


def synthesise_kernel(
    slot, low, apart, more, partial, me_ref, sign_ref, here_ref, there_ref, own_ref, other_ref, table_ref, *rest
):
    rows, members, _ = own_ref.shape
    step = pl.program_id(0)
    if partial:
        partial_ref, rest = rest[0], rest[1:]
    if more:
        sums_out, mixed = rest
    elif apart:
        outs, mate_out, mixed, held, sems = rest[:-4], rest[-4], rest[-3], rest[-2], rest[-1]
    else:
        own_out, mate_out, mixed = rest

    @pl.when(step == 0)
    def _():
        count = own_ref.shape[2]
        for n in range(0, count, 128):
            lanes = slice(low + n, low + n + 128)
            lines = [
                here_ref[entry, slot : slot + 1, lanes] + there_ref[entry, slot : slot + 1, lanes]
                for entry in range(2 * rows * rows)
            ]
            lines[rows * rows :] = [sign_ref[0] * line for line in lines[rows * rows :]]
            for e in range(0, members, 32):
                part = (slice(e, e + 32), slice(n, n + 128))
                owns = [own_ref[(g,) + part].astype(F32) for g in range(rows)]
                others = [other_ref[(g,) + part].astype(F32) for g in range(rows)]
                for f in range(rows):
                    total = 0.0
                    for g in range(rows):
                        total = total + lines[f * rows + g] * owns[g]
                        total = total + lines[rows * rows + f * rows + g] * others[g]
                    mixed[f * members + e : f * members + e + 32, n : n + 128] = total.astype(BF16)

    sums = jnp.dot(mixed[...], table_ref[0], preferred_element_type=F32)
    if partial:
        sums = sums + partial_ref[...]
    if more:
        sums_out[...] = sums
        return
    lats = mate_out.shape[2]
    each = mate_out.shape[0]
    for r in range(rows):
        turned = sums[r * members : (r + 1) * members, :].astype(BF16).T
        values = [turned[i : i + lats] for i in range(0, turned.shape[0], lats)]
        mine, others = split_cores(values, me_ref[0] % CORES)
        for i, (a, b) in enumerate(zip(mine, others)):
            if apart:
                held[step * each + i, r] = a
            else:
                own_out[i, 0, r] = a
            mate_out[i, r] = b

    if apart:
        chip, core = me_ref[0] // CORES, me_ref[0] % CORES
        copies = []
        for i, (k, out) in enumerate(zip(partners(len(outs)), outs)):
            copies.append(pltpu.make_async_copy(held.at[chip ^ k], out.at[core], sems.at[i]))
            pl.when((chip ^ k) // each == step)(copies[-1].start)

        @pl.when(step == pl.num_programs(0) - 1)
        def _():
            for copy in copies:
                copy.wait()


def synthesise(here, there, sign, own, other, table, me, slot, low, lats, apart, more, partial):
    rows, members, count = own.shape
    nlat = table.shape[2]
    width = math.lcm(CORES * lats, 128)
    chips, each = nlat // lats // CORES, width // lats // CORES
    matrix = pl.BlockSpec(here.shape, lambda j, m: (0, 0, 0))
    whole = pl.BlockSpec((rows, members, count), lambda j, m: (0, 0, 0))
    smem = pl.BlockSpec(memory_space=pltpu.SMEM)
    shapes = [jax.ShapeDtypeStruct((chips, CORES, rows, lats, members), BF16)]
    specs = [pl.BlockSpec((each, 1, rows, lats, members), lambda j, m: (j, m[0] % CORES, 0, 0, 0))]
    scratch = [pltpu.VMEM((rows * members, count), BF16)]
    shapes += [jax.ShapeDtypeStruct((chips, rows, lats, members), BF16)]
    specs += [pl.BlockSpec((each, rows, lats, members), lambda j, m: (j, 0, 0, 0))]
    sums = pl.BlockSpec((rows * members, width), lambda j, m: (0, j))
    if more:
        shapes, specs = [jax.ShapeDtypeStruct((rows * members, nlat), F32)], [sums]
    elif apart:
        shapes[:1] = [jax.ShapeDtypeStruct((CORES, rows, lats, members), BF16)] * chips
        specs[:1] = [ANYWHERE] * chips
        scratch += [pltpu.VMEM((chips, rows, lats, members), BF16), pltpu.SemaphoreType.DMA((chips,))]
    return call(
        functools.partial(synthesise_kernel, slot, low, apart, more, len(partial)),
        "synthesise",
        2 * count * nlat * rows * members,
        2 * count * nlat,
        out_shape=shapes,
        grid_spec=pltpu.PrefetchScalarGridSpec(
            num_scalar_prefetch=1,
            grid=(nlat // width,),
            in_specs=[
                smem,
                matrix,
                matrix,
                whole,
                whole,
                pl.BlockSpec((1, count, width), lambda j, m: (slot, low // count, j)),
            ]
            + [sums] * len(partial),
            out_specs=specs,
            scratch_shapes=scratch,
        ),
    )(me, sign, here, there, own, other, table, *partial)


def assemble_kernel(counts, me_ref, *rest):
    ins, out_ref, (held, done, in_sems, out_sems) = rest[: sum(counts)], rest[-5], rest[-4:]
    rows, lats, slots, members = done.shape
    local_slots = len(counts)
    chip = me_ref[0] // CORES
    each = out_sems.shape[1]
    size = lats // each
    depth, breadth = math.gcd(size, 16), 16
    copies, whole = [], {}
    for r in range(rows):
        copies.append([])
        used = 0
        for slot, count in enumerate(counts):
            refs = ins[used : used + count]
            used += count
            if count == 1:
                whole[slot] = refs[0]
                continue
            if r == 0:
                held[slot, chip] = refs[0][...]
            for i, (k, ref) in list(enumerate(zip(partners(count), refs)))[1:]:
                target = held.at[slot, chip ^ k, :, r]
                copies[r].append(pltpu.make_async_copy(ref.at[:, r], target, in_sems.at[r, slot, i]))
        for copy in copies[r]:
            copy.start()
    matrix = swap_matrix(breadth, depth, 1, 0)
    results = []
    for r in range(rows):
        for copy in copies[r]:
            copy.wait()
        for start in range(0, lats, depth):
            j = slice(start, start + depth)
            for s in range(0, slots, 2 * breadth):
                halves = []
                for h in (0, breadth):
                    columns = [divmod(i, local_slots) for i in range(s + h, s + h + breadth)]
                    columns = [
                        whole.get(slot, held.at[slot])[owner // CORES, owner % CORES, r, j, :]
                        for owner, slot in columns
                    ]
                    halves.append(jnp.concatenate(columns, axis=0))
                turned = jnp.dot(matrix, jnp.concatenate(halves, axis=1), preferred_element_type=F32).astype(BF16)
                for h in range(2):
                    value = turned[:, h * members : (h + 1) * members].reshape(depth, breadth, members)
                    done[r, j, s + h * breadth : s + (h + 1) * breadth, :] = value
            if (start + depth) % size == 0:
                part = pl.ds(start + depth - size, size)
                target = out_ref.at[r, part]
                results.append(pltpu.make_async_copy(done.at[r, part], target, out_sems.at[r, start // size]))
                results[-1].start()
    for copy in results:
        copy.wait()


def assemble(pieces, me):
    rows, lats, members = pieces[0][0].shape[-3:]
    chips = max(len(p) if len(p) > 1 else p[0].shape[0] for p in pieces)
    slots = len(pieces) * chips * CORES
    flat = [block for slot in pieces for block in slot]
    return call(
        functools.partial(assemble_kernel, [len(p) for p in pieces]),
        "assemble",
        2 * 256 * rows * lats * slots * members,
        4 * rows * lats * slots * members,
        out_shape=jax.ShapeDtypeStruct((rows, lats, slots, members), BF16),
        in_specs=[IN_SMEM]
        + [IN_VMEM if i == 0 else IN_HBM for p in pieces for i in range(len(p))],
        out_specs=IN_HBM,
        scratch_shapes=[
            pltpu.VMEM((len(pieces), chips, CORES, rows, lats, members), BF16),
            pltpu.VMEM((rows, lats, slots, members), BF16),
            pltpu.SemaphoreType.DMA((rows, len(pieces), chips)),
            pltpu.SemaphoreType.DMA((rows, lats // lat_block(lats))),
        ],
    )(me, *flat)


def between_cores(blocks, owners):
    return lax.ppermute(blocks, "wave", [(d, d ^ 1) for d in range(owners)])


def by_permutes(messages):
    owners = len(messages) * CORES
    got = [messages[0]]
    for k, message in list(zip(partners(len(messages)), messages))[1:]:
        got.append(lax.ppermute(message, "wave", [(d, d ^ (k * CORES)) for d in range(owners)]))
    return got


def between_chips(blocks, owners):
    groups = [list(range(core, owners, CORES)) for core in range(CORES)]
    return lax.all_to_all(blocks, "wave", split_axis=0, concat_axis=0, axis_index_groups=groups, tiled=True)


def per_device(
    tendency, spectral_state, legendre, gauss_weights, block_inverses, pole_coeffs, wavenumbers
):
    rows, lats, slots, members = tendency.shape
    local_slots, nspec, nlat = legendre.shape
    owners = slots // local_slots
    me = lax.axis_index("wave").astype(jnp.int32).reshape(1)
    pole_index = lax.axis_index("pole")
    sign = (2 * pole_index - 1).astype(F32).reshape(1)
    order = list(range(local_slots))[::-1]
    received, waits = {}, []
    for slot in order:
        early = slot == order[0]
        *blocks, token = weigh(tendency, gauss_weights[None], me, slot, local_slots, not early, waits)
        if early:
            received[slot] = between_chips(blocks[0], owners)
            here = sum_pairs(block_inverses, pole_coeffs, token)
            there = lax.ppermute(here, "pole", [(0, 1), (1, 0)])
            waits = [there]
        else:
            blocks, token = pair(blocks[0], between_cores(blocks[1], owners), me)
            received[slot] = between_chips(blocks, owners)

    sent = {}
    for slot in order:
        half = nspec // 2
        lows = [half] if slot % 2 else [0, half]
        blocks = [received[slot]]
        if slot == order[0]:
            blocks.append(between_cores(pick(blocks[0], me, token), owners))
        forced = [analyse(blocks, legendre, spectral_state, wavenumbers, me, token, slot, low, half) for low in lows]
        others = [lax.ppermute(part, "pole", [(0, 1), (1, 0)]) for part in forced]
        last = slot == order[-1]
        own = []
        for low, part, other in zip(lows, forced, others):
            more = low != lows[-1]
            own = synthesise(here, there, sign, part, other, legendre, me, slot, low, lats, last, more, own)
        *own, for_mate = own
        mate = between_cores(for_mate, owners)
        if last:
            far = len(own) // 2 + 1
            own = list(pair_messages(own[:far], mate, me, 0, [])) + list(
                pair_messages(own[far:], mate, me, far, sent[order[0]])
            )
            sent[slot] = by_permutes(own)
        else:
            blocks, token = pair(own[0], mate, me)
            sent[slot] = [between_chips(blocks, owners)]
    return assemble([sent[slot] for slot in range(local_slots)], me)


def solution(mesh):
    in_specs = (
        P("pole", "wave", None, None),
        P("pole", "wave", None, None),
        P("wave", None, None),
        P("wave"),
        P("pole", None, "wave", None),
        P("pole", None),
        P("wave"),
    )
    out_specs = P("pole", "wave", None, None)
    return jax.shard_map(
        per_device, mesh=mesh, in_specs=in_specs, out_specs=out_specs, check_vma=False
    )
```

```python
import functools
import math

import jax
import jax.numpy as jnp
from jax import lax
from jax.experimental import pallas as pl
from jax.experimental.pallas import tpu as pltpu
from jax.sharding import PartitionSpec as P

BF16 = jnp.bfloat16
F32 = jnp.float32
CORES = 2
ANYWHERE = pl.BlockSpec(memory_space=pl.ANY)
IN_SMEM = pl.BlockSpec(memory_space=pltpu.SMEM)
IN_HBM = pl.BlockSpec(memory_space=pltpu.HBM)
IN_VMEM = pl.BlockSpec(memory_space=pltpu.VMEM)
TOKEN = jax.ShapeDtypeStruct((8, 128), F32)


def call(kernel, name, flops, size, mib=40, **kwargs):
    return pl.pallas_call(
        kernel,
        name=name,
        compiler_params=pltpu.CompilerParams(vmem_limit_bytes=mib * 1024 * 1024),
        cost_estimate=pl.CostEstimate(flops=int(flops), bytes_accessed=int(size), transcendentals=0),
        **kwargs,
    )


def in_hbm(array):
    return pltpu.with_memory_space_constraint(array, pltpu.HBM)


def run_copies(copies):
    for copy in copies:
        copy.start()
    for copy in copies:
        copy.wait()


def partners(chips):
    return [0] + list(range(chips // 2, chips)) + list(range(1, chips // 2))


def split_cores(values, core):
    even = [values[i] for i in range(0, len(values), CORES)]
    odd = [values[i] for i in range(1, len(values), CORES)]
    mine = [jnp.where(core == 0, a, b) for a, b in zip(even, odd)]
    others = [jnp.where(core == 0, b, a) for a, b in zip(even, odd)]
    return mine, others


def swap_matrix(rows, columns, step, skip):
    shape = (rows * columns // step, rows * columns)
    shift = rows.bit_length() - 1
    target = lax.broadcasted_iota(jnp.int32, shape, 0)
    source = lax.broadcasted_iota(jnp.int32, shape, 1)
    wanted = (target & (rows - 1)) * columns + (target >> shift) * step + skip
    return jnp.where(source == wanted, 1.0, 0.0).astype(BF16)


def weigh_kernel(slot, local_slots, split, waits, me_ref, gauss_any, tendency_ref, *rest):
    outs, token_ref, (gauss_ref, column, held, done, gauss_sem, in_sems, out_sems) = rest[waits:-8], rest[-8], rest[-7:]
    line_copy = pltpu.make_async_copy(gauss_any, gauss_ref, gauss_sem)
    line_copy.start()
    rows, lats, slots, members = held.shape
    each = in_sems.shape[1]
    size = lats // each
    copies = []
    for r in range(rows):
        for i in range(each):
            part = pl.ds(i * size, size)
            copies.append(pltpu.make_async_copy(tendency_ref.at[r, part], held.at[r, part], in_sems.at[r, i]))
            copies[-1].start()
    token_ref[...] = jnp.zeros_like(token_ref)
    depth, breadth = math.gcd(size, 16), 16
    matrix = swap_matrix(depth, breadth, local_slots, slot)
    owners = breadth // local_slots
    core = me_ref[0] % CORES
    line_copy.wait()
    for j in range(0, lats, depth):
        line = jnp.broadcast_to(gauss_ref[...], (depth, lats))
        here = lax.broadcasted_iota(jnp.int32, line.shape, 0) + j
        mine = lax.broadcasted_iota(jnp.int32, line.shape, 1) == here
        value = jnp.sum(jnp.where(mine, line, 0.0), axis=1, keepdims=True)
        column[j : j + depth, :] = jnp.broadcast_to(value, (depth, members))
    results = []
    for r in range(rows):
        for j in range(0, lats, depth):
            if j % size == 0:
                copies[r * each + j // size].wait()
            scale = column[j : j + depth, :]
            for s in range(0, slots, 2 * breadth):
                halves = [
                    held[r, j : j + depth, s + h : s + h + breadth, :].reshape(depth * breadth, members)
                    for h in (0, breadth)
                ]
                turned = jnp.dot(matrix, jnp.concatenate(halves, axis=1), preferred_element_type=F32)
                values = [
                    turned[i * depth : (i + 1) * depth, h * members : (h + 1) * members] * scale
                    for h in range(2)
                    for i in range(owners)
                ]
                start = s // local_slots
                if split:
                    mine, others = split_cores(values, core)
                    for i, (a, b) in enumerate(zip(mine, others)):
                        done[start // CORES + i, 0, r, j : j + depth, :] = a.astype(BF16)
                        done[start // CORES + i, 1, r, j : j + depth, :] = b.astype(BF16)
                else:
                    for i, value in enumerate(values):
                        chip, target = divmod(start + i, CORES)
                        done[chip, target, r, j : j + depth, :] = value.astype(BF16)
            if (j + depth) % size == 0:
                part = pl.ds(j + depth - size, size)
                source, target = done.at[:, :, r, part], outs[0].at[:, :, r, part]
                if split:
                    source, target = done.at[:, 0, r, part], outs[0].at[:, core, r, part]
                    other = pltpu.make_async_copy(
                        done.at[:, 1, r, part], outs[1].at[:, r, part], out_sems.at[1, r, j // size]
                    )
                    other.start()
                    results.append(other)
                results.append(pltpu.make_async_copy(source, target, out_sems.at[0, r, j // size]))
                results[-1].start()
    for copy in results:
        copy.wait()


def lat_block(lats):
    return lats // 2 if lats % 32 == 0 else lats


def weigh(tendency, gauss, me, slot, local_slots, split, waits):
    rows, lats, slots, members = tendency.shape
    each = lats // lat_block(lats)
    chips = slots // local_slots // CORES
    shapes = [jax.ShapeDtypeStruct((chips, CORES, rows, lats, members), BF16)]
    if split:
        shapes += [jax.ShapeDtypeStruct((chips, rows, lats, members), BF16)]
    return call(
        functools.partial(weigh_kernel, slot, local_slots, split, len(waits)),
        "weigh",
        2 * 128 * tendency.size,
        3 * tendency.size,
        58,
        out_shape=shapes + [TOKEN],
        in_specs=[IN_SMEM] + [ANYWHERE] * (2 + len(waits)),
        out_specs=[ANYWHERE] * len(shapes) + [pl.BlockSpec(TOKEN.shape, lambda: (0, 0))],
        scratch_shapes=[
            pltpu.VMEM((1, lats), F32),
            pltpu.VMEM((lats, members), F32),
            pltpu.VMEM((rows, lats, slots, members), BF16),
            pltpu.VMEM((chips, CORES, rows, lats, members), BF16),
            pltpu.SemaphoreType.DMA,
            pltpu.SemaphoreType.DMA((rows, each)),
            pltpu.SemaphoreType.DMA((CORES, rows, each)),
        ],
    )(me, gauss, tendency, *waits)


def pick_kernel(me_ref, token_ref, in_ref, out_ref, held, in_sems, out_sems):
    other = CORES - 1 - me_ref[0] % CORES
    rows = held.shape[1]
    fetched = [pltpu.make_async_copy(in_ref.at[:, other, r], held.at[:, r], in_sems.at[r]) for r in range(rows)]
    stored = [pltpu.make_async_copy(held.at[:, r], out_ref.at[:, r], out_sems.at[r]) for r in range(rows)]
    for copy in fetched:
        copy.start()
    for fetch, store in zip(fetched, stored):
        fetch.wait()
        store.start()
    for copy in stored:
        copy.wait()


def pick(blocks, me, token):
    chips, _, rows, lats, members = blocks.shape
    shape = (chips, rows, lats, members)
    return call(
        pick_kernel,
        "pick",
        0,
        2 * blocks.size,
        out_shape=jax.ShapeDtypeStruct(shape, BF16),
        in_specs=[IN_SMEM, ANYWHERE, IN_HBM],
        out_specs=IN_HBM,
        scratch_shapes=[
            pltpu.VMEM(shape, BF16),
            pltpu.SemaphoreType.DMA((rows,)),
            pltpu.SemaphoreType.DMA((rows,)),
        ],
    )(me, token, in_hbm(blocks))


def pair_kernel(me_ref, mate_ref, blocks_ref, out_ref, token_ref, sem):
    token_ref[...] = jnp.zeros_like(token_ref)
    other = CORES - 1 - me_ref[0] % CORES
    run_copies([pltpu.make_async_copy(mate_ref, out_ref.at[:, other], sem)])


def pair(blocks, mate, me):
    return call(
        pair_kernel,
        "pair",
        0,
        4 * mate.size,
        out_shape=[jax.ShapeDtypeStruct(blocks.shape, blocks.dtype), TOKEN],
        in_specs=[IN_SMEM, pl.BlockSpec(mate.shape, lambda: (0, 0, 0, 0)), ANYWHERE],
        out_specs=[ANYWHERE, pl.BlockSpec(TOKEN.shape, lambda: (0, 0))],
        scratch_shapes=[pltpu.SemaphoreType.DMA],
        input_output_aliases={2: 0},
    )(me, mate, blocks)


def pair_messages_kernel(first, waits, me_ref, mate_ref, *rest):
    count = (len(rest) - 1 - waits) // 2
    outs, sems = rest[-1 - count : -1], rest[-1]
    chip, other = me_ref[0] // CORES, CORES - 1 - me_ref[0] % CORES
    wanted = partners(mate_ref.shape[0])[first : first + count]
    run_copies(
        [
            pltpu.make_async_copy(mate_ref.at[chip ^ k], out.at[other], sems.at[i])
            for i, (k, out) in enumerate(zip(wanted, outs))
        ]
    )


def pair_messages(messages, mate, me, first, waits):
    count = len(messages)
    return call(
        functools.partial(pair_messages_kernel, first, len(waits)),
        "pair",
        0,
        4 * mate.size,
        out_shape=[jax.ShapeDtypeStruct(m.shape, m.dtype) for m in messages],
        in_specs=[IN_SMEM, pl.BlockSpec(mate.shape, lambda: (0, 0, 0, 0))] + [ANYWHERE] * (count + len(waits)),
        out_specs=[ANYWHERE] * count,
        scratch_shapes=[pltpu.SemaphoreType.DMA((count,))],
        input_output_aliases={i + 2: i for i in range(count)},
    )(me, mate, *messages, *waits)


def analyse_kernel(slot, low, me_ref, wave_ref, token_ref, table_ref, state_ref, *rest):
    blocks, out, (grid, table, state, table_sems, state_sem, block_sems) = rest[:-7], rest[-7], rest[-6:]
    rows, members, width = out.shape
    chips, cores, lats, _ = grid.shape
    core = me_ref[0] % CORES
    moves = []
    for r in range(rows):
        lanes = pl.ds(r * members, members)
        if len(blocks) == 1:
            moves.append(pltpu.make_async_copy(blocks[0].at[:, :, r], grid.at[:, :, :, lanes], block_sems.at[0, r]))
        else:
            target = grid.at[:, core, :, lanes]
            moves.append(pltpu.make_async_copy(blocks[0].at[:, core, r], target, block_sems.at[0, r]))
            target = grid.at[:, CORES - 1 - core, :, lanes]
            moves.append(pltpu.make_async_copy(blocks[1].at[:, r], target, block_sems.at[1, r]))
    cuts = sorted(set([0] + list(range(width % 256, width + 1, 256))))
    copies = []
    for i, (start, end) in enumerate(zip(cuts, cuts[1:])):
        source = table_ref.at[slot, pl.ds(low + start, end - start)]
        copies.append(pltpu.make_async_copy(source, table.at[pl.ds(start, end - start)], table_sems.at[i]))
    state_copy = pltpu.make_async_copy(state_ref.at[:, slot, :, pl.ds(low, width)], state, state_sem)
    for move in moves + copies + [state_copy]:
        move.start()
    for move in moves:
        move.wait()
    field = grid[...].reshape(chips * cores * lats, rows * members)
    state_copy.wait()
    for copy, start, end in zip(copies, cuts, cuts[1:]):
        copy.wait()
        sums = jnp.dot(table[start:end], field, preferred_element_type=F32)
        degree = lax.broadcasted_iota(jnp.int32, (members, end - start), 1) + (low + start)
        live = degree >= wave_ref[slot]
        for r in range(rows):
            total = state[r, :, start:end].astype(F32) + sums[:, r * members : (r + 1) * members].T
            out[r, :, start:end] = jnp.where(live, total, 0.0).astype(BF16)


def analyse(blocks, table, state, wave, me, token, slot, low, width):
    chips, _, rows, lats, members = blocks[0].shape
    nlat = table.shape[2]
    cores = CORES
    if lats % 16:
        if len(blocks) > 1:
            core = me[0] % CORES
            own = lax.dynamic_index_in_dim(blocks[0], core, 1, keepdims=False)
            pairs = [jnp.where(core == 0, own, blocks[1]), jnp.where(core == 0, blocks[1], own)]
            blocks = [jnp.stack(pairs, axis=1)]
        laid = jnp.transpose(blocks[0], (2, 0, 1, 3, 4)).reshape(1, 1, rows, nlat, members)
        blocks, chips, cores, lats = [laid], 1, 1, nlat
    return call(
        functools.partial(analyse_kernel, slot, low),
        "analyse",
        2 * width * nlat * rows * members,
        2 * width * nlat,
        out_shape=jax.ShapeDtypeStruct((rows, members, width), BF16),
        grid_spec=pltpu.PrefetchScalarGridSpec(
            num_scalar_prefetch=1,
            grid=(1,),
            in_specs=[IN_SMEM, ANYWHERE] + [IN_HBM] * (2 + len(blocks)),
            out_specs=pl.BlockSpec((rows, members, width), lambda i, m: (0, 0, 0)),
            scratch_shapes=[
                pltpu.VMEM((chips, cores, lats, rows * members), BF16),
                pltpu.VMEM((width, nlat), BF16),
                pltpu.VMEM((rows, members, width), BF16),
                pltpu.SemaphoreType.DMA((width // 256 + 1,)),
                pltpu.SemaphoreType.DMA,
                pltpu.SemaphoreType.DMA((CORES, rows)),
            ],
        ),
    )(me, wave, token, in_hbm(table), in_hbm(state), in_hbm(blocks[0]), *blocks[1:])


def sum_pairs_kernel(coeff_ref, token_ref, inverse_ref, out_ref):
    pairs, entries = inverse_ref.shape[:2]
    half = entries // 2

    def one(entry, carry):
        real = imag = 0.0
        for k in range(pairs):
            first, second = inverse_ref[k, entry].astype(F32), inverse_ref[k, half + entry].astype(F32)
            a, b = coeff_ref[k, 0], coeff_ref[k, 1]
            real = real + (a * first - b * second)
            imag = imag + (a * second + b * first)
        out_ref[entry] = real
        out_ref[half + entry] = imag
        return carry

    lax.fori_loop(0, half, one, 0)


def sum_pairs(block_inverses, pole_coeffs, token):
    return call(
        sum_pairs_kernel,
        "sum_pairs",
        4 * block_inverses.size,
        2 * block_inverses.size,
        out_shape=jax.ShapeDtypeStruct(block_inverses.shape[1:], F32),
        in_specs=[IN_SMEM, ANYWHERE, pl.BlockSpec(block_inverses.shape, lambda: (0, 0, 0, 0))],
        out_specs=pl.BlockSpec(block_inverses.shape[1:], lambda: (0, 0, 0)),
    )(pole_coeffs, token, block_inverses)


def synthesise_kernel(
    slot, low, apart, more, partial, me_ref, sign_ref, here_ref, there_ref, own_ref, other_ref, table_ref, *rest
):
    rows, members, _ = own_ref.shape
    step = pl.program_id(0)
    if partial:
        partial_ref, rest = rest[0], rest[1:]
    if more:
        sums_out, mixed = rest
    elif apart:
        outs, mate_out, mixed, held, sems = rest[:-4], rest[-4], rest[-3], rest[-2], rest[-1]
    else:
        own_out, mate_out, mixed = rest

    @pl.when(step == 0)
    def _():
        count = own_ref.shape[2]
        for n in range(0, count, 128):
            lanes = slice(low + n, low + n + 128)
            lines = [
                here_ref[entry, slot : slot + 1, lanes] + there_ref[entry, slot : slot + 1, lanes]
                for entry in range(2 * rows * rows)
            ]
            lines[rows * rows :] = [sign_ref[0] * line for line in lines[rows * rows :]]
            for e in range(0, members, 32):
                part = (slice(e, e + 32), slice(n, n + 128))
                owns = [own_ref[(g,) + part].astype(F32) for g in range(rows)]
                others = [other_ref[(g,) + part].astype(F32) for g in range(rows)]
                for f in range(rows):
                    total = 0.0
                    for g in range(rows):
                        total = total + lines[f * rows + g] * owns[g]
                        total = total + lines[rows * rows + f * rows + g] * others[g]
                    mixed[f * members + e : f * members + e + 32, n : n + 128] = total.astype(BF16)

    sums = jnp.dot(mixed[...], table_ref[0], preferred_element_type=F32)
    if partial:
        sums = sums + partial_ref[...]
    if more:
        sums_out[...] = sums
        return
    lats = mate_out.shape[2]
    each = mate_out.shape[0]
    for r in range(rows):
        turned = sums[r * members : (r + 1) * members, :].astype(BF16).T
        values = [turned[i : i + lats] for i in range(0, turned.shape[0], lats)]
        mine, others = split_cores(values, me_ref[0] % CORES)
        for i, (a, b) in enumerate(zip(mine, others)):
            if apart:
                held[step * each + i, r] = a
            else:
                own_out[i, 0, r] = a
            mate_out[i, r] = b

    if apart:
        chip, core = me_ref[0] // CORES, me_ref[0] % CORES
        copies = []
        for i, (k, out) in enumerate(zip(partners(len(outs)), outs)):
            copies.append(pltpu.make_async_copy(held.at[chip ^ k], out.at[core], sems.at[i]))
            pl.when((chip ^ k) // each == step)(copies[-1].start)

        @pl.when(step == pl.num_programs(0) - 1)
        def _():
            for copy in copies:
                copy.wait()


def synthesise(here, there, sign, own, other, table, me, slot, low, lats, apart, more, partial):
    rows, members, count = own.shape
    nlat = table.shape[2]
    width = math.lcm(CORES * lats, 128)
    chips, each = nlat // lats // CORES, width // lats // CORES
    matrix = pl.BlockSpec(here.shape, lambda j, m: (0, 0, 0))
    whole = pl.BlockSpec((rows, members, count), lambda j, m: (0, 0, 0))
    smem = pl.BlockSpec(memory_space=pltpu.SMEM)
    shapes = [jax.ShapeDtypeStruct((chips, CORES, rows, lats, members), BF16)]
    specs = [pl.BlockSpec((each, 1, rows, lats, members), lambda j, m: (j, m[0] % CORES, 0, 0, 0))]
    scratch = [pltpu.VMEM((rows * members, count), BF16)]
    shapes += [jax.ShapeDtypeStruct((chips, rows, lats, members), BF16)]
    specs += [pl.BlockSpec((each, rows, lats, members), lambda j, m: (j, 0, 0, 0))]
    sums = pl.BlockSpec((rows * members, width), lambda j, m: (0, j))
    if more:
        shapes, specs = [jax.ShapeDtypeStruct((rows * members, nlat), F32)], [sums]
    elif apart:
        shapes[:1] = [jax.ShapeDtypeStruct((CORES, rows, lats, members), BF16)] * chips
        specs[:1] = [ANYWHERE] * chips
        scratch += [pltpu.VMEM((chips, rows, lats, members), BF16), pltpu.SemaphoreType.DMA((chips,))]
    return call(
        functools.partial(synthesise_kernel, slot, low, apart, more, len(partial)),
        "synthesise",
        2 * count * nlat * rows * members,
        2 * count * nlat,
        out_shape=shapes,
        grid_spec=pltpu.PrefetchScalarGridSpec(
            num_scalar_prefetch=1,
            grid=(nlat // width,),
            in_specs=[
                smem,
                matrix,
                matrix,
                whole,
                whole,
                pl.BlockSpec((1, count, width), lambda j, m: (slot, low // count, j)),
            ]
            + [sums] * len(partial),
            out_specs=specs,
            scratch_shapes=scratch,
        ),
    )(me, sign, here, there, own, other, table, *partial)


def assemble_kernel(far, moved, count, me_ref, blocks_ref, *rest):
    messages, out_ref, (held, done, in_sems, out_sems) = rest[:count], rest[-5], rest[-4:]
    rows, lats, slots, members = done.shape
    half = held.shape[0]
    local_slots = slots // half // CORES
    chip = me_ref[0] // CORES
    side = chip // half if not far else 1 - chip // half
    each = out_sems.shape[1]
    size = lats // each
    depth, breadth = math.gcd(size, 16), 16
    wanted = [k for k in partners(2 * half) if (k >= half) == far]
    copies = []
    for r in range(rows):
        copies.append([])
        for i, (k, ref) in enumerate(zip(wanted, messages)):
            target = held.at[(chip ^ k) & (half - 1), :, r]
            copies[r].append(pltpu.make_async_copy(ref.at[:, r], target, in_sems.at[r, i]))
            copies[r][-1].start()
    matrix = swap_matrix(breadth, depth, 1, 0)
    results = []

    def tile(r, start, s):
        parts = []
        for i in range(s, s + breadth):
            owner, slot = divmod(i, local_slots)
            place = owner // CORES
            if slot == moved:
                parts.append(held[place, owner % CORES, r, start : start + depth, :])
            else:
                parts.append(blocks_ref[side * half + place, owner % CORES, r, start : start + depth, :])
        return jnp.concatenate(parts, axis=0)

    for r in range(rows):
        for copy in copies[r]:
            copy.wait()
        for part in range(each):
            starts = range(part * size, (part + 1) * size, depth)
            tiles = [(start, s) for start in starts for s in range(0, slots, breadth)]
            for i in range(0, len(tiles), 2):
                both = tiles[i : i + 2]
                wide = jnp.concatenate([tile(r, *place) for place in both], axis=1)
                turned = jnp.dot(matrix, wide, preferred_element_type=F32).astype(BF16)
                for n, (start, s) in enumerate(both):
                    value = turned[:, n * members : (n + 1) * members].reshape(depth, breadth, members)
                    done[r, start : start + depth, s : s + breadth, :] = value
            lines = pl.ds(part * size, size)
            target = out_ref.at[r, lines, pl.ds(pl.multiple_of(side * slots, slots), slots)]
            results.append(pltpu.make_async_copy(done.at[r, lines], target, out_sems.at[r, part]))
            results[-1].start()
    for copy in results:
        copy.wait()


def assemble(blocks, messages, me, moved, local_slots, far, output):
    chips, _, rows, lats, members = blocks.shape
    half = chips // 2
    slots = local_slots * half * CORES
    return call(
        functools.partial(assemble_kernel, far, moved, len(messages)),
        "assemble",
        2 * 256 * rows * lats * slots * members,
        4 * rows * lats * slots * members,
        out_shape=jax.ShapeDtypeStruct((rows, lats, 2 * slots, members), BF16),
        in_specs=[IN_SMEM, IN_VMEM] + [IN_HBM] * (len(messages) + len(output)),
        out_specs=IN_HBM,
        scratch_shapes=[
            pltpu.VMEM((half, CORES, rows, lats, members), BF16),
            pltpu.VMEM((rows, lats, slots, members), BF16),
            pltpu.SemaphoreType.DMA((rows, half)),
            pltpu.SemaphoreType.DMA((rows, lats // lat_block(lats))),
        ],
        input_output_aliases={len(messages) + 2: 0} if output else {},
    )(me, blocks, *messages, *output)


def between_cores(blocks, owners):
    return lax.ppermute(blocks, "wave", [(d, d ^ 1) for d in range(owners)])


def by_permutes(messages):
    owners = len(messages) * CORES
    got = [messages[0]]
    for k, message in list(zip(partners(len(messages)), messages))[1:]:
        got.append(lax.ppermute(message, "wave", [(d, d ^ (k * CORES)) for d in range(owners)]))
    return got


def between_chips(blocks, owners):
    groups = [list(range(core, owners, CORES)) for core in range(CORES)]
    return lax.all_to_all(blocks, "wave", split_axis=0, concat_axis=0, axis_index_groups=groups, tiled=True)


def per_device(
    tendency, spectral_state, legendre, gauss_weights, block_inverses, pole_coeffs, wavenumbers
):
    rows, lats, slots, members = tendency.shape
    local_slots, nspec, nlat = legendre.shape
    owners = slots // local_slots
    me = lax.axis_index("wave").astype(jnp.int32).reshape(1)
    pole_index = lax.axis_index("pole")
    sign = (2 * pole_index - 1).astype(F32).reshape(1)
    order = list(range(local_slots))[::-1]
    received, waits = {}, []
    for slot in order:
        early = slot == order[0]
        *blocks, token = weigh(tendency, gauss_weights[None], me, slot, local_slots, not early, waits)
        if early:
            received[slot] = between_chips(blocks[0], owners)
            here = sum_pairs(block_inverses, pole_coeffs, token)
            there = lax.ppermute(here, "pole", [(0, 1), (1, 0)])
            waits = [there]
        else:
            blocks, token = pair(blocks[0], between_cores(blocks[1], owners), me)
            received[slot] = between_chips(blocks, owners)

    sent = {}
    for slot in order:
        half = nspec // 2
        lows = [half] if slot % 2 else [0, half]
        blocks = [received[slot]]
        if slot == order[0]:
            blocks.append(between_cores(pick(blocks[0], me, token), owners))
        forced = [analyse(blocks, legendre, spectral_state, wavenumbers, me, token, slot, low, half) for low in lows]
        others = [lax.ppermute(part, "pole", [(0, 1), (1, 0)]) for part in forced]
        last = slot == order[-1]
        own = []
        for low, part, other in zip(lows, forced, others):
            more = low != lows[-1]
            own = synthesise(here, there, sign, part, other, legendre, me, slot, low, lats, last, more, own)
        *own, for_mate = own
        mate = between_cores(for_mate, owners)
        if last:
            own = pair_messages(own, mate, me, 0, [])
            sent[slot] = by_permutes(own)
        else:
            blocks, token = pair(own[0], mate, me)
            sent[slot] = [between_chips(blocks, owners)]
    blocks, messages = sent[order[0]][0], sent[order[-1]]
    far = len(messages) // 2 + 1
    near = assemble(blocks, messages[:1] + messages[far:], me, order[-1], local_slots, False, [])
    return assemble(blocks, messages[1:far], me, order[-1], local_slots, True, [near])


def solution(mesh):
    in_specs = (
        P("pole", "wave", None, None),
        P("pole", "wave", None, None),
        P("wave", None, None),
        P("wave"),
        P("pole", None, "wave", None),
        P("pole", None),
        P("wave"),
    )
    out_specs = P("pole", "wave", None, None)
    return jax.shard_map(
        per_device, mesh=mesh, in_specs=in_specs, out_specs=out_specs, check_vma=False
    )
```

```python
import functools
import math

import jax
import jax.numpy as jnp
from jax import lax
from jax.experimental import pallas as pl
from jax.experimental.pallas import tpu as pltpu
from jax.sharding import PartitionSpec as P

BF16 = jnp.bfloat16
F32 = jnp.float32
CORES = 2
ANYWHERE = pl.BlockSpec(memory_space=pl.ANY)
IN_SMEM = pl.BlockSpec(memory_space=pltpu.SMEM)
IN_HBM = pl.BlockSpec(memory_space=pltpu.HBM)
IN_VMEM = pl.BlockSpec(memory_space=pltpu.VMEM)
TOKEN = jax.ShapeDtypeStruct((8, 128), F32)


def call(kernel, name, flops, size, mib=40, **kwargs):
    return pl.pallas_call(
        kernel,
        name=name,
        compiler_params=pltpu.CompilerParams(vmem_limit_bytes=mib * 1024 * 1024),
        cost_estimate=pl.CostEstimate(flops=int(flops), bytes_accessed=int(size), transcendentals=0),
        **kwargs,
    )


def in_hbm(array):
    return pltpu.with_memory_space_constraint(array, pltpu.HBM)


def run_copies(copies):
    for copy in copies:
        copy.start()
    for copy in copies:
        copy.wait()


def messages_of(chips, rows):
    near, far = range(1, chips // 2), range(chips // 2, chips)
    first = [(k, 0, rows - 1) for k in far]
    return [(0, 0, rows)] + first + [(k, rows - 1, 1) for k in far] + [(k, 0, rows) for k in near]


def split_cores(values, core):
    even = [values[i] for i in range(0, len(values), CORES)]
    odd = [values[i] for i in range(1, len(values), CORES)]
    mine = [jnp.where(core == 0, a, b) for a, b in zip(even, odd)]
    others = [jnp.where(core == 0, b, a) for a, b in zip(even, odd)]
    return mine, others


def swap_matrix(rows, columns, step, skip):
    shape = (rows * columns // step, rows * columns)
    shift = rows.bit_length() - 1
    target = lax.broadcasted_iota(jnp.int32, shape, 0)
    source = lax.broadcasted_iota(jnp.int32, shape, 1)
    wanted = (target & (rows - 1)) * columns + (target >> shift) * step + skip
    return jnp.where(source == wanted, 1.0, 0.0).astype(BF16)


def weigh_kernel(slot, local_slots, split, waits, me_ref, gauss_any, tendency_ref, *rest):
    outs, token_ref, (gauss_ref, column, held, done, gauss_sem, in_sems, out_sems) = rest[waits:-8], rest[-8], rest[-7:]
    line_copy = pltpu.make_async_copy(gauss_any, gauss_ref, gauss_sem)
    line_copy.start()
    rows, lats, slots, members = held.shape
    each = in_sems.shape[1]
    size = lats // each
    copies = []
    for r in range(rows):
        for i in range(each):
            part = pl.ds(i * size, size)
            copies.append(pltpu.make_async_copy(tendency_ref.at[r, part], held.at[r, part], in_sems.at[r, i]))
            copies[-1].start()
    token_ref[...] = jnp.zeros_like(token_ref)
    depth, breadth = math.gcd(size, 16), 16
    matrix = swap_matrix(depth, breadth, local_slots, slot)
    owners = breadth // local_slots
    core = me_ref[0] % CORES
    line_copy.wait()
    for j in range(0, lats, depth):
        line = jnp.broadcast_to(gauss_ref[...], (depth, lats))
        here = lax.broadcasted_iota(jnp.int32, line.shape, 0) + j
        mine = lax.broadcasted_iota(jnp.int32, line.shape, 1) == here
        value = jnp.sum(jnp.where(mine, line, 0.0), axis=1, keepdims=True)
        column[j : j + depth, :] = jnp.broadcast_to(value, (depth, members))
    results = []
    for r in range(rows):
        for j in range(0, lats, depth):
            if j % size == 0:
                copies[r * each + j // size].wait()
            scale = column[j : j + depth, :]
            for s in range(0, slots, 2 * breadth):
                halves = [
                    held[r, j : j + depth, s + h : s + h + breadth, :].reshape(depth * breadth, members)
                    for h in (0, breadth)
                ]
                turned = jnp.dot(matrix, jnp.concatenate(halves, axis=1), preferred_element_type=F32)
                values = [
                    turned[i * depth : (i + 1) * depth, h * members : (h + 1) * members] * scale
                    for h in range(2)
                    for i in range(owners)
                ]
                start = s // local_slots
                if split:
                    mine, others = split_cores(values, core)
                    for i, (a, b) in enumerate(zip(mine, others)):
                        done[start // CORES + i, 0, r, j : j + depth, :] = a.astype(BF16)
                        done[start // CORES + i, 1, r, j : j + depth, :] = b.astype(BF16)
                else:
                    for i, value in enumerate(values):
                        chip, target = divmod(start + i, CORES)
                        done[chip, target, r, j : j + depth, :] = value.astype(BF16)
            if (j + depth) % size == 0:
                part = pl.ds(j + depth - size, size)
                source, target = done.at[:, :, r, part], outs[0].at[:, :, r, part]
                if split:
                    source, target = done.at[:, 0, r, part], outs[0].at[:, core, r, part]
                    other = pltpu.make_async_copy(
                        done.at[:, 1, r, part], outs[1].at[:, r, part], out_sems.at[1, r, j // size]
                    )
                    other.start()
                    results.append(other)
                results.append(pltpu.make_async_copy(source, target, out_sems.at[0, r, j // size]))
                results[-1].start()
    for copy in results:
        copy.wait()


def lat_block(lats):
    return 32 if lats % 32 == 0 else lats


def weigh(tendency, gauss, me, slot, local_slots, split, waits):
    rows, lats, slots, members = tendency.shape
    each = lats // lat_block(lats)
    chips = slots // local_slots // CORES
    shapes = [jax.ShapeDtypeStruct((chips, CORES, rows, lats, members), BF16)]
    if split:
        shapes += [jax.ShapeDtypeStruct((chips, rows, lats, members), BF16)]
    return call(
        functools.partial(weigh_kernel, slot, local_slots, split, len(waits)),
        "weigh",
        2 * 128 * tendency.size,
        3 * tendency.size,
        58,
        out_shape=shapes + [TOKEN],
        in_specs=[IN_SMEM] + [ANYWHERE] * (2 + len(waits)),
        out_specs=[ANYWHERE] * len(shapes) + [pl.BlockSpec(TOKEN.shape, lambda: (0, 0))],
        scratch_shapes=[
            pltpu.VMEM((1, lats), F32),
            pltpu.VMEM((lats, members), F32),
            pltpu.VMEM((rows, lats, slots, members), BF16),
            pltpu.VMEM((chips, CORES, rows, lats, members), BF16),
            pltpu.SemaphoreType.DMA,
            pltpu.SemaphoreType.DMA((rows, each)),
            pltpu.SemaphoreType.DMA((CORES, rows, each)),
        ],
    )(me, gauss, tendency, *waits)


def pick_kernel(me_ref, token_ref, in_ref, out_ref, held, in_sems, out_sems):
    other = CORES - 1 - me_ref[0] % CORES
    rows = held.shape[1]
    fetched = [pltpu.make_async_copy(in_ref.at[:, other, r], held.at[:, r], in_sems.at[r]) for r in range(rows)]
    stored = [pltpu.make_async_copy(held.at[:, r], out_ref.at[:, r], out_sems.at[r]) for r in range(rows)]
    for copy in fetched:
        copy.start()
    for fetch, store in zip(fetched, stored):
        fetch.wait()
        store.start()
    for copy in stored:
        copy.wait()


def pick(blocks, me, token):
    chips, _, rows, lats, members = blocks.shape
    shape = (chips, rows, lats, members)
    return call(
        pick_kernel,
        "pick",
        0,
        2 * blocks.size,
        out_shape=jax.ShapeDtypeStruct(shape, BF16),
        in_specs=[IN_SMEM, ANYWHERE, IN_HBM],
        out_specs=IN_HBM,
        scratch_shapes=[
            pltpu.VMEM(shape, BF16),
            pltpu.SemaphoreType.DMA((rows,)),
            pltpu.SemaphoreType.DMA((rows,)),
        ],
    )(me, token, in_hbm(blocks))


def pair_kernel(me_ref, mate_ref, blocks_ref, out_ref, token_ref, sem):
    token_ref[...] = jnp.zeros_like(token_ref)
    other = CORES - 1 - me_ref[0] % CORES
    run_copies([pltpu.make_async_copy(mate_ref, out_ref.at[:, other], sem)])


def pair(blocks, mate, me):
    return call(
        pair_kernel,
        "pair",
        0,
        4 * mate.size,
        out_shape=[jax.ShapeDtypeStruct(blocks.shape, blocks.dtype), TOKEN],
        in_specs=[IN_SMEM, pl.BlockSpec(mate.shape, lambda: (0, 0, 0, 0)), ANYWHERE],
        out_specs=[ANYWHERE, pl.BlockSpec(TOKEN.shape, lambda: (0, 0))],
        scratch_shapes=[pltpu.SemaphoreType.DMA],
        input_output_aliases={2: 0},
    )(me, mate, blocks)


def pair_messages_kernel(me_ref, mate_ref, *rest):
    outs, sems = rest[len(rest) // 2 : -1], rest[-1]
    chip, other = me_ref[0] // CORES, CORES - 1 - me_ref[0] % CORES
    copies = []
    for i, (k, row, rows) in enumerate(messages_of(*mate_ref.shape[:2])):
        source = mate_ref.at[chip ^ k, pl.ds(row, rows)]
        copies.append(pltpu.make_async_copy(source, outs[i].at[other], sems.at[i]))
    run_copies(copies)


def pair_messages(messages, mate, me):
    count = len(messages)
    return call(
        pair_messages_kernel,
        "pair",
        0,
        4 * mate.size,
        out_shape=[jax.ShapeDtypeStruct(m.shape, m.dtype) for m in messages],
        in_specs=[IN_SMEM, pl.BlockSpec(mate.shape, lambda: (0, 0, 0, 0))] + [ANYWHERE] * count,
        out_specs=[ANYWHERE] * count,
        scratch_shapes=[pltpu.SemaphoreType.DMA((count,))],
        input_output_aliases={i + 2: i for i in range(count)},
    )(me, mate, *messages)


def analyse_kernel(slot, low, me_ref, wave_ref, token_ref, table_ref, state_ref, *rest):
    blocks, out, (grid, table, state, table_sems, state_sem, block_sems) = rest[:-7], rest[-7], rest[-6:]
    rows, members, width = out.shape
    chips, cores, lats, _ = grid.shape
    core = me_ref[0] % CORES
    moves = []
    for r in range(rows):
        lanes = pl.ds(r * members, members)
        if len(blocks) == 1:
            moves.append(pltpu.make_async_copy(blocks[0].at[:, :, r], grid.at[:, :, :, lanes], block_sems.at[0, r]))
        else:
            target = grid.at[:, core, :, lanes]
            moves.append(pltpu.make_async_copy(blocks[0].at[:, core, r], target, block_sems.at[0, r]))
            target = grid.at[:, CORES - 1 - core, :, lanes]
            moves.append(pltpu.make_async_copy(blocks[1].at[:, r], target, block_sems.at[1, r]))
    cuts = sorted(set([0] + list(range(width % 256, width + 1, 256))))
    copies = []
    for i, (start, end) in enumerate(zip(cuts, cuts[1:])):
        source = table_ref.at[slot, pl.ds(low + start, end - start)]
        copies.append(pltpu.make_async_copy(source, table.at[pl.ds(start, end - start)], table_sems.at[i]))
    state_copy = pltpu.make_async_copy(state_ref.at[:, slot, :, pl.ds(low, width)], state, state_sem)
    for move in moves + copies + [state_copy]:
        move.start()
    for move in moves:
        move.wait()
    field = grid[...].reshape(chips * cores * lats, rows * members)
    state_copy.wait()
    for copy, start, end in zip(copies, cuts, cuts[1:]):
        copy.wait()
        sums = jnp.dot(table[start:end], field, preferred_element_type=F32)
        degree = lax.broadcasted_iota(jnp.int32, (members, end - start), 1) + (low + start)
        live = degree >= wave_ref[slot]
        for r in range(rows):
            total = state[r, :, start:end].astype(F32) + sums[:, r * members : (r + 1) * members].T
            out[r, :, start:end] = jnp.where(live, total, 0.0).astype(BF16)


def analyse(blocks, table, state, wave, me, token, slot, low, width):
    chips, _, rows, lats, members = blocks[0].shape
    nlat = table.shape[2]
    cores = CORES
    if lats % 16:
        if len(blocks) > 1:
            core = me[0] % CORES
            own = lax.dynamic_index_in_dim(blocks[0], core, 1, keepdims=False)
            pairs = [jnp.where(core == 0, own, blocks[1]), jnp.where(core == 0, blocks[1], own)]
            blocks = [jnp.stack(pairs, axis=1)]
        laid = jnp.transpose(blocks[0], (2, 0, 1, 3, 4)).reshape(1, 1, rows, nlat, members)
        blocks, chips, cores, lats = [laid], 1, 1, nlat
    return call(
        functools.partial(analyse_kernel, slot, low),
        "analyse",
        2 * width * nlat * rows * members,
        2 * width * nlat,
        out_shape=jax.ShapeDtypeStruct((rows, members, width), BF16),
        grid_spec=pltpu.PrefetchScalarGridSpec(
            num_scalar_prefetch=1,
            grid=(1,),
            in_specs=[IN_SMEM, ANYWHERE] + [IN_HBM] * (2 + len(blocks)),
            out_specs=pl.BlockSpec((rows, members, width), lambda i, m: (0, 0, 0)),
            scratch_shapes=[
                pltpu.VMEM((chips, cores, lats, rows * members), BF16),
                pltpu.VMEM((width, nlat), BF16),
                pltpu.VMEM((rows, members, width), BF16),
                pltpu.SemaphoreType.DMA((width // 256 + 1,)),
                pltpu.SemaphoreType.DMA,
                pltpu.SemaphoreType.DMA((CORES, rows)),
            ],
        ),
    )(me, wave, token, in_hbm(table), in_hbm(state), in_hbm(blocks[0]), *blocks[1:])


def sum_pairs_kernel(coeff_ref, token_ref, inverse_ref, out_ref):
    pairs, entries = inverse_ref.shape[:2]
    half = entries // 2

    def one(entry, carry):
        real = imag = 0.0
        for k in range(pairs):
            first, second = inverse_ref[k, entry].astype(F32), inverse_ref[k, half + entry].astype(F32)
            a, b = coeff_ref[k, 0], coeff_ref[k, 1]
            real = real + (a * first - b * second)
            imag = imag + (a * second + b * first)
        out_ref[entry] = real
        out_ref[half + entry] = imag
        return carry

    lax.fori_loop(0, half, one, 0)


def sum_pairs(block_inverses, pole_coeffs, token):
    return call(
        sum_pairs_kernel,
        "sum_pairs",
        4 * block_inverses.size,
        2 * block_inverses.size,
        out_shape=jax.ShapeDtypeStruct(block_inverses.shape[1:], F32),
        in_specs=[IN_SMEM, ANYWHERE, pl.BlockSpec(block_inverses.shape, lambda: (0, 0, 0, 0))],
        out_specs=pl.BlockSpec(block_inverses.shape[1:], lambda: (0, 0, 0)),
    )(pole_coeffs, token, block_inverses)


def synthesise_kernel(
    slot, low, apart, more, partial, me_ref, sign_ref, here_ref, there_ref, own_ref, other_ref, table_ref, *rest
):
    rows, members, _ = own_ref.shape
    step = pl.program_id(0)
    if partial:
        partial_ref, rest = rest[0], rest[1:]
    if more:
        sums_out, mixed = rest
    elif apart:
        outs, mate_out, mixed, held, sems = rest[:-4], rest[-4], rest[-3], rest[-2], rest[-1]
    else:
        own_out, mate_out, mixed = rest

    @pl.when(step == 0)
    def _():
        count = own_ref.shape[2]
        for n in range(0, count, 128):
            lanes = slice(low + n, low + n + 128)
            lines = [
                here_ref[entry, slot : slot + 1, lanes] + there_ref[entry, slot : slot + 1, lanes]
                for entry in range(2 * rows * rows)
            ]
            lines[rows * rows :] = [sign_ref[0] * line for line in lines[rows * rows :]]
            for e in range(0, members, 32):
                part = (slice(e, e + 32), slice(n, n + 128))
                owns = [own_ref[(g,) + part].astype(F32) for g in range(rows)]
                others = [other_ref[(g,) + part].astype(F32) for g in range(rows)]
                for f in range(rows):
                    total = 0.0
                    for g in range(rows):
                        total = total + lines[f * rows + g] * owns[g]
                        total = total + lines[rows * rows + f * rows + g] * others[g]
                    mixed[f * members + e : f * members + e + 32, n : n + 128] = total.astype(BF16)

    sums = jnp.dot(mixed[...], table_ref[0], preferred_element_type=F32)
    if partial:
        sums = sums + partial_ref[...]
    if more:
        sums_out[...] = sums
        return
    lats = mate_out.shape[2]
    each = mate_out.shape[0]
    for r in range(rows):
        turned = sums[r * members : (r + 1) * members, :].astype(BF16).T
        values = [turned[i : i + lats] for i in range(0, turned.shape[0], lats)]
        mine, others = split_cores(values, me_ref[0] % CORES)
        for i, (a, b) in enumerate(zip(mine, others)):
            if apart:
                held[step * each + i, r] = a
            else:
                own_out[i, 0, r] = a
            mate_out[i, r] = b

    if apart:
        chip, core = me_ref[0] // CORES, me_ref[0] % CORES
        copies = []
        for i, (k, row, some) in enumerate(messages_of(held.shape[0], rows)):
            source = held.at[chip ^ k, pl.ds(row, some)]
            copies.append(pltpu.make_async_copy(source, outs[i].at[core], sems.at[i]))
            pl.when((chip ^ k) // each == step)(copies[-1].start)

        @pl.when(step == pl.num_programs(0) - 1)
        def _():
            for copy in copies:
                copy.wait()


def synthesise(here, there, sign, own, other, table, me, slot, low, lats, apart, more, partial):
    rows, members, count = own.shape
    nlat = table.shape[2]
    width = math.lcm(CORES * lats, 128)
    chips, each = nlat // lats // CORES, width // lats // CORES
    matrix = pl.BlockSpec(here.shape, lambda j, m: (0, 0, 0))
    whole = pl.BlockSpec((rows, members, count), lambda j, m: (0, 0, 0))
    smem = pl.BlockSpec(memory_space=pltpu.SMEM)
    shapes = [jax.ShapeDtypeStruct((chips, CORES, rows, lats, members), BF16)]
    specs = [pl.BlockSpec((each, 1, rows, lats, members), lambda j, m: (j, m[0] % CORES, 0, 0, 0))]
    scratch = [pltpu.VMEM((rows * members, count), BF16)]
    shapes += [jax.ShapeDtypeStruct((chips, rows, lats, members), BF16)]
    specs += [pl.BlockSpec((each, rows, lats, members), lambda j, m: (j, 0, 0, 0))]
    sums = pl.BlockSpec((rows * members, width), lambda j, m: (0, j))
    if more:
        shapes, specs = [jax.ShapeDtypeStruct((rows * members, nlat), F32)], [sums]
    elif apart:
        counts = [some for _, _, some in messages_of(chips, rows)]
        shapes[:1] = [jax.ShapeDtypeStruct((CORES, some, lats, members), BF16) for some in counts]
        specs[:1] = [ANYWHERE] * len(counts)
        scratch += [pltpu.VMEM((chips, rows, lats, members), BF16), pltpu.SemaphoreType.DMA((len(counts),))]
    return call(
        functools.partial(synthesise_kernel, slot, low, apart, more, len(partial)),
        "synthesise",
        2 * count * nlat * rows * members,
        2 * count * nlat,
        out_shape=shapes,
        grid_spec=pltpu.PrefetchScalarGridSpec(
            num_scalar_prefetch=1,
            grid=(nlat // width,),
            in_specs=[
                smem,
                matrix,
                matrix,
                whole,
                whole,
                pl.BlockSpec((1, count, width), lambda j, m: (slot, low // count, j)),
            ]
            + [sums] * len(partial),
            out_specs=specs,
            scratch_shapes=scratch,
        ),
    )(me, sign, here, there, own, other, table, *partial)


def assemble_kernel(far, moved, wanted, me_ref, blocks_ref, *rest):
    messages, out_ref, (held, done, in_sems, out_sems) = rest[: len(wanted)], rest[-5], rest[-4:]
    rows, lats, slots, members = done.shape
    first = wanted[0][1]
    half = held.shape[0]
    local_slots = slots // half // CORES
    chip = me_ref[0] // CORES
    side = chip // half if not far else 1 - chip // half
    each = out_sems.shape[1]
    size = lats // each
    depth, breadth = math.gcd(size, 16), 16
    copies = []
    for r in range(rows):
        copies.append([])
        for i, ((k, _, _), ref) in enumerate(zip(wanted, messages)):
            target = held.at[(chip ^ k) & (half - 1), :, r]
            copies[r].append(pltpu.make_async_copy(ref.at[:, r], target, in_sems.at[r, i]))
            copies[r][-1].start()
    matrix = swap_matrix(breadth, depth, 1, 0)
    results = []

    def tile(r, start, s):
        parts = []
        for i in range(s, s + breadth):
            owner, slot = divmod(i, local_slots)
            place = owner // CORES
            if slot == moved:
                parts.append(held[place, owner % CORES, r, start : start + depth, :])
            else:
                parts.append(blocks_ref[side * half + place, owner % CORES, first + r, start : start + depth, :])
        return jnp.concatenate(parts, axis=0)

    for r in range(rows):
        for copy in copies[r]:
            copy.wait()
        for part in range(each):
            starts = range(part * size, (part + 1) * size, depth)
            tiles = [(start, s) for start in starts for s in range(0, slots, breadth)]
            for i in range(0, len(tiles), 2):
                both = tiles[i : i + 2]
                wide = jnp.concatenate([tile(r, *place) for place in both], axis=1)
                turned = jnp.dot(matrix, wide, preferred_element_type=F32).astype(BF16)
                for n, (start, s) in enumerate(both):
                    value = turned[:, n * members : (n + 1) * members].reshape(depth, breadth, members)
                    done[r, start : start + depth, s : s + breadth, :] = value
            lines = pl.ds(part * size, size)
            target = out_ref.at[first + r, lines, pl.ds(pl.multiple_of(side * slots, slots), slots)]
            results.append(pltpu.make_async_copy(done.at[r, lines], target, out_sems.at[r, part]))
            results[-1].start()
    for copy in results:
        copy.wait()


def assemble(blocks, messages, me, moved, local_slots, far, first, output):
    chips, _, rows, lats, members = blocks.shape
    half = chips // 2
    slots = local_slots * half * CORES
    parts = zip(messages_of(chips, rows), messages)
    parts = [(part, m) for part, m in parts if (part[0] >= half) == far and part[1] == first]
    wanted, used = [part for part, _ in parts], [m for _, m in parts]
    some = wanted[0][2]
    return call(
        functools.partial(assemble_kernel, far, moved, wanted),
        "assemble",
        2 * 256 * some * lats * slots * members,
        4 * some * lats * slots * members,
        out_shape=jax.ShapeDtypeStruct((rows, lats, 2 * slots, members), BF16),
        in_specs=[IN_SMEM, IN_VMEM] + [IN_HBM] * (len(used) + len(output)),
        out_specs=IN_HBM,
        scratch_shapes=[
            pltpu.VMEM((half, CORES, some, lats, members), BF16),
            pltpu.VMEM((some, lats, slots, members), BF16),
            pltpu.SemaphoreType.DMA((some, half)),
            pltpu.SemaphoreType.DMA((some, lats // lat_block(lats))),
        ],
        input_output_aliases={len(used) + 2: 0} if output else {},
    )(me, blocks, *used, *output)


def between_cores(blocks, owners):
    return lax.ppermute(blocks, "wave", [(d, d ^ 1) for d in range(owners)])


def by_permutes(messages, chips, rows):
    got = []
    for (k, _, _), message in zip(messages_of(chips, rows), messages):
        moves = [(d, d ^ (k * CORES)) for d in range(chips * CORES)]
        got.append(lax.ppermute(message, "wave", moves) if k else message)
    return got


def between_chips(blocks, owners):
    groups = [list(range(core, owners, CORES)) for core in range(CORES)]
    return lax.all_to_all(blocks, "wave", split_axis=0, concat_axis=0, axis_index_groups=groups, tiled=True)


def per_device(
    tendency, spectral_state, legendre, gauss_weights, block_inverses, pole_coeffs, wavenumbers
):
    rows, lats, slots, members = tendency.shape
    local_slots, nspec, nlat = legendre.shape
    owners = slots // local_slots
    me = lax.axis_index("wave").astype(jnp.int32).reshape(1)
    pole_index = lax.axis_index("pole")
    sign = (2 * pole_index - 1).astype(F32).reshape(1)
    order = list(range(local_slots))[::-1]
    received, waits = {}, []
    for slot in order:
        early = slot == order[0]
        *blocks, token = weigh(tendency, gauss_weights[None], me, slot, local_slots, not early, waits)
        if early:
            received[slot] = between_chips(blocks[0], owners)
            here = sum_pairs(block_inverses, pole_coeffs, token)
            there = lax.ppermute(here, "pole", [(0, 1), (1, 0)])
            waits = [there]
        else:
            blocks, token = pair(blocks[0], between_cores(blocks[1], owners), me)
            received[slot] = between_chips(blocks, owners)

    sent = {}
    for slot in order:
        half = nspec // 2
        lows = [half] if slot % 2 else [0, half]
        blocks = [received[slot]]
        if slot == order[0]:
            blocks.append(between_cores(pick(blocks[0], me, token), owners))
        forced = [analyse(blocks, legendre, spectral_state, wavenumbers, me, token, slot, low, half) for low in lows]
        others = [lax.ppermute(part, "pole", [(0, 1), (1, 0)]) for part in forced]
        last = slot == order[-1]
        own = []
        for low, part, other in zip(lows, forced, others):
            more = low != lows[-1]
            own = synthesise(here, there, sign, part, other, legendre, me, slot, low, lats, last, more, own)
        *own, for_mate = own
        mate = between_cores(for_mate, owners)
        if last:
            sent[slot] = by_permutes(pair_messages(own, mate, me), owners // CORES, rows)
        else:
            blocks, token = pair(own[0], mate, me)
            sent[slot] = [between_chips(blocks, owners)]
    blocks, messages = sent[order[0]][0], sent[order[-1]]
    output = []
    for far, first in ((False, 0), (True, 0), (True, rows - 1)):
        output = [assemble(blocks, messages, me, order[-1], local_slots, far, first, output)]
    return output[0]


def solution(mesh):
    in_specs = (
        P("pole", "wave", None, None),
        P("pole", "wave", None, None),
        P("wave", None, None),
        P("wave"),
        P("pole", None, "wave", None),
        P("pole", None),
        P("wave"),
    )
    out_specs = P("pole", "wave", None, None)
    return jax.shard_map(
        per_device, mesh=mesh, in_specs=in_specs, out_specs=out_specs, check_vma=False
    )
```

```python
import functools
import math

import jax
import jax.numpy as jnp
from jax import lax
from jax.experimental import pallas as pl
from jax.experimental.pallas import tpu as pltpu
from jax.sharding import PartitionSpec as P

BF16 = jnp.bfloat16
F32 = jnp.float32
CORES = 2
ANYWHERE = pl.BlockSpec(memory_space=pl.ANY)
IN_SMEM = pl.BlockSpec(memory_space=pltpu.SMEM)
IN_HBM = pl.BlockSpec(memory_space=pltpu.HBM)
IN_VMEM = pl.BlockSpec(memory_space=pltpu.VMEM)
TOKEN = jax.ShapeDtypeStruct((8, 128), F32)


def call(kernel, name, flops, size, mib=40, **kwargs):
    return pl.pallas_call(
        kernel,
        name=name,
        compiler_params=pltpu.CompilerParams(vmem_limit_bytes=mib * 1024 * 1024),
        cost_estimate=pl.CostEstimate(flops=int(flops), bytes_accessed=int(size), transcendentals=0),
        **kwargs,
    )


def in_hbm(array):
    return pltpu.with_memory_space_constraint(array, pltpu.HBM)


def run_copies(copies):
    for copy in copies:
        copy.start()
    for copy in copies:
        copy.wait()


def messages_of(chips, rows):
    near, far = range(1, chips // 2), range(chips // 2, chips)
    first = [(k, 0, rows - 1) for k in far]
    return [(0, 0, rows)] + first + [(k, rows - 1, 1) for k in far] + [(k, 0, rows) for k in near]


def split_cores(values, core):
    even = [values[i] for i in range(0, len(values), CORES)]
    odd = [values[i] for i in range(1, len(values), CORES)]
    mine = [jnp.where(core == 0, a, b) for a, b in zip(even, odd)]
    others = [jnp.where(core == 0, b, a) for a, b in zip(even, odd)]
    return mine, others


def swap_matrix(rows, columns, step, skip):
    shape = (rows * columns // step, rows * columns)
    shift = rows.bit_length() - 1
    target = lax.broadcasted_iota(jnp.int32, shape, 0)
    source = lax.broadcasted_iota(jnp.int32, shape, 1)
    wanted = (target & (rows - 1)) * columns + (target >> shift) * step + skip
    return jnp.where(source == wanted, 1.0, 0.0).astype(BF16)


def weigh_kernel(slot, local_slots, split, waits, me_ref, gauss_any, tendency_ref, *rest):
    outs, token_ref, (gauss_ref, column, held, done, gauss_sem, in_sems, out_sems) = rest[waits:-8], rest[-8], rest[-7:]
    line_copy = pltpu.make_async_copy(gauss_any, gauss_ref, gauss_sem)
    line_copy.start()
    rows, lats, slots, members = held.shape
    each = in_sems.shape[1]
    size = lats // each
    copies = []
    for r in range(rows):
        for i in range(each):
            part = pl.ds(i * size, size)
            copies.append(pltpu.make_async_copy(tendency_ref.at[r, part], held.at[r, part], in_sems.at[r, i]))
            copies[-1].start()
    token_ref[...] = jnp.zeros_like(token_ref)
    depth, breadth = math.gcd(size, 16), 16
    matrix = swap_matrix(depth, breadth, local_slots, slot)
    owners = breadth // local_slots
    core = me_ref[0] % CORES
    line_copy.wait()
    for j in range(0, lats, depth):
        line = jnp.broadcast_to(gauss_ref[...], (depth, lats))
        here = lax.broadcasted_iota(jnp.int32, line.shape, 0) + j
        mine = lax.broadcasted_iota(jnp.int32, line.shape, 1) == here
        value = jnp.sum(jnp.where(mine, line, 0.0), axis=1, keepdims=True)
        column[j : j + depth, :] = jnp.broadcast_to(value, (depth, members))
    results = []
    for r in range(rows):
        for j in range(0, lats, depth):
            if j % size == 0:
                copies[r * each + j // size].wait()
            scale = column[j : j + depth, :]
            for s in range(0, slots, 2 * breadth):
                halves = [
                    held[r, j : j + depth, s + h : s + h + breadth, :].reshape(depth * breadth, members)
                    for h in (0, breadth)
                ]
                turned = jnp.dot(matrix, jnp.concatenate(halves, axis=1), preferred_element_type=F32)
                values = [
                    turned[i * depth : (i + 1) * depth, h * members : (h + 1) * members] * scale
                    for h in range(2)
                    for i in range(owners)
                ]
                start = s // local_slots
                if split:
                    mine, others = split_cores(values, core)
                    for i, (a, b) in enumerate(zip(mine, others)):
                        done[start // CORES + i, 0, r, j : j + depth, :] = a.astype(BF16)
                        done[start // CORES + i, 1, r, j : j + depth, :] = b.astype(BF16)
                else:
                    for i, value in enumerate(values):
                        chip, target = divmod(start + i, CORES)
                        done[chip, target, r, j : j + depth, :] = value.astype(BF16)
            if (j + depth) % size == 0:
                part = pl.ds(j + depth - size, size)
                source, target = done.at[:, :, r, part], outs[0].at[:, :, r, part]
                if split:
                    source, target = done.at[:, 0, r, part], outs[0].at[:, core, r, part]
                    other = pltpu.make_async_copy(
                        done.at[:, 1, r, part], outs[1].at[:, r, part], out_sems.at[1, r, j // size]
                    )
                    other.start()
                    results.append(other)
                results.append(pltpu.make_async_copy(source, target, out_sems.at[0, r, j // size]))
                results[-1].start()
    for copy in results:
        copy.wait()


def weigh(tendency, gauss, me, slot, local_slots, split, waits):
    rows, lats, slots, members = tendency.shape
    each = 1
    chips = slots // local_slots // CORES
    shapes = [jax.ShapeDtypeStruct((chips, CORES, rows, lats, members), BF16)]
    if split:
        shapes += [jax.ShapeDtypeStruct((chips, rows, lats, members), BF16)]
    return call(
        functools.partial(weigh_kernel, slot, local_slots, split, len(waits)),
        "weigh",
        2 * 128 * tendency.size,
        3 * tendency.size,
        58,
        out_shape=shapes + [TOKEN],
        in_specs=[IN_SMEM] + [ANYWHERE] * (2 + len(waits)),
        out_specs=[ANYWHERE] * len(shapes) + [pl.BlockSpec(TOKEN.shape, lambda: (0, 0))],
        scratch_shapes=[
            pltpu.VMEM((1, lats), F32),
            pltpu.VMEM((lats, members), F32),
            pltpu.VMEM((rows, lats, slots, members), BF16),
            pltpu.VMEM((chips, CORES, rows, lats, members), BF16),
            pltpu.SemaphoreType.DMA,
            pltpu.SemaphoreType.DMA((rows, each)),
            pltpu.SemaphoreType.DMA((CORES, rows, each)),
        ],
    )(me, gauss, tendency, *waits)


def pick_kernel(me_ref, token_ref, in_ref, out_ref, held, in_sems, out_sems):
    other = CORES - 1 - me_ref[0] % CORES
    rows = held.shape[1]
    fetched = [pltpu.make_async_copy(in_ref.at[:, other, r], held.at[:, r], in_sems.at[r]) for r in range(rows)]
    stored = [pltpu.make_async_copy(held.at[:, r], out_ref.at[:, r], out_sems.at[r]) for r in range(rows)]
    for copy in fetched:
        copy.start()
    for fetch, store in zip(fetched, stored):
        fetch.wait()
        store.start()
    for copy in stored:
        copy.wait()


def pick(blocks, me, token):
    chips, _, rows, lats, members = blocks.shape
    shape = (chips, rows, lats, members)
    return call(
        pick_kernel,
        "pick",
        0,
        2 * blocks.size,
        out_shape=jax.ShapeDtypeStruct(shape, BF16),
        in_specs=[IN_SMEM, ANYWHERE, IN_HBM],
        out_specs=IN_HBM,
        scratch_shapes=[
            pltpu.VMEM(shape, BF16),
            pltpu.SemaphoreType.DMA((rows,)),
            pltpu.SemaphoreType.DMA((rows,)),
        ],
    )(me, token, in_hbm(blocks))


def pair_kernel(me_ref, mate_ref, blocks_ref, out_ref, token_ref, sem):
    token_ref[...] = jnp.zeros_like(token_ref)
    other = CORES - 1 - me_ref[0] % CORES
    run_copies([pltpu.make_async_copy(mate_ref, out_ref.at[:, other], sem)])


def pair(blocks, mate, me):
    return call(
        pair_kernel,
        "pair",
        0,
        4 * mate.size,
        out_shape=[jax.ShapeDtypeStruct(blocks.shape, blocks.dtype), TOKEN],
        in_specs=[IN_SMEM, pl.BlockSpec(mate.shape, lambda: (0, 0, 0, 0)), ANYWHERE],
        out_specs=[ANYWHERE, pl.BlockSpec(TOKEN.shape, lambda: (0, 0))],
        scratch_shapes=[pltpu.SemaphoreType.DMA],
        input_output_aliases={2: 0},
    )(me, mate, blocks)


def pair_messages_kernel(me_ref, mate_ref, *rest):
    outs, sems = rest[len(rest) // 2 : -1], rest[-1]
    chip, other = me_ref[0] // CORES, CORES - 1 - me_ref[0] % CORES
    copies = []
    for i, (k, row, rows) in enumerate(messages_of(*mate_ref.shape[:2])):
        source = mate_ref.at[chip ^ k, pl.ds(row, rows)]
        copies.append(pltpu.make_async_copy(source, outs[i].at[other], sems.at[i]))
    run_copies(copies)


def pair_messages(messages, mate, me):
    count = len(messages)
    return call(
        pair_messages_kernel,
        "pair",
        0,
        4 * mate.size,
        out_shape=[jax.ShapeDtypeStruct(m.shape, m.dtype) for m in messages],
        in_specs=[IN_SMEM, pl.BlockSpec(mate.shape, lambda: (0, 0, 0, 0))] + [ANYWHERE] * count,
        out_specs=[ANYWHERE] * count,
        scratch_shapes=[pltpu.SemaphoreType.DMA((count,))],
        input_output_aliases={i + 2: i for i in range(count)},
    )(me, mate, *messages)


def analyse_kernel(slot, low, me_ref, wave_ref, token_ref, table_ref, state_ref, *rest):
    blocks, out, (grid, table, state, table_sems, state_sem, block_sems) = rest[:-7], rest[-7], rest[-6:]
    rows, members, width = out.shape
    chips, cores, lats, _ = grid.shape
    core = me_ref[0] % CORES
    moves = []
    for r in range(rows):
        lanes = pl.ds(r * members, members)
        if len(blocks) == 1:
            moves.append(pltpu.make_async_copy(blocks[0].at[:, :, r], grid.at[:, :, :, lanes], block_sems.at[0, r]))
        else:
            target = grid.at[:, core, :, lanes]
            moves.append(pltpu.make_async_copy(blocks[0].at[:, core, r], target, block_sems.at[0, r]))
            target = grid.at[:, CORES - 1 - core, :, lanes]
            moves.append(pltpu.make_async_copy(blocks[1].at[:, r], target, block_sems.at[1, r]))
    cuts = sorted(set([0] + list(range(width % 256, width + 1, 256))))
    copies = []
    for i, (start, end) in enumerate(zip(cuts, cuts[1:])):
        source = table_ref.at[slot, pl.ds(low + start, end - start)]
        copies.append(pltpu.make_async_copy(source, table.at[pl.ds(start, end - start)], table_sems.at[i]))
    state_copy = pltpu.make_async_copy(state_ref.at[:, slot, :, pl.ds(low, width)], state, state_sem)
    for move in moves + copies + [state_copy]:
        move.start()
    for move in moves:
        move.wait()
    field = grid[...].reshape(chips * cores * lats, rows * members)
    state_copy.wait()
    for copy, start, end in zip(copies, cuts, cuts[1:]):
        copy.wait()
        sums = jnp.dot(table[start:end], field, preferred_element_type=F32)
        degree = lax.broadcasted_iota(jnp.int32, (members, end - start), 1) + (low + start)
        live = degree >= wave_ref[slot]
        for r in range(rows):
            total = state[r, :, start:end].astype(F32) + sums[:, r * members : (r + 1) * members].T
            out[r, :, start:end] = jnp.where(live, total, 0.0).astype(BF16)


def analyse(blocks, table, state, wave, me, token, slot, low, width):
    chips, _, rows, lats, members = blocks[0].shape
    nlat = table.shape[2]
    cores = CORES
    if lats % 16:
        if len(blocks) > 1:
            core = me[0] % CORES
            own = lax.dynamic_index_in_dim(blocks[0], core, 1, keepdims=False)
            pairs = [jnp.where(core == 0, own, blocks[1]), jnp.where(core == 0, blocks[1], own)]
            blocks = [jnp.stack(pairs, axis=1)]
        laid = jnp.transpose(blocks[0], (2, 0, 1, 3, 4)).reshape(1, 1, rows, nlat, members)
        blocks, chips, cores, lats = [laid], 1, 1, nlat
    return call(
        functools.partial(analyse_kernel, slot, low),
        "analyse",
        2 * width * nlat * rows * members,
        2 * width * nlat,
        out_shape=jax.ShapeDtypeStruct((rows, members, width), BF16),
        grid_spec=pltpu.PrefetchScalarGridSpec(
            num_scalar_prefetch=1,
            grid=(1,),
            in_specs=[IN_SMEM, ANYWHERE] + [IN_HBM] * (2 + len(blocks)),
            out_specs=pl.BlockSpec((rows, members, width), lambda i, m: (0, 0, 0)),
            scratch_shapes=[
                pltpu.VMEM((chips, cores, lats, rows * members), BF16),
                pltpu.VMEM((width, nlat), BF16),
                pltpu.VMEM((rows, members, width), BF16),
                pltpu.SemaphoreType.DMA((width // 256 + 1,)),
                pltpu.SemaphoreType.DMA,
                pltpu.SemaphoreType.DMA((CORES, rows)),
            ],
        ),
    )(me, wave, token, in_hbm(table), in_hbm(state), in_hbm(blocks[0]), *blocks[1:])


def sum_pairs_kernel(coeff_ref, token_ref, inverse_ref, out_ref):
    pairs, entries = inverse_ref.shape[:2]
    half = entries // 2

    def one(entry, carry):
        real = imag = 0.0
        for k in range(pairs):
            first, second = inverse_ref[k, entry].astype(F32), inverse_ref[k, half + entry].astype(F32)
            a, b = coeff_ref[k, 0], coeff_ref[k, 1]
            real = real + (a * first - b * second)
            imag = imag + (a * second + b * first)
        out_ref[entry] = real
        out_ref[half + entry] = imag
        return carry

    lax.fori_loop(0, half, one, 0)


def sum_pairs(block_inverses, pole_coeffs, token):
    return call(
        sum_pairs_kernel,
        "sum_pairs",
        4 * block_inverses.size,
        2 * block_inverses.size,
        out_shape=jax.ShapeDtypeStruct(block_inverses.shape[1:], F32),
        in_specs=[IN_SMEM, ANYWHERE, pl.BlockSpec(block_inverses.shape, lambda: (0, 0, 0, 0))],
        out_specs=pl.BlockSpec(block_inverses.shape[1:], lambda: (0, 0, 0)),
    )(pole_coeffs, token, block_inverses)


def synthesise_kernel(
    slot, low, apart, more, partial, me_ref, sign_ref, here_ref, there_ref, own_ref, other_ref, table_ref, *rest
):
    rows, members, _ = own_ref.shape
    step = pl.program_id(0)
    if partial:
        partial_ref, rest = rest[0], rest[1:]
    if more:
        sums_out, mixed = rest
    elif apart:
        outs, mate_out, mixed, held, sems = rest[:-4], rest[-4], rest[-3], rest[-2], rest[-1]
    else:
        own_out, mate_out, mixed = rest

    @pl.when(step == 0)
    def _():
        count = own_ref.shape[2]
        for n in range(0, count, 128):
            lanes = slice(low + n, low + n + 128)
            lines = [
                here_ref[entry, slot : slot + 1, lanes] + there_ref[entry, slot : slot + 1, lanes]
                for entry in range(2 * rows * rows)
            ]
            lines[rows * rows :] = [sign_ref[0] * line for line in lines[rows * rows :]]
            for e in range(0, members, 32):
                part = (slice(e, e + 32), slice(n, n + 128))
                owns = [own_ref[(g,) + part].astype(F32) for g in range(rows)]
                others = [other_ref[(g,) + part].astype(F32) for g in range(rows)]
                for f in range(rows):
                    total = 0.0
                    for g in range(rows):
                        total = total + lines[f * rows + g] * owns[g]
                        total = total + lines[rows * rows + f * rows + g] * others[g]
                    mixed[f * members + e : f * members + e + 32, n : n + 128] = total.astype(BF16)

    sums = jnp.dot(mixed[...], table_ref[0], preferred_element_type=F32)
    if partial:
        sums = sums + partial_ref[...]
    if more:
        sums_out[...] = sums
        return
    lats = mate_out.shape[2]
    each = mate_out.shape[0]
    for r in range(rows):
        turned = sums[r * members : (r + 1) * members, :].astype(BF16).T
        values = [turned[i : i + lats] for i in range(0, turned.shape[0], lats)]
        mine, others = split_cores(values, me_ref[0] % CORES)
        for i, (a, b) in enumerate(zip(mine, others)):
            if apart:
                held[step * each + i, r] = a
            else:
                own_out[i, 0, r] = a
            mate_out[i, r] = b

    if apart:
        chip, core = me_ref[0] // CORES, me_ref[0] % CORES
        copies = []
        for i, (k, row, some) in enumerate(messages_of(held.shape[0], rows)):
            source = held.at[chip ^ k, pl.ds(row, some)]
            copies.append(pltpu.make_async_copy(source, outs[i].at[core], sems.at[i]))
            pl.when((chip ^ k) // each == step)(copies[-1].start)

        @pl.when(step == pl.num_programs(0) - 1)
        def _():
            for copy in copies:
                copy.wait()


def synthesise(here, there, sign, own, other, table, me, slot, low, lats, apart, more, partial):
    rows, members, count = own.shape
    nlat = table.shape[2]
    width = math.lcm(CORES * lats, 128)
    chips, each = nlat // lats // CORES, width // lats // CORES
    matrix = pl.BlockSpec(here.shape, lambda j, m: (0, 0, 0))
    whole = pl.BlockSpec((rows, members, count), lambda j, m: (0, 0, 0))
    smem = pl.BlockSpec(memory_space=pltpu.SMEM)
    shapes = [jax.ShapeDtypeStruct((chips, CORES, rows, lats, members), BF16)]
    specs = [pl.BlockSpec((each, 1, rows, lats, members), lambda j, m: (j, m[0] % CORES, 0, 0, 0))]
    scratch = [pltpu.VMEM((rows * members, count), BF16)]
    shapes += [jax.ShapeDtypeStruct((chips, rows, lats, members), BF16)]
    specs += [pl.BlockSpec((each, rows, lats, members), lambda j, m: (j, 0, 0, 0))]
    sums = pl.BlockSpec((rows * members, width), lambda j, m: (0, j))
    if more:
        shapes, specs = [jax.ShapeDtypeStruct((rows * members, nlat), F32)], [sums]
    elif apart:
        counts = [some for _, _, some in messages_of(chips, rows)]
        shapes[:1] = [jax.ShapeDtypeStruct((CORES, some, lats, members), BF16) for some in counts]
        specs[:1] = [ANYWHERE] * len(counts)
        scratch += [pltpu.VMEM((chips, rows, lats, members), BF16), pltpu.SemaphoreType.DMA((len(counts),))]
    return call(
        functools.partial(synthesise_kernel, slot, low, apart, more, len(partial)),
        "synthesise",
        2 * count * nlat * rows * members,
        2 * count * nlat,
        out_shape=shapes,
        grid_spec=pltpu.PrefetchScalarGridSpec(
            num_scalar_prefetch=1,
            grid=(nlat // width,),
            in_specs=[
                smem,
                matrix,
                matrix,
                whole,
                whole,
                pl.BlockSpec((1, count, width), lambda j, m: (slot, low // count, j)),
            ]
            + [sums] * len(partial),
            out_specs=specs,
            scratch_shapes=scratch,
        ),
    )(me, sign, here, there, own, other, table, *partial)


def assemble_kernel(far, moved, wanted, me_ref, blocks_ref, *rest):
    messages, out_ref, (held, done, in_sems, out_sems) = rest[: len(wanted)], rest[-5], rest[-4:]
    rows, lats, slots, members = done.shape
    first = wanted[0][1]
    half = held.shape[0]
    local_slots = slots // half // CORES
    chip = me_ref[0] // CORES
    side = chip // half if not far else 1 - chip // half
    each = out_sems.shape[1]
    size = lats // each
    depth, breadth = math.gcd(size, 16), 16
    copies = []
    for r in range(rows):
        copies.append([])
        for i, ((k, _, _), ref) in enumerate(zip(wanted, messages)):
            target = held.at[(chip ^ k) & (half - 1), :, r]
            copies[r].append(pltpu.make_async_copy(ref.at[:, r], target, in_sems.at[r, i]))
            copies[r][-1].start()
    matrix = swap_matrix(breadth, depth, 1, 0)
    results = []

    def tile(r, start, s):
        parts = []
        for i in range(s, s + breadth):
            owner, slot = divmod(i, local_slots)
            place = owner // CORES
            if slot == moved:
                parts.append(held[place, owner % CORES, r, start : start + depth, :])
            else:
                parts.append(blocks_ref[side * half + place, owner % CORES, first + r, start : start + depth, :])
        return jnp.concatenate(parts, axis=0)

    for r in range(rows):
        for copy in copies[r]:
            copy.wait()
        for part in range(each):
            starts = range(part * size, (part + 1) * size, depth)
            tiles = [(start, s) for start in starts for s in range(0, slots, breadth)]
            for i in range(0, len(tiles), 2):
                both = tiles[i : i + 2]
                wide = jnp.concatenate([tile(r, *place) for place in both], axis=1)
                turned = jnp.dot(matrix, wide, preferred_element_type=F32).astype(BF16)
                for n, (start, s) in enumerate(both):
                    value = turned[:, n * members : (n + 1) * members].reshape(depth, breadth, members)
                    done[r, start : start + depth, s : s + breadth, :] = value
            lines = pl.ds(part * size, size)
            target = out_ref.at[first + r, lines, pl.ds(pl.multiple_of(side * slots, slots), slots)]
            results.append(pltpu.make_async_copy(done.at[r, lines], target, out_sems.at[r, part]))
            results[-1].start()
    for copy in results:
        copy.wait()


def assemble(blocks, messages, me, moved, local_slots, far, first, output):
    chips, _, rows, lats, members = blocks.shape
    half = chips // 2
    slots = local_slots * half * CORES
    parts = zip(messages_of(chips, rows), messages)
    parts = [(part, m) for part, m in parts if (part[0] >= half) == far and part[1] == first]
    wanted, used = [part for part, _ in parts], [m for _, m in parts]
    some = wanted[0][2]
    return call(
        functools.partial(assemble_kernel, far, moved, wanted),
        "assemble",
        2 * 256 * some * lats * slots * members,
        4 * some * lats * slots * members,
        out_shape=jax.ShapeDtypeStruct((rows, lats, 2 * slots, members), BF16),
        in_specs=[IN_SMEM, IN_VMEM] + [IN_HBM] * (len(used) + len(output)),
        out_specs=IN_HBM,
        scratch_shapes=[
            pltpu.VMEM((half, CORES, some, lats, members), BF16),
            pltpu.VMEM((some, lats, slots, members), BF16),
            pltpu.SemaphoreType.DMA((some, half)),
            pltpu.SemaphoreType.DMA((some, 1)),
        ],
        input_output_aliases={len(used) + 2: 0} if output else {},
    )(me, blocks, *used, *output)


def between_cores(blocks, owners):
    return lax.ppermute(blocks, "wave", [(d, d ^ 1) for d in range(owners)])


def by_permutes(messages, chips, rows):
    got = []
    for (k, _, _), message in zip(messages_of(chips, rows), messages):
        moves = [(d, d ^ (k * CORES)) for d in range(chips * CORES)]
        got.append(lax.ppermute(message, "wave", moves) if k else message)
    return got


def between_chips(blocks, owners):
    groups = [list(range(core, owners, CORES)) for core in range(CORES)]
    return lax.all_to_all(blocks, "wave", split_axis=0, concat_axis=0, axis_index_groups=groups, tiled=True)


def per_device(
    tendency, spectral_state, legendre, gauss_weights, block_inverses, pole_coeffs, wavenumbers
):
    rows, lats, slots, members = tendency.shape
    local_slots, nspec, nlat = legendre.shape
    owners = slots // local_slots
    me = lax.axis_index("wave").astype(jnp.int32).reshape(1)
    pole_index = lax.axis_index("pole")
    sign = (2 * pole_index - 1).astype(F32).reshape(1)
    order = list(range(local_slots))[::-1]
    received, waits = {}, []
    for slot in order:
        early = slot == order[0]
        *blocks, token = weigh(tendency, gauss_weights[None], me, slot, local_slots, not early, waits)
        if early:
            received[slot] = between_chips(blocks[0], owners)
            here = sum_pairs(block_inverses, pole_coeffs, token)
            there = lax.ppermute(here, "pole", [(0, 1), (1, 0)])
            waits = [there]
        else:
            blocks, token = pair(blocks[0], between_cores(blocks[1], owners), me)
            received[slot] = between_chips(blocks, owners)

    sent = {}
    for slot in order:
        half = nspec // 2
        lows = [half] if slot % 2 else [0, half]
        blocks = [received[slot]]
        if slot == order[0]:
            blocks.append(between_cores(pick(blocks[0], me, token), owners))
        forced = [analyse(blocks, legendre, spectral_state, wavenumbers, me, token, slot, low, half) for low in lows]
        others = [lax.ppermute(part, "pole", [(0, 1), (1, 0)]) for part in forced]
        last = slot == order[-1]
        own = []
        for low, part, other in zip(lows, forced, others):
            more = low != lows[-1]
            own = synthesise(here, there, sign, part, other, legendre, me, slot, low, lats, last, more, own)
        *own, for_mate = own
        mate = between_cores(for_mate, owners)
        if last:
            sent[slot] = by_permutes(pair_messages(own, mate, me), owners // CORES, rows)
        else:
            blocks, token = pair(own[0], mate, me)
            sent[slot] = [between_chips(blocks, owners)]
    blocks, messages = sent[order[0]][0], sent[order[-1]]
    output = []
    for far, first in ((False, 0), (True, 0), (True, rows - 1)):
        output = [assemble(blocks, messages, me, order[-1], local_slots, far, first, output)]
    return output[0]


def solution(mesh):
    in_specs = (
        P("pole", "wave", None, None),
        P("pole", "wave", None, None),
        P("wave", None, None),
        P("wave"),
        P("pole", None, "wave", None),
        P("pole", None),
        P("wave"),
    )
    out_specs = P("pole", "wave", None, None)
    return jax.shard_map(
        per_device, mesh=mesh, in_specs=in_specs, out_specs=out_specs, check_vma=False
    )
```

```python
import functools
import math

import jax
import jax.numpy as jnp
from jax import lax
from jax.experimental import pallas as pl
from jax.experimental.pallas import tpu as pltpu
from jax.sharding import PartitionSpec as P

BF16 = jnp.bfloat16
F32 = jnp.float32
CORES = 2
PLANES = (0, 2, 1, 3)
ANYWHERE = pl.BlockSpec(memory_space=pl.ANY)
IN_SMEM = pl.BlockSpec(memory_space=pltpu.SMEM)
IN_HBM = pl.BlockSpec(memory_space=pltpu.HBM)
IN_VMEM = pl.BlockSpec(memory_space=pltpu.VMEM)
TOKEN = jax.ShapeDtypeStruct((8, 128), F32)


def call(kernel, name, flops, size, mib=40, **kwargs):
    return pl.pallas_call(
        kernel,
        name=name,
        compiler_params=pltpu.CompilerParams(vmem_limit_bytes=mib * 1024 * 1024),
        cost_estimate=pl.CostEstimate(flops=int(flops), bytes_accessed=int(size), transcendentals=0),
        **kwargs,
    )


def in_hbm(array):
    return pltpu.with_memory_space_constraint(array, pltpu.HBM)


def run_copies(copies):
    for copy in copies:
        copy.start()
    for copy in copies:
        copy.wait()


def place_of(chip, chips):
    quarter = chips // len(PLANES)
    return PLANES[chip // quarter] * quarter + chip % quarter


def messages_of(chips, rows):
    near, far = range(1, chips // 2), range(chips // 2, chips)
    first = [(k, 0, rows - 1) for k in far]
    return [(0, 0, rows)] + first + [(k, rows - 1, 1) for k in far] + [(k, 0, rows) for k in near]


def split_cores(values, core):
    even = [values[i] for i in range(0, len(values), CORES)]
    odd = [values[i] for i in range(1, len(values), CORES)]
    mine = [jnp.where(core == 0, a, b) for a, b in zip(even, odd)]
    others = [jnp.where(core == 0, b, a) for a, b in zip(even, odd)]
    return mine, others


def swap_matrix(rows, columns, step, skip):
    shape = (rows * columns // step, rows * columns)
    shift = rows.bit_length() - 1
    target = lax.broadcasted_iota(jnp.int32, shape, 0)
    source = lax.broadcasted_iota(jnp.int32, shape, 1)
    wanted = (target & (rows - 1)) * columns + (target >> shift) * step + skip
    return jnp.where(source == wanted, 1.0, 0.0).astype(BF16)


def weigh_kernel(slot, local_slots, split, waits, me_ref, gauss_any, tendency_ref, *rest):
    outs, token_ref, (gauss_ref, column, held, done, gauss_sem, in_sems, out_sems) = rest[waits:-8], rest[-8], rest[-7:]
    line_copy = pltpu.make_async_copy(gauss_any, gauss_ref, gauss_sem)
    line_copy.start()
    rows, lats, slots, members = held.shape
    each = in_sems.shape[1]
    size = lats // each
    copies = []
    for r in range(rows):
        for i in range(each):
            part = pl.ds(i * size, size)
            copies.append(pltpu.make_async_copy(tendency_ref.at[r, part], held.at[r, part], in_sems.at[r, i]))
            copies[-1].start()
    token_ref[...] = jnp.zeros_like(token_ref)
    depth, breadth = math.gcd(size, 16), 16
    matrix = swap_matrix(depth, breadth, local_slots, slot)
    owners = breadth // local_slots
    core = me_ref[0] % CORES
    line_copy.wait()
    for j in range(0, lats, depth):
        line = jnp.broadcast_to(gauss_ref[...], (depth, lats))
        here = lax.broadcasted_iota(jnp.int32, line.shape, 0) + j
        mine = lax.broadcasted_iota(jnp.int32, line.shape, 1) == here
        value = jnp.sum(jnp.where(mine, line, 0.0), axis=1, keepdims=True)
        column[j : j + depth, :] = jnp.broadcast_to(value, (depth, members))
    results = []
    for r in range(rows):
        for j in range(0, lats, depth):
            if j % size == 0:
                copies[r * each + j // size].wait()
            scale = column[j : j + depth, :]
            for s in range(0, slots, 2 * breadth):
                halves = [
                    held[r, j : j + depth, s + h : s + h + breadth, :].reshape(depth * breadth, members)
                    for h in (0, breadth)
                ]
                turned = jnp.dot(matrix, jnp.concatenate(halves, axis=1), preferred_element_type=F32)
                values = [
                    turned[i * depth : (i + 1) * depth, h * members : (h + 1) * members] * scale
                    for h in range(2)
                    for i in range(owners)
                ]
                start = s // local_slots
                if split:
                    mine, others = split_cores(values, core)
                    for i, (a, b) in enumerate(zip(mine, others)):
                        place = place_of(start // CORES + i, done.shape[0])
                        done[place, 0, r, j : j + depth, :] = a.astype(BF16)
                        done[place, 1, r, j : j + depth, :] = b.astype(BF16)
                else:
                    for i, value in enumerate(values):
                        chip, target = divmod(start + i, CORES)
                        done[place_of(chip, done.shape[0]), target, r, j : j + depth, :] = value.astype(BF16)
            if (j + depth) % size == 0:
                part = pl.ds(j + depth - size, size)
                source, target = done.at[:, :, r, part], outs[0].at[:, :, r, part]
                if split:
                    source, target = done.at[:, 0, r, part], outs[0].at[:, core, r, part]
                    other = pltpu.make_async_copy(
                        done.at[:, 1, r, part], outs[1].at[:, r, part], out_sems.at[1, r, j // size]
                    )
                    other.start()
                    results.append(other)
                results.append(pltpu.make_async_copy(source, target, out_sems.at[0, r, j // size]))
                results[-1].start()
    for copy in results:
        copy.wait()


def weigh(tendency, gauss, me, slot, local_slots, split, waits):
    rows, lats, slots, members = tendency.shape
    each = 1
    chips = slots // local_slots // CORES
    shapes = [jax.ShapeDtypeStruct((chips, CORES, rows, lats, members), BF16)]
    if split:
        shapes += [jax.ShapeDtypeStruct((chips, rows, lats, members), BF16)]
    return call(
        functools.partial(weigh_kernel, slot, local_slots, split, len(waits)),
        "weigh",
        2 * 128 * tendency.size,
        3 * tendency.size,
        58,
        out_shape=shapes + [TOKEN],
        in_specs=[IN_SMEM] + [ANYWHERE] * (2 + len(waits)),
        out_specs=[ANYWHERE] * len(shapes) + [pl.BlockSpec(TOKEN.shape, lambda: (0, 0))],
        scratch_shapes=[
            pltpu.VMEM((1, lats), F32),
            pltpu.VMEM((lats, members), F32),
            pltpu.VMEM((rows, lats, slots, members), BF16),
            pltpu.VMEM((chips, CORES, rows, lats, members), BF16),
            pltpu.SemaphoreType.DMA,
            pltpu.SemaphoreType.DMA((rows, each)),
            pltpu.SemaphoreType.DMA((CORES, rows, each)),
        ],
    )(me, gauss, tendency, *waits)


def pick_kernel(me_ref, token_ref, in_ref, out_ref, held, in_sems, out_sems):
    other = CORES - 1 - me_ref[0] % CORES
    rows = held.shape[1]
    fetched = [pltpu.make_async_copy(in_ref.at[:, other, r], held.at[:, r], in_sems.at[r]) for r in range(rows)]
    stored = [pltpu.make_async_copy(held.at[:, r], out_ref.at[:, r], out_sems.at[r]) for r in range(rows)]
    for copy in fetched:
        copy.start()
    for fetch, store in zip(fetched, stored):
        fetch.wait()
        store.start()
    for copy in stored:
        copy.wait()


def pick(blocks, me, token):
    chips, _, rows, lats, members = blocks.shape
    shape = (chips, rows, lats, members)
    return call(
        pick_kernel,
        "pick",
        0,
        2 * blocks.size,
        out_shape=jax.ShapeDtypeStruct(shape, BF16),
        in_specs=[IN_SMEM, ANYWHERE, IN_HBM],
        out_specs=IN_HBM,
        scratch_shapes=[
            pltpu.VMEM(shape, BF16),
            pltpu.SemaphoreType.DMA((rows,)),
            pltpu.SemaphoreType.DMA((rows,)),
        ],
    )(me, token, in_hbm(blocks))


def pair_kernel(me_ref, mate_ref, blocks_ref, out_ref, token_ref, sem):
    token_ref[...] = jnp.zeros_like(token_ref)
    other = CORES - 1 - me_ref[0] % CORES
    run_copies([pltpu.make_async_copy(mate_ref, out_ref.at[:, other], sem)])


def pair(blocks, mate, me):
    return call(
        pair_kernel,
        "pair",
        0,
        4 * mate.size,
        out_shape=[jax.ShapeDtypeStruct(blocks.shape, blocks.dtype), TOKEN],
        in_specs=[IN_SMEM, pl.BlockSpec(mate.shape, lambda: (0, 0, 0, 0)), ANYWHERE],
        out_specs=[ANYWHERE, pl.BlockSpec(TOKEN.shape, lambda: (0, 0))],
        scratch_shapes=[pltpu.SemaphoreType.DMA],
        input_output_aliases={2: 0},
    )(me, mate, blocks)


def pair_messages_kernel(me_ref, mate_ref, *rest):
    outs, sems = rest[len(rest) // 2 : -1], rest[-1]
    chip, other = me_ref[0] // CORES, CORES - 1 - me_ref[0] % CORES
    copies = []
    for i, (k, row, rows) in enumerate(messages_of(*mate_ref.shape[:2])):
        source = mate_ref.at[chip ^ k, pl.ds(row, rows)]
        copies.append(pltpu.make_async_copy(source, outs[i].at[other], sems.at[i]))
    run_copies(copies)


def pair_messages(messages, mate, me):
    count = len(messages)
    return call(
        pair_messages_kernel,
        "pair",
        0,
        4 * mate.size,
        out_shape=[jax.ShapeDtypeStruct(m.shape, m.dtype) for m in messages],
        in_specs=[IN_SMEM, pl.BlockSpec(mate.shape, lambda: (0, 0, 0, 0))] + [ANYWHERE] * count,
        out_specs=[ANYWHERE] * count,
        scratch_shapes=[pltpu.SemaphoreType.DMA((count,))],
        input_output_aliases={i + 2: i for i in range(count)},
    )(me, mate, *messages)


def analyse_kernel(slot, low, me_ref, wave_ref, token_ref, table_ref, state_ref, *rest):
    blocks, out, (grid, table, state, table_sems, state_sem, block_sems) = rest[:-7], rest[-7], rest[-6:]
    rows, members, width = out.shape
    chips, cores, lats, _ = grid.shape
    core = me_ref[0] % CORES
    moves = []
    quarter = max(chips // len(PLANES), 1)
    for q in range(chips // quarter):
        here, there = pl.ds(q * quarter, quarter), pl.ds(place_of(q * quarter, chips) if chips > 1 else 0, quarter)
        for r in range(rows):
            lanes = pl.ds(r * members, members)
            if len(blocks) == 1:
                source, target = blocks[0].at[there, :, r], grid.at[here, :, :, lanes]
                moves.append(pltpu.make_async_copy(source, target, block_sems.at[0, r, q]))
            else:
                source, target = blocks[0].at[there, core, r], grid.at[here, core, :, lanes]
                moves.append(pltpu.make_async_copy(source, target, block_sems.at[0, r, q]))
                source, target = blocks[1].at[there, r], grid.at[here, CORES - 1 - core, :, lanes]
                moves.append(pltpu.make_async_copy(source, target, block_sems.at[1, r, q]))
    cuts = sorted(set([0] + list(range(width % 256, width + 1, 256))))
    copies = []
    for i, (start, end) in enumerate(zip(cuts, cuts[1:])):
        source = table_ref.at[slot, pl.ds(low + start, end - start)]
        copies.append(pltpu.make_async_copy(source, table.at[pl.ds(start, end - start)], table_sems.at[i]))
    state_copy = pltpu.make_async_copy(state_ref.at[:, slot, :, pl.ds(low, width)], state, state_sem)
    for move in moves + copies + [state_copy]:
        move.start()
    for move in moves:
        move.wait()
    field = grid[...].reshape(chips * cores * lats, rows * members)
    state_copy.wait()
    for copy, start, end in zip(copies, cuts, cuts[1:]):
        copy.wait()
        sums = jnp.dot(table[start:end], field, preferred_element_type=F32)
        degree = lax.broadcasted_iota(jnp.int32, (members, end - start), 1) + (low + start)
        live = degree >= wave_ref[slot]
        for r in range(rows):
            total = state[r, :, start:end].astype(F32) + sums[:, r * members : (r + 1) * members].T
            out[r, :, start:end] = jnp.where(live, total, 0.0).astype(BF16)


def analyse(blocks, table, state, wave, me, token, slot, low, width):
    chips, _, rows, lats, members = blocks[0].shape
    nlat = table.shape[2]
    cores = CORES
    if lats % 16:
        if len(blocks) > 1:
            core = me[0] % CORES
            own = lax.dynamic_index_in_dim(blocks[0], core, 1, keepdims=False)
            pairs = [jnp.where(core == 0, own, blocks[1]), jnp.where(core == 0, blocks[1], own)]
            blocks = [jnp.stack(pairs, axis=1)]
        quarter = chips // len(PLANES)
        laid = jnp.concatenate([blocks[0][q * quarter : (q + 1) * quarter] for q in PLANES])
        laid = jnp.transpose(laid, (2, 0, 1, 3, 4)).reshape(1, 1, rows, nlat, members)
        blocks, chips, cores, lats = [laid], 1, 1, nlat
    return call(
        functools.partial(analyse_kernel, slot, low),
        "analyse",
        2 * width * nlat * rows * members,
        2 * width * nlat,
        out_shape=jax.ShapeDtypeStruct((rows, members, width), BF16),
        grid_spec=pltpu.PrefetchScalarGridSpec(
            num_scalar_prefetch=1,
            grid=(1,),
            in_specs=[IN_SMEM, ANYWHERE] + [IN_HBM] * (2 + len(blocks)),
            out_specs=pl.BlockSpec((rows, members, width), lambda i, m: (0, 0, 0)),
            scratch_shapes=[
                pltpu.VMEM((chips, cores, lats, rows * members), BF16),
                pltpu.VMEM((width, nlat), BF16),
                pltpu.VMEM((rows, members, width), BF16),
                pltpu.SemaphoreType.DMA((width // 256 + 1,)),
                pltpu.SemaphoreType.DMA,
                pltpu.SemaphoreType.DMA((CORES, rows, len(PLANES))),
            ],
        ),
    )(me, wave, token, in_hbm(table), in_hbm(state), in_hbm(blocks[0]), *blocks[1:])


def sum_pairs_kernel(coeff_ref, token_ref, inverse_ref, out_ref):
    pairs, entries = inverse_ref.shape[:2]
    half = entries // 2

    def one(entry, carry):
        real = imag = 0.0
        for k in range(pairs):
            first, second = inverse_ref[k, entry].astype(F32), inverse_ref[k, half + entry].astype(F32)
            a, b = coeff_ref[k, 0], coeff_ref[k, 1]
            real = real + (a * first - b * second)
            imag = imag + (a * second + b * first)
        out_ref[entry] = real
        out_ref[half + entry] = imag
        return carry

    lax.fori_loop(0, half, one, 0)


def sum_pairs(block_inverses, pole_coeffs, token):
    return call(
        sum_pairs_kernel,
        "sum_pairs",
        4 * block_inverses.size,
        2 * block_inverses.size,
        out_shape=jax.ShapeDtypeStruct(block_inverses.shape[1:], F32),
        in_specs=[IN_SMEM, ANYWHERE, pl.BlockSpec(block_inverses.shape, lambda: (0, 0, 0, 0))],
        out_specs=pl.BlockSpec(block_inverses.shape[1:], lambda: (0, 0, 0)),
    )(pole_coeffs, token, block_inverses)


def synthesise_kernel(
    slot, low, apart, more, partial, me_ref, sign_ref, here_ref, there_ref, own_ref, other_ref, table_ref, *rest
):
    rows, members, _ = own_ref.shape
    step = pl.program_id(0)
    if partial:
        partial_ref, rest = rest[0], rest[1:]
    if more:
        sums_out, mixed = rest
    elif apart:
        outs, mate_out, mixed, held, sems = rest[:-4], rest[-4], rest[-3], rest[-2], rest[-1]
    else:
        own_out, mate_out, mixed = rest

    @pl.when(step == 0)
    def _():
        count = own_ref.shape[2]
        for n in range(0, count, 128):
            lanes = slice(low + n, low + n + 128)
            lines = [
                here_ref[entry, slot : slot + 1, lanes] + there_ref[entry, slot : slot + 1, lanes]
                for entry in range(2 * rows * rows)
            ]
            lines[rows * rows :] = [sign_ref[0] * line for line in lines[rows * rows :]]
            for e in range(0, members, 32):
                part = (slice(e, e + 32), slice(n, n + 128))
                owns = [own_ref[(g,) + part].astype(F32) for g in range(rows)]
                others = [other_ref[(g,) + part].astype(F32) for g in range(rows)]
                for f in range(rows):
                    total = 0.0
                    for g in range(rows):
                        total = total + lines[f * rows + g] * owns[g]
                        total = total + lines[rows * rows + f * rows + g] * others[g]
                    mixed[f * members + e : f * members + e + 32, n : n + 128] = total.astype(BF16)

    sums = jnp.dot(mixed[...], table_ref[0], preferred_element_type=F32)
    if partial:
        sums = sums + partial_ref[...]
    if more:
        sums_out[...] = sums
        return
    lats = mate_out.shape[2]
    each = mate_out.shape[0]
    for r in range(rows):
        turned = sums[r * members : (r + 1) * members, :].astype(BF16).T
        values = [turned[i : i + lats] for i in range(0, turned.shape[0], lats)]
        mine, others = split_cores(values, me_ref[0] % CORES)
        for i, (a, b) in enumerate(zip(mine, others)):
            if apart:
                held[step * each + i, r] = a
            else:
                own_out[i, 0, r] = a
            mate_out[i, r] = b

    if apart:
        chip, core = me_ref[0] // CORES, me_ref[0] % CORES
        copies = []
        for i, (k, row, some) in enumerate(messages_of(held.shape[0], rows)):
            source = held.at[chip ^ k, pl.ds(row, some)]
            copies.append(pltpu.make_async_copy(source, outs[i].at[core], sems.at[i]))
            pl.when((chip ^ k) // each == step)(copies[-1].start)

        @pl.when(step == pl.num_programs(0) - 1)
        def _():
            for copy in copies:
                copy.wait()


def synthesise(here, there, sign, own, other, table, me, slot, low, lats, apart, more, partial):
    rows, members, count = own.shape
    nlat = table.shape[2]
    width = math.lcm(CORES * lats, 128)
    chips, each = nlat // lats // CORES, width // lats // CORES
    matrix = pl.BlockSpec(here.shape, lambda j, m: (0, 0, 0))
    whole = pl.BlockSpec((rows, members, count), lambda j, m: (0, 0, 0))
    smem = pl.BlockSpec(memory_space=pltpu.SMEM)
    shapes = [jax.ShapeDtypeStruct((chips, CORES, rows, lats, members), BF16)]

    def place(j):
        per = chips // len(PLANES) // each
        q = j // per
        return j if apart else jnp.where(q == 1, j + per, jnp.where(q == 2, j - per, j))

    specs = [pl.BlockSpec((each, 1, rows, lats, members), lambda j, m: (place(j), m[0] % CORES, 0, 0, 0))]
    scratch = [pltpu.VMEM((rows * members, count), BF16)]
    shapes += [jax.ShapeDtypeStruct((chips, rows, lats, members), BF16)]
    specs += [pl.BlockSpec((each, rows, lats, members), lambda j, m: (place(j), 0, 0, 0))]
    sums = pl.BlockSpec((rows * members, width), lambda j, m: (0, j))
    if more:
        shapes, specs = [jax.ShapeDtypeStruct((rows * members, nlat), F32)], [sums]
    elif apart:
        counts = [some for _, _, some in messages_of(chips, rows)]
        shapes[:1] = [jax.ShapeDtypeStruct((CORES, some, lats, members), BF16) for some in counts]
        specs[:1] = [ANYWHERE] * len(counts)
        scratch += [pltpu.VMEM((chips, rows, lats, members), BF16), pltpu.SemaphoreType.DMA((len(counts),))]
    return call(
        functools.partial(synthesise_kernel, slot, low, apart, more, len(partial)),
        "synthesise",
        2 * count * nlat * rows * members,
        2 * count * nlat,
        out_shape=shapes,
        grid_spec=pltpu.PrefetchScalarGridSpec(
            num_scalar_prefetch=1,
            grid=(nlat // width,),
            in_specs=[
                smem,
                matrix,
                matrix,
                whole,
                whole,
                pl.BlockSpec((1, count, width), lambda j, m: (slot, low // count, j)),
            ]
            + [sums] * len(partial),
            out_specs=specs,
            scratch_shapes=scratch,
        ),
    )(me, sign, here, there, own, other, table, *partial)


def assemble_kernel(far, moved, wanted, me_ref, blocks_ref, *rest):
    messages, out_ref, (held, done, in_sems, out_sems) = rest[: len(wanted)], rest[-5], rest[-4:]
    rows, lats, slots, members = done.shape
    first = wanted[0][1]
    half = held.shape[0]
    local_slots = slots // half // CORES
    chip = me_ref[0] // CORES
    side = chip // half if not far else 1 - chip // half
    each = out_sems.shape[1]
    size = lats // each
    depth, breadth = math.gcd(size, 16), 16
    copies = []
    for r in range(rows):
        copies.append([])
        for i, ((k, _, _), ref) in enumerate(zip(wanted, messages)):
            target = held.at[(chip ^ k) & (half - 1), :, r]
            copies[r].append(pltpu.make_async_copy(ref.at[:, r], target, in_sems.at[r, i]))
            copies[r][-1].start()
    matrix = swap_matrix(breadth, depth, 1, 0)
    results = []

    def tile(r, start, s):
        parts = []
        for i in range(s, s + breadth):
            owner, slot = divmod(i, local_slots)
            place = owner // CORES
            if slot == moved:
                parts.append(held[place, owner % CORES, r, start : start + depth, :])
            else:
                plane, rest = divmod(place, half // 2)
                there = (side + 2 * plane) * (half // 2) + rest
                parts.append(blocks_ref[there, owner % CORES, first + r, start : start + depth, :])
        return jnp.concatenate(parts, axis=0)

    for r in range(rows):
        for copy in copies[r]:
            copy.wait()
        for part in range(each):
            starts = range(part * size, (part + 1) * size, depth)
            tiles = [(start, s) for start in starts for s in range(0, slots, breadth)]
            for i in range(0, len(tiles), 2):
                both = tiles[i : i + 2]
                wide = jnp.concatenate([tile(r, *place) for place in both], axis=1)
                turned = jnp.dot(matrix, wide, preferred_element_type=F32).astype(BF16)
                for n, (start, s) in enumerate(both):
                    value = turned[:, n * members : (n + 1) * members].reshape(depth, breadth, members)
                    done[r, start : start + depth, s : s + breadth, :] = value
            lines = pl.ds(part * size, size)
            target = out_ref.at[first + r, lines, pl.ds(pl.multiple_of(side * slots, slots), slots)]
            results.append(pltpu.make_async_copy(done.at[r, lines], target, out_sems.at[r, part]))
            results[-1].start()
    for copy in results:
        copy.wait()


def assemble(blocks, messages, me, moved, local_slots, far, first, output):
    chips, _, rows, lats, members = blocks.shape
    half = chips // 2
    slots = local_slots * half * CORES
    parts = zip(messages_of(chips, rows), messages)
    parts = [(part, m) for part, m in parts if (part[0] >= half) == far and part[1] == first]
    wanted, used = [part for part, _ in parts], [m for _, m in parts]
    some = wanted[0][2]
    return call(
        functools.partial(assemble_kernel, far, moved, wanted),
        "assemble",
        2 * 256 * some * lats * slots * members,
        4 * some * lats * slots * members,
        out_shape=jax.ShapeDtypeStruct((rows, lats, 2 * slots, members), BF16),
        in_specs=[IN_SMEM, IN_VMEM] + [IN_HBM] * (len(used) + len(output)),
        out_specs=IN_HBM,
        scratch_shapes=[
            pltpu.VMEM((half, CORES, some, lats, members), BF16),
            pltpu.VMEM((some, lats, slots, members), BF16),
            pltpu.SemaphoreType.DMA((some, half)),
            pltpu.SemaphoreType.DMA((some, 1)),
        ],
        input_output_aliases={len(used) + 2: 0} if output else {},
    )(me, blocks, *used, *output)


def between_cores(blocks, owners):
    return lax.ppermute(blocks, "wave", [(d, d ^ 1) for d in range(owners)])


def by_permutes(messages, chips, rows):
    got = []
    for (k, _, _), message in zip(messages_of(chips, rows), messages):
        moves = [(d, d ^ (k * CORES)) for d in range(chips * CORES)]
        got.append(lax.ppermute(message, "wave", moves) if k else message)
    return got


def between_chips(blocks, owners):
    chips = owners // CORES
    groups = [[place_of(i, chips) * CORES + core for i in range(chips)] for core in range(CORES)]
    return lax.all_to_all(blocks, "wave", split_axis=0, concat_axis=0, axis_index_groups=groups, tiled=True)


def per_device(
    tendency, spectral_state, legendre, gauss_weights, block_inverses, pole_coeffs, wavenumbers
):
    rows, lats, slots, members = tendency.shape
    local_slots, nspec, nlat = legendre.shape
    owners = slots // local_slots
    me = lax.axis_index("wave").astype(jnp.int32).reshape(1)
    pole_index = lax.axis_index("pole")
    sign = (2 * pole_index - 1).astype(F32).reshape(1)
    order = list(range(local_slots))[::-1]
    received, waits = {}, []
    for slot in order:
        early = slot == order[0]
        *blocks, token = weigh(tendency, gauss_weights[None], me, slot, local_slots, not early, waits)
        if early:
            received[slot] = between_chips(blocks[0], owners)
            here = sum_pairs(block_inverses, pole_coeffs, token)
            there = lax.ppermute(here, "pole", [(0, 1), (1, 0)])
            waits = [there]
        else:
            blocks, token = pair(blocks[0], between_cores(blocks[1], owners), me)
            received[slot] = between_chips(blocks, owners)

    sent = {}
    for slot in order:
        half = nspec // 2
        lows = [half] if slot % 2 else [0, half]
        blocks = [received[slot]]
        if slot == order[0]:
            blocks.append(between_cores(pick(blocks[0], me, token), owners))
        forced = [analyse(blocks, legendre, spectral_state, wavenumbers, me, token, slot, low, half) for low in lows]
        others = [lax.ppermute(part, "pole", [(0, 1), (1, 0)]) for part in forced]
        last = slot == order[-1]
        own = []
        for low, part, other in zip(lows, forced, others):
            more = low != lows[-1]
            own = synthesise(here, there, sign, part, other, legendre, me, slot, low, lats, last, more, own)
        *own, for_mate = own
        mate = between_cores(for_mate, owners)
        if last:
            sent[slot] = by_permutes(pair_messages(own, mate, me), owners // CORES, rows)
        else:
            blocks, token = pair(own[0], mate, me)
            sent[slot] = [between_chips(blocks, owners)]
    blocks, messages = sent[order[0]][0], sent[order[-1]]
    output = []
    for far, first in ((False, 0), (True, 0), (True, rows - 1)):
        output = [assemble(blocks, messages, me, order[-1], local_slots, far, first, output)]
    return output[0]


def solution(mesh):
    in_specs = (
        P("pole", "wave", None, None),
        P("pole", "wave", None, None),
        P("wave", None, None),
        P("wave"),
        P("pole", None, "wave", None),
        P("pole", None),
        P("wave"),
    )
    out_specs = P("pole", "wave", None, None)
    return jax.shard_map(
        per_device, mesh=mesh, in_specs=in_specs, out_specs=out_specs, check_vma=False
    )
```

```python
import functools
import math

import jax
import jax.numpy as jnp
from jax import lax
from jax.experimental import pallas as pl
from jax.experimental.pallas import tpu as pltpu
from jax.sharding import PartitionSpec as P

BF16 = jnp.bfloat16
F32 = jnp.float32
CORES = 2
PLANES = (0, 1, 3, 2)
ANYWHERE = pl.BlockSpec(memory_space=pl.ANY)
IN_SMEM = pl.BlockSpec(memory_space=pltpu.SMEM)
IN_HBM = pl.BlockSpec(memory_space=pltpu.HBM)
IN_VMEM = pl.BlockSpec(memory_space=pltpu.VMEM)
TOKEN = jax.ShapeDtypeStruct((8, 128), F32)


def call(kernel, name, flops, size, mib=40, **kwargs):
    return pl.pallas_call(
        kernel,
        name=name,
        compiler_params=pltpu.CompilerParams(vmem_limit_bytes=mib * 1024 * 1024),
        cost_estimate=pl.CostEstimate(flops=int(flops), bytes_accessed=int(size), transcendentals=0),
        **kwargs,
    )


def in_hbm(array):
    return pltpu.with_memory_space_constraint(array, pltpu.HBM)


def run_copies(copies):
    for copy in copies:
        copy.start()
    for copy in copies:
        copy.wait()


def place_of(chip, chips):
    quarter = chips // len(PLANES)
    return PLANES[chip // quarter] * quarter + chip % quarter


def messages_of(chips, rows):
    near, far = range(1, chips // 2), range(chips // 2, chips)
    first = [(k, 0, rows - 1) for k in far]
    return [(0, 0, rows)] + first + [(k, rows - 1, 1) for k in far] + [(k, 0, rows) for k in near]


def split_cores(values, core):
    even = [values[i] for i in range(0, len(values), CORES)]
    odd = [values[i] for i in range(1, len(values), CORES)]
    mine = [jnp.where(core == 0, a, b) for a, b in zip(even, odd)]
    others = [jnp.where(core == 0, b, a) for a, b in zip(even, odd)]
    return mine, others


def swap_matrix(rows, columns, step, skip):
    shape = (rows * columns // step, rows * columns)
    shift = rows.bit_length() - 1
    target = lax.broadcasted_iota(jnp.int32, shape, 0)
    source = lax.broadcasted_iota(jnp.int32, shape, 1)
    wanted = (target & (rows - 1)) * columns + (target >> shift) * step + skip
    return jnp.where(source == wanted, 1.0, 0.0).astype(BF16)


def weigh_kernel(slot, local_slots, split, waits, me_ref, gauss_any, tendency_ref, *rest):
    outs, token_ref, (gauss_ref, column, held, done, gauss_sem, in_sems, out_sems) = rest[waits:-8], rest[-8], rest[-7:]
    line_copy = pltpu.make_async_copy(gauss_any, gauss_ref, gauss_sem)
    line_copy.start()
    rows, lats, slots, members = held.shape
    each = in_sems.shape[1]
    size = lats // each
    copies = []
    for r in range(rows):
        for i in range(each):
            part = pl.ds(i * size, size)
            copies.append(pltpu.make_async_copy(tendency_ref.at[r, part], held.at[r, part], in_sems.at[r, i]))
            copies[-1].start()
    token_ref[...] = jnp.zeros_like(token_ref)
    depth, breadth = math.gcd(size, 16), 16
    matrix = swap_matrix(depth, breadth, local_slots, slot)
    owners = breadth // local_slots
    core = me_ref[0] % CORES
    line_copy.wait()
    for j in range(0, lats, depth):
        line = jnp.broadcast_to(gauss_ref[...], (depth, lats))
        here = lax.broadcasted_iota(jnp.int32, line.shape, 0) + j
        mine = lax.broadcasted_iota(jnp.int32, line.shape, 1) == here
        value = jnp.sum(jnp.where(mine, line, 0.0), axis=1, keepdims=True)
        column[j : j + depth, :] = jnp.broadcast_to(value, (depth, members))
    results = []
    for r in range(rows):
        for j in range(0, lats, depth):
            if j % size == 0:
                copies[r * each + j // size].wait()
            scale = column[j : j + depth, :]
            for s in range(0, slots, 2 * breadth):
                halves = [
                    held[r, j : j + depth, s + h : s + h + breadth, :].reshape(depth * breadth, members)
                    for h in (0, breadth)
                ]
                turned = jnp.dot(matrix, jnp.concatenate(halves, axis=1), preferred_element_type=F32)
                values = [
                    turned[i * depth : (i + 1) * depth, h * members : (h + 1) * members] * scale
                    for h in range(2)
                    for i in range(owners)
                ]
                start = s // local_slots
                if split:
                    mine, others = split_cores(values, core)
                    for i, (a, b) in enumerate(zip(mine, others)):
                        place = place_of(start // CORES + i, done.shape[0])
                        done[place, 0, r, j : j + depth, :] = a.astype(BF16)
                        done[place, 1, r, j : j + depth, :] = b.astype(BF16)
                else:
                    for i, value in enumerate(values):
                        chip, target = divmod(start + i, CORES)
                        done[place_of(chip, done.shape[0]), target, r, j : j + depth, :] = value.astype(BF16)
            if (j + depth) % size == 0:
                part = pl.ds(j + depth - size, size)
                source, target = done.at[:, :, r, part], outs[0].at[:, :, r, part]
                if split:
                    source, target = done.at[:, 0, r, part], outs[0].at[:, core, r, part]
                    other = pltpu.make_async_copy(
                        done.at[:, 1, r, part], outs[1].at[:, r, part], out_sems.at[1, r, j // size]
                    )
                    other.start()
                    results.append(other)
                results.append(pltpu.make_async_copy(source, target, out_sems.at[0, r, j // size]))
                results[-1].start()
    for copy in results:
        copy.wait()


def weigh(tendency, gauss, me, slot, local_slots, split, waits):
    rows, lats, slots, members = tendency.shape
    each = 1
    chips = slots // local_slots // CORES
    shapes = [jax.ShapeDtypeStruct((chips, CORES, rows, lats, members), BF16)]
    if split:
        shapes += [jax.ShapeDtypeStruct((chips, rows, lats, members), BF16)]
    return call(
        functools.partial(weigh_kernel, slot, local_slots, split, len(waits)),
        "weigh",
        2 * 128 * tendency.size,
        3 * tendency.size,
        58,
        out_shape=shapes + [TOKEN],
        in_specs=[IN_SMEM] + [ANYWHERE] * (2 + len(waits)),
        out_specs=[ANYWHERE] * len(shapes) + [pl.BlockSpec(TOKEN.shape, lambda: (0, 0))],
        scratch_shapes=[
            pltpu.VMEM((1, lats), F32),
            pltpu.VMEM((lats, members), F32),
            pltpu.VMEM((rows, lats, slots, members), BF16),
            pltpu.VMEM((chips, CORES, rows, lats, members), BF16),
            pltpu.SemaphoreType.DMA,
            pltpu.SemaphoreType.DMA((rows, each)),
            pltpu.SemaphoreType.DMA((CORES, rows, each)),
        ],
    )(me, gauss, tendency, *waits)


def pick_kernel(me_ref, token_ref, in_ref, out_ref, held, in_sems, out_sems):
    other = CORES - 1 - me_ref[0] % CORES
    rows = held.shape[1]
    fetched = [pltpu.make_async_copy(in_ref.at[:, other, r], held.at[:, r], in_sems.at[r]) for r in range(rows)]
    stored = [pltpu.make_async_copy(held.at[:, r], out_ref.at[:, r], out_sems.at[r]) for r in range(rows)]
    for copy in fetched:
        copy.start()
    for fetch, store in zip(fetched, stored):
        fetch.wait()
        store.start()
    for copy in stored:
        copy.wait()


def pick(blocks, me, token):
    chips, _, rows, lats, members = blocks.shape
    shape = (chips, rows, lats, members)
    return call(
        pick_kernel,
        "pick",
        0,
        2 * blocks.size,
        out_shape=jax.ShapeDtypeStruct(shape, BF16),
        in_specs=[IN_SMEM, ANYWHERE, IN_HBM],
        out_specs=IN_HBM,
        scratch_shapes=[
            pltpu.VMEM(shape, BF16),
            pltpu.SemaphoreType.DMA((rows,)),
            pltpu.SemaphoreType.DMA((rows,)),
        ],
    )(me, token, in_hbm(blocks))


def pair_kernel(me_ref, mate_ref, blocks_ref, out_ref, token_ref, sem):
    token_ref[...] = jnp.zeros_like(token_ref)
    other = CORES - 1 - me_ref[0] % CORES
    run_copies([pltpu.make_async_copy(mate_ref, out_ref.at[:, other], sem)])


def pair(blocks, mate, me):
    return call(
        pair_kernel,
        "pair",
        0,
        4 * mate.size,
        out_shape=[jax.ShapeDtypeStruct(blocks.shape, blocks.dtype), TOKEN],
        in_specs=[IN_SMEM, pl.BlockSpec(mate.shape, lambda: (0, 0, 0, 0)), ANYWHERE],
        out_specs=[ANYWHERE, pl.BlockSpec(TOKEN.shape, lambda: (0, 0))],
        scratch_shapes=[pltpu.SemaphoreType.DMA],
        input_output_aliases={2: 0},
    )(me, mate, blocks)


def pair_messages_kernel(me_ref, mate_ref, *rest):
    outs, sems = rest[len(rest) // 2 : -1], rest[-1]
    chip, other = me_ref[0] // CORES, CORES - 1 - me_ref[0] % CORES
    copies = []
    for i, (k, row, rows) in enumerate(messages_of(*mate_ref.shape[:2])):
        source = mate_ref.at[chip ^ k, pl.ds(row, rows)]
        copies.append(pltpu.make_async_copy(source, outs[i].at[other], sems.at[i]))
    run_copies(copies)


def pair_messages(messages, mate, me):
    count = len(messages)
    return call(
        pair_messages_kernel,
        "pair",
        0,
        4 * mate.size,
        out_shape=[jax.ShapeDtypeStruct(m.shape, m.dtype) for m in messages],
        in_specs=[IN_SMEM, pl.BlockSpec(mate.shape, lambda: (0, 0, 0, 0))] + [ANYWHERE] * count,
        out_specs=[ANYWHERE] * count,
        scratch_shapes=[pltpu.SemaphoreType.DMA((count,))],
        input_output_aliases={i + 2: i for i in range(count)},
    )(me, mate, *messages)


def analyse_kernel(slot, low, me_ref, wave_ref, token_ref, table_ref, state_ref, *rest):
    blocks, out, (grid, table, state, table_sems, state_sem, block_sems) = rest[:-7], rest[-7], rest[-6:]
    rows, members, width = out.shape
    chips, cores, lats, _ = grid.shape
    core = me_ref[0] % CORES
    moves = []
    quarter = max(chips // len(PLANES), 1)
    for q in range(chips // quarter):
        here, there = pl.ds(q * quarter, quarter), pl.ds(place_of(q * quarter, chips) if chips > 1 else 0, quarter)
        for r in range(rows):
            lanes = pl.ds(r * members, members)
            if len(blocks) == 1:
                source, target = blocks[0].at[there, :, r], grid.at[here, :, :, lanes]
                moves.append(pltpu.make_async_copy(source, target, block_sems.at[0, r, q]))
            else:
                source, target = blocks[0].at[there, core, r], grid.at[here, core, :, lanes]
                moves.append(pltpu.make_async_copy(source, target, block_sems.at[0, r, q]))
                source, target = blocks[1].at[there, r], grid.at[here, CORES - 1 - core, :, lanes]
                moves.append(pltpu.make_async_copy(source, target, block_sems.at[1, r, q]))
    cuts = sorted(set([0] + list(range(width % 256, width + 1, 256))))
    copies = []
    for i, (start, end) in enumerate(zip(cuts, cuts[1:])):
        source = table_ref.at[slot, pl.ds(low + start, end - start)]
        copies.append(pltpu.make_async_copy(source, table.at[pl.ds(start, end - start)], table_sems.at[i]))
    state_copy = pltpu.make_async_copy(state_ref.at[:, slot, :, pl.ds(low, width)], state, state_sem)
    for move in moves + copies + [state_copy]:
        move.start()
    for move in moves:
        move.wait()
    field = grid[...].reshape(chips * cores * lats, rows * members)
    state_copy.wait()
    for copy, start, end in zip(copies, cuts, cuts[1:]):
        copy.wait()
        sums = jnp.dot(table[start:end], field, preferred_element_type=F32)
        degree = lax.broadcasted_iota(jnp.int32, (members, end - start), 1) + (low + start)
        live = degree >= wave_ref[slot]
        for r in range(rows):
            total = state[r, :, start:end].astype(F32) + sums[:, r * members : (r + 1) * members].T
            out[r, :, start:end] = jnp.where(live, total, 0.0).astype(BF16)


def analyse(blocks, table, state, wave, me, token, slot, low, width):
    chips, _, rows, lats, members = blocks[0].shape
    nlat = table.shape[2]
    cores = CORES
    if lats % 16:
        if len(blocks) > 1:
            core = me[0] % CORES
            own = lax.dynamic_index_in_dim(blocks[0], core, 1, keepdims=False)
            pairs = [jnp.where(core == 0, own, blocks[1]), jnp.where(core == 0, blocks[1], own)]
            blocks = [jnp.stack(pairs, axis=1)]
        quarter = chips // len(PLANES)
        laid = jnp.concatenate([blocks[0][q * quarter : (q + 1) * quarter] for q in PLANES])
        laid = jnp.transpose(laid, (2, 0, 1, 3, 4)).reshape(1, 1, rows, nlat, members)
        blocks, chips, cores, lats = [laid], 1, 1, nlat
    return call(
        functools.partial(analyse_kernel, slot, low),
        "analyse",
        2 * width * nlat * rows * members,
        2 * width * nlat,
        out_shape=jax.ShapeDtypeStruct((rows, members, width), BF16),
        grid_spec=pltpu.PrefetchScalarGridSpec(
            num_scalar_prefetch=1,
            grid=(1,),
            in_specs=[IN_SMEM, ANYWHERE] + [IN_HBM] * (2 + len(blocks)),
            out_specs=pl.BlockSpec((rows, members, width), lambda i, m: (0, 0, 0)),
            scratch_shapes=[
                pltpu.VMEM((chips, cores, lats, rows * members), BF16),
                pltpu.VMEM((width, nlat), BF16),
                pltpu.VMEM((rows, members, width), BF16),
                pltpu.SemaphoreType.DMA((width // 256 + 1,)),
                pltpu.SemaphoreType.DMA,
                pltpu.SemaphoreType.DMA((CORES, rows, len(PLANES))),
            ],
        ),
    )(me, wave, token, in_hbm(table), in_hbm(state), in_hbm(blocks[0]), *blocks[1:])


def sum_pairs_kernel(coeff_ref, token_ref, inverse_ref, out_ref):
    pairs, entries = inverse_ref.shape[:2]
    half = entries // 2

    def one(entry, carry):
        real = imag = 0.0
        for k in range(pairs):
            first, second = inverse_ref[k, entry].astype(F32), inverse_ref[k, half + entry].astype(F32)
            a, b = coeff_ref[k, 0], coeff_ref[k, 1]
            real = real + (a * first - b * second)
            imag = imag + (a * second + b * first)
        out_ref[entry] = real
        out_ref[half + entry] = imag
        return carry

    lax.fori_loop(0, half, one, 0)


def sum_pairs(block_inverses, pole_coeffs, token):
    return call(
        sum_pairs_kernel,
        "sum_pairs",
        4 * block_inverses.size,
        2 * block_inverses.size,
        out_shape=jax.ShapeDtypeStruct(block_inverses.shape[1:], F32),
        in_specs=[IN_SMEM, ANYWHERE, pl.BlockSpec(block_inverses.shape, lambda: (0, 0, 0, 0))],
        out_specs=pl.BlockSpec(block_inverses.shape[1:], lambda: (0, 0, 0)),
    )(pole_coeffs, token, block_inverses)


def synthesise_kernel(
    slot, low, apart, more, partial, me_ref, sign_ref, here_ref, there_ref, own_ref, other_ref, table_ref, *rest
):
    rows, members, _ = own_ref.shape
    step = pl.program_id(0)
    if partial:
        partial_ref, rest = rest[0], rest[1:]
    if more:
        sums_out, mixed = rest
    elif apart:
        outs, mate_out, mixed, held, sems = rest[:-4], rest[-4], rest[-3], rest[-2], rest[-1]
    else:
        own_out, mate_out, mixed = rest

    @pl.when(step == 0)
    def _():
        count = own_ref.shape[2]
        for n in range(0, count, 128):
            lanes = slice(low + n, low + n + 128)
            lines = [
                here_ref[entry, slot : slot + 1, lanes] + there_ref[entry, slot : slot + 1, lanes]
                for entry in range(2 * rows * rows)
            ]
            lines[rows * rows :] = [sign_ref[0] * line for line in lines[rows * rows :]]
            for e in range(0, members, 32):
                part = (slice(e, e + 32), slice(n, n + 128))
                owns = [own_ref[(g,) + part].astype(F32) for g in range(rows)]
                others = [other_ref[(g,) + part].astype(F32) for g in range(rows)]
                for f in range(rows):
                    total = 0.0
                    for g in range(rows):
                        total = total + lines[f * rows + g] * owns[g]
                        total = total + lines[rows * rows + f * rows + g] * others[g]
                    mixed[f * members + e : f * members + e + 32, n : n + 128] = total.astype(BF16)

    sums = jnp.dot(mixed[...], table_ref[0], preferred_element_type=F32)
    if partial:
        sums = sums + partial_ref[...]
    if more:
        sums_out[...] = sums
        return
    lats = mate_out.shape[2]
    each = mate_out.shape[0]
    for r in range(rows):
        turned = sums[r * members : (r + 1) * members, :].astype(BF16).T
        values = [turned[i : i + lats] for i in range(0, turned.shape[0], lats)]
        mine, others = split_cores(values, me_ref[0] % CORES)
        for i, (a, b) in enumerate(zip(mine, others)):
            if apart:
                held[step * each + i, r] = a
            else:
                own_out[i, 0, r] = a
            mate_out[i, r] = b

    if apart:
        chip, core = me_ref[0] // CORES, me_ref[0] % CORES
        copies = []
        for i, (k, row, some) in enumerate(messages_of(held.shape[0], rows)):
            source = held.at[chip ^ k, pl.ds(row, some)]
            copies.append(pltpu.make_async_copy(source, outs[i].at[core], sems.at[i]))
            pl.when((chip ^ k) // each == step)(copies[-1].start)

        @pl.when(step == pl.num_programs(0) - 1)
        def _():
            for copy in copies:
                copy.wait()


def synthesise(here, there, sign, own, other, table, me, slot, low, lats, apart, more, partial):
    rows, members, count = own.shape
    nlat = table.shape[2]
    width = math.lcm(CORES * lats, 128)
    chips, each = nlat // lats // CORES, width // lats // CORES
    matrix = pl.BlockSpec(here.shape, lambda j, m: (0, 0, 0))
    whole = pl.BlockSpec((rows, members, count), lambda j, m: (0, 0, 0))
    smem = pl.BlockSpec(memory_space=pltpu.SMEM)
    shapes = [jax.ShapeDtypeStruct((chips, CORES, rows, lats, members), BF16)]

    def place(j):
        per = chips // len(PLANES) // each
        q = j // per
        return j if apart else jnp.where(q == 2, j + per, jnp.where(q == 3, j - per, j))

    specs = [pl.BlockSpec((each, 1, rows, lats, members), lambda j, m: (place(j), m[0] % CORES, 0, 0, 0))]
    scratch = [pltpu.VMEM((rows * members, count), BF16)]
    shapes += [jax.ShapeDtypeStruct((chips, rows, lats, members), BF16)]
    specs += [pl.BlockSpec((each, rows, lats, members), lambda j, m: (place(j), 0, 0, 0))]
    sums = pl.BlockSpec((rows * members, width), lambda j, m: (0, j))
    if more:
        shapes, specs = [jax.ShapeDtypeStruct((rows * members, nlat), F32)], [sums]
    elif apart:
        counts = [some for _, _, some in messages_of(chips, rows)]
        shapes[:1] = [jax.ShapeDtypeStruct((CORES, some, lats, members), BF16) for some in counts]
        specs[:1] = [ANYWHERE] * len(counts)
        scratch += [pltpu.VMEM((chips, rows, lats, members), BF16), pltpu.SemaphoreType.DMA((len(counts),))]
    return call(
        functools.partial(synthesise_kernel, slot, low, apart, more, len(partial)),
        "synthesise",
        2 * count * nlat * rows * members,
        2 * count * nlat,
        out_shape=shapes,
        grid_spec=pltpu.PrefetchScalarGridSpec(
            num_scalar_prefetch=1,
            grid=(nlat // width,),
            in_specs=[
                smem,
                matrix,
                matrix,
                whole,
                whole,
                pl.BlockSpec((1, count, width), lambda j, m: (slot, low // count, j)),
            ]
            + [sums] * len(partial),
            out_specs=specs,
            scratch_shapes=scratch,
        ),
    )(me, sign, here, there, own, other, table, *partial)


def assemble_kernel(far, moved, wanted, me_ref, blocks_ref, *rest):
    messages, out_ref, (held, done, in_sems, out_sems) = rest[: len(wanted)], rest[-5], rest[-4:]
    rows, lats, slots, members = done.shape
    first = wanted[0][1]
    half = held.shape[0]
    local_slots = slots // half // CORES
    chip = me_ref[0] // CORES
    side = chip // half if not far else 1 - chip // half
    each = out_sems.shape[1]
    size = lats // each
    depth, breadth = math.gcd(size, 16), 16
    copies = []
    for r in range(rows):
        copies.append([])
        for i, ((k, _, _), ref) in enumerate(zip(wanted, messages)):
            target = held.at[(chip ^ k) & (half - 1), :, r]
            copies[r].append(pltpu.make_async_copy(ref.at[:, r], target, in_sems.at[r, i]))
            copies[r][-1].start()
    matrix = swap_matrix(breadth, depth, 1, 0)
    results = []

    def tile(r, start, s):
        parts = []
        for i in range(s, s + breadth):
            owner, slot = divmod(i, local_slots)
            place = owner // CORES
            if slot == moved:
                parts.append(held[place, owner % CORES, r, start : start + depth, :])
            else:
                plane, rest = divmod(place, half // 2)
                there = (2 * side + plane + side * (1 - 2 * plane)) * (half // 2) + rest
                parts.append(blocks_ref[there, owner % CORES, first + r, start : start + depth, :])
        return jnp.concatenate(parts, axis=0)

    for r in range(rows):
        for copy in copies[r]:
            copy.wait()
        for part in range(each):
            starts = range(part * size, (part + 1) * size, depth)
            tiles = [(start, s) for start in starts for s in range(0, slots, breadth)]
            for i in range(0, len(tiles), 2):
                both = tiles[i : i + 2]
                wide = jnp.concatenate([tile(r, *place) for place in both], axis=1)
                turned = jnp.dot(matrix, wide, preferred_element_type=F32).astype(BF16)
                for n, (start, s) in enumerate(both):
                    value = turned[:, n * members : (n + 1) * members].reshape(depth, breadth, members)
                    done[r, start : start + depth, s : s + breadth, :] = value
            lines = pl.ds(part * size, size)
            target = out_ref.at[first + r, lines, pl.ds(pl.multiple_of(side * slots, slots), slots)]
            results.append(pltpu.make_async_copy(done.at[r, lines], target, out_sems.at[r, part]))
            results[-1].start()
    for copy in results:
        copy.wait()


def assemble(blocks, messages, me, moved, local_slots, far, first, output):
    chips, _, rows, lats, members = blocks.shape
    half = chips // 2
    slots = local_slots * half * CORES
    parts = zip(messages_of(chips, rows), messages)
    parts = [(part, m) for part, m in parts if (part[0] >= half) == far and part[1] == first]
    wanted, used = [part for part, _ in parts], [m for _, m in parts]
    some = wanted[0][2]
    return call(
        functools.partial(assemble_kernel, far, moved, wanted),
        "assemble",
        2 * 256 * some * lats * slots * members,
        4 * some * lats * slots * members,
        out_shape=jax.ShapeDtypeStruct((rows, lats, 2 * slots, members), BF16),
        in_specs=[IN_SMEM, IN_VMEM] + [IN_HBM] * (len(used) + len(output)),
        out_specs=IN_HBM,
        scratch_shapes=[
            pltpu.VMEM((half, CORES, some, lats, members), BF16),
            pltpu.VMEM((some, lats, slots, members), BF16),
            pltpu.SemaphoreType.DMA((some, half)),
            pltpu.SemaphoreType.DMA((some, 1)),
        ],
        input_output_aliases={len(used) + 2: 0} if output else {},
    )(me, blocks, *used, *output)


def between_cores(blocks, owners):
    return lax.ppermute(blocks, "wave", [(d, d ^ 1) for d in range(owners)])


def by_permutes(messages, chips, rows):
    got = []
    for (k, _, _), message in zip(messages_of(chips, rows), messages):
        moves = [(d, d ^ (k * CORES)) for d in range(chips * CORES)]
        got.append(lax.ppermute(message, "wave", moves) if k else message)
    return got


def between_chips(blocks, owners):
    chips = owners // CORES
    groups = [[place_of(i, chips) * CORES + core for i in range(chips)] for core in range(CORES)]
    return lax.all_to_all(blocks, "wave", split_axis=0, concat_axis=0, axis_index_groups=groups, tiled=True)


def per_device(
    tendency, spectral_state, legendre, gauss_weights, block_inverses, pole_coeffs, wavenumbers
):
    rows, lats, slots, members = tendency.shape
    local_slots, nspec, nlat = legendre.shape
    owners = slots // local_slots
    me = lax.axis_index("wave").astype(jnp.int32).reshape(1)
    pole_index = lax.axis_index("pole")
    sign = (2 * pole_index - 1).astype(F32).reshape(1)
    order = list(range(local_slots))[::-1]
    received, waits = {}, []
    for slot in order:
        early = slot == order[0]
        *blocks, token = weigh(tendency, gauss_weights[None], me, slot, local_slots, not early, waits)
        if early:
            received[slot] = between_chips(blocks[0], owners)
            here = sum_pairs(block_inverses, pole_coeffs, token)
            there = lax.ppermute(here, "pole", [(0, 1), (1, 0)])
            waits = [there]
        else:
            blocks, token = pair(blocks[0], between_cores(blocks[1], owners), me)
            received[slot] = between_chips(blocks, owners)

    sent = {}
    for slot in order:
        half = nspec // 2
        lows = [half] if slot % 2 else [0, half]
        blocks = [received[slot]]
        if slot == order[0]:
            blocks.append(between_cores(pick(blocks[0], me, token), owners))
        forced = [analyse(blocks, legendre, spectral_state, wavenumbers, me, token, slot, low, half) for low in lows]
        others = [lax.ppermute(part, "pole", [(0, 1), (1, 0)]) for part in forced]
        last = slot == order[-1]
        own = []
        for low, part, other in zip(lows, forced, others):
            more = low != lows[-1]
            own = synthesise(here, there, sign, part, other, legendre, me, slot, low, lats, last, more, own)
        *own, for_mate = own
        mate = between_cores(for_mate, owners)
        if last:
            sent[slot] = by_permutes(pair_messages(own, mate, me), owners // CORES, rows)
        else:
            blocks, token = pair(own[0], mate, me)
            sent[slot] = [between_chips(blocks, owners)]
    blocks, messages = sent[order[0]][0], sent[order[-1]]
    output = []
    for far, first in ((False, 0), (True, 0), (True, rows - 1)):
        output = [assemble(blocks, messages, me, order[-1], local_slots, far, first, output)]
    return output[0]


def solution(mesh):
    in_specs = (
        P("pole", "wave", None, None),
        P("pole", "wave", None, None),
        P("wave", None, None),
        P("wave"),
        P("pole", None, "wave", None),
        P("pole", None),
        P("wave"),
    )
    out_specs = P("pole", "wave", None, None)
    return jax.shard_map(
        per_device, mesh=mesh, in_specs=in_specs, out_specs=out_specs, check_vma=False
    )
```

```python
import functools
import math

import jax
import jax.numpy as jnp
from jax import lax
from jax.experimental import pallas as pl
from jax.experimental.pallas import tpu as pltpu
from jax.sharding import PartitionSpec as P

BF16 = jnp.bfloat16
F32 = jnp.float32
CORES = 2
PLANES = (0, 1, 3, 2)
ANYWHERE = pl.BlockSpec(memory_space=pl.ANY)
IN_SMEM = pl.BlockSpec(memory_space=pltpu.SMEM)
IN_HBM = pl.BlockSpec(memory_space=pltpu.HBM)
IN_VMEM = pl.BlockSpec(memory_space=pltpu.VMEM)
TOKEN = jax.ShapeDtypeStruct((8, 128), F32)


def call(kernel, name, flops, size, mib=40, **kwargs):
    return pl.pallas_call(
        kernel,
        name=name,
        compiler_params=pltpu.CompilerParams(vmem_limit_bytes=mib * 1024 * 1024),
        cost_estimate=pl.CostEstimate(flops=int(flops), bytes_accessed=int(size), transcendentals=0),
        **kwargs,
    )


def in_hbm(array):
    return pltpu.with_memory_space_constraint(array, pltpu.HBM)


def run_copies(copies):
    for copy in copies:
        copy.start()
    for copy in copies:
        copy.wait()


def place_of(chip, chips):
    quarter = chips // len(PLANES)
    return PLANES[chip // quarter] * quarter + chip % quarter


def messages_of(chips, rows):
    near, far = range(1, chips // 2), range(chips - 1, chips // 2 - 1, -1)
    first = [(k, 0, rows - 1) for k in far]
    return [(0, 0, rows)] + first + [(k, rows - 1, 1) for k in far] + [(k, 0, rows) for k in near]


def split_cores(values, core):
    even = [values[i] for i in range(0, len(values), CORES)]
    odd = [values[i] for i in range(1, len(values), CORES)]
    mine = [jnp.where(core == 0, a, b) for a, b in zip(even, odd)]
    others = [jnp.where(core == 0, b, a) for a, b in zip(even, odd)]
    return mine, others


def swap_matrix(rows, columns, step, skip):
    shape = (rows * columns // step, rows * columns)
    shift = rows.bit_length() - 1
    target = lax.broadcasted_iota(jnp.int32, shape, 0)
    source = lax.broadcasted_iota(jnp.int32, shape, 1)
    wanted = (target & (rows - 1)) * columns + (target >> shift) * step + skip
    return jnp.where(source == wanted, 1.0, 0.0).astype(BF16)


def weigh_kernel(slot, local_slots, split, waits, me_ref, gauss_any, tendency_ref, *rest):
    outs, token_ref, (gauss_ref, column, held, done, gauss_sem, in_sems, out_sems) = rest[waits:-8], rest[-8], rest[-7:]
    line_copy = pltpu.make_async_copy(gauss_any, gauss_ref, gauss_sem)
    line_copy.start()
    rows, lats, slots, members = held.shape
    each = in_sems.shape[1]
    size = lats // each
    copies = []
    for r in range(rows):
        for i in range(each):
            part = pl.ds(i * size, size)
            copies.append(pltpu.make_async_copy(tendency_ref.at[r, part], held.at[r, part], in_sems.at[r, i]))
            copies[-1].start()
    token_ref[...] = jnp.zeros_like(token_ref)
    depth, breadth = math.gcd(size, 16), 16
    matrix = swap_matrix(depth, breadth, local_slots, slot)
    owners = breadth // local_slots
    core = me_ref[0] % CORES
    line_copy.wait()
    for j in range(0, lats, depth):
        line = jnp.broadcast_to(gauss_ref[...], (depth, lats))
        here = lax.broadcasted_iota(jnp.int32, line.shape, 0) + j
        mine = lax.broadcasted_iota(jnp.int32, line.shape, 1) == here
        value = jnp.sum(jnp.where(mine, line, 0.0), axis=1, keepdims=True)
        column[j : j + depth, :] = jnp.broadcast_to(value, (depth, members))
    results = []
    for r in range(rows):
        for j in range(0, lats, depth):
            if j % size == 0:
                copies[r * each + j // size].wait()
            scale = column[j : j + depth, :]
            for s in range(0, slots, 2 * breadth):
                halves = [
                    held[r, j : j + depth, s + h : s + h + breadth, :].reshape(depth * breadth, members)
                    for h in (0, breadth)
                ]
                turned = jnp.dot(matrix, jnp.concatenate(halves, axis=1), preferred_element_type=F32)
                values = [
                    turned[i * depth : (i + 1) * depth, h * members : (h + 1) * members] * scale
                    for h in range(2)
                    for i in range(owners)
                ]
                start = s // local_slots
                if split:
                    mine, others = split_cores(values, core)
                    for i, (a, b) in enumerate(zip(mine, others)):
                        place = place_of(start // CORES + i, done.shape[0])
                        done[place, 0, r, j : j + depth, :] = a.astype(BF16)
                        done[place, 1, r, j : j + depth, :] = b.astype(BF16)
                else:
                    for i, value in enumerate(values):
                        chip, target = divmod(start + i, CORES)
                        done[place_of(chip, done.shape[0]), target, r, j : j + depth, :] = value.astype(BF16)
            if (j + depth) % size == 0:
                part = pl.ds(j + depth - size, size)
                source, target = done.at[:, :, r, part], outs[0].at[:, :, r, part]
                if split:
                    source, target = done.at[:, 0, r, part], outs[0].at[:, core, r, part]
                    other = pltpu.make_async_copy(
                        done.at[:, 1, r, part], outs[1].at[:, r, part], out_sems.at[1, r, j // size]
                    )
                    other.start()
                    results.append(other)
                results.append(pltpu.make_async_copy(source, target, out_sems.at[0, r, j // size]))
                results[-1].start()
    for copy in results:
        copy.wait()


def weigh(tendency, gauss, me, slot, local_slots, split, waits):
    rows, lats, slots, members = tendency.shape
    each = 1
    chips = slots // local_slots // CORES
    shapes = [jax.ShapeDtypeStruct((chips, CORES, rows, lats, members), BF16)]
    if split:
        shapes += [jax.ShapeDtypeStruct((chips, rows, lats, members), BF16)]
    return call(
        functools.partial(weigh_kernel, slot, local_slots, split, len(waits)),
        "weigh",
        2 * 128 * tendency.size,
        3 * tendency.size,
        58,
        out_shape=shapes + [TOKEN],
        in_specs=[IN_SMEM] + [ANYWHERE] * (2 + len(waits)),
        out_specs=[ANYWHERE] * len(shapes) + [pl.BlockSpec(TOKEN.shape, lambda: (0, 0))],
        scratch_shapes=[
            pltpu.VMEM((1, lats), F32),
            pltpu.VMEM((lats, members), F32),
            pltpu.VMEM((rows, lats, slots, members), BF16),
            pltpu.VMEM((chips, CORES, rows, lats, members), BF16),
            pltpu.SemaphoreType.DMA,
            pltpu.SemaphoreType.DMA((rows, each)),
            pltpu.SemaphoreType.DMA((CORES, rows, each)),
        ],
    )(me, gauss, tendency, *waits)


def pick_kernel(me_ref, token_ref, in_ref, out_ref, held, in_sems, out_sems):
    other = CORES - 1 - me_ref[0] % CORES
    rows = held.shape[1]
    fetched = [pltpu.make_async_copy(in_ref.at[:, other, r], held.at[:, r], in_sems.at[r]) for r in range(rows)]
    stored = [pltpu.make_async_copy(held.at[:, r], out_ref.at[:, r], out_sems.at[r]) for r in range(rows)]
    for copy in fetched:
        copy.start()
    for fetch, store in zip(fetched, stored):
        fetch.wait()
        store.start()
    for copy in stored:
        copy.wait()


def pick(blocks, me, token):
    chips, _, rows, lats, members = blocks.shape
    shape = (chips, rows, lats, members)
    return call(
        pick_kernel,
        "pick",
        0,
        2 * blocks.size,
        out_shape=jax.ShapeDtypeStruct(shape, BF16),
        in_specs=[IN_SMEM, ANYWHERE, IN_HBM],
        out_specs=IN_HBM,
        scratch_shapes=[
            pltpu.VMEM(shape, BF16),
            pltpu.SemaphoreType.DMA((rows,)),
            pltpu.SemaphoreType.DMA((rows,)),
        ],
    )(me, token, in_hbm(blocks))


def pair_kernel(me_ref, mate_ref, blocks_ref, out_ref, token_ref, sem):
    token_ref[...] = jnp.zeros_like(token_ref)
    other = CORES - 1 - me_ref[0] % CORES
    run_copies([pltpu.make_async_copy(mate_ref, out_ref.at[:, other], sem)])


def pair(blocks, mate, me):
    return call(
        pair_kernel,
        "pair",
        0,
        4 * mate.size,
        out_shape=[jax.ShapeDtypeStruct(blocks.shape, blocks.dtype), TOKEN],
        in_specs=[IN_SMEM, pl.BlockSpec(mate.shape, lambda: (0, 0, 0, 0)), ANYWHERE],
        out_specs=[ANYWHERE, pl.BlockSpec(TOKEN.shape, lambda: (0, 0))],
        scratch_shapes=[pltpu.SemaphoreType.DMA],
        input_output_aliases={2: 0},
    )(me, mate, blocks)


def pair_messages_kernel(me_ref, mate_ref, *rest):
    outs, sems = rest[len(rest) // 2 : -1], rest[-1]
    chip, other = me_ref[0] // CORES, CORES - 1 - me_ref[0] % CORES
    copies = []
    for i, (k, row, rows) in enumerate(messages_of(*mate_ref.shape[:2])):
        source = mate_ref.at[chip ^ k, pl.ds(row, rows)]
        copies.append(pltpu.make_async_copy(source, outs[i].at[other], sems.at[i]))
    run_copies(copies)


def pair_messages(messages, mate, me):
    count = len(messages)
    return call(
        pair_messages_kernel,
        "pair",
        0,
        4 * mate.size,
        out_shape=[jax.ShapeDtypeStruct(m.shape, m.dtype) for m in messages],
        in_specs=[IN_SMEM, pl.BlockSpec(mate.shape, lambda: (0, 0, 0, 0))] + [ANYWHERE] * count,
        out_specs=[ANYWHERE] * count,
        scratch_shapes=[pltpu.SemaphoreType.DMA((count,))],
        input_output_aliases={i + 2: i for i in range(count)},
    )(me, mate, *messages)


def analyse_kernel(slot, low, me_ref, wave_ref, token_ref, table_ref, state_ref, *rest):
    blocks, out, (grid, table, state, table_sems, state_sem, block_sems) = rest[:-7], rest[-7], rest[-6:]
    rows, members, width = out.shape
    chips, cores, lats, _ = grid.shape
    core = me_ref[0] % CORES
    moves = []
    quarter = max(chips // len(PLANES), 1)
    for q in range(chips // quarter):
        here, there = pl.ds(q * quarter, quarter), pl.ds(place_of(q * quarter, chips) if chips > 1 else 0, quarter)
        for r in range(rows):
            lanes = pl.ds(r * members, members)
            if len(blocks) == 1:
                source, target = blocks[0].at[there, :, r], grid.at[here, :, :, lanes]
                moves.append(pltpu.make_async_copy(source, target, block_sems.at[0, r, q]))
            else:
                source, target = blocks[0].at[there, core, r], grid.at[here, core, :, lanes]
                moves.append(pltpu.make_async_copy(source, target, block_sems.at[0, r, q]))
                source, target = blocks[1].at[there, r], grid.at[here, CORES - 1 - core, :, lanes]
                moves.append(pltpu.make_async_copy(source, target, block_sems.at[1, r, q]))
    cuts = sorted(set([0] + list(range(width % 256, width + 1, 256))))
    copies = []
    for i, (start, end) in enumerate(zip(cuts, cuts[1:])):
        source = table_ref.at[slot, pl.ds(low + start, end - start)]
        copies.append(pltpu.make_async_copy(source, table.at[pl.ds(start, end - start)], table_sems.at[i]))
    state_copy = pltpu.make_async_copy(state_ref.at[:, slot, :, pl.ds(low, width)], state, state_sem)
    for move in moves + copies + [state_copy]:
        move.start()
    for move in moves:
        move.wait()
    field = grid[...].reshape(chips * cores * lats, rows * members)
    state_copy.wait()
    for copy, start, end in zip(copies, cuts, cuts[1:]):
        copy.wait()
        sums = jnp.dot(table[start:end], field, preferred_element_type=F32)
        degree = lax.broadcasted_iota(jnp.int32, (members, end - start), 1) + (low + start)
        live = degree >= wave_ref[slot]
        for r in range(rows):
            total = state[r, :, start:end].astype(F32) + sums[:, r * members : (r + 1) * members].T
            out[r, :, start:end] = jnp.where(live, total, 0.0).astype(BF16)


def analyse(blocks, table, state, wave, me, token, slot, low, width):
    chips, _, rows, lats, members = blocks[0].shape
    nlat = table.shape[2]
    cores = CORES
    if lats % 16:
        if len(blocks) > 1:
            core = me[0] % CORES
            own = lax.dynamic_index_in_dim(blocks[0], core, 1, keepdims=False)
            pairs = [jnp.where(core == 0, own, blocks[1]), jnp.where(core == 0, blocks[1], own)]
            blocks = [jnp.stack(pairs, axis=1)]
        quarter = chips // len(PLANES)
        laid = jnp.concatenate([blocks[0][q * quarter : (q + 1) * quarter] for q in PLANES])
        laid = jnp.transpose(laid, (2, 0, 1, 3, 4)).reshape(1, 1, rows, nlat, members)
        blocks, chips, cores, lats = [laid], 1, 1, nlat
    return call(
        functools.partial(analyse_kernel, slot, low),
        "analyse",
        2 * width * nlat * rows * members,
        2 * width * nlat,
        out_shape=jax.ShapeDtypeStruct((rows, members, width), BF16),
        grid_spec=pltpu.PrefetchScalarGridSpec(
            num_scalar_prefetch=1,
            grid=(1,),
            in_specs=[IN_SMEM, ANYWHERE] + [IN_HBM] * (2 + len(blocks)),
            out_specs=pl.BlockSpec((rows, members, width), lambda i, m: (0, 0, 0)),
            scratch_shapes=[
                pltpu.VMEM((chips, cores, lats, rows * members), BF16),
                pltpu.VMEM((width, nlat), BF16),
                pltpu.VMEM((rows, members, width), BF16),
                pltpu.SemaphoreType.DMA((width // 256 + 1,)),
                pltpu.SemaphoreType.DMA,
                pltpu.SemaphoreType.DMA((CORES, rows, len(PLANES))),
            ],
        ),
    )(me, wave, token, in_hbm(table), in_hbm(state), in_hbm(blocks[0]), *blocks[1:])


def sum_pairs_kernel(coeff_ref, token_ref, inverse_ref, out_ref):
    pairs, entries = inverse_ref.shape[:2]
    half = entries // 2

    def one(entry, carry):
        real = imag = 0.0
        for k in range(pairs):
            first, second = inverse_ref[k, entry].astype(F32), inverse_ref[k, half + entry].astype(F32)
            a, b = coeff_ref[k, 0], coeff_ref[k, 1]
            real = real + (a * first - b * second)
            imag = imag + (a * second + b * first)
        out_ref[entry] = real
        out_ref[half + entry] = imag
        return carry

    lax.fori_loop(0, half, one, 0)


def sum_pairs(block_inverses, pole_coeffs, token):
    return call(
        sum_pairs_kernel,
        "sum_pairs",
        4 * block_inverses.size,
        2 * block_inverses.size,
        out_shape=jax.ShapeDtypeStruct(block_inverses.shape[1:], F32),
        in_specs=[IN_SMEM, ANYWHERE, pl.BlockSpec(block_inverses.shape, lambda: (0, 0, 0, 0))],
        out_specs=pl.BlockSpec(block_inverses.shape[1:], lambda: (0, 0, 0)),
    )(pole_coeffs, token, block_inverses)


def synthesise_kernel(
    slot, low, apart, more, partial, me_ref, sign_ref, here_ref, there_ref, own_ref, other_ref, table_ref, *rest
):
    rows, members, _ = own_ref.shape
    step = pl.program_id(0)
    if partial:
        partial_ref, rest = rest[0], rest[1:]
    if more:
        sums_out, mixed = rest
    elif apart:
        outs, mate_out, mixed, held, sems = rest[:-4], rest[-4], rest[-3], rest[-2], rest[-1]
    else:
        own_out, mate_out, mixed = rest

    @pl.when(step == 0)
    def _():
        count = own_ref.shape[2]
        for n in range(0, count, 128):
            lanes = slice(low + n, low + n + 128)
            lines = [
                here_ref[entry, slot : slot + 1, lanes] + there_ref[entry, slot : slot + 1, lanes]
                for entry in range(2 * rows * rows)
            ]
            lines[rows * rows :] = [sign_ref[0] * line for line in lines[rows * rows :]]
            for e in range(0, members, 32):
                part = (slice(e, e + 32), slice(n, n + 128))
                owns = [own_ref[(g,) + part].astype(F32) for g in range(rows)]
                others = [other_ref[(g,) + part].astype(F32) for g in range(rows)]
                for f in range(rows):
                    total = 0.0
                    for g in range(rows):
                        total = total + lines[f * rows + g] * owns[g]
                        total = total + lines[rows * rows + f * rows + g] * others[g]
                    mixed[f * members + e : f * members + e + 32, n : n + 128] = total.astype(BF16)

    sums = jnp.dot(mixed[...], table_ref[0], preferred_element_type=F32)
    if partial:
        sums = sums + partial_ref[...]
    if more:
        sums_out[...] = sums
        return
    lats = mate_out.shape[2]
    each = mate_out.shape[0]
    for r in range(rows):
        turned = sums[r * members : (r + 1) * members, :].astype(BF16).T
        values = [turned[i : i + lats] for i in range(0, turned.shape[0], lats)]
        mine, others = split_cores(values, me_ref[0] % CORES)
        for i, (a, b) in enumerate(zip(mine, others)):
            if apart:
                held[step * each + i, r] = a
            else:
                own_out[i, 0, r] = a
            mate_out[i, r] = b

    if apart:
        chip, core = me_ref[0] // CORES, me_ref[0] % CORES
        copies = []
        for i, (k, row, some) in enumerate(messages_of(held.shape[0], rows)):
            source = held.at[chip ^ k, pl.ds(row, some)]
            copies.append(pltpu.make_async_copy(source, outs[i].at[core], sems.at[i]))
            pl.when((chip ^ k) // each == step)(copies[-1].start)

        @pl.when(step == pl.num_programs(0) - 1)
        def _():
            for copy in copies:
                copy.wait()


def synthesise(here, there, sign, own, other, table, me, slot, low, lats, apart, more, partial):
    rows, members, count = own.shape
    nlat = table.shape[2]
    width = math.lcm(CORES * lats, 128)
    chips, each = nlat // lats // CORES, width // lats // CORES
    matrix = pl.BlockSpec(here.shape, lambda j, m: (0, 0, 0))
    whole = pl.BlockSpec((rows, members, count), lambda j, m: (0, 0, 0))
    smem = pl.BlockSpec(memory_space=pltpu.SMEM)
    shapes = [jax.ShapeDtypeStruct((chips, CORES, rows, lats, members), BF16)]

    def place(j):
        per = chips // len(PLANES) // each
        q = j // per
        return j if apart else jnp.where(q == 2, j + per, jnp.where(q == 3, j - per, j))

    specs = [pl.BlockSpec((each, 1, rows, lats, members), lambda j, m: (place(j), m[0] % CORES, 0, 0, 0))]
    scratch = [pltpu.VMEM((rows * members, count), BF16)]
    shapes += [jax.ShapeDtypeStruct((chips, rows, lats, members), BF16)]
    specs += [pl.BlockSpec((each, rows, lats, members), lambda j, m: (place(j), 0, 0, 0))]
    sums = pl.BlockSpec((rows * members, width), lambda j, m: (0, j))
    if more:
        shapes, specs = [jax.ShapeDtypeStruct((rows * members, nlat), F32)], [sums]
    elif apart:
        counts = [some for _, _, some in messages_of(chips, rows)]
        shapes[:1] = [jax.ShapeDtypeStruct((CORES, some, lats, members), BF16) for some in counts]
        specs[:1] = [ANYWHERE] * len(counts)
        scratch += [pltpu.VMEM((chips, rows, lats, members), BF16), pltpu.SemaphoreType.DMA((len(counts),))]
    return call(
        functools.partial(synthesise_kernel, slot, low, apart, more, len(partial)),
        "synthesise",
        2 * count * nlat * rows * members,
        2 * count * nlat,
        out_shape=shapes,
        grid_spec=pltpu.PrefetchScalarGridSpec(
            num_scalar_prefetch=1,
            grid=(nlat // width,),
            in_specs=[
                smem,
                matrix,
                matrix,
                whole,
                whole,
                pl.BlockSpec((1, count, width), lambda j, m: (slot, low // count, j)),
            ]
            + [sums] * len(partial),
            out_specs=specs,
            scratch_shapes=scratch,
        ),
    )(me, sign, here, there, own, other, table, *partial)


def assemble_kernel(far, moved, wanted, me_ref, blocks_ref, *rest):
    messages, out_ref, (held, done, in_sems, out_sems) = rest[: len(wanted)], rest[-5], rest[-4:]
    rows, lats, slots, members = done.shape
    first = wanted[0][1]
    half = held.shape[0]
    local_slots = slots // half // CORES
    chip = me_ref[0] // CORES
    side = chip // half if not far else 1 - chip // half
    each = out_sems.shape[1]
    size = lats // each
    depth, breadth = math.gcd(size, 16), 16
    copies = []
    for r in range(rows):
        copies.append([])
        for i, ((k, _, _), ref) in enumerate(zip(wanted, messages)):
            target = held.at[(chip ^ k) & (half - 1), :, r]
            copies[r].append(pltpu.make_async_copy(ref.at[:, r], target, in_sems.at[r, i]))
            copies[r][-1].start()
    matrix = swap_matrix(breadth, depth, 1, 0)
    results = []

    def tile(r, start, s):
        parts = []
        for i in range(s, s + breadth):
            owner, slot = divmod(i, local_slots)
            place = owner // CORES
            if slot == moved:
                parts.append(held[place, owner % CORES, r, start : start + depth, :])
            else:
                plane, rest = divmod(place, half // 2)
                there = (2 * side + plane + side * (1 - 2 * plane)) * (half // 2) + rest
                parts.append(blocks_ref[there, owner % CORES, first + r, start : start + depth, :])
        return jnp.concatenate(parts, axis=0)

    for r in range(rows):
        for copy in copies[r]:
            copy.wait()
        for part in range(each):
            starts = range(part * size, (part + 1) * size, depth)
            tiles = [(start, s) for start in starts for s in range(0, slots, breadth)]
            for i in range(0, len(tiles), 2):
                both = tiles[i : i + 2]
                wide = jnp.concatenate([tile(r, *place) for place in both], axis=1)
                turned = jnp.dot(matrix, wide, preferred_element_type=F32).astype(BF16)
                for n, (start, s) in enumerate(both):
                    value = turned[:, n * members : (n + 1) * members].reshape(depth, breadth, members)
                    done[r, start : start + depth, s : s + breadth, :] = value
            lines = pl.ds(part * size, size)
            target = out_ref.at[first + r, lines, pl.ds(pl.multiple_of(side * slots, slots), slots)]
            results.append(pltpu.make_async_copy(done.at[r, lines], target, out_sems.at[r, part]))
            results[-1].start()
    for copy in results:
        copy.wait()


def assemble(blocks, messages, me, moved, local_slots, far, first, output):
    chips, _, rows, lats, members = blocks.shape
    half = chips // 2
    slots = local_slots * half * CORES
    parts = zip(messages_of(chips, rows), messages)
    parts = [(part, m) for part, m in parts if (part[0] >= half) == far and part[1] == first]
    wanted, used = [part for part, _ in parts], [m for _, m in parts]
    some = wanted[0][2]
    return call(
        functools.partial(assemble_kernel, far, moved, wanted),
        "assemble",
        2 * 256 * some * lats * slots * members,
        4 * some * lats * slots * members,
        out_shape=jax.ShapeDtypeStruct((rows, lats, 2 * slots, members), BF16),
        in_specs=[IN_SMEM, IN_VMEM] + [IN_HBM] * (len(used) + len(output)),
        out_specs=IN_HBM,
        scratch_shapes=[
            pltpu.VMEM((half, CORES, some, lats, members), BF16),
            pltpu.VMEM((some, lats, slots, members), BF16),
            pltpu.SemaphoreType.DMA((some, half)),
            pltpu.SemaphoreType.DMA((some, 1)),
        ],
        input_output_aliases={len(used) + 2: 0} if output else {},
    )(me, blocks, *used, *output)


def between_cores(blocks, owners):
    return lax.ppermute(blocks, "wave", [(d, d ^ 1) for d in range(owners)])


def by_permutes(messages, chips, rows):
    got = []
    for (k, _, _), message in zip(messages_of(chips, rows), messages):
        moves = [(d, d ^ (k * CORES)) for d in range(chips * CORES)]
        got.append(lax.ppermute(message, "wave", moves) if k else message)
    return got


def between_chips(blocks, owners):
    chips = owners // CORES
    groups = [[place_of(i, chips) * CORES + core for i in range(chips)] for core in range(CORES)]
    return lax.all_to_all(blocks, "wave", split_axis=0, concat_axis=0, axis_index_groups=groups, tiled=True)


def per_device(
    tendency, spectral_state, legendre, gauss_weights, block_inverses, pole_coeffs, wavenumbers
):
    rows, lats, slots, members = tendency.shape
    local_slots, nspec, nlat = legendre.shape
    owners = slots // local_slots
    me = lax.axis_index("wave").astype(jnp.int32).reshape(1)
    pole_index = lax.axis_index("pole")
    sign = (2 * pole_index - 1).astype(F32).reshape(1)
    order = list(range(local_slots))[::-1]
    received, waits = {}, []
    for slot in order:
        early = slot == order[0]
        *blocks, token = weigh(tendency, gauss_weights[None], me, slot, local_slots, not early, waits)
        if early:
            received[slot] = between_chips(blocks[0], owners)
            here = sum_pairs(block_inverses, pole_coeffs, token)
            there = lax.ppermute(here, "pole", [(0, 1), (1, 0)])
            waits = [there]
        else:
            blocks, token = pair(blocks[0], between_cores(blocks[1], owners), me)
            received[slot] = between_chips(blocks, owners)

    sent = {}
    for slot in order:
        half = nspec // 2
        lows = [half] if slot % 2 else [0, half]
        blocks = [received[slot]]
        if slot == order[0]:
            blocks.append(between_cores(pick(blocks[0], me, token), owners))
        forced = [analyse(blocks, legendre, spectral_state, wavenumbers, me, token, slot, low, half) for low in lows]
        others = [lax.ppermute(part, "pole", [(0, 1), (1, 0)]) for part in forced]
        last = slot == order[-1]
        own = []
        for low, part, other in zip(lows, forced, others):
            more = low != lows[-1]
            own = synthesise(here, there, sign, part, other, legendre, me, slot, low, lats, last, more, own)
        *own, for_mate = own
        mate = between_cores(for_mate, owners)
        if last:
            sent[slot] = by_permutes(pair_messages(own, mate, me), owners // CORES, rows)
        else:
            blocks, token = pair(own[0], mate, me)
            sent[slot] = [between_chips(blocks, owners)]
    blocks, messages = sent[order[0]][0], sent[order[-1]]
    output = []
    for far, first in ((False, 0), (True, 0), (True, rows - 1)):
        output = [assemble(blocks, messages, me, order[-1], local_slots, far, first, output)]
    return output[0]


def solution(mesh):
    in_specs = (
        P("pole", "wave", None, None),
        P("pole", "wave", None, None),
        P("wave", None, None),
        P("wave"),
        P("pole", None, "wave", None),
        P("pole", None),
        P("wave"),
    )
    out_specs = P("pole", "wave", None, None)
    return jax.shard_map(
        per_device, mesh=mesh, in_specs=in_specs, out_specs=out_specs, check_vma=False
    )
```
